32 devices in a mesh: dp: 16 (over z, y, x), fsdp: 2 (over core).
Axes of the slice: x: 2, y: 2, z: 4, core: 2. Of those that a mesh axis runs over, the one named last changes fastest.
Arguments:
- acts: bfloat16 [64, 128, 768], P(('dp', 'fsdp')), may hold values from -6 to 6
- cotangent: bfloat16 [64, 128, 768], P(('dp', 'fsdp')), may hold values from -6 to 6
- mask: int32 [64, 512], P(('dp', 'fsdp')), may hold values from 0 to 1, as said below
- shape_id: int32 [64], P(('dp', 'fsdp')), may hold values from 0 to 1
- weights: float32 [32, 221609], P(('dp', 'fsdp'))
- momenta: float32 [32, 221609], P(('dp', 'fsdp'))
- averages: float32 [32, 221609], P(('dp', 'fsdp'))
Outputs:
- activations: bfloat16 [64, 128, 768], P(('dp', 'fsdp'))
- input_grad: float32 [64, 128, 768], P(('dp', 'fsdp'))
- momenta_new: float32 [32, 221609], P(('dp', 'fsdp'))
- averages_new: float32 [32, 221609], P(('dp', 'fsdp'))
- weights_new: float32 [32, 221609], P(('dp', 'fsdp'))
- weights_copy: bfloat16 [32, 221609], P(('dp', 'fsdp'))
The draws below stay inside these ranges and needn't reach their ends.
Inputs may be any that keep to these rules, and one draw needn't show every extreme that they name: `mask`: each clip's row has 64 to 128 ones, and some clip has exactly 128. `shape_id`: 0 marks a grid of 8 bands, 1 a grid of 4 bands.
All inputs are finite; a program needn't handle non-finite values.
Results may differ from the reference program's by a relative error of at most 0.012.
Values may be sent and summed in bfloat16 or wider, within the bound.
No kernel may reach another device: no remote copies, remote signals or barrier semaphores. Data moves between devices by JAX's collectives and lax.ppermute only.
A program may use at most 192 MiB of HBM per device.

```python
import math
import jax
import jax.numpy as jnp
import numpy as np
from jax import lax

D = 768
H = 12
HD = 64
FF = 3072
NB = 320
P_SIZE = 512
CAP = 128
SHARDS = 32
CLIPS = 64
TOKENS = 8192
NPOS = 4372
PIECE_POS = 137
PIECE = 221609


def draw_mask(key, part):
    key = jax.random.fold_in(key, 3)
    counts = jax.random.randint(jax.random.fold_in(key, 1), (CLIPS,), CAP // 2, CAP + 1)
    chosen = jax.random.randint(jax.random.fold_in(key, 2), (), 0, CLIPS)
    counts = jnp.where(jnp.arange(CLIPS) == chosen, CAP, counts)
    ranking = jax.random.permutation(jax.random.fold_in(key, 4), jnp.broadcast_to(jnp.arange(P_SIZE), (CLIPS, P_SIZE)), axis=1, independent=True)
    return (ranking < counts[:, None]).astype(jnp.int32)


def section_law():
    shard_rows = jnp.arange(SHARDS)[:, None]
    lengths = [3 * D * D // SHARDS, D * D // SHARDS, D * FF // SHARDS, FF * D // SHARDS]
    factors = [D ** (-0.5), 3.0 * D ** (-0.5), D ** (-0.5), 3.0 * FF ** (-0.5)]
    scales = [jnp.full((SHARDS, length), factor, jnp.float32) for length, factor in zip(lengths, factors)]
    shifts = [jnp.zeros((SHARDS, length), jnp.float32) for length in lengths]
    vector_width = 12 * D // SHARDS
    vector_rows = (shard_rows * vector_width + jnp.arange(vector_width)[None, :]) // D
    gain_mask = (vector_rows == 3) | (vector_rows == 6)
    scales.append(jnp.where(gain_mask, 0.1, 0.2).astype(jnp.float32))
    shifts.append(jnp.where(gain_mask, 1.0, 0.0).astype(jnp.float32))
    position_index = shard_rows * PIECE_POS + jnp.arange(PIECE_POS)[None, :]
    table_end = NB * H
    matrix_end = table_end + HD * 8
    bias_end = matrix_end + 8
    scale_end = bias_end + H
    position_scale = jnp.where(position_index < table_end, 1.0, jnp.where(position_index < matrix_end, HD ** (-0.5), jnp.where(position_index < bias_end, 0.5, jnp.where(position_index < scale_end, 0.2, 0.1))))
    scales.append(position_scale.astype(jnp.float32))
    shifts.append(jnp.where((position_index >= bias_end) & (position_index < scale_end), 1.0, 0.0).astype(jnp.float32))
    return (jnp.concatenate(shifts, axis=1), jnp.concatenate(scales, axis=1))


def draw_weights(key, part):
    key = jax.random.fold_in(key, 5)
    shifts, scales = section_law()
    noise = jax.random.normal(key, (SHARDS, PIECE), jnp.float32)
    return shifts + scales * noise


def draw_averages(key, part):
    key = jax.random.fold_in(key, 7)
    shifts, scales = section_law()
    noise = jax.random.normal(key, (SHARDS, PIECE), jnp.float32)
    return shifts + scales * noise


def draw_momenta(key, part):
    key = jax.random.fold_in(key, 9)
    size_scale = 0.25 * math.sqrt(TOKENS)
    noise = jax.random.normal(key, (SHARDS, PIECE), jnp.float32)
    return size_scale * noise


def set_ends(values, key, least, top_value):
    shape = values.shape
    index_at = [jax.random.randint(jax.random.fold_in(key, axis), (), 0, shape[axis]) for axis in range(len(shape))]
    values = values.at[tuple(index_at)].set(least)
    longest = shape.index(max(shape))
    index_at[longest] = (index_at[longest] + 1) % shape[longest]
    return values.at[tuple(index_at)].set(top_value)


def steps_of(key, shape, cuts, least, top_value):
    level, own = 1.0, jax.random.fold_in(key, 6)
    for axis_at, blocks in cuts:
        steps = jnp.exp(jax.random.uniform(jax.random.fold_in(own, axis_at), (blocks,), jnp.float32, least / len(cuts), top_value / len(cuts)))
        level = level * jnp.repeat(steps, shape[axis_at] // blocks).reshape([-1 if axis == axis_at else 1 for axis in range(len(shape))])
    return level


def normal_values(key, extent, deviation, most, cuts=(), kind=jnp.bfloat16):
    level = steps_of(key, extent, cuts, -0.22, 0.18) if cuts else 1.0
    values = jax.random.normal(key, extent, jnp.float32) * deviation * level
    return jnp.minimum(jnp.maximum(values, -most), most).astype(kind)


def setup_inputs(seed: int = 0) -> dict:
    key_list = jax.random.split(jax.random.key(seed), 8)
    return {
        "acts": normal_values(key_list[0], (CLIPS, CAP, D), 1.0, 6.0, ((0, 32),)),
        "cotangent": normal_values(key_list[1], (CLIPS, CAP, D), 1.0, 6.0, ((0, 32),)),
        "mask": draw_mask(jax.random.fold_in(key_list[7], 71), 0),
        "shape_id": set_ends(jax.random.randint(key_list[3], (CLIPS,), 0, 2), jax.random.fold_in(key_list[3], 1), 0, 1).astype(jnp.int32),
        "weights": draw_weights(jax.random.fold_in(key_list[7], 71), 0),
        "momenta": draw_momenta(jax.random.fold_in(key_list[7], 71), 0),
        "averages": draw_averages(jax.random.fold_in(key_list[7], 71), 0),
    }


deep_alpha = 24.0 ** 0.25
layer_epsilon = 1e-05
masked_score = -1000000000.0
far_distance = 800
gate_units = 8
momentum_rate = 0.9
average_rate = 0.8
decay_rate = 0.0001
rate_scale = 0.04

@jax.custom_vjp
def low(v):
    return lax.optimization_barrier(v.astype(jnp.bfloat16)).astype(jnp.float32)

@jax.custom_vjp
def low_back(v):
    return v

def low_keep(v):
    return (low(v), None)

def low_pass(kept, grad):
    return (grad,)

def back_keep(v):
    return (v, None)

def back_low(kept, grad):
    return (low(grad),)
low.defvjp(low_keep, low_pass)
low_back.defvjp(back_keep, back_low)

def bucket_table(buckets, span):
    offsets = np.arange(-span, span + 1)
    half_count = buckets // 2
    exact_count = half_count // 2
    distance = np.abs(offsets)
    logscale = np.log(np.maximum(distance, 1) / exact_count) / np.log(far_distance / exact_count) * (half_count - exact_count)
    beyond = np.minimum(exact_count + np.floor(logscale).astype(np.int64), half_count - 1)
    result = np.where(offsets > 0, half_count, 0) + np.where(distance < exact_count, distance, beyond)
    return jnp.asarray(result.astype(np.int32))

def slot_layout(mask_rows, shape_rows, slot_count):
    visible = mask_rows.astype(jnp.int32)
    ranking = jnp.cumsum(visible, axis=1) - 1
    counts = lax.optimization_barrier(jnp.sum(visible, axis=1))
    patches = jnp.arange(mask_rows.shape[1], dtype=jnp.int32)
    slot_ids = jnp.arange(slot_count, dtype=jnp.int32)
    matches = (ranking[:, None, :] == slot_ids[None, :, None]) & (visible[:, None, :] == 1)
    patch_ids = lax.optimization_barrier(jnp.sum(jnp.where(matches, patches[None, None, :], 0), axis=2)).astype(jnp.int32)
    band_count = (8 - 4 * shape_rows).astype(jnp.int32)[:, None]
    places = patch_ids // band_count * 8 + patch_ids % band_count
    valid_slots = slot_ids[None, :] < counts[:, None]
    return (places.astype(jnp.int32), valid_slots)

def layer_norm(entries, gain_row, shift_row):
    centre = entries - lax.optimization_barrier(jnp.mean(entries, axis=-1, keepdims=True))
    spread = lax.optimization_barrier(jnp.mean(centre * centre, axis=-1, keepdims=True))
    return centre * lax.rsqrt(spread + layer_epsilon) * gain_row + shift_row

def gate_values(inputs, gate_matrix, gate_bias, gate_scale):
    split_heads = inputs.reshape(inputs.shape[0], inputs.shape[1], H, HD)
    logits = jnp.einsum('gihd,de->gihe', split_heads, gate_matrix, precision=lax.Precision.HIGHEST) + gate_bias
    first_gate = jax.nn.sigmoid(lax.optimization_barrier(jnp.sum(logits[..., :4], axis=-1)))
    second_gate = jax.nn.sigmoid(lax.optimization_barrier(jnp.sum(logits[..., 4:], axis=-1)))
    return first_gate * (second_gate * gate_scale - 1.0) + 2.0

def split_position(position):
    table_size = NB * H
    matrix_end = table_size + HD * gate_units
    bias_end = matrix_end + gate_units
    table_values = position[:table_size].reshape(NB, H)
    gate_matrix = position[table_size:matrix_end].reshape(HD, gate_units)
    return (table_values, gate_matrix, position[matrix_end:bias_end], position[bias_end:bias_end + H])

def sections(block, shards):
    widths = [3 * D * D // shards, D * D // shards, D * FF // shards, FF * D // shards]
    pieces = []
    offset = 0
    for span_width in widths:
        pieces.append(block[:, offset:offset + span_width])
        offset = offset + span_width
    pieces.append(block[:, offset:])
    return pieces

def unpack(gathered, shards):
    vector_width = 12 * D // shards
    vectors = gathered[4][:, :vector_width].astype(jnp.float32).reshape(12, D)
    position = gathered[4][:, vector_width:].astype(jnp.float32).reshape(-1)[:NPOS]
    return (gathered[0].reshape(D, 3 * D), gathered[1].reshape(D, D), gathered[2].reshape(D, FF), gathered[3].reshape(FF, D), vectors, position)

def pack_grads(grads, shards):
    position_width = (NPOS + shards - 1) // shards
    padded = jnp.pad(grads[5], (0, shards * position_width - NPOS))
    small_part = jnp.concatenate([grads[4].reshape(shards, -1), padded.reshape(shards, -1)], axis=1)
    return (grads[0].reshape(shards, -1), grads[1].reshape(shards, -1), grads[2].reshape(shards, -1), grads[3].reshape(shards, -1), small_part)

def forward(w_qkv, w_out, w_in, w_down, vectors, position, inputs, bucket_ids, valid_slots):
    highest = lax.Precision.HIGHEST
    clip_count = inputs.shape[0]
    input_rows = inputs.reshape(-1, D)
    table_values, gate_matrix, gate_bias, gate_scale = split_position(position)
    zero_bias = jnp.zeros((D,), jnp.float32)
    joined = jnp.dot(input_rows, w_qkv, precision=highest) + jnp.concatenate([vectors[0], zero_bias, vectors[1]])
    joined = low(low_back(joined)).reshape(clip_count, CAP, 3, H, HD)
    query_heads, key_heads, value_heads = (joined[:, :, 0], joined[:, :, 1], joined[:, :, 2])
    gate_heads = gate_values(inputs, gate_matrix, gate_bias, gate_scale)
    relative = jnp.transpose(table_values[bucket_ids], (0, 3, 1, 2))
    scores = jnp.einsum('gihd,gjhd->ghij', query_heads, key_heads, precision=highest) / math.sqrt(HD)
    scores = scores + jnp.transpose(gate_heads, (0, 2, 1))[:, :, :, None] * relative
    scores = low_back(scores)
    scores = jnp.where(valid_slots[:, None, None, :], scores, masked_score)
    row_top = lax.optimization_barrier(jnp.max(scores, axis=-1, keepdims=True))
    powers = jnp.exp(scores - row_top)
    probability = powers / lax.optimization_barrier(jnp.sum(powers, axis=-1, keepdims=True))
    mixed_heads = jnp.einsum('ghij,gjhd->gihd', low(probability), value_heads, precision=highest)
    mixed_rows = low(low_back(mixed_heads)).reshape(-1, D)
    branch = low_back(jnp.dot(mixed_rows, w_out, precision=highest) + vectors[2])
    first_norm = layer_norm(deep_alpha * input_rows + branch, vectors[3], vectors[4])
    first_low = low(low_back(first_norm))
    hidden = low_back(jnp.dot(first_low, w_in, precision=highest) + vectors[8:12].reshape(-1))
    active = low(jax.nn.gelu(hidden, approximate=False))
    returned = low(low_back(jnp.dot(active, w_down, precision=highest) + vectors[5]))
    final_norm = layer_norm(deep_alpha * first_norm + returned, vectors[6], vectors[7])
    final_norm = jnp.where(valid_slots.reshape(-1, 1), final_norm, 0.0)
    return final_norm.reshape(clip_count, CAP, D)

def reference(acts, cotangent, mask, shape_id, weights, momenta, averages):
    copies = weights.astype(jnp.bfloat16).astype(jnp.float32)
    params = unpack(sections(copies, SHARDS), SHARDS)
    group_size = math.gcd(CLIPS, max(1, 4096 // CAP))
    buckets_all = bucket_table(NB, 2 * P_SIZE)

    def group_step(totals, group_items):
        inputs16, cot16, mask_rows, shape_rows = group_items
        places, valid_slots = slot_layout(mask_rows, shape_rows, CAP)
        bucket_ids = buckets_all[places[:, None, :] - places[:, :, None] + 2 * P_SIZE]

        def layer_pass(w_qkv, w_out, w_in, w_down, vectors, position, inputs):
            return forward(w_qkv, w_out, w_in, w_down, vectors, position, inputs, bucket_ids, valid_slots)
        outputs, pullback = jax.vjp(layer_pass, params[0], params[1], params[2], params[3], params[4], params[5], inputs16.astype(jnp.float32))
        grads = pullback(cot16.astype(jnp.float32))
        totals = tuple((running + increment for running, increment in zip(totals, grads[:6])))
        return (totals, (outputs.astype(jnp.bfloat16), grads[6]))

    def regroup(array):
        return array.reshape((CLIPS // group_size, group_size) + array.shape[1:])
    starts = tuple((jnp.zeros_like(parameter) for parameter in params))
    totals, (outputs, input_grads) = lax.scan(group_step, starts, (regroup(acts), regroup(cotangent), regroup(mask), regroup(shape_id)))
    grad_block = jnp.concatenate(pack_grads(totals, SHARDS), axis=1)
    learning = rate_scale / math.sqrt(TOKENS)
    decayed = grad_block + decay_rate * weights
    momenta_new = momentum_rate * momenta + decayed
    weights_new = weights - learning * (decayed + momentum_rate * momenta_new)
    averages_new = average_rate * averages + (1.0 - average_rate) * weights_new
    return (outputs.reshape(CLIPS, CAP, D), input_grads.reshape(CLIPS, CAP, D), momenta_new, averages_new, weights_new, weights_new.astype(jnp.bfloat16))
```

```python
from functools import partial
import math

import jax
import jax.numpy as jnp
import numpy as np
from jax import lax
from jax.experimental import pallas as pl
from jax.experimental.pallas import tpu as pltpu
from jax.sharding import PartitionSpec as P

D = 768
H = 12
HD = 64
FF = 3072
NB = 320
HALF = NB // 2
P_SIZE = 512
NPOS = 4372
LANES = 128
KEYS = 384
BF = jnp.bfloat16
F32 = jnp.float32

deep_alpha = 24.0**0.25
layer_epsilon = 1e-05
masked_score = -1000000000.0
far_distance = 800
gate_units = 8
momentum_rate = 0.9
average_rate = 0.8
decay_rate = 0.0001
rate_scale = 0.04
far_place = 1 << 20


def bucket_levels(span):
    distance = np.arange(0, span + 1)
    exact = HALF // 2
    logscale = (
        np.log(np.maximum(distance, 1) / exact) / np.log(far_distance / exact) * (HALF - exact)
    )
    beyond = np.minimum(exact + np.floor(logscale).astype(np.int64), HALF - 1)
    return np.where(distance < exact, distance, beyond)


def far_marks():
    levels = bucket_levels(2 * P_SIZE)
    rises = np.diff(levels)
    marks = np.repeat(np.arange(1, 2 * P_SIZE + 1), rises)
    return [int(m) for m in marks[HALF // 2 :]]


def key_ends():
    span = 2 * P_SIZE
    levels = bucket_levels(span)
    offsets = np.arange(-span, span + 1)
    level = levels[np.abs(offsets)]
    keys = np.where(offsets > 0, HALF + level, HALF - 1 - level)
    ends = np.full((KEYS,), far_place // 2, np.int32)
    for key in range(NB - 1):
        below = offsets[keys <= key]
        ends[key] = below.max() if below.size else -(far_place // 2)
    return ends


def exchange(value, axis, mask):
    count = lax.axis_size(axis)
    return lax.ppermute(value, axis, [(i, i ^ mask) for i in range(count)])


def high_groups(count):
    bits = count.bit_length() - 1
    groups = []
    shift = 2
    while shift < bits:
        size = min(2, bits - shift)
        groups.append((shift, size))
        shift += size
    return groups


def gather_class(piece):
    count = lax.axis_size("dp")
    column = piece
    for shift, size in high_groups(count):
        column = jnp.concatenate(
            [column] + [exchange(column, "dp", d << shift) for d in range(1, 1 << size)], axis=0
        )
    half = column.shape[0] // 2
    near = exchange(column, "dp", 1)
    side = exchange(column, "dp", 2)
    first = exchange(near[:half], "dp", 2)
    second = exchange(side[half:], "dp", 1)
    return jnp.concatenate([column, near, side, first, second], axis=0)


def add_low(one, two):
    return (one.astype(F32) + two.astype(F32)).astype(BF)


def scatter_class(stack):
    count = lax.axis_size("dp")
    size = stack.shape[0] // 4
    half = size // 2
    own, near, side = stack[:size], stack[size : 2 * size], stack[2 * size : 3 * size]
    first = exchange(stack[3 * size : 3 * size + half], "dp", 2)
    second = exchange(stack[3 * size + half :], "dp", 1)
    near = jnp.concatenate([add_low(near[:half], first), near[half:]], axis=0)
    side = jnp.concatenate([side[:half], add_low(side[half:], second)], axis=0)
    near = exchange(near, "dp", 1)
    side = exchange(side, "dp", 2)
    column = own.astype(F32) + near.astype(F32) + side.astype(F32)
    for shift, bits in reversed(high_groups(count)):
        parts = 1 << bits
        size = column.shape[0] // parts
        low = column.astype(BF)
        total = column[:size]
        for d in range(1, parts):
            total = total + exchange(low[d * size : (d + 1) * size], "dp", d << shift).astype(F32)
        column = total
    return column


def slot_order(dp, core, count):
    high = count // 4
    core_step, low, up = np.meshgrid(np.arange(2), np.arange(4), np.arange(high), indexing="ij")
    distance = jnp.asarray((up * 4 + low).reshape(-1).astype(np.int32))
    core_distance = jnp.asarray(core_step.reshape(-1).astype(np.int32))
    return (distance ^ dp) * 2 + (core_distance ^ core)


def prep_kernel(marks, places_ref, column_ref, row_ref, ends_ref, bucket_ref, rank_ref):
    clips, slots = row_ref.shape[0], row_ref.shape[2]
    for clip in range(clips):
        offset = row_ref[clip] - column_ref[clip]
        distance = jnp.abs(offset)
        level = jnp.minimum(distance, HALF // 2)
        for mark in marks:
            level = level + (distance >= mark).astype(jnp.int32)
        bucket_ref[clip] = level + jnp.where(offset > 0, HALF, 0)
        limit = column_ref[clip] + ends_ref[...]

        def count(j, total):
            return total + (limit >= places_ref[clip, j]).astype(jnp.int32)

        rank_ref[clip] = lax.fori_loop(0, slots, count, jnp.zeros(limit.shape, jnp.int32), unroll=8)


def prep(places, valid_slots):
    clips, slots = places.shape
    row = places[:, None, :]
    column = places[:, :, None]
    counted = jnp.where(valid_slots, places, far_place)
    ends = jnp.asarray(key_ends())[None, :]
    vmem = pl.BlockSpec(memory_space=pltpu.VMEM)
    return pl.pallas_call(
        partial(prep_kernel, far_marks()),
        out_shape=(
            jax.ShapeDtypeStruct((clips, slots, slots), jnp.int32),
            jax.ShapeDtypeStruct((clips, slots, KEYS), jnp.int32),
        ),
        in_specs=[pl.BlockSpec(memory_space=pltpu.SMEM), vmem, vmem, vmem],
        out_specs=(vmem, vmem),
        name="prep",
    )(counted, column, row, ends)


def lookup(table_ref, head, index, block):
    out = None
    for part in range(KEYS // LANES):
        row = jnp.broadcast_to(table_ref[head : head + 1, part * LANES : (part + 1) * LANES], index.shape)
        found = jnp.take_along_axis(row, index, axis=1, mode="promise_in_bounds")
        out = found if out is None else jnp.where(block == part, found, out)
    return out


def nt(a, b):
    return lax.dot_general(a, b, (((1,), (1,)), ((), ())), preferred_element_type=F32)


def tn(a, b):
    return lax.dot_general(a, b, (((0,), (0,)), ((), ())), preferred_element_type=F32)


def attention_kernel(joined_ref, gate_ref, bucket_ref, valid_ref, table_ref, mixed_ref, prob_ref, rel_ref):
    clips, slots = bucket_ref.shape[0], bucket_ref.shape[1]
    for clip in range(clips):
        rows = slice(clip * slots, (clip + 1) * slots)
        index = bucket_ref[clip] & (LANES - 1)
        block = bucket_ref[clip] >> 7
        valid = valid_ref[clip] > 0
        for head in range(H):
            cols = slice(head * HD, (head + 1) * HD)
            query = joined_ref[rows, head * HD : (head + 1) * HD]
            key = joined_ref[rows, D + head * HD : D + (head + 1) * HD]
            value = joined_ref[rows, 2 * D + head * HD : 2 * D + (head + 1) * HD]
            rel = lookup(table_ref, head, index, block)
            rel_ref[clip, head] = rel
            score = nt(query, key) * (1.0 / math.sqrt(HD)) + gate_ref[rows, head : head + 1] * rel
            score = jnp.where(valid, score, masked_score)
            top = jnp.max(score, axis=-1, keepdims=True)
            power = jnp.exp(score - top)
            prob = power / jnp.sum(power, axis=-1, keepdims=True)
            prob_ref[clip, head] = prob
            mixed_ref[rows, cols] = jnp.dot(
                prob.astype(BF), value, preferred_element_type=F32
            ).astype(BF)


def attention(joined, gate, bucket, valid, table):
    clips, slots = bucket.shape[0], bucket.shape[1]
    vmem = pl.BlockSpec(memory_space=pltpu.VMEM)
    return pl.pallas_call(
        attention_kernel,
        out_shape=(
            jax.ShapeDtypeStruct((clips * slots, D), BF),
            jax.ShapeDtypeStruct((clips, H, slots, slots), F32),
            jax.ShapeDtypeStruct((clips, H, slots, slots), F32),
        ),
        in_specs=[vmem] * 5,
        out_specs=(vmem,) * 3,
        compiler_params=pltpu.CompilerParams(vmem_limit_bytes=40 * 1024 * 1024),
        name="attention",
    )(joined, gate, bucket, valid, table)


def attention_back_kernel(
    joined_ref, gate_ref, rank_ref, prob_ref, rel_ref, grad_ref, tri_ref, joined_grad_ref, gate_grad_ref, table_grad_ref
):
    clips, slots = rank_ref.shape[0], rank_ref.shape[1]
    scale = 1.0 / math.sqrt(HD)
    gate_grad_ref[...] = jnp.zeros(gate_grad_ref.shape, F32)
    table_grad_ref[...] = jnp.zeros(table_grad_ref.shape, F32)
    for clip in range(clips):
        rows = slice(clip * slots, (clip + 1) * slots)
        for head in range(H):
            cols = slice(head * HD, (head + 1) * HD)
            key_cols = slice(D + head * HD, D + (head + 1) * HD)
            value_cols = slice(2 * D + head * HD, 2 * D + (head + 1) * HD)
            query = joined_ref[rows, cols]
            key = joined_ref[rows, key_cols]
            value = joined_ref[rows, value_cols]
            grad = grad_ref[rows, cols]
            prob = prob_ref[clip, head]
            joined_grad_ref[rows, value_cols] = tn(prob.astype(BF), grad).astype(BF)
            prob_grad = nt(grad, value)
            weighted = prob * prob_grad
            low = (weighted - prob * jnp.sum(weighted, axis=-1, keepdims=True)).astype(BF)
            joined_grad_ref[rows, cols] = (
                jnp.dot(low, key, preferred_element_type=F32) * scale
            ).astype(BF)
            joined_grad_ref[rows, key_cols] = (tn(low, query) * scale).astype(BF)
            wide = low.astype(F32)
            gate_grad_ref[rows, head : head + 1] = jnp.sum(
                wide * rel_ref[clip, head], axis=-1, keepdims=True
            )
            gated = wide * gate_ref[rows, head : head + 1]
            high = gated.astype(BF)
            rest = (gated - high.astype(F32)).astype(BF)
            running = jnp.dot(high, tri_ref[...], preferred_element_type=F32) + jnp.dot(
                rest, tri_ref[...], preferred_element_type=F32
            )
            for part in range(KEYS // LANES):
                lanes = slice(part * LANES, (part + 1) * LANES)
                rank = rank_ref[clip, :, lanes]
                found = jnp.take_along_axis(
                    running, jnp.maximum(rank - 1, 0), axis=1, mode="promise_in_bounds"
                )
                total = jnp.sum(jnp.where(rank > 0, found, 0.0), axis=0, keepdims=True)
                table_grad_ref[head : head + 1, lanes] += total


def attention_back(joined, gate, rank, prob, rel, grad):
    clips, slots = rank.shape[0], rank.shape[1]
    vmem = pl.BlockSpec(memory_space=pltpu.VMEM)
    tri = jnp.asarray(np.triu(np.ones((slots, slots), np.float32)), BF)
    return pl.pallas_call(
        attention_back_kernel,
        out_shape=(
            jax.ShapeDtypeStruct((clips * slots, 3 * D), BF),
            jax.ShapeDtypeStruct((clips * slots, LANES), F32),
            jax.ShapeDtypeStruct((16, KEYS), F32),
        ),
        in_specs=[vmem] * 7,
        out_specs=(vmem,) * 3,
        compiler_params=pltpu.CompilerParams(vmem_limit_bytes=40 * 1024 * 1024),
        name="attention_back",
    )(joined, gate, rank, prob, rel, grad, tri)


def slot_layout(mask_rows, shape_rows, slot_count):
    ranking = jnp.cumsum(mask_rows, axis=1) - 1
    counts = jnp.sum(mask_rows, axis=1)
    patches = jnp.arange(mask_rows.shape[1], dtype=jnp.int32)
    slot_ids = jnp.arange(slot_count, dtype=jnp.int32)
    matches = (ranking[:, None, :] == slot_ids[None, :, None]) & (mask_rows[:, None, :] == 1)
    patch_ids = jnp.sum(jnp.where(matches, patches[None, None, :], 0), axis=2)
    band_count = (8 - 4 * shape_rows)[:, None]
    places = patch_ids // band_count * 8 + patch_ids % band_count
    valid_slots = slot_ids[None, :] < counts[:, None]
    return (places, valid_slots)


def layer_norm(entries, gain_row, shift_row):
    centre = entries - jnp.mean(entries, axis=-1, keepdims=True)
    spread = jnp.mean(centre * centre, axis=-1, keepdims=True)
    return centre * lax.rsqrt(spread + layer_epsilon) * gain_row + shift_row


def gate_values(inputs, gate_matrix, gate_bias, gate_scale):
    rows = inputs.shape[0]
    spread = jnp.einsum("de,hk->hdek", gate_matrix.astype(BF), jnp.eye(H, dtype=BF)).reshape(D, gate_units * H)
    logits = jnp.dot(inputs, spread, preferred_element_type=F32).reshape(rows, gate_units, H) + gate_bias[None, :, None]
    first = jax.nn.sigmoid(jnp.sum(logits[:, :4], axis=1))
    second = jax.nn.sigmoid(jnp.sum(logits[:, 4:], axis=1))
    return first, second, first * (second * gate_scale - 1.0) + 2.0


def gate_back(inputs, gate_matrix, gate_scale, first, second, grad):
    highest = lax.Precision.HIGHEST
    grad_first = grad * (second * gate_scale - 1.0) * first * (1.0 - first)
    grad_second = grad * first * gate_scale * second * (1.0 - second)
    grad_scale = jnp.sum(grad * first * second, axis=0)
    sums = jnp.stack([jnp.sum(gate_matrix[:, :4], axis=1), jnp.sum(gate_matrix[:, 4:], axis=1)])
    spread = jnp.einsum("ed,hk->ehkd", sums, jnp.eye(H, dtype=F32)).reshape(2 * H, D)
    both = jnp.concatenate([grad_first, grad_second], axis=1)
    grad_inputs = jnp.dot(both, spread, precision=highest)
    wide = lax.dot_general(
        both, inputs.astype(F32), (((0,), (0,)), ((), ())), precision=highest
    ).reshape(2, H, H, HD)
    parts = jnp.einsum("ehkd,hk->ed", wide, jnp.eye(H, dtype=F32), precision=highest)
    grad_matrix = jnp.repeat(parts, 4, axis=0).T
    grad_bias = jnp.repeat(jnp.sum(both.reshape(-1, 2, H), axis=(0, 2)), 4)
    return grad_inputs, grad_matrix, grad_bias, grad_scale


def split_position(position):
    table_size = NB * H
    matrix_end = table_size + HD * gate_units
    bias_end = matrix_end + gate_units
    table_values = position[:table_size].reshape(NB, H)
    gate_matrix = position[table_size:matrix_end].reshape(HD, gate_units)
    return (
        table_values,
        gate_matrix,
        position[matrix_end:bias_end],
        position[bias_end : bias_end + H],
    )


def body(acts, cotangent, mask, shape_id, weights, momenta, averages):
    shards = lax.axis_size(("dp", "fsdp"))
    count = lax.axis_size("dp")
    dp, core = lax.axis_index("dp"), lax.axis_index("fsdp")
    clips, slots = acts.shape[0], acts.shape[1]
    rows = clips * slots
    total_tokens = rows * shards
    piece_rows = D // shards
    wide_rows = FF // shards
    vector_width = 12 * D // shards
    position_width = (NPOS + shards - 1) // shards
    small_width = vector_width + position_width

    low = weights.reshape(-1).astype(BF)
    sizes = [3 * D * D // shards, D * D // shards, D * FF // shards, FF * D // shards]
    ends = np.cumsum([0] + sizes)
    small = jnp.pad(low[int(ends[4]) :], (0, piece_rows * LANES - small_width)).reshape(piece_rows, LANES)
    piece_first = jnp.concatenate(
        [
            low[int(ends[0]) : int(ends[1])].reshape(piece_rows, 3 * D),
            low[int(ends[1]) : int(ends[2])].reshape(piece_rows, D),
            small,
        ],
        axis=1,
    )
    piece_in = low[int(ends[2]) : int(ends[3])].reshape(piece_rows, FF)
    piece_down = low[int(ends[3]) : int(ends[4])].reshape(wide_rows, D)

    def both_cores(piece):
        mine = gather_class(piece)
        return jnp.concatenate([mine, exchange(mine, "fsdp", 1)], axis=0)

    full_first = both_cores(piece_first)
    full_in = both_cores(piece_in)
    full_down = both_cores(piece_down)

    order = slot_order(dp, core, count)
    row_order = (order[:, None] * piece_rows + jnp.arange(piece_rows, dtype=jnp.int32)).reshape(-1)
    turn = (jnp.arange(D, dtype=jnp.int32)[:, None] == row_order[None, :]).astype(BF)
    piece_turn = (jnp.arange(shards, dtype=jnp.int32)[:, None] == order[None, :]).astype(BF)

    def to_slots(value):
        return jnp.dot(value, turn, preferred_element_type=F32).astype(BF)

    def from_slots(value):
        return jnp.dot(value, turn.T, preferred_element_type=F32).astype(BF)

    w_qkv = full_first[:, : 3 * D]
    w_out = full_first[:, 3 * D : 4 * D]
    small_all = full_first[:, 4 * D :].reshape(shards, piece_rows * LANES)[:, :small_width]
    small_all = jnp.dot(piece_turn, small_all, preferred_element_type=F32)
    vectors = small_all[:, :vector_width].reshape(12, D)
    position = small_all[:, vector_width:].reshape(-1)[:NPOS]
    table_values, gate_matrix, gate_bias, gate_scale = split_position(position)
    table = jnp.pad(table_values.T, ((0, 16 - H), (0, KEYS - NB)))

    places, valid_slots = slot_layout(mask, shape_id, slots)
    bucket, rank = prep(places, valid_slots)
    valid_rows = valid_slots.reshape(-1, 1)
    valid_wide = valid_slots.astype(jnp.int32)[:, None, :]

    inputs_low = acts.reshape(rows, D)
    inputs = inputs_low.astype(F32)
    inputs_slots = to_slots(inputs_low)
    joined_bias = jnp.concatenate([vectors[0], jnp.zeros((D,), F32), vectors[1]])
    joined = (jnp.dot(inputs_slots, w_qkv, preferred_element_type=F32) + joined_bias).astype(BF)
    first, second, gate = gate_values(inputs_low, gate_matrix, gate_bias, gate_scale)
    gate_wide = jnp.pad(gate, ((0, 0), (0, LANES - H)))
    mixed, prob, rel = attention(joined, gate_wide, bucket, valid_wide, table)
    mixed_slots = to_slots(mixed)
    branch = jnp.dot(mixed_slots, w_out, preferred_element_type=F32) + vectors[2]
    first_norm, first_pull = jax.vjp(layer_norm, deep_alpha * inputs + branch, vectors[3], vectors[4])
    first_slots = to_slots(first_norm.astype(BF))
    hidden = jnp.dot(first_slots, full_in, preferred_element_type=F32) + vectors[8:12].reshape(-1)
    hidden = jnp.take(hidden.T.reshape(shards, wide_rows, rows), order, axis=0).reshape(FF, rows)
    active, gelu_pull = jax.vjp(partial(jax.nn.gelu, approximate=False), hidden)
    active = active.astype(BF)
    returned = (tn(active, full_down) + vectors[5]).astype(BF)
    final_norm, second_pull = jax.vjp(
        layer_norm, deep_alpha * first_norm + returned.astype(F32), vectors[6], vectors[7]
    )
    activations = jnp.where(valid_rows, final_norm, 0.0).astype(BF)

    grad_final = jnp.where(valid_rows, cotangent.reshape(rows, D).astype(F32), 0.0)
    grad_second, grad_gain_two, grad_shift_two = second_pull(grad_final)
    grad_made = grad_second.astype(BF)
    grad_down = jnp.dot(active, grad_made, preferred_element_type=F32).astype(BF)

    def both_back(grads):
        half = grads.shape[0] // 2
        return scatter_class(add_low(grads[:half], exchange(grads[half:], "fsdp", 1)))

    sum_down = both_back(grad_down)
    grad_bias_down = jnp.sum(grad_made.astype(F32), axis=0)
    grad_hidden = gelu_pull(nt(full_down, grad_made))[0].astype(BF)
    back_order = jnp.dot(piece_turn.astype(F32), jnp.arange(shards, dtype=F32)).astype(jnp.int32)
    grad_hidden = jnp.take(grad_hidden.reshape(shards, wide_rows, rows), back_order, axis=0).reshape(FF, rows)
    grad_bias_in = jnp.sum(grad_hidden.astype(F32), axis=1)
    grad_in = lax.dot_general(
        first_slots, grad_hidden, (((0,), (1,)), ((), ())), preferred_element_type=F32
    ).astype(BF)
    sum_in = both_back(grad_in)
    grad_first_ffn = lax.dot_general(
        grad_hidden, full_in, (((0,), (1,)), ((), ())), preferred_element_type=F32
    ).astype(BF)
    grad_first_ffn = from_slots(grad_first_ffn)
    grad_first = deep_alpha * grad_second + grad_first_ffn.astype(F32)
    grad_first_sum, grad_gain_one, grad_shift_one = first_pull(grad_first)
    grad_branch = grad_first_sum.astype(BF)
    grad_bias_out = jnp.sum(grad_branch.astype(F32), axis=0)
    grad_out = tn(mixed_slots, grad_branch).astype(BF)
    grad_mixed = from_slots(nt(grad_branch, w_out).astype(BF))
    grad_joined, gate_grad, key_sums = attention_back(joined, gate_wide, rank, prob, rel, grad_mixed)
    key_sums = key_sums[:H, :NB]
    key_grad = key_sums - jnp.pad(key_sums, ((0, 0), (1, 0)))[:, :NB]
    table_grad = jnp.concatenate([key_grad[:, HALF - 1 :: -1], key_grad[:, HALF:]], axis=1).T
    grad_gate_inputs, grad_matrix, grad_bias, grad_scale = gate_back(
        inputs_low, gate_matrix, gate_scale, first, second, gate_grad[:, :H]
    )
    grad_qkv = tn(inputs_slots, grad_joined).astype(BF)
    wide_joined = grad_joined.astype(F32)
    grad_bias_query = jnp.sum(wide_joined[:, :D], axis=0)
    grad_bias_value = jnp.sum(wide_joined[:, 2 * D :], axis=0)
    grad_vectors = jnp.concatenate(
        [
            jnp.stack(
                [
                    grad_bias_query,
                    grad_bias_value,
                    grad_bias_out,
                    grad_gain_one,
                    grad_shift_one,
                    grad_bias_down,
                    grad_gain_two,
                    grad_shift_two,
                ]
            ),
            grad_bias_in.reshape(4, D),
        ],
        axis=0,
    )
    grad_position = jnp.concatenate([table_grad.reshape(-1), grad_matrix.reshape(-1), grad_bias, grad_scale])
    grad_position = jnp.pad(grad_position, (0, shards * position_width - NPOS))
    grad_small = jnp.concatenate(
        [grad_vectors.reshape(shards, -1), grad_position.reshape(shards, -1)], axis=1
    ).astype(BF)
    grad_small = jnp.dot(piece_turn.T, grad_small, preferred_element_type=F32).astype(BF)
    grad_small = jnp.pad(grad_small, ((0, 0), (0, piece_rows * LANES - small_width))).reshape(D, LANES)
    sum_first = both_back(jnp.concatenate([grad_qkv, grad_out, grad_small], axis=1))
    grad_rows = nt(grad_joined, w_qkv)
    grad_rows = jnp.dot(grad_rows, turn.T.astype(F32), precision=lax.Precision.HIGHEST)
    input_grad = grad_rows + deep_alpha * grad_first_sum + grad_gate_inputs

    grad_block = jnp.concatenate(
        [
            sum_first[:, : 3 * D].reshape(-1),
            sum_first[:, 3 * D : 4 * D].reshape(-1),
            sum_in.reshape(-1),
            sum_down.reshape(-1),
            sum_first[:, 4 * D :].reshape(-1)[:small_width],
        ]
    ).reshape(weights.shape)
    learning = rate_scale / math.sqrt(total_tokens)
    decayed = grad_block + decay_rate * weights
    momenta_new = momentum_rate * momenta + decayed
    weights_new = weights - learning * (decayed + momentum_rate * momenta_new)
    averages_new = average_rate * averages + (1.0 - average_rate) * weights_new
    return (
        activations.reshape(acts.shape),
        input_grad.reshape(acts.shape),
        momenta_new,
        averages_new,
        weights_new,
        weights_new.astype(BF),
    )


def solution(mesh):
    split = ("dp", "fsdp")
    in_specs = (
        P(split, None, None),
        P(split, None, None),
        P(split, None),
        P(split),
        P(split, None),
        P(split, None),
        P(split, None),
    )
    out_specs = (
        P(split, None, None),
        P(split, None, None),
        P(split, None),
        P(split, None),
        P(split, None),
        P(split, None),
    )
    return jax.shard_map(body, mesh=mesh, in_specs=in_specs, out_specs=out_specs, check_vma=False)
```

```python
from functools import partial
import math

import jax
import jax.numpy as jnp
import numpy as np
from jax import lax
from jax.experimental import pallas as pl
from jax.experimental.pallas import tpu as pltpu
from jax.sharding import PartitionSpec as P

D = 768
H = 12
HD = 64
FF = 3072
NB = 320
HALF = NB // 2
P_SIZE = 512
NPOS = 4372
LANES = 128
KEYS = 384
BF = jnp.bfloat16
F32 = jnp.float32

deep_alpha = 24.0**0.25
layer_epsilon = 1e-05
masked_score = -1000000000.0
far_distance = 800
gate_units = 8
momentum_rate = 0.9
average_rate = 0.8
decay_rate = 0.0001
rate_scale = 0.04
far_place = 1 << 20


def bucket_levels(span):
    distance = np.arange(0, span + 1)
    exact = HALF // 2
    logscale = (
        np.log(np.maximum(distance, 1) / exact) / np.log(far_distance / exact) * (HALF - exact)
    )
    beyond = np.minimum(exact + np.floor(logscale).astype(np.int64), HALF - 1)
    return np.where(distance < exact, distance, beyond)


def far_marks():
    levels = bucket_levels(2 * P_SIZE)
    rises = np.diff(levels)
    marks = np.repeat(np.arange(1, 2 * P_SIZE + 1), rises)
    return [int(m) for m in marks[HALF // 2 :]]


def key_ends():
    span = 2 * P_SIZE
    levels = bucket_levels(span)
    offsets = np.arange(-span, span + 1)
    level = levels[np.abs(offsets)]
    keys = np.where(offsets > 0, HALF + level, HALF - 1 - level)
    ends = np.full((KEYS,), far_place // 2, np.int32)
    for key in range(NB - 1):
        below = offsets[keys <= key]
        ends[key] = below.max() if below.size else -(far_place // 2)
    return ends


def exchange(value, axis, mask):
    count = lax.axis_size(axis)
    return lax.ppermute(value, axis, [(i, i ^ mask) for i in range(count)])


def high_groups(count):
    bits = count.bit_length() - 1
    groups = []
    shift = 2
    while shift < bits:
        size = min(2, bits - shift)
        groups.append((shift, size))
        shift += size
    return groups


def after(value, *others):
    return lax.optimization_barrier((value,) + others)[0]


def gather_column(piece):
    column = piece
    for shift, size in high_groups(lax.axis_size("dp")):
        column = stack([column] + [exchange(column, "dp", d << shift) for d in range(1, 1 << size)])
    return column


def high_bits(count):
    return list(range(2, count.bit_length() - 1))


def gather_bits(column, bits):
    parts = (column,)
    for bit in bits:
        column = stack(parts)
        parts = (column, exchange(column, "dp", 1 << bit))
    return parts


def gather_sides(column):
    return exchange(column, "dp", 1), exchange(column, "dp", 2)


def gather_corner(near, side):
    first, second = halves(near, side)
    return exchange(first, "dp", 2), exchange(second, "dp", 1)


def other_core(parts):
    return exchange(stack(list(parts)), "fsdp", 1)


def scatter_corner(first, second):
    return exchange(first, "dp", 2), exchange(second, "dp", 1)


def scatter_sides(near, side):
    return exchange(near, "dp", 1), exchange(side, "dp", 2)


def scatter_bits(parts, bits):
    for bit in reversed(bits):
        keep, send = halve(parts)
        parts = (keep, exchange(send, "dp", 1 << bit))
    return parts


def scatter_high(cut, size):
    groups = high_groups(lax.axis_size("dp"))
    if len(groups) == 1:
        shift = groups[0][0]
        return [cut[0]] + [exchange(part, "dp", d << shift) for d, part in enumerate(cut) if d]
    total = jnp.concatenate([part.astype(F32) for part in cut], axis=0)
    for shift, bits in reversed(groups):
        size = total.shape[0] >> bits
        low = total.astype(BF)
        total = total[:size]
        for d in range(1, 1 << bits):
            total = total + exchange(low[d * size : (d + 1) * size], "dp", d << shift).astype(F32)
    return [total]


def slot_order(dp, core, count):
    high = count // 4
    core_step, low, up = np.meshgrid(np.arange(2), np.arange(4), np.arange(high), indexing="ij")
    distance = jnp.asarray((up * 4 + low).reshape(-1).astype(np.int32))
    core_distance = jnp.asarray(core_step.reshape(-1).astype(np.int32))
    return (distance ^ dp) * 2 + (core_distance ^ core)


def prep_kernel(marks, shape_ref, mask_ref, ends_ref, bucket_ref, rank_ref, valid_ref, valid_row_ref):
    clips, patches = mask_ref.shape
    slots = bucket_ref.shape[1]
    mask = mask_ref[...]
    up = lax.broadcasted_iota(jnp.int32, (patches, patches), 0)
    across = lax.broadcasted_iota(jnp.int32, (patches, patches), 1)
    running = wide_dot(mask.astype(F32).astype(BF), (up <= across).astype(F32).astype(BF))
    ranks = jnp.where(mask == 1, running.astype(jnp.int32) - 1, -1)
    slot = lax.broadcasted_iota(jnp.int32, (slots, patches), 0)
    patch = lax.broadcasted_iota(jnp.int32, (slots, patches), 1)
    pair = lax.broadcasted_iota(jnp.int32, (8, patches), 1)
    halves = jnp.where(lax.broadcasted_iota(jnp.int32, (8, patches), 0) == 0, pair >> 4, pair & 15)
    halves = halves.astype(F32).astype(BF)
    for clip in range(clips):
        found = ranks[clip : clip + 1, :] == slot
        column = jnp.sum(jnp.where(found, patch, 0), axis=1, keepdims=True)
        both = nt(halves, found.astype(F32).astype(BF)).astype(jnp.int32)
        row = 16 * both[0:1, :] + both[1:2, :]
        narrow = shape_ref[clip] > 0
        column = jnp.where(narrow, 8 * (column >> 2) + (column & 3), column)
        row = jnp.where(narrow, 8 * (row >> 2) + (row & 3), row)
        count = jnp.sum(mask[clip : clip + 1, :], axis=1, keepdims=True)
        valid = lax.broadcasted_iota(jnp.int32, (slots, 1), 0) < count
        valid_ref[clip * slots : (clip + 1) * slots, :] = valid.astype(F32)
        valid_row_ref[clip] = (lax.broadcasted_iota(jnp.int32, (1, slots), 1) < count).astype(jnp.int32)
        offset = row - column
        distance = jnp.abs(offset)
        level = jnp.minimum(distance, HALF // 2)
        for mark in marks:
            level = level + (distance >= mark).astype(jnp.int32)
        bucket_ref[clip] = level + jnp.where(offset > 0, HALF, 0)
        away = jnp.where(valid, column - row, far_place)
        for first in range(slots):
            seen = away[:, first : first + 1] <= ends_ref[...]
            rank_ref[clip, first : first + 1, :] = jnp.sum(seen.astype(jnp.int32), axis=0, keepdims=True)


def prep(mask, shape_id, slots):
    clips = mask.shape[0]
    ends = jnp.asarray(key_ends())[None, :]
    return call(
        partial(prep_kernel, far_marks()),
        (mask, ends),
        (
            shaped((clips, slots, slots), jnp.int32),
            shaped((clips, slots, KEYS), jnp.int32),
            shaped((clips * slots, 1), F32),
            shaped((clips, 1, slots), jnp.int32),
        ),
        8,
        "prep",
        scalars=(shape_id,),
    )


def position_rows(shards, by_key):
    width = (NPOS + shards - 1) // shards
    index = np.full((24, KEYS), -1, np.int64)
    for head in range(H):
        for lane in range(NB):
            bucket = (HALF - 1 - lane if lane < HALF else lane) if by_key else lane
            index[head, lane] = bucket * H + head
    for unit in range(gate_units):
        index[12 + unit, :HD] = NB * H + np.arange(HD) * gate_units + unit
    index[20, :gate_units] = (NB + 0) * H + HD * gate_units + np.arange(gate_units)
    index[21, :H] = NB * H + (HD + 1) * gate_units + np.arange(H)
    pieces = np.where(index >= 0, index // width, -1).astype(np.int32)
    columns = np.where(index >= 0, 12 * D // shards + index % width, -1).astype(np.int32)
    return jnp.asarray(pieces), jnp.asarray(columns)


def vector_chunks(shards):
    width = 12 * D // shards
    size = math.gcd(width, D)
    each, across = width // size, D // size
    return size, [
        (g // each, g % each * size, g // across, g % across * size) for g in range(12 * across)
    ]


def unpack_kernel(shards, turn_ref, pieces_ref, columns_ref, *refs):
    parts = refs[:-7]
    vectors_ref, bias_ref, table_ref, stack_ref, natural_ref, small_ref, _ = refs[-7:]
    at = 0
    for part in parts:
        stack_ref[at : at + part.shape[0], :] = part[:, 4 * D :]
        at += part.shape[0]
    natural_ref[...] = wide_dot(turn_ref[...], stack_ref[...])
    each = D // shards
    wide = small_ref.shape[1]
    for k in range(wide // LANES):
        small_ref[:, k * LANES : (k + 1) * LANES] = natural_ref[pl.ds(k, shards, stride=each), :]
    size, chunks = vector_chunks(shards)
    for piece, column, row, place in chunks:
        value = small_ref[piece : piece + 1, column : column + size]
        if row < 8:
            vectors_ref[row : row + 1, place : place + size] = value
        else:
            bias_ref[:, (row - 8) * D + place : (row - 8) * D + place + size] = value
    start = 12 * D // shards // LANES * LANES
    small = small_ref[:, start:].astype(BF)
    piece_ids = lax.broadcasted_iota(jnp.int32, (shards, KEYS), 0)
    column_ids = lax.broadcasted_iota(jnp.int32, (wide - start, KEYS), 0) + start
    for row in range(22):
        chosen = (piece_ids == pieces_ref[row : row + 1, :]).astype(F32).astype(BF)
        spread = tn(small, chosen)
        table_ref[row : row + 1, :] = jnp.sum(
            jnp.where(column_ids == columns_ref[row : row + 1, :], spread, 0.0), axis=0, keepdims=True
        )
    table_ref[22:24, :] = jnp.zeros((2, KEYS), F32)


def small_lanes(shards):
    return -(-(12 * D // shards + (NPOS + shards - 1) // shards) // LANES) * LANES


def unpack(shards, turn, parts):
    pieces, columns = position_rows(shards, False)
    return call(
        partial(unpack_kernel, shards),
        (turn, pieces, columns, *parts),
        (shaped((8, D), F32), shaped((1, FF), F32), shaped((24, KEYS), F32)),
        8,
        "unpack",
        scratch=(
            pltpu.VMEM((D, LANES), BF),
            pltpu.VMEM((D, LANES), F32),
            pltpu.VMEM((shards, small_lanes(shards)), F32),
            pltpu.VMEM((8, LANES), F32),
        ),
    )


def pack_kernel(shards, turn_ref, pieces_ref, columns_ref, attention_ref, first_ref, second_ref, bias_ref, table_ref, out_ref, natural_ref, small_ref):
    each = D // shards
    wide = small_ref.shape[1]
    table = table_ref[...]
    lane = lax.broadcasted_iota(jnp.int32, table.shape, 1)
    row_id = lax.broadcasted_iota(jnp.int32, table.shape, 0)
    before = jnp.where((lane > 0) & (row_id < H), pltpu.roll(table, 1, 1), 0.0)
    table = table - before
    piece_ids = lax.broadcasted_iota(jnp.int32, (shards, KEYS), 0)
    start = 12 * D // shards // LANES * LANES
    column_ids = lax.broadcasted_iota(jnp.int32, (wide - start, KEYS), 0) + start
    total = jnp.zeros((shards, wide - start), F32)
    for row in range(22):
        chosen = jnp.where(piece_ids == pieces_ref[row : row + 1, :], table[row : row + 1, :], 0.0).astype(BF)
        spread = (column_ids == columns_ref[row : row + 1, :]).astype(F32).astype(BF)
        total = total + nt(chosen, spread)
    small_ref[...] = jnp.zeros(small_ref.shape, F32)
    small_ref[:, start:] = total
    rows = [(attention_ref, 0), (attention_ref, 1)]
    rows += [(first_ref, i) for i in range(3)] + [(second_ref, i) for i in range(3)]
    size, chunks = vector_chunks(shards)
    for piece, column, row, place in chunks:
        if row < 8:
            ref, at = rows[row]
            value = ref[at : at + 1, place : place + size]
        else:
            value = bias_ref[:, (row - 8) * D + place : (row - 8) * D + place + size]
        small_ref[piece : piece + 1, column : column + size] = value
    natural_ref[...] = jnp.zeros(natural_ref.shape, F32)
    for k in range(wide // LANES):
        natural_ref[pl.ds(k, shards, stride=each), :] = small_ref[:, k * LANES : (k + 1) * LANES]
    out_ref[...] = tn(turn_ref[...], natural_ref[...].astype(BF)).astype(BF)


def pack(shards, turn, sums_attention, sums_first, sums_second, bias, table):
    pieces, columns = position_rows(shards, True)
    return call(
        partial(pack_kernel, shards),
        (turn, pieces, columns, sums_attention, sums_first, sums_second, bias, table),
        (shaped((D, LANES), BF),),
        8,
        "pack",
        scratch=(pltpu.VMEM((D, LANES), F32), pltpu.VMEM((shards, small_lanes(shards)), F32)),
    )[0]


def lookup(table_ref, head, index, block):
    out = None
    for part in range(KEYS // LANES):
        row = jnp.broadcast_to(table_ref[head : head + 1, part * LANES : (part + 1) * LANES], index.shape)
        found = jnp.take_along_axis(row, index, axis=1, mode="promise_in_bounds")
        out = found if out is None else jnp.where(block == part, found, out)
    return out


def nt(a, b):
    return lax.dot_general(a, b, (((1,), (1,)), ((), ())), preferred_element_type=F32)


def tn(a, b):
    return lax.dot_general(a, b, (((0,), (0,)), ((), ())), preferred_element_type=F32)


def vmem(count):
    return [pl.BlockSpec(memory_space=pltpu.VMEM)] * count


def limits(mib):
    return pltpu.CompilerParams(vmem_limit_bytes=mib * 1024 * 1024)


def shaped(shape, dtype):
    return jax.ShapeDtypeStruct(tuple(shape), dtype)


def call(kernel, operands, outs, mib, name, scalars=(), scratch=()):
    return pl.pallas_call(
        kernel,
        out_shape=tuple(outs),
        in_specs=[pl.BlockSpec(memory_space=pltpu.SMEM)] * len(scalars) + vmem(len(operands)),
        out_specs=tuple(vmem(len(outs))),
        scratch_shapes=list(scratch),
        compiler_params=limits(mib),
        cost_estimate=pl.CostEstimate(flops=1, bytes_accessed=1, transcendentals=0),
        name=name,
    )(*scalars, *operands)


def stack_rows(parts, whole_ref):
    at = 0
    for part in parts:
        size = part.shape[0]
        whole_ref[at : at + size, :] = part[...]
        at += size


def stack_kernel(*refs):
    stack_rows(refs[:-1], refs[-1])


def stack(parts):
    if len(parts) == 1:
        return parts[0]
    if any(part.shape[0] % 8 for part in parts):
        return jnp.concatenate(parts, axis=0)
    rows = sum(part.shape[0] for part in parts)
    return call(stack_kernel, parts, (shaped((rows, parts[0].shape[1]), BF),), 4, "stack")[0]


def halves_kernel(near_ref, side_ref, first_ref, second_ref):
    half = first_ref.shape[0]
    first_ref[...] = near_ref[:half, :]
    second_ref[...] = side_ref[half:, :]


def halves(near, side):
    if near.shape[0] % 16:
        return near[: near.shape[0] // 2], side[near.shape[0] // 2 :]
    out = shaped((near.shape[0] // 2, near.shape[1]), BF)
    return call(halves_kernel, (near, side), (out, out), 4, "halves")


def normal(entries):
    centre = entries - jnp.mean(entries, axis=-1, keepdims=True)
    scale = lax.rsqrt(jnp.mean(centre * centre, axis=-1, keepdims=True) + layer_epsilon)
    return centre * scale, scale


def normal_back(grad, unit, scale):
    return scale * (
        grad
        - jnp.mean(grad, axis=-1, keepdims=True)
        - unit * jnp.mean(grad * unit, axis=-1, keepdims=True)
    )


def wide_dot(a, b):
    return jnp.dot(a, b, preferred_element_type=F32)


def split(value, count):
    parts = []
    for _ in range(count):
        parts.append(value.astype(BF))
        value = value - parts[-1].astype(F32)
    return parts


def joined_kernel(*refs):
    x_ref, turn_ref, vectors_ref, table_ref = refs[:4]
    parts = refs[4:-5]
    whole_ref, slots_ref, joined_ref, gate_ref, logits_ref = refs[-5:]
    stack_rows(parts, whole_ref)
    slots_ref[...] = wide_dot(x_ref[...], turn_ref[...]).astype(BF)
    for part in range(3):
        cols = slice(part * D, (part + 1) * D)
        made = wide_dot(slots_ref[...], whole_ref[:, cols])
        if part != 1:
            made = made + vectors_ref[part // 2 : part // 2 + 1, :]
        joined_ref[:, cols] = made.astype(BF)
    units = table_ref[12:20, :HD].astype(BF)
    logits_ref[...] = jnp.zeros(logits_ref.shape, F32)
    for head in range(H):
        logits_ref[:, head * gate_units : (head + 1) * gate_units] = (
            nt(x_ref[:, head * HD : (head + 1) * HD], units) + table_ref[20:21, :gate_units]
        )
    up = lax.broadcasted_iota(jnp.int32, (LANES, LANES), 0)
    across = lax.broadcasted_iota(jnp.int32, (LANES, LANES), 1)
    logits = split(logits_ref[...], 3)
    gates = []
    for side in range(2):
        chosen = ((up >> 3) == across) & (((up >> 2) & 1) == side)
        chosen = chosen.astype(F32).astype(BF)
        gates.append(jax.nn.sigmoid(sum(wide_dot(part, chosen) for part in logits)))
    first, second = gates
    gate_ref[0] = first * (second * table_ref[21:22, :LANES] - 1.0) + 2.0
    gate_ref[1] = first
    gate_ref[2] = second


def joined_forward(x, turn, vectors, table, parts):
    rows = x.shape[0]
    return call(
        joined_kernel,
        (x, turn, vectors, table, *parts),
        (
            shaped((D, parts[0].shape[1]), BF),
            shaped((rows, D), BF),
            shaped((rows, 3 * D), BF),
            shaped((3, rows, LANES), F32),
        ),
        8,
        "joined_forward",
        scratch=(pltpu.VMEM((rows, LANES), F32),),
    )


def attention_kernel(
    x_ref, turn_ref, vectors_ref, bucket_ref, valid_ref, table_ref, joined_ref, gate_ref, whole_ref,
    prob_ref, rel_ref, mixed_ref, unit_ref, scale_ref,
):
    clips, slots = bucket_ref.shape[0], bucket_ref.shape[1]
    for clip in range(clips):
        rows = slice(clip * slots, (clip + 1) * slots)
        index = bucket_ref[clip] & (LANES - 1)
        block = bucket_ref[clip] >> 7
        valid = valid_ref[clip] > 0
        for head in range(H):
            cols = slice(head * HD, (head + 1) * HD)
            query = joined_ref[rows, cols]
            key = joined_ref[rows, D + head * HD : D + (head + 1) * HD]
            value = joined_ref[rows, 2 * D + head * HD : 2 * D + (head + 1) * HD]
            rel = lookup(table_ref, head, index, block)
            rel_ref[clip, head] = rel
            score = nt(query, key) * (1.0 / math.sqrt(HD)) + gate_ref[0, rows, head : head + 1] * rel
            score = jnp.where(valid, score, masked_score)
            top = jnp.max(score, axis=-1, keepdims=True)
            power = jnp.exp(score - top)
            prob = power / jnp.sum(power, axis=-1, keepdims=True)
            prob_ref[clip, head] = prob
            mixed_ref[rows, cols] = wide_dot(prob.astype(BF), value).astype(BF)
    mixed_ref[...] = wide_dot(mixed_ref[...], turn_ref[...]).astype(BF)
    branch = wide_dot(mixed_ref[...], whole_ref[:, 3 * D : 4 * D]) + vectors_ref[2:3, :]
    unit, scale = normal(deep_alpha * x_ref[...].astype(F32) + branch)
    unit_ref[...] = unit
    scale_ref[...] = scale


def attention(x, turn, vectors, bucket, valid, table, joined, gate, whole):
    clips, slots = bucket.shape[0], bucket.shape[1]
    rows = clips * slots
    return call(
        attention_kernel,
        (x, turn, vectors, bucket, valid, table, joined, gate, whole),
        (
            shaped((clips, H, slots, slots), F32),
            shaped((clips, H, slots, slots), F32),
            shaped((rows, D), BF),
            shaped((rows, D), F32),
            shaped((rows, 1), F32),
        ),
        6,
        "attention",
    )


def attention_back_kernel(
    x_ref, table_ref, joined_ref, gate_ref, rank_ref, prob_ref, rel_ref, grad_ref, tri_ref,
    joined_grad_ref, x_grad_ref, table_grad_ref, sums_ref, gate_grad_ref,
):
    clips, slots = rank_ref.shape[0], rank_ref.shape[1]
    scale = 1.0 / math.sqrt(HD)
    gate_grad_ref[...] = jnp.zeros(gate_grad_ref.shape, F32)
    table_grad_ref[...] = jnp.zeros(table_grad_ref.shape, F32)
    for clip in range(clips):
        rows = slice(clip * slots, (clip + 1) * slots)
        for head in range(H):
            cols = slice(head * HD, (head + 1) * HD)
            key_cols = slice(D + head * HD, D + (head + 1) * HD)
            value_cols = slice(2 * D + head * HD, 2 * D + (head + 1) * HD)
            query = joined_ref[rows, cols]
            key = joined_ref[rows, key_cols]
            value = joined_ref[rows, value_cols]
            grad = grad_ref[rows, cols]
            prob = prob_ref[clip, head]
            joined_grad_ref[rows, value_cols] = tn(prob.astype(BF), grad).astype(BF)
            prob_grad = nt(grad, value)
            weighted = prob * prob_grad
            low = (weighted - prob * jnp.sum(weighted, axis=-1, keepdims=True)).astype(BF)
            joined_grad_ref[rows, cols] = (wide_dot(low, key) * scale).astype(BF)
            joined_grad_ref[rows, key_cols] = (tn(low, query) * scale).astype(BF)
            wide = low.astype(F32)
            gate_grad_ref[rows, head : head + 1] = jnp.sum(
                wide * rel_ref[clip, head], axis=-1, keepdims=True
            )
            gated = wide * gate_ref[0, rows, head : head + 1]
            high = gated.astype(BF)
            rest = (gated - high.astype(F32)).astype(BF)
            running = wide_dot(high, tri_ref[...]) + wide_dot(rest, tri_ref[...])
            for part in range(KEYS // LANES):
                lanes = slice(part * LANES, (part + 1) * LANES)
                rank = rank_ref[clip, :, lanes]
                found = jnp.take_along_axis(
                    running, jnp.maximum(rank - 1, 0), axis=1, mode="promise_in_bounds"
                )
                total = jnp.sum(jnp.where(rank > 0, found, 0.0), axis=0, keepdims=True)
                table_grad_ref[head : head + 1, lanes] += total
    sums_ref[0:1, :] = jnp.sum(joined_grad_ref[:, :D].astype(F32), axis=0, keepdims=True)
    sums_ref[1:2, :] = jnp.sum(joined_grad_ref[:, 2 * D :].astype(F32), axis=0, keepdims=True)
    units = [jnp.sum(table_ref[12 + 4 * i : 16 + 4 * i, :HD], axis=0, keepdims=True) for i in range(2)]
    unit_grads = [jnp.zeros((1, HD), F32), jnp.zeros((1, HD), F32)]
    bias_grads = [jnp.zeros((1, 1), F32), jnp.zeros((1, 1), F32)]
    grad, first, second = gate_grad_ref[...], gate_ref[1], gate_ref[2]
    size = table_ref[21:22, :LANES]
    grads = (
        grad * (second * size - 1.0) * first * (1.0 - first),
        grad * first * size * second * (1.0 - second),
    )
    table_grad_ref[21:22, :LANES] = jnp.sum(grad * first * second, axis=0, keepdims=True)
    for i in range(2):
        bias_grads[i] = jnp.sum(jnp.sum(grads[i], axis=0, keepdims=True), axis=1, keepdims=True)
    for head in range(H):
        cols = slice(head * HD, (head + 1) * HD)
        x = x_ref[:, cols].astype(F32)
        sides = [grads[i][:, head : head + 1] for i in range(2)]
        x_grad_ref[:, cols] = sides[0] * units[0] + sides[1] * units[1]
        for i in range(2):
            unit_grads[i] = unit_grads[i] + jnp.sum(x * sides[i], axis=0, keepdims=True)
    for unit in range(gate_units):
        table_grad_ref[12 + unit : 13 + unit, :HD] = unit_grads[unit // 4]
        table_grad_ref[20:21, unit : unit + 1] = bias_grads[unit // 4]


def attention_back(x, table, joined, gate, rank, prob, rel, grad):
    clips, slots = rank.shape[0], rank.shape[1]
    tri = jnp.asarray(np.triu(np.ones((slots, slots), np.float32)), BF)
    return call(
        attention_back_kernel,
        (x, table, joined, gate, rank, prob, rel, grad, tri),
        (
            shaped((clips * slots, 3 * D), BF),
            shaped((clips * slots, D), F32),
            shaped((24, KEYS), F32),
            shaped((8, D), F32),
        ),
        6,
        "attention_back",
        scratch=(pltpu.VMEM((clips * slots, LANES), F32),),
    )


def gelu_pair(u):
    size = jnp.abs(u) * math.sqrt(0.5)
    t = 1.0 / (1.0 + 0.3275911 * size)
    poly = ((((1.061405429 * t - 1.453152027) * t + 1.421413741) * t - 0.284496736) * t + 0.254829592) * t
    bell = jnp.exp(-0.5 * u * u)
    tail = 0.5 * poly * bell
    below = jnp.where(u < 0, tail, 1.0 - tail)
    return u * below, below + u * bell * (1.0 / math.sqrt(2.0 * math.pi))


def hidden_kernel(*refs):
    unit_ref, vectors_ref, turn_ref, bias_ref = refs[:4]
    parts = refs[4:-4]
    whole_ref, slots_ref, active_ref, slope_ref = refs[-4:]
    stack_rows(parts, whole_ref)
    low = (unit_ref[...] * vectors_ref[3:4, :] + vectors_ref[4:5, :]).astype(BF)
    slots_ref[...] = wide_dot(low, turn_ref[...]).astype(BF)
    width = FF // 8
    for block in range(8):
        cols = slice(block * width, (block + 1) * width)
        u = wide_dot(slots_ref[...], whole_ref[:, cols]) + bias_ref[:, cols]
        active, slope = gelu_pair(u)
        active_ref[:, cols] = active.astype(BF)
        slope_ref[:, cols] = slope


def hidden_forward(unit, vectors, turn, bias, parts):
    rows = unit.shape[0]
    return call(
        hidden_kernel,
        (unit, vectors, turn, bias, *parts),
        (shaped((D, FF), BF), shaped((rows, D), BF), shaped((rows, FF), BF), shaped((rows, FF), F32)),
        10,
        "hidden_forward",
    )


def turn_kernel(chunk, *refs):
    at_ref, active_ref, unit_ref, vectors_ref, valid_ref, cot_ref = refs[:6]
    parts = refs[6:-5]
    whole_ref, out_ref, second_ref, low_ref, sums_ref = refs[-5:]
    slot = 0
    for part in parts:
        for first in range(0, part.shape[0], chunk):
            place = pl.multiple_of(at_ref[slot], 16)
            whole_ref[pl.ds(place, chunk), :] = part[first : first + chunk, :]
            slot += 1
    made = wide_dot(active_ref[...], whole_ref[...]) + vectors_ref[5:6, :]
    first_norm = unit_ref[...] * vectors_ref[3:4, :] + vectors_ref[4:5, :]
    unit, scale = normal(deep_alpha * first_norm + made.astype(BF).astype(F32))
    valid = valid_ref[...]
    gain = vectors_ref[6:7, :]
    out_ref[...] = ((unit * gain + vectors_ref[7:8, :]) * valid).astype(BF)
    grad = cot_ref[...].astype(F32) * valid
    second = normal_back(grad * gain, unit, scale)
    second_ref[...] = second
    low = second.astype(BF)
    low_ref[...] = low
    sums_ref[0:1, :] = jnp.sum(low.astype(F32), axis=0, keepdims=True)
    sums_ref[1:2, :] = jnp.sum(grad * unit, axis=0, keepdims=True)
    sums_ref[2:3, :] = jnp.sum(grad, axis=0, keepdims=True)


def turn_back(at, chunk, active, unit, vectors, valid, cot, parts):
    rows = unit.shape[0]
    return call(
        partial(turn_kernel, chunk),
        (active, unit, vectors, valid, cot, *parts),
        (shaped((FF, D), BF), shaped((rows, D), BF), shaped((rows, D), F32), shaped((rows, D), BF), shaped((8, D), F32)),
        10,
        "turn_back",
        scalars=(at,),
    )


def down_back_kernel(chunk, at_ref, active_ref, low_ref, mine_ref, other_ref, made_ref):
    for first in range(0, FF, FF // 8):
        made_ref[first : first + FF // 8, :] = tn(
            active_ref[:, first : first + FF // 8], low_ref[...]
        ).astype(BF)
    half = FF // 2
    for slot in range(FF // chunk):
        ref = mine_ref if slot * chunk < half else other_ref
        place = pl.multiple_of(at_ref[slot], chunk)
        ref[slot * chunk % half : slot * chunk % half + chunk, :] = made_ref[pl.ds(place, chunk), :]


def down_back(at, chunk, active, low):
    rows = low.shape[0]
    return call(
        partial(down_back_kernel, chunk),
        (active, low),
        (shaped((FF // 2, D), BF), shaped((FF // 2, D), BF)),
        10,
        "down_back",
        scalars=(at,),
        scratch=(pltpu.VMEM((FF, D), BF),),
    )


def hidden_back_kernel(low_ref, down_ref, slope_ref, grad_ref, bias_ref):
    width = FF // 8
    for block in range(8):
        cols = slice(block * width, (block + 1) * width)
        grad = (nt(low_ref[...], down_ref[cols, :]) * slope_ref[:, cols]).astype(BF)
        grad_ref[:, cols] = grad
        bias_ref[:, cols] = jnp.sum(grad.astype(F32), axis=0, keepdims=True)


def hidden_back(low, down, slope):
    rows = low.shape[0]
    return call(
        hidden_back_kernel,
        (low, down, slope),
        (shaped((rows, FF), BF), shaped((1, FF), F32)),
        6,
        "hidden_back",
    )


def in_back_kernel(slots_ref, grad_ref, mine_ref, other_ref):
    width = FF // 4
    for block in range(4):
        cols = slice(block * width, (block + 1) * width)
        made = tn(slots_ref[...], grad_ref[:, cols]).astype(BF)
        mine_ref[:, cols] = made[: D // 2]
        other_ref[:, cols] = made[D // 2 :]


def in_back(slots, grad):
    rows = slots.shape[0]
    return call(
        in_back_kernel,
        (slots, grad),
        (shaped((D // 2, FF), BF), shaped((D // 2, FF), BF)),
        6,
        "in_back",
    )


def out_back_kernel(
    grad_ref, in_ref, turn_ref, second_ref, unit_ref, scale_ref, vectors_ref, mixed_ref, out_ref,
    first_ref, weight_ref, mixed_grad_ref, sums_ref,
):
    low = nt(grad_ref[...], in_ref[...]).astype(BF)
    grad = deep_alpha * second_ref[...] + nt(low, turn_ref[...]).astype(BF).astype(F32)
    unit = unit_ref[...]
    first = normal_back(grad * vectors_ref[3:4, :], unit, scale_ref[...])
    first_ref[...] = first
    branch = first.astype(BF)
    sums_ref[0:1, :] = jnp.sum(branch.astype(F32), axis=0, keepdims=True)
    sums_ref[1:2, :] = jnp.sum(grad * unit, axis=0, keepdims=True)
    sums_ref[2:3, :] = jnp.sum(grad, axis=0, keepdims=True)
    weight_ref[...] = tn(mixed_ref[...], branch).astype(BF)
    back = nt(branch, out_ref[:, 3 * D : 4 * D]).astype(BF)
    mixed_grad_ref[...] = nt(back, turn_ref[...]).astype(BF)


def out_back(grad, w_in, turn, second, unit, scale, vectors, mixed, w_first):
    rows = unit.shape[0]
    return call(
        out_back_kernel,
        (grad, w_in, turn, second, unit, scale, vectors, mixed, w_first),
        (shaped((rows, D), F32), shaped((D, D), BF), shaped((rows, D), BF), shaped((8, D), F32)),
        6,
        "out_back",
    )


def first_back_kernel(slots_ref, grad_ref, out_ref, small_ref, mine_ref, other_ref):
    half = D // 2
    for part in range(3):
        cols = slice(part * D, (part + 1) * D)
        made = tn(slots_ref[...], grad_ref[:, cols]).astype(BF)
        mine_ref[:, cols] = made[:half]
        other_ref[:, cols] = made[half:]
    for ref, rows in ((mine_ref, slice(0, half)), (other_ref, slice(half, D))):
        ref[:, 3 * D : 4 * D] = out_ref[rows, :]
        ref[:, 4 * D :] = small_ref[rows, :]


def first_back(slots, grad, weight_out, small):
    rows = slots.shape[0]
    wide = 4 * D + small.shape[1]
    return call(
        first_back_kernel,
        (slots, grad, weight_out, small),
        (shaped((D // 2, wide), BF), shaped((D // 2, wide), BF)),
        6,
        "first_back",
    )


def rows_back_kernel(grad_ref, first_ref, turn_ref, branch_ref, gate_ref, out_ref):
    made = nt(grad_ref[...], first_ref[:, : 3 * D])
    high = made.astype(BF)
    rest = made - high.astype(F32)
    middle = rest.astype(BF)
    last = (rest - middle.astype(F32)).astype(BF)
    turned = nt(high, turn_ref[...]) + nt(middle, turn_ref[...]) + nt(last, turn_ref[...])
    out_ref[...] = turned + deep_alpha * branch_ref[...] + gate_ref[...]


def rows_back(grad, w_first, turn, branch, gate):
    rows = grad.shape[0]
    return call(
        rows_back_kernel,
        (grad, w_first, turn, branch, gate),
        (shaped((rows, D), F32),),
        8,
        "rows_back",
    )[0]


def join_kernel(mine_ref, other_ref, *outs):
    at = 0
    for out in outs:
        rows = slice(at, at + out.shape[0])
        out[...] = (mine_ref[rows, :].astype(F32) + other_ref[rows, :].astype(F32)).astype(BF)
        at += out.shape[0]


def join(mine, other):
    size, wide = mine.shape[0] // 4, mine.shape[1]
    cuts = (size, size, size, size // 2, size // 2)
    return call(join_kernel, (mine, other), [shaped((cut, wide), BF) for cut in cuts], 4, "join")


def bend_kernel(near_ref, side_ref, first_ref, second_ref, near_out, side_out):
    half = first_ref.shape[0]
    near_out[...] = near_ref[...]
    side_out[...] = side_ref[...]
    near_out[:half, :] = (near_ref[:half, :].astype(F32) + first_ref[...].astype(F32)).astype(BF)
    side_out[half:, :] = (side_ref[half:, :].astype(F32) + second_ref[...].astype(F32)).astype(BF)


def bend(near, side, first, second):
    return call(bend_kernel, (near, side, first, second), (shaped(near.shape, BF),) * 2, 4, "bend")


def flat_cuts(each, wide_rows):
    cuts = [(0, row, 0, 3 * D) for row in range(each)]
    cuts += [(0, row, 3 * D, 4 * D) for row in range(each)]
    cuts += [(1, row, 0, FF) for row in range(each)]
    cuts += [(2, row, 0, D) for row in range(wide_rows)]
    return cuts + [(0, row, 4 * D, 4 * D + LANES) for row in range(each)]


def flat_runs(each, wide_rows, width):
    at = 0
    for which, row, first, last in flat_cuts(each, wide_rows):
        size = min(last - first, width - at)
        if size > 0:
            yield which, row, first, size, at
        at += last - first


def pieces_kernel(flat_ref, first_ref, in_ref, down_ref, *lows):
    refs = (first_ref, in_ref, down_ref)
    first_ref[:, 4 * D :] = jnp.zeros((first_ref.shape[0], LANES), F32)
    for which, row, first, size, at in flat_runs(first_ref.shape[0], down_ref.shape[0], flat_ref.shape[1]):
        refs[which][row : row + 1, first : first + size] = flat_ref[:, at : at + size]
    for ref, low in zip(refs, lows):
        low[...] = ref[...].astype(BF)


def pieces(flat, each, wide_rows, low):
    shapes = ((each, 4 * D + LANES), (each, FF), (wide_rows, D))
    outs = [shaped(shape, F32) for shape in shapes] + [shaped(shape, BF) for shape in shapes if low]
    return call(pieces_kernel, (flat,), outs, 6, "pieces")


def update_kernel(learning, counts, *refs):
    sums, at = [], 0
    for count in counts:
        sums.append(refs[at : at + count])
        at += count
    weights, momenta, averages = refs[at : at + 3], refs[at + 3 : at + 6], refs[at + 6 : at + 9]
    outs, rows = refs[at + 9 : at + 12], refs[at + 12 :]
    grads = [sum(ref[...].astype(F32) for ref in part) for part in sums]
    for i in range(3):
        weight = weights[i][...]
        decayed = grads[i] + decay_rate * weight
        momentum = momentum_rate * momenta[i][...] + decayed
        weight = weight - learning * (decayed + momentum_rate * momentum)
        rows[i][...] = momentum
        rows[3 + i][...] = average_rate * averages[i][...] + (1.0 - average_rate) * weight
        rows[6 + i][...] = weight
    for out, which in zip(outs, (0, 3, 6)):
        for section, row, first, size, at in flat_runs(rows[0].shape[0], rows[2].shape[0], out.shape[1]):
            out[:, at : at + size] = rows[which + section][row : row + 1, first : first + size]


def update(learning, sums, weights, momenta, averages, width):
    operands = [ref for part in sums for ref in part] + [*weights, *momenta, *averages]
    rows = [pltpu.VMEM(part.shape, F32) for part in weights] * 3
    return call(
        partial(update_kernel, learning, [len(part) for part in sums]),
        operands,
        (shaped((1, width), F32),) * 3,
        8,
        "update",
        scratch=rows,
    )


def halve_kernel(*refs):
    *parts, keep_ref, send_ref = refs
    half = keep_ref.shape[0]
    for out, rows in ((keep_ref, slice(0, half)), (send_ref, slice(half, 2 * half))):
        out[...] = sum(part[rows, :].astype(F32) for part in parts).astype(BF)


def halve(parts):
    half, wide = parts[0].shape[0] // 2, parts[0].shape[1]
    if half % 8:
        total = sum(part.astype(F32) for part in parts).astype(BF)
        return total[:half], total[half:]
    return call(halve_kernel, parts, (shaped((half, wide), BF),) * 2, 4, "halve")


def column_kernel(own_ref, near_ref, side_ref, *outs):
    size = outs[0].shape[0]
    for at, out in enumerate(outs):
        rows = slice(at * size, (at + 1) * size)
        total = own_ref[rows, :].astype(F32) + near_ref[rows, :].astype(F32) + side_ref[rows, :].astype(F32)
        out[...] = total.astype(out.dtype)


def column_parts(own, near, side, parts):
    size, wide = own.shape[0] // parts, own.shape[1]
    outs = [shaped((size, wide), BF)] * parts
    if size % 8:
        total = own.astype(F32) + near.astype(F32) + side.astype(F32)
        return [total[i * size : (i + 1) * size].astype(out.dtype) for i, out in enumerate(outs)]
    return call(column_kernel, (own, near, side), outs, 4, "column_parts")


def body(acts, cotangent, mask, shape_id, weights, momenta, averages):
    shards = lax.axis_size(("dp", "fsdp"))
    count = lax.axis_size("dp")
    dp, core = lax.axis_index("dp"), lax.axis_index("fsdp")
    clips, slots = acts.shape[0], acts.shape[1]
    rows = clips * slots
    total_tokens = rows * shards
    piece_rows = D // shards
    wide_rows = FF // shards
    vector_width = 12 * D // shards
    position_width = (NPOS + shards - 1) // shards
    small_width = vector_width + position_width

    weight_rows = pieces(weights, piece_rows, wide_rows, True)
    weight_rows, (piece_first, piece_in, piece_down) = weight_rows[:3], weight_rows[3:]

    order = slot_order(dp, core, count)
    row_order = (order[:, None] * piece_rows + jnp.arange(piece_rows, dtype=jnp.int32)).reshape(-1)
    turn = (jnp.arange(D, dtype=jnp.int32)[:, None] == row_order[None, :]).astype(BF)
    piece_turn = (jnp.arange(shards, dtype=jnp.int32)[:, None] == order[None, :]).astype(BF)

    back_order = jnp.dot(piece_turn.astype(F32), jnp.arange(shards, dtype=F32)).astype(jnp.int32)

    def both_cores(parts):
        return tuple(parts) + tuple(exchange(part, "fsdp", 1) for part in parts)

    inputs_low = acts.reshape(rows, D)
    together = lax.optimization_barrier
    chunk = wide_rows
    at = order * wide_rows
    bits = high_bits(count)
    low_bits, top_bits = bits[: len(bits) // 2], bits[len(bits) // 2 :]

    column_first = gather_column(piece_first)
    column_in = gather_bits(piece_in, low_bits)
    momenta_rows = pieces(momenta, piece_rows, wide_rows, False)
    averages_rows = pieces(averages, piece_rows, wide_rows, False)
    column_first, column_in, piece_down, mask, turn, at, momenta_rows, averages_rows = together(
        (column_first, column_in, piece_down, mask, turn, at, momenta_rows, averages_rows)
    )

    sides_first = gather_sides(column_first)
    column_in = gather_bits(stack(column_in), top_bits)
    bucket, rank, valid_rows, valid_wide = prep(mask, shape_id, slots)
    sides_first, column_in, piece_down, bucket, rank, valid_rows, valid_wide = together(
        (sides_first, column_in, piece_down, bucket, rank, valid_rows, valid_wide)
    )

    corner_first = gather_corner(*sides_first)
    column_down = gather_bits(piece_down, low_bits)
    early_first = other_core((column_first, *sides_first))
    corner_first, early_first, column_in, column_down = together(
        (corner_first, early_first, column_in, column_down)
    )

    column_in = stack(column_in)
    sides_in = gather_sides(column_in)
    column_down = gather_bits(stack(column_down), top_bits)
    parts_first = (column_first, *sides_first, *corner_first, early_first, other_core(corner_first))
    vectors, bias_in, table = unpack(shards, turn, parts_first)
    w_first, inputs_slots, joined, gate = joined_forward(inputs_low, turn, vectors, table, parts_first)
    prob, rel, mixed_slots, unit, unit_scale = attention(
        inputs_low, turn, vectors, bucket, valid_wide, table, joined, gate, w_first
    )
    sides_in, column_down, unit = together((sides_in, column_down, unit))

    column_down = stack(column_down)
    corner_in = gather_corner(*sides_in)
    sides_down = gather_sides(column_down)
    early_in = other_core((column_in, *sides_in))
    corner_in, sides_down, early_in = together((corner_in, sides_down, early_in))

    corner_down = gather_corner(*sides_down)
    early_down = other_core((column_down, *sides_down))
    parts_in = (column_in, *sides_in, *corner_in, early_in, other_core(corner_in))
    w_in, first_slots, active, slope = hidden_forward(unit, vectors, turn, bias_in, parts_in)
    corner_down, early_down, active = together((corner_down, early_down, active))

    parts_down = (column_down, *sides_down, *corner_down, early_down, other_core(corner_down))
    if chunk % 16:
        stacked = jnp.concatenate(parts_down, axis=0).reshape(shards, wide_rows, D)
        parts_down = (jnp.take(stacked, back_order, axis=0).reshape(FF, D),)
        chunk = FF
        at = jnp.zeros((1,), jnp.int32)
    w_down, activations, grad_second, grad_made, sums_second = turn_back(
        at, chunk, active, unit, vectors, valid_rows, cotangent.reshape(rows, D), parts_down
    )

    if chunk == FF:
        grad_down = tn(active, grad_made).astype(BF).reshape(shards, wide_rows, D)
        grad_down = jnp.take(grad_down, order, axis=0).reshape(FF, D)
        down_mine, down_other = grad_down[: FF // 2], grad_down[FF // 2 :]
    else:
        down_mine, down_other = down_back(at, chunk, active, grad_made)
    down_mine, down_other, grad_made = together((down_mine, down_other, grad_made))

    down_other = exchange(down_other, "fsdp", 1)
    grad_hidden, grad_bias_in = hidden_back(grad_made, w_down, slope)
    in_mine, in_other = in_back(first_slots, grad_hidden)
    down_other, grad_hidden, in_mine, in_other = together((down_other, grad_hidden, in_mine, in_other))

    down_own, down_near, down_side, *down_corner = join(down_mine, down_other)
    down_corner = scatter_corner(*down_corner)
    in_other = exchange(in_other, "fsdp", 1)
    grad_first_sum, grad_out, grad_mixed, sums_first = out_back(
        grad_hidden, w_in, turn, grad_second, unit, unit_scale, vectors, mixed_slots, w_first
    )
    down_corner, in_other, grad_mixed = together((down_corner, in_other, grad_mixed))

    down_sides = scatter_sides(*bend(down_near, down_side, *down_corner))
    in_own, in_near, in_side, *in_corner = join(in_mine, in_other)
    in_corner = scatter_corner(*in_corner)
    grad_joined, grad_gate_inputs, table_grad, sums_attention = attention_back(
        inputs_low, table, joined, gate, rank, prob, rel, grad_mixed
    )
    grad_small = pack(shards, turn, sums_attention, sums_first, sums_second, grad_bias_in, table_grad)
    first_mine, first_other = first_back(inputs_slots, grad_joined, grad_out, grad_small)
    down_sides, in_corner, first_mine, first_other, grad_joined = together(
        (down_sides, in_corner, first_mine, first_other, grad_joined)
    )

    in_sides = scatter_sides(*bend(in_near, in_side, *in_corner))
    down_sums = scatter_bits((down_own, *down_sides), top_bits)
    first_other = exchange(first_other, "fsdp", 1)
    first_own, first_near, first_side, *first_corner = join(first_mine, first_other)
    first_corner = scatter_corner(*first_corner)
    input_grad = rows_back(grad_joined, w_first, turn, grad_first_sum, grad_gate_inputs)
    in_sides, down_sums, first_corner, input_grad = together((in_sides, down_sums, first_corner, input_grad))

    first_sides = scatter_sides(*bend(first_near, first_side, *first_corner))
    in_sums = scatter_bits((in_own, *in_sides), top_bits)
    down_sums = scatter_bits(down_sums, low_bits)
    first_sides, in_sums, down_sums = together((first_sides, in_sums, down_sums))

    first_sums = scatter_high(column_parts(first_own, *first_sides, count // 4), piece_rows)
    in_sums = scatter_bits(in_sums, low_bits)

    learning = rate_scale / math.sqrt(total_tokens)
    momenta_new, averages_new, weights_new = update(
        learning,
        (first_sums, in_sums, down_sums),
        weight_rows,
        momenta_rows,
        averages_rows,
        weights.shape[1],
    )
    return (
        activations.reshape(acts.shape),
        input_grad.reshape(acts.shape),
        momenta_new,
        averages_new,
        weights_new,
        weights_new.astype(BF),
    )


def solution(mesh):
    split = ("dp", "fsdp")
    in_specs = (
        P(split, None, None),
        P(split, None, None),
        P(split, None),
        P(split),
        P(split, None),
        P(split, None),
        P(split, None),
    )
    out_specs = (
        P(split, None, None),
        P(split, None, None),
        P(split, None),
        P(split, None),
        P(split, None),
        P(split, None),
    )
    return jax.shard_map(body, mesh=mesh, in_specs=in_specs, out_specs=out_specs, check_vma=False)
```

```python
from functools import partial
import math

import jax
import jax.numpy as jnp
import numpy as np
from jax import lax
from jax.experimental import pallas as pl
from jax.experimental.pallas import tpu as pltpu
from jax.sharding import PartitionSpec as P

D = 768
H = 12
HD = 64
FF = 3072
NB = 320
HALF = NB // 2
P_SIZE = 512
NPOS = 4372
LANES = 128
KEYS = 384
BF = jnp.bfloat16
F32 = jnp.float32

deep_alpha = 24.0**0.25
layer_epsilon = 1e-05
masked_score = -1000000000.0
far_distance = 800
gate_units = 8
momentum_rate = 0.9
average_rate = 0.8
decay_rate = 0.0001
rate_scale = 0.04
far_place = 1 << 20


def bucket_levels(span):
    distance = np.arange(0, span + 1)
    exact = HALF // 2
    logscale = (
        np.log(np.maximum(distance, 1) / exact) / np.log(far_distance / exact) * (HALF - exact)
    )
    beyond = np.minimum(exact + np.floor(logscale).astype(np.int64), HALF - 1)
    return np.where(distance < exact, distance, beyond)


def far_marks():
    levels = bucket_levels(2 * P_SIZE)
    rises = np.diff(levels)
    marks = np.repeat(np.arange(1, 2 * P_SIZE + 1), rises)
    return [int(m) for m in marks[HALF // 2 :]]


def key_ends():
    span = 2 * P_SIZE
    levels = bucket_levels(span)
    offsets = np.arange(-span, span + 1)
    level = levels[np.abs(offsets)]
    keys = np.where(offsets > 0, HALF + level, HALF - 1 - level)
    ends = np.full((KEYS,), far_place // 2, np.int32)
    for key in range(NB - 1):
        below = offsets[keys <= key]
        ends[key] = below.max() if below.size else -(far_place // 2)
    return ends


def exchange(value, axis, mask):
    count = lax.axis_size(axis)
    return lax.ppermute(value, axis, [(i, i ^ mask) for i in range(count)])


def high_bits(count):
    return list(range(2, count.bit_length() - 1))


def exchange_sides(pair):
    return exchange(pair[0], "dp", 1), exchange(pair[1], "dp", 2)


def exchange_core(value):
    return exchange(value, "fsdp", 1)


def slot_order(dp, core, count):
    high = count // 4
    core_step, low, up = np.meshgrid(np.arange(2), np.arange(4), np.arange(high), indexing="ij")
    distance = jnp.asarray((up * 4 + low).reshape(-1).astype(np.int32))
    core_distance = jnp.asarray(core_step.reshape(-1).astype(np.int32))
    return (distance ^ dp) * 2 + (core_distance ^ core)


def prep_kernel(marks, shape_ref, mask_ref, ends_ref, bucket_ref, rank_ref, valid_ref, valid_row_ref):
    clips, patches = mask_ref.shape
    slots = bucket_ref.shape[1]
    mask = mask_ref[...]
    up = lax.broadcasted_iota(jnp.int32, (patches, patches), 0)
    across = lax.broadcasted_iota(jnp.int32, (patches, patches), 1)
    running = wide_dot(mask.astype(F32).astype(BF), (up <= across).astype(F32).astype(BF))
    ranks = jnp.where(mask == 1, running.astype(jnp.int32) - 1, -1)
    slot = lax.broadcasted_iota(jnp.int32, (slots, patches), 0)
    patch = lax.broadcasted_iota(jnp.int32, (slots, patches), 1)
    pair = lax.broadcasted_iota(jnp.int32, (8, patches), 1)
    halves = jnp.where(lax.broadcasted_iota(jnp.int32, (8, patches), 0) == 0, pair >> 4, pair & 15)
    halves = halves.astype(F32).astype(BF)
    for clip in range(clips):
        found = ranks[clip : clip + 1, :] == slot
        column = jnp.sum(jnp.where(found, patch, 0), axis=1, keepdims=True)
        both = nt(halves, found.astype(F32).astype(BF)).astype(jnp.int32)
        row = 16 * both[0:1, :] + both[1:2, :]
        narrow = shape_ref[clip] > 0
        column = jnp.where(narrow, 8 * (column >> 2) + (column & 3), column)
        row = jnp.where(narrow, 8 * (row >> 2) + (row & 3), row)
        count = jnp.sum(mask[clip : clip + 1, :], axis=1, keepdims=True)
        valid = lax.broadcasted_iota(jnp.int32, (slots, 1), 0) < count
        valid_ref[clip * slots : (clip + 1) * slots, :] = valid.astype(F32)
        valid_row_ref[clip] = (lax.broadcasted_iota(jnp.int32, (1, slots), 1) < count).astype(jnp.int32)
        offset = row - column
        distance = jnp.abs(offset)
        level = jnp.minimum(distance, HALF // 2)
        for mark in marks:
            level = level + (distance >= mark).astype(jnp.int32)
        bucket_ref[clip] = level + jnp.where(offset > 0, HALF, 0)
        away = jnp.where(valid, column - row, far_place)
        for first in range(slots):
            seen = away[:, first : first + 1] <= ends_ref[...]
            rank_ref[clip, first : first + 1, :] = jnp.sum(seen.astype(jnp.int32), axis=0, keepdims=True)


def prep(mask, shape_id, slots):
    clips = mask.shape[0]
    ends = jnp.asarray(key_ends())[None, :]
    return call(
        partial(prep_kernel, far_marks()),
        (mask, ends),
        (
            shaped((clips, slots, slots), jnp.int32),
            shaped((clips, slots, KEYS), jnp.int32),
            shaped((clips * slots, 1), F32),
            shaped((clips, 1, slots), jnp.int32),
        ),
        8,
        "prep",
        scalars=(shape_id,),
    )


def position_rows(shards, by_key):
    width = (NPOS + shards - 1) // shards
    index = np.full((24, KEYS), -1, np.int64)
    for head in range(H):
        for lane in range(NB):
            bucket = (HALF - 1 - lane if lane < HALF else lane) if by_key else lane
            index[head, lane] = bucket * H + head
    for unit in range(gate_units):
        index[12 + unit, :HD] = NB * H + np.arange(HD) * gate_units + unit
    index[20, :gate_units] = (NB + 0) * H + HD * gate_units + np.arange(gate_units)
    index[21, :H] = NB * H + (HD + 1) * gate_units + np.arange(H)
    pieces = np.where(index >= 0, index // width, -1).astype(np.int32)
    columns = np.where(index >= 0, 12 * D // shards + index % width, -1).astype(np.int32)
    return jnp.asarray(pieces), jnp.asarray(columns)


def vector_chunks(shards):
    width = 12 * D // shards
    size = math.gcd(width, D)
    each, across = width // size, D // size
    return size, [
        (g // each, g % each * size, g // across, g % across * size) for g in range(12 * across)
    ]


def unpack_kernel(shards, turn_ref, pieces_ref, columns_ref, *refs):
    whole_ref, vectors_ref, bias_ref, table_ref, natural_ref, small_ref = refs
    natural_ref[...] = wide_dot(turn_ref[...], whole_ref[:, 4 * D :])
    each = D // shards
    wide = small_ref.shape[1]
    for k in range(wide // LANES):
        small_ref[:, k * LANES : (k + 1) * LANES] = natural_ref[pl.ds(k, shards, stride=each), :]
    size, chunks = vector_chunks(shards)
    for piece, column, row, place in chunks:
        value = small_ref[piece : piece + 1, column : column + size]
        if row < 8:
            vectors_ref[row : row + 1, place : place + size] = value
        else:
            bias_ref[:, (row - 8) * D + place : (row - 8) * D + place + size] = value
    start = 12 * D // shards // LANES * LANES
    small = small_ref[:, start:].astype(BF)
    piece_ids = lax.broadcasted_iota(jnp.int32, (shards, KEYS), 0)
    column_ids = lax.broadcasted_iota(jnp.int32, (wide - start, KEYS), 0) + start
    for row in range(22):
        chosen = (piece_ids == pieces_ref[row : row + 1, :]).astype(F32).astype(BF)
        spread = tn(small, chosen)
        table_ref[row : row + 1, :] = jnp.sum(
            jnp.where(column_ids == columns_ref[row : row + 1, :], spread, 0.0), axis=0, keepdims=True
        )
    table_ref[22:24, :] = jnp.zeros((2, KEYS), F32)


def small_lanes(shards):
    return -(-(12 * D // shards + (NPOS + shards - 1) // shards) // LANES) * LANES


def unpack(shards, turn, whole):
    pieces, columns = position_rows(shards, False)
    return call(
        partial(unpack_kernel, shards),
        (turn, pieces, columns, whole),
        (shaped((8, D), F32), shaped((1, FF), F32), shaped((24, KEYS), F32)),
        8,
        "unpack",
        scratch=(
            pltpu.VMEM((D, LANES), F32),
            pltpu.VMEM((shards, small_lanes(shards)), F32),
        ),
    )


def pack_kernel(shards, turn_ref, pieces_ref, columns_ref, attention_ref, first_ref, second_ref, bias_ref, table_ref, out_ref, natural_ref, small_ref):
    each = D // shards
    wide = small_ref.shape[1]
    table = table_ref[...]
    lane = lax.broadcasted_iota(jnp.int32, table.shape, 1)
    row_id = lax.broadcasted_iota(jnp.int32, table.shape, 0)
    before = jnp.where((lane > 0) & (row_id < H), pltpu.roll(table, 1, 1), 0.0)
    table = table - before
    piece_ids = lax.broadcasted_iota(jnp.int32, (shards, KEYS), 0)
    start = 12 * D // shards // LANES * LANES
    column_ids = lax.broadcasted_iota(jnp.int32, (wide - start, KEYS), 0) + start
    total = jnp.zeros((shards, wide - start), F32)
    for row in range(22):
        chosen = jnp.where(piece_ids == pieces_ref[row : row + 1, :], table[row : row + 1, :], 0.0).astype(BF)
        spread = (column_ids == columns_ref[row : row + 1, :]).astype(F32).astype(BF)
        total = total + nt(chosen, spread)
    small_ref[...] = jnp.zeros(small_ref.shape, F32)
    small_ref[:, start:] = total
    rows = [(attention_ref, 0), (attention_ref, 1)]
    rows += [(first_ref, i) for i in range(3)] + [(second_ref, i) for i in range(3)]
    size, chunks = vector_chunks(shards)
    for piece, column, row, place in chunks:
        if row < 8:
            ref, at = rows[row]
            value = ref[at : at + 1, place : place + size]
        else:
            value = bias_ref[:, (row - 8) * D + place : (row - 8) * D + place + size]
        small_ref[piece : piece + 1, column : column + size] = value
    natural_ref[...] = jnp.zeros(natural_ref.shape, F32)
    for k in range(wide // LANES):
        natural_ref[pl.ds(k, shards, stride=each), :] = small_ref[:, k * LANES : (k + 1) * LANES]
    out_ref[...] = tn(turn_ref[...], natural_ref[...].astype(BF)).astype(BF)


def pack(shards, turn, sums_attention, sums_first, sums_second, bias, table):
    pieces, columns = position_rows(shards, True)
    return call(
        partial(pack_kernel, shards),
        (turn, pieces, columns, sums_attention, sums_first, sums_second, bias, table),
        (shaped((D, LANES), BF),),
        8,
        "pack",
        scratch=(pltpu.VMEM((D, LANES), F32), pltpu.VMEM((shards, small_lanes(shards)), F32)),
    )[0]


def lookup(table_ref, head, index, block):
    out = None
    for part in range(KEYS // LANES):
        row = jnp.broadcast_to(table_ref[head : head + 1, part * LANES : (part + 1) * LANES], index.shape)
        found = jnp.take_along_axis(row, index, axis=1, mode="promise_in_bounds")
        out = found if out is None else jnp.where(block == part, found, out)
    return out


def nt(a, b):
    return lax.dot_general(a, b, (((1,), (1,)), ((), ())), preferred_element_type=F32)


def tn(a, b):
    return lax.dot_general(a, b, (((0,), (0,)), ((), ())), preferred_element_type=F32)


def vmem(count):
    return [pl.BlockSpec(memory_space=pltpu.VMEM)] * count


def limits(mib):
    return pltpu.CompilerParams(vmem_limit_bytes=mib * 1024 * 1024)


def shaped(shape, dtype):
    return jax.ShapeDtypeStruct(tuple(shape), dtype)


def call(kernel, operands, outs, mib, name, scalars=(), scratch=()):
    return pl.pallas_call(
        kernel,
        out_shape=tuple(outs),
        in_specs=[pl.BlockSpec(memory_space=pltpu.SMEM)] * len(scalars) + vmem(len(operands)),
        out_specs=tuple(vmem(len(outs))),
        scratch_shapes=list(scratch),
        compiler_params=limits(mib),
        cost_estimate=pl.CostEstimate(flops=1, bytes_accessed=1, transcendentals=0),
        name=name,
    )(*scalars, *operands)


def build_kernel(plans, count, *refs):
    sources, outs = refs[:count], refs[count:]
    for out, (whole, items) in zip(outs, plans):
        if not whole:
            out[...] = jnp.zeros(out.shape, out.dtype)
        for row, column, rows, columns, views in items:
            values = [
                sources[which][first : first + rows, left : left + columns] for which, first, left in views
            ]
            if len(values) > 1:
                values = [sum(value.astype(F32) for value in values)]
            out[row : row + rows, column : column + columns] = values[0].astype(out.dtype)


def build(*outs):
    sources, plans = [], []
    for shape, items in outs:
        plan = []
        for row, column, rows, columns, views in items:
            found = []
            for array, first, left in views:
                at = next((i for i, source in enumerate(sources) if source is array), None)
                if at is None:
                    at = len(sources)
                    sources.append(array)
                found.append((at, first, left))
            plan.append((row, column, rows, columns, found))
        plans.append((sum(item[2] * item[3] for item in items) == math.prod(shape), plan))
    return call(
        partial(build_kernel, plans, len(sources)), sources, [shaped(shape, BF) for shape, _ in outs], 8, "build"
    )


def stack(parts):
    items, at = [], 0
    for array, row, rows, column, columns in parts:
        items.append((at, 0, rows, columns, [(array, row, column)]))
        at += rows
    return (at, parts[0][4]), items


def whole_of(array):
    return (array, 0, array.shape[0], 0, array.shape[1])


def normal(entries):
    centre = entries - jnp.mean(entries, axis=-1, keepdims=True)
    scale = lax.rsqrt(jnp.mean(centre * centre, axis=-1, keepdims=True) + layer_epsilon)
    return centre * scale, scale


def normal_back(grad, unit, scale):
    return scale * (
        grad
        - jnp.mean(grad, axis=-1, keepdims=True)
        - unit * jnp.mean(grad * unit, axis=-1, keepdims=True)
    )


def wide_dot(a, b):
    return jnp.dot(a, b, preferred_element_type=F32)


def split(value, count):
    parts = []
    for _ in range(count):
        parts.append(value.astype(BF))
        value = value - parts[-1].astype(F32)
    return parts


def joined_kernel(
    x_ref, turn_ref, vectors_ref, table_ref, whole_ref, slots_ref, joined_ref, gate_ref, logits_ref
):
    slots_ref[...] = wide_dot(x_ref[...], turn_ref[...]).astype(BF)
    for part in range(3):
        cols = slice(part * D, (part + 1) * D)
        made = wide_dot(slots_ref[...], whole_ref[:, cols])
        if part != 1:
            made = made + vectors_ref[part // 2 : part // 2 + 1, :]
        joined_ref[:, cols] = made.astype(BF)
    units = table_ref[12:20, :HD].astype(BF)
    logits_ref[...] = jnp.zeros(logits_ref.shape, F32)
    for head in range(H):
        logits_ref[:, head * gate_units : (head + 1) * gate_units] = (
            nt(x_ref[:, head * HD : (head + 1) * HD], units) + table_ref[20:21, :gate_units]
        )
    up = lax.broadcasted_iota(jnp.int32, (LANES, LANES), 0)
    across = lax.broadcasted_iota(jnp.int32, (LANES, LANES), 1)
    logits = split(logits_ref[...], 3)
    gates = []
    for side in range(2):
        chosen = ((up >> 3) == across) & (((up >> 2) & 1) == side)
        chosen = chosen.astype(F32).astype(BF)
        gates.append(jax.nn.sigmoid(sum(wide_dot(part, chosen) for part in logits)))
    first, second = gates
    gate_ref[0] = first * (second * table_ref[21:22, :LANES] - 1.0) + 2.0
    gate_ref[1] = first
    gate_ref[2] = second


def joined_forward(x, turn, vectors, table, whole):
    rows = x.shape[0]
    return call(
        joined_kernel,
        (x, turn, vectors, table, whole),
        (
            shaped((rows, D), BF),
            shaped((rows, 3 * D), BF),
            shaped((3, rows, LANES), F32),
        ),
        8,
        "joined_forward",
        scratch=(pltpu.VMEM((rows, LANES), F32),),
    )


def attention_kernel(clip, bucket_ref, valid_ref, table_ref, joined_ref, gate_ref, prob_ref, rel_ref, mixed_ref):
    slots = bucket_ref.shape[1]
    rows = slice(clip * slots, (clip + 1) * slots)
    index = bucket_ref[clip] & (LANES - 1)
    block = bucket_ref[clip] >> 7
    valid = valid_ref[clip] > 0
    for head in range(H):
        cols = slice(head * HD, (head + 1) * HD)
        query = joined_ref[rows, cols]
        key = joined_ref[rows, D + head * HD : D + (head + 1) * HD]
        value = joined_ref[rows, 2 * D + head * HD : 2 * D + (head + 1) * HD]
        rel = lookup(table_ref, head, index, block)
        rel_ref[head] = rel
        score = nt(query, key) * (1.0 / math.sqrt(HD)) + gate_ref[0, rows, head : head + 1] * rel
        score = jnp.where(valid, score, masked_score)
        top = jnp.max(score, axis=-1, keepdims=True)
        power = jnp.exp(score - top)
        prob = power / jnp.sum(power, axis=-1, keepdims=True)
        prob_ref[head] = prob
        mixed_ref[:, cols] = wide_dot(prob.astype(BF), value).astype(BF)


def attention(clip, bucket, valid, table, joined, gate):
    slots = bucket.shape[1]
    return call(
        partial(attention_kernel, clip),
        (bucket, valid, table, joined, gate),
        (shaped((H, slots, slots), F32), shaped((H, slots, slots), F32), shaped((slots, D), BF)),
        4,
        "attention",
    )


def out_kernel(x_ref, turn_ref, vectors_ref, whole_ref, *refs):
    mixed_ref, unit_ref, scale_ref = refs[-3:]
    at = 0
    for part in refs[:-3]:
        rows = slice(at, at + part.shape[0])
        mixed_ref[rows, :] = wide_dot(part[...], turn_ref[...]).astype(BF)
        at += part.shape[0]
    branch = wide_dot(mixed_ref[...], whole_ref[:, 3 * D : 4 * D]) + vectors_ref[2:3, :]
    unit, scale = normal(deep_alpha * x_ref[...].astype(F32) + branch)
    unit_ref[...] = unit
    scale_ref[...] = scale


def out_forward(x, turn, vectors, whole, mixed):
    rows = x.shape[0]
    return call(
        out_kernel,
        (x, turn, vectors, whole, *mixed),
        (shaped((rows, D), BF), shaped((rows, D), F32), shaped((rows, 1), F32)),
        6,
        "out_forward",
    )


def attention_back_kernel(
    clip, joined_ref, gate_ref, rank_ref, prob_ref, rel_ref, grad_ref, tri_ref,
    joined_grad_ref, gate_grad_ref, table_grad_ref,
):
    slots = rank_ref.shape[1]
    rows = slice(clip * slots, (clip + 1) * slots)
    scale = 1.0 / math.sqrt(HD)
    gate_grad_ref[...] = jnp.zeros(gate_grad_ref.shape, F32)
    for head in range(H):
        cols = slice(head * HD, (head + 1) * HD)
        key_cols = slice(D + head * HD, D + (head + 1) * HD)
        value_cols = slice(2 * D + head * HD, 2 * D + (head + 1) * HD)
        query = joined_ref[rows, cols]
        key = joined_ref[rows, key_cols]
        value = joined_ref[rows, value_cols]
        grad = grad_ref[rows, cols]
        prob = prob_ref[head]
        joined_grad_ref[:, value_cols] = tn(prob.astype(BF), grad).astype(BF)
        prob_grad = nt(grad, value)
        weighted = prob * prob_grad
        low = (weighted - prob * jnp.sum(weighted, axis=-1, keepdims=True)).astype(BF)
        joined_grad_ref[:, cols] = (wide_dot(low, key) * scale).astype(BF)
        joined_grad_ref[:, key_cols] = (tn(low, query) * scale).astype(BF)
        wide = low.astype(F32)
        gate_grad_ref[:, head : head + 1] = jnp.sum(wide * rel_ref[head], axis=-1, keepdims=True)
        gated = wide * gate_ref[0, rows, head : head + 1]
        high = gated.astype(BF)
        rest = (gated - high.astype(F32)).astype(BF)
        running = wide_dot(high, tri_ref[...]) + wide_dot(rest, tri_ref[...])
        for part in range(KEYS // LANES):
            lanes = slice(part * LANES, (part + 1) * LANES)
            rank = rank_ref[clip, :, lanes]
            found = jnp.take_along_axis(
                running, jnp.maximum(rank - 1, 0), axis=1, mode="promise_in_bounds"
            )
            table_grad_ref[head : head + 1, lanes] = jnp.sum(
                jnp.where(rank > 0, found, 0.0), axis=0, keepdims=True
            )
    table_grad_ref[H:, :] = jnp.zeros((16 - H, KEYS), F32)


def attention_back(clip, joined, gate, rank, prob, rel, grad):
    slots = rank.shape[1]
    tri = jnp.asarray(np.triu(np.ones((slots, slots), np.float32)), BF)
    return call(
        partial(attention_back_kernel, clip),
        (joined, gate, rank, prob, rel, grad, tri),
        (shaped((slots, 3 * D), BF), shaped((slots, LANES), F32), shaped((16, KEYS), F32)),
        4,
        "attention_back",
    )


def gate_back_kernel(count, x_ref, table_ref, gate_ref, *refs):
    joined_grads, gate_grads, table_grads = refs[:count], refs[count : 2 * count], refs[2 * count : 3 * count]
    x_grad_ref, table_grad_ref, sums_ref = refs[3 * count :]
    table_grad_ref[...] = jnp.zeros(table_grad_ref.shape, F32)
    table_grad_ref[:16, :] = sum(ref[...] for ref in table_grads)
    sums_ref[0:1, :] = sum(jnp.sum(ref[:, :D].astype(F32), axis=0, keepdims=True) for ref in joined_grads)
    sums_ref[1:2, :] = sum(jnp.sum(ref[:, 2 * D :].astype(F32), axis=0, keepdims=True) for ref in joined_grads)
    units = [jnp.sum(table_ref[12 + 4 * i : 16 + 4 * i, :HD], axis=0, keepdims=True) for i in range(2)]
    unit_grads = [jnp.zeros((1, HD), F32), jnp.zeros((1, HD), F32)]
    grad = jnp.concatenate([ref[...] for ref in gate_grads], axis=0)
    first, second = gate_ref[1], gate_ref[2]
    size = table_ref[21:22, :LANES]
    grads = (
        grad * (second * size - 1.0) * first * (1.0 - first),
        grad * first * size * second * (1.0 - second),
    )
    table_grad_ref[21:22, :LANES] = jnp.sum(grad * first * second, axis=0, keepdims=True)
    bias_grads = [jnp.sum(jnp.sum(g, axis=0, keepdims=True), axis=1, keepdims=True) for g in grads]
    for head in range(H):
        cols = slice(head * HD, (head + 1) * HD)
        x = x_ref[:, cols].astype(F32)
        sides = [g[:, head : head + 1] for g in grads]
        x_grad_ref[:, cols] = sides[0] * units[0] + sides[1] * units[1]
        for i in range(2):
            unit_grads[i] = unit_grads[i] + jnp.sum(x * sides[i], axis=0, keepdims=True)
    for unit in range(gate_units):
        table_grad_ref[12 + unit : 13 + unit, :HD] = unit_grads[unit // 4]
        table_grad_ref[20:21, unit : unit + 1] = bias_grads[unit // 4]


def gate_back(x, table, gate, joined_grads, gate_grads, table_grads):
    return call(
        partial(gate_back_kernel, len(joined_grads)),
        (x, table, gate, *joined_grads, *gate_grads, *table_grads),
        (shaped(x.shape, F32), shaped((24, KEYS), F32), shaped((8, D), F32)),
        6,
        "gate_back",
    )


def gelu_pair(u):
    size = jnp.abs(u) * math.sqrt(0.5)
    t = 1.0 / (1.0 + 0.3275911 * size)
    poly = ((((1.061405429 * t - 1.453152027) * t + 1.421413741) * t - 0.284496736) * t + 0.254829592) * t
    bell = jnp.exp(-0.5 * u * u)
    tail = 0.5 * poly * bell
    below = jnp.where(u < 0, tail, 1.0 - tail)
    return u * below, below + u * bell * (1.0 / math.sqrt(2.0 * math.pi))


def hidden_kernel(
    unit_ref, vectors_ref, turn_ref, bias_ref, whole_ref, slots_ref, active_ref, slope_ref
):
    low = (unit_ref[...] * vectors_ref[3:4, :] + vectors_ref[4:5, :]).astype(BF)
    slots_ref[...] = wide_dot(low, turn_ref[...]).astype(BF)
    width = FF // 8
    for block in range(8):
        cols = slice(block * width, (block + 1) * width)
        u = wide_dot(slots_ref[...], whole_ref[:, cols]) + bias_ref[:, cols]
        active, slope = gelu_pair(u)
        active_ref[:, cols] = active.astype(BF)
        slope_ref[:, cols] = slope


def hidden_forward(unit, vectors, turn, bias, whole):
    rows = unit.shape[0]
    return call(
        hidden_kernel,
        (unit, vectors, turn, bias, whole),
        (shaped((rows, D), BF), shaped((rows, FF), BF), shaped((rows, FF), F32)),
        10,
        "hidden_forward",
    )


def turn_kernel(slots, *refs):
    at_ref, active_ref, unit_ref, vectors_ref, valid_ref, cot_ref = refs[:6]
    parts = refs[6:-5]
    whole_ref, out_ref, second_ref, low_ref, sums_ref = refs[-5:]
    for slot, (which, row, rows, column) in enumerate(slots):
        place = pl.multiple_of(at_ref[slot], 16)
        if parts[which].shape[1] == D:
            whole_ref[pl.ds(place, rows), :] = parts[which][row : row + rows, :]
            continue
        blocks = [
            parts[which][row : row + rows, column + j * D : column + (j + 1) * D] for j in range(FF // D)
        ]
        whole_ref[pl.ds(place, rows * len(blocks)), :] = jnp.concatenate(blocks, axis=0)
    made = wide_dot(active_ref[...], whole_ref[...]) + vectors_ref[5:6, :]
    first_norm = unit_ref[...] * vectors_ref[3:4, :] + vectors_ref[4:5, :]
    unit, scale = normal(deep_alpha * first_norm + made.astype(BF).astype(F32))
    valid = valid_ref[...]
    gain = vectors_ref[6:7, :]
    out_ref[...] = ((unit * gain + vectors_ref[7:8, :]) * valid).astype(BF)
    grad = cot_ref[...].astype(F32) * valid
    second = normal_back(grad * gain, unit, scale)
    second_ref[...] = second
    low = second.astype(BF)
    low_ref[...] = low
    sums_ref[0:1, :] = jnp.sum(low.astype(F32), axis=0, keepdims=True)
    sums_ref[1:2, :] = jnp.sum(grad * unit, axis=0, keepdims=True)
    sums_ref[2:3, :] = jnp.sum(grad, axis=0, keepdims=True)


def turn_back(at, slots, active, unit, vectors, valid, cot, parts):
    rows = unit.shape[0]
    return call(
        partial(turn_kernel, slots),
        (active, unit, vectors, valid, cot, *parts),
        (shaped((FF, D), BF), shaped((rows, D), BF), shaped((rows, D), F32), shaped((rows, D), BF), shaped((8, D), F32)),
        10,
        "turn_back",
        scalars=(at,),
    )


def down_back_kernel(rows, at_ref, active_ref, low_ref, mine_ref, other_ref, made_ref):
    for first in range(0, FF, FF // 8):
        made_ref[first : first + FF // 8, :] = tn(
            active_ref[:, first : first + FF // 8], low_ref[...]
        ).astype(BF)
    chunk = rows * FF // D
    half = D // 2
    for slot in range(FF // chunk):
        ref = mine_ref if slot * rows < half else other_ref
        made = made_ref[pl.ds(pl.multiple_of(at_ref[slot], 16), chunk), :]
        to = slot * rows % half
        for j in range(FF // D):
            ref[to : to + rows, j * D : (j + 1) * D] = made[j * rows : (j + 1) * rows, :]


def down_back(at, rows, active, low):
    return call(
        partial(down_back_kernel, rows),
        (active, low),
        (shaped((D // 2, FF), BF), shaped((D // 2, FF), BF)),
        10,
        "down_back",
        scalars=(at,),
        scratch=(pltpu.VMEM((FF, D), BF),),
    )


def hidden_back_kernel(low_ref, down_ref, slope_ref, grad_ref, bias_ref):
    width = FF // 8
    for block in range(8):
        cols = slice(block * width, (block + 1) * width)
        grad = (nt(low_ref[...], down_ref[cols, :]) * slope_ref[:, cols]).astype(BF)
        grad_ref[:, cols] = grad
        bias_ref[:, cols] = jnp.sum(grad.astype(F32), axis=0, keepdims=True)


def hidden_back(low, down, slope):
    rows = low.shape[0]
    return call(
        hidden_back_kernel,
        (low, down, slope),
        (shaped((rows, FF), BF), shaped((1, FF), F32)),
        6,
        "hidden_back",
    )


def in_back_kernel(slots_ref, grad_ref, mine_ref, other_ref):
    width = FF // 4
    for block in range(4):
        cols = slice(block * width, (block + 1) * width)
        made = tn(slots_ref[...], grad_ref[:, cols]).astype(BF)
        mine_ref[:, cols] = made[: D // 2]
        other_ref[:, cols] = made[D // 2 :]


def in_back(slots, grad):
    rows = slots.shape[0]
    return call(
        in_back_kernel,
        (slots, grad),
        (shaped((D // 2, FF), BF), shaped((D // 2, FF), BF)),
        6,
        "in_back",
    )


def out_back_kernel(
    grad_ref, in_ref, turn_ref, second_ref, unit_ref, scale_ref, vectors_ref, mixed_ref, out_ref,
    first_ref, weight_ref, mixed_grad_ref, sums_ref,
):
    low = nt(grad_ref[...], in_ref[...]).astype(BF)
    grad = deep_alpha * second_ref[...] + nt(low, turn_ref[...]).astype(BF).astype(F32)
    unit = unit_ref[...]
    first = normal_back(grad * vectors_ref[3:4, :], unit, scale_ref[...])
    first_ref[...] = first
    branch = first.astype(BF)
    sums_ref[0:1, :] = jnp.sum(branch.astype(F32), axis=0, keepdims=True)
    sums_ref[1:2, :] = jnp.sum(grad * unit, axis=0, keepdims=True)
    sums_ref[2:3, :] = jnp.sum(grad, axis=0, keepdims=True)
    weight_ref[...] = tn(mixed_ref[...], branch).astype(BF)
    back = nt(branch, out_ref[:, 3 * D : 4 * D]).astype(BF)
    mixed_grad_ref[...] = nt(back, turn_ref[...]).astype(BF)


def out_back(grad, w_in, turn, second, unit, scale, vectors, mixed, w_first):
    rows = unit.shape[0]
    return call(
        out_back_kernel,
        (grad, w_in, turn, second, unit, scale, vectors, mixed, w_first),
        (shaped((rows, D), F32), shaped((D, D), BF), shaped((rows, D), BF), shaped((8, D), F32)),
        6,
        "out_back",
    )


def first_back_kernel(slots_ref, out_ref, small_ref, *refs):
    *grads, mine_ref, other_ref, grad_ref = refs
    at = 0
    for grad in grads:
        grad_ref[at : at + grad.shape[0], :] = grad[...]
        at += grad.shape[0]
    half = D // 2
    for part in range(3):
        cols = slice(part * D, (part + 1) * D)
        made = tn(slots_ref[...], grad_ref[:, cols]).astype(BF)
        mine_ref[:, cols] = made[:half]
        other_ref[:, cols] = made[half:]
    for ref, rows in ((mine_ref, slice(0, half)), (other_ref, slice(half, D))):
        ref[:, 3 * D : 4 * D] = out_ref[rows, :]
        ref[:, 4 * D :] = small_ref[rows, :]


def first_back(slots, weight_out, small, grads):
    rows = slots.shape[0]
    wide = 4 * D + small.shape[1]
    return call(
        first_back_kernel,
        (slots, weight_out, small, *grads),
        (shaped((D // 2, wide), BF), shaped((D // 2, wide), BF), shaped((rows, 3 * D), BF)),
        6,
        "first_back",
    )


def rows_back_kernel(grad_ref, first_ref, turn_ref, branch_ref, gate_ref, out_ref):
    made = nt(grad_ref[...], first_ref[:, : 3 * D])
    high = made.astype(BF)
    rest = made - high.astype(F32)
    middle = rest.astype(BF)
    last = (rest - middle.astype(F32)).astype(BF)
    turned = nt(high, turn_ref[...]) + nt(middle, turn_ref[...]) + nt(last, turn_ref[...])
    out_ref[...] = turned + deep_alpha * branch_ref[...] + gate_ref[...]


def rows_back(grad, w_first, turn, branch, gate):
    rows = grad.shape[0]
    return call(
        rows_back_kernel,
        (grad, w_first, turn, branch, gate),
        (shaped((rows, D), F32),),
        8,
        "rows_back",
    )[0]


def flat_cuts(each):
    cuts = [(0, row, 0, 3 * D) for row in range(each)]
    cuts += [(0, row, 3 * D, 4 * D) for row in range(each)]
    cuts += [(1, row, 0, FF) for row in range(each)]
    cuts += [(2, row, j * D, (j + 1) * D) for j in range(FF // D) for row in range(each)]
    return cuts + [(0, row, 4 * D, 4 * D + LANES) for row in range(each)]


def flat_runs(each, width):
    at = 0
    for which, row, first, last in flat_cuts(each):
        size = min(last - first, width - at)
        if size > 0:
            yield which, row, first, size, at
        at += last - first


def rows_kernel(flat_ref, first_ref, in_ref, down_ref):
    refs = (first_ref, in_ref, down_ref)
    first_ref[:, 4 * D :] = jnp.zeros((first_ref.shape[0], LANES), F32)
    for which, row, first, size, at in flat_runs(first_ref.shape[0], flat_ref.shape[1]):
        refs[which][row : row + 1, first : first + size] = flat_ref[:, at : at + size]


def pieces_kernel(flat_ref, first_ref, in_ref, down_ref, all_ref, *refs):
    rows_kernel(flat_ref, *refs)
    at = 0
    for ref, low in zip(refs, (first_ref, in_ref, down_ref)):
        low[...] = ref[...].astype(BF)
        all_ref[:, at : at + low.shape[1]] = low[...]
        at += low.shape[1]


def row_widths():
    return (4 * D + LANES, FF, FF)


def flat_rows(flat, each):
    return call(rows_kernel, (flat,), [shaped((each, width), F32) for width in row_widths()], 6, "flat_rows")


def pieces(flat, each):
    widths = row_widths()
    return call(
        pieces_kernel,
        (flat,),
        [shaped((each, width), BF) for width in (*widths, sum(widths))],
        6,
        "pieces",
        scratch=[pltpu.VMEM((each, width), F32) for width in widths],
    )


def update_kernel(learning, plan, count, *refs):
    sums = refs[:count]
    refs = refs[count:]
    weights, momenta, averages, outs, rows = refs[:3], refs[3:6], refs[6:9], refs[9:12], refs[12:]
    for i in range(3):
        each, wide = weights[i].shape
        grad = sum(
            sums[which][row : row + each, column : column + wide].astype(F32) for which, row, column in plan[i]
        )
        weight = weights[i][...]
        decayed = grad + decay_rate * weight
        momentum = momentum_rate * momenta[i][...] + decayed
        weight = weight - learning * (decayed + momentum_rate * momentum)
        rows[i][...] = momentum
        rows[3 + i][...] = average_rate * averages[i][...] + (1.0 - average_rate) * weight
        rows[6 + i][...] = weight
    for out, which in zip(outs, (0, 3, 6)):
        for section, row, first, size, at in flat_runs(rows[0].shape[0], out.shape[1]):
            out[:, at : at + size] = rows[which + section][row : row + 1, first : first + size]


def update(learning, sums, weights, momenta, averages, width):
    arrays, plan = [], []
    for views in sums:
        found = []
        for array, row, column in views:
            at = next((i for i, known in enumerate(arrays) if known is array), None)
            if at is None:
                at = len(arrays)
                arrays.append(array)
            found.append((at, row, column))
        plan.append(found)
    rows = [pltpu.VMEM(part.shape, F32) for part in weights] * 3
    return call(
        partial(update_kernel, learning, plan, len(arrays)),
        [*arrays, *weights, *momenta, *averages],
        (shaped((1, width), F32),) * 3,
        8,
        "update",
        scratch=rows,
    )


def body(acts, cotangent, mask, shape_id, weights, momenta, averages):
    shards = lax.axis_size(("dp", "fsdp"))
    count = lax.axis_size("dp")
    dp, core = lax.axis_index("dp"), lax.axis_index("fsdp")
    clips, slots = acts.shape[0], acts.shape[1]
    rows = clips * slots
    total_tokens = rows * shards
    piece_rows = D // shards
    wide_rows = FF // shards
    vector_width = 12 * D // shards
    position_width = (NPOS + shards - 1) // shards
    small_width = vector_width + position_width

    piece_first, piece_in, piece_down, piece_all = pieces(weights, piece_rows)

    order = slot_order(dp, core, count)
    row_order = (order[:, None] * piece_rows + jnp.arange(piece_rows, dtype=jnp.int32)).reshape(-1)
    turn = (jnp.arange(D, dtype=jnp.int32)[:, None] == row_order[None, :]).astype(BF)
    piece_turn = (jnp.arange(shards, dtype=jnp.int32)[:, None] == order[None, :]).astype(BF)

    back_order = jnp.dot(piece_turn.astype(F32), jnp.arange(shards, dtype=F32)).astype(jnp.int32)

    together = lax.optimization_barrier
    bits = high_bits(count)
    staged = len(bits) == 2
    n = piece_rows
    rest = D // 8 - n
    widths = (piece_first.shape[1], FF, FF)
    lefts = (0, widths[0], widths[0] + FF)
    cuts = (13 * LANES, FF // 2, FF // 2)
    wide_all, cut_all = sum(widths), 37 * LANES
    third = (13 * LANES, 12 * LANES, 12 * LANES), (12 * LANES,) * 3
    at = order * wide_rows
    inputs_low = acts.reshape(rows, D)

    def gather_high(piece):
        if staged:
            return [exchange(piece, "dp", d << 2) for d in (1, 2, 3)]
        column = piece
        for bit in bits:
            column = jnp.concatenate([column, exchange(column, "dp", 1 << bit)], axis=0)
        return [column[n:]]

    def thirds(side, views):
        left = widths[0]
        items, column = [], 0
        for i, size in enumerate(third[side]):
            items += views(i * n, left, column, size)
            column += size
        return items

    own_sides = exchange_sides((piece_all, piece_all))
    high_first = gather_high(piece_first)
    own_sides, high_first, piece_in, mask, turn, at = together(
        (own_sides, high_first, piece_in, mask, turn, at)
    )

    items = stack([whole_of(part) for part in high_first])[1]
    sends = build(
        ((rest, widths[0]), items),
        (
            (rest, widths[0] + third[1][0]),
            items + thirds(1, lambda row, left, c, w: [(row, left, n, w, [(own_sides[1], 0, cut_all + c)])]),
        ),
        (
            (rest, widths[0] + third[0][0]),
            items + thirds(0, lambda row, left, c, w: [(row, left, n, w, [(own_sides[0], 0, c)])]),
        ),
    )
    rest_first, sends = sends[0], sends[1:]
    sides_first = exchange_sides(sends)
    high_in = gather_high(piece_in)
    bucket, rank, valid_rows, valid_wide = prep(mask, shape_id, slots)
    sides_first, high_in, piece_down, bucket, rank, valid_rows, valid_wide = together(
        (sides_first, high_in, piece_down, bucket, rank, valid_rows, valid_wide)
    )

    def corner_sends(unit, sides):
        wide, half = widths[unit], cuts[unit]
        return (
            ((rest, wide - half), [(0, 0, rest, wide - half, [(sides[1], 0, half)])]),
            ((rest, half), [(0, 0, rest, half, [(sides[0], 0, 0)])]),
        )

    def corner_items(unit, corner):
        wide, half = widths[unit], cuts[unit]
        (second, left_second), (first, left_first) = corner
        return [
            (0, 0, rest, half, [(first, 0, left_first)]),
            (0, half, rest, wide - half, [(second, 0, left_second)]),
        ]

    def early_rows(unit, piece, high, sides):
        wide = widths[unit]
        return stack([whole_of(piece), whole_of(high)] + [(side, 0, rest, 0, wide) for side in sides])

    def shifted(items, row):
        return [(row + item[0], *item[1:]) for item in items]

    def slots_of(unit, piece, high, sides, corner, early, late):
        wide, left = widths[unit], lefts[unit]
        own_mine, own_other = own
        items = [(0, 0, n, wide, [(piece, 0, 0)]), (n, 0, rest, wide, [(high, 0, 0)])]
        eighth = D // 8
        for i in range(3):
            items.append(((i + 1) * eighth, 0, n, wide, [(own_mine, i * n, left)]))
        for i, side in enumerate(sides):
            items.append(((i + 1) * eighth + n, 0, rest, wide, [(side, 0, 0)]))
        items += shifted(corner_items(unit, corner), 3 * eighth + n)
        base = D // 2
        items.append((base, 0, n, wide, [(early, 0, 0)]))
        items.append((base + n, 0, rest, wide, [(early, n, 0)]))
        for i in range(3):
            items.append((base + (i + 1) * eighth, 0, n, wide, [(own_other, i * n, left)]))
            view = (late, 0, 0) if i == 2 else (early, n + (i + 1) * rest, 0)
            items.append((base + (i + 1) * eighth + n, 0, rest, wide, [view]))
        return items

    def own_corner(row, half, side, column):
        return [(row, column + c, n, w, [(side, i * n, widths[0])]) for i, (c, w) in enumerate(half)]

    def spans(side):
        edges = np.cumsum((0, *third[side]))
        return [(int(a), int(b - a)) for a, b in zip(edges[:-1], edges[1:])]

    items = [(0, 0, n, wide_all, [(own_sides[0], 0, 0)]), (n, 0, n, wide_all, [(own_sides[1], 0, 0)])]
    items += own_corner(2 * n, spans(0), sides_first[1], 0) + own_corner(2 * n, spans(1), sides_first[0], cut_all)
    own_mine, early, *sends = build(
        ((3 * n, wide_all), items),
        early_rows(0, piece_first, rest_first, sides_first),
        *corner_sends(0, sides_first),
    )
    corner_first = exchange_sides(sends)
    early_first = exchange_core(early)
    own = (own_mine, exchange_core(own_mine))
    corner_first, early_first, own, high_in, piece_down = together(
        (corner_first, early_first, own, high_in, piece_down)
    )

    corner_first = [(part, 0) for part in corner_first]
    rest_in, late = build(
        stack([whole_of(part) for part in high_in]),
        ((rest, widths[0]), corner_items(0, corner_first)),
    )
    sides_in = exchange_sides((rest_in, rest_in))
    high_down = gather_high(piece_down)
    late = exchange_core(late)
    items = slots_of(0, piece_first, rest_first, sides_first, corner_first, early_first, late)
    w_first = build(((D, widths[0]), items))[0]
    vectors, bias_in, table = unpack(shards, turn, w_first)
    inputs_slots, joined, gate = joined_forward(inputs_low, turn, vectors, table, w_first)
    made = [attention(0, bucket, valid_wide, table, joined, gate)]
    sides_in, high_down, joined, made = together((sides_in, high_down, joined, made))

    wide, half = widths[1], cuts[1]
    items = stack([whole_of(part) for part in high_down])[1]
    rest_down, early, *sends = build(
        ((rest, FF), items),
        early_rows(1, piece_in, rest_in, sides_in),
        *(
            (
                (rest, FF + width),
                items + [(0, FF, rest, width, [view])],
            )
            for width, view in ((wide - half, (sides_in[1], 0, half)), (half, (sides_in[0], 0, 0)))
        ),
    )
    sides_down = exchange_sides(sends)
    early_in = exchange_core(early)
    made += [attention(clip, bucket, valid_wide, table, joined, gate) for clip in range(1, clips)]
    mixed_slots, unit, unit_scale = out_forward(inputs_low, turn, vectors, w_first, [m[2] for m in made])
    sides_down, early_in, unit = together((sides_down, early_in, unit))

    corner_in = [(part, FF) for part in sides_down]
    late, early, *sends = build(
        ((rest, FF), corner_items(1, corner_in)),
        early_rows(2, piece_down, rest_down, sides_down),
        *corner_sends(2, sides_down),
    )
    corner_down = exchange_sides(sends)
    late = exchange_core(late)
    early_down = exchange_core(early)
    items = slots_of(1, piece_in, rest_in, sides_in, corner_in, early_in, late)
    w_in = build(((D, FF), items))[0]
    first_slots, active, slope = hidden_forward(unit, vectors, turn, bias_in, w_in)
    corner_down, early_down, active = together((corner_down, early_down, active))

    corner_down = [(part, 0) for part in corner_down]
    corner = build(((rest, FF), corner_items(2, corner_down)))[0]
    late = exchange_core(corner)
    items = slots_of(2, piece_down, rest_down, sides_down, [(corner, cuts[2]), (corner, 0)], early_down, late)
    arrays, places = [], [None] * shards
    for row, column, size, _, [(array, first, left)] in items:
        if column:
            continue
        which = next((i for i, known in enumerate(arrays) if known is array), len(arrays))
        if which == len(arrays):
            arrays.append(array)
        for step in range(size // n):
            places[row // n + step] = (which, first + step * n, n, left)
    to = at
    if wide_rows % 16:
        parts = [arrays[which][row : row + n, left : left + FF] for which, row, _, left in places]
        stacked = jnp.stack(parts).reshape(shards, n, FF // D, D).transpose(0, 2, 1, 3).reshape(shards, wide_rows, D)
        arrays, places = [jnp.take(stacked, back_order, axis=0).reshape(FF, D)], [(0, 0, FF, 0)]
        to = jnp.zeros((1,), jnp.int32)
    w_down, activations, grad_second, grad_made, sums_second = turn_back(
        to, places, active, unit, vectors, valid_rows, cotangent.reshape(rows, D), arrays
    )

    if wide_rows % 16:
        grad_down = tn(active, grad_made).astype(BF).reshape(shards, wide_rows, D)
        grad_down = jnp.take(grad_down, order, axis=0).reshape(shards, FF // D, n, D).transpose(0, 2, 1, 3)
        grad_down = grad_down.reshape(D, FF)
        down_mine, down_other = grad_down[: D // 2], grad_down[D // 2 :]
    else:
        down_mine, down_other = down_back(at, n, active, grad_made)
    down_mine, down_other, grad_made = together((down_mine, down_other, grad_made))

    eighth = D // 8

    def both(pair, row, column):
        return [(array, row, column) for array in pair]

    def corner_out(unit, pair):
        wide, half = widths[unit], cuts[unit]
        row = 3 * eighth + n
        return (
            (wide - half, [(0, 0, rest, wide - half, both(pair, row, half))]),
            (half, [(0, 0, rest, half, both(pair, row, 0))]),
        )

    def sides_out(unit, pair, corner):
        wide, half = widths[unit], cuts[unit]
        (second, left_second), (first, left_first) = corner
        near, side = eighth + n, 2 * eighth + n
        return (
            (
                wide,
                [
                    (0, 0, rest, half, both(pair, near, 0) + [(first, 0, left_first)]),
                    (0, half, rest, wide - half, both(pair, near, half)),
                ],
            ),
            (
                wide,
                [
                    (0, 0, rest, half, both(pair, side, 0)),
                    (0, half, rest, wide - half, both(pair, side, half) + [(second, 0, left_second)]),
                ],
            ),
        )

    def beside(one, two):
        return [
            ((rest, a[0] + b[0]), a[1] + [(item[0], a[0] + item[1], *item[2:]) for item in b[1]])
            for a, b in zip(one, two)
        ]

    def alone(one):
        return [((rest, wide), items) for wide, items in one]

    def column_views(unit, pair, sides, row):
        return both(pair, row, 0) + [(side, row - n, 0) for side in sides]

    def high_out(unit, pair, sides, first, count, *more):
        wide = widths[unit]
        views = column_views(unit, pair, sides, first * n)
        if more:
            views = views + [(more[0], n, 0)]
        return ((count * n, wide), [(0, 0, count * n, wide, views)])

    def scatter_high(unit, pair, sides):
        total = sum(part[n:eighth].astype(F32) for part in pair)
        total = total + sum(side[:, : widths[unit]].astype(F32) for side in sides)
        total = jnp.concatenate([jnp.zeros((n, widths[unit]), F32), total], axis=0)
        for bit in reversed(bits):
            size = total.shape[0] // 2
            total = total[:size] + exchange(total[size:].astype(BF), "dp", 1 << bit).astype(F32)
        return [total]

    def scatter_far(unit, pair, sides):
        if not staged:
            return scatter_high(unit, pair, sides)
        return [exchange(build(high_out(unit, pair, sides, 2, 2))[0], "dp", 8)]

    down = (down_mine, exchange_core(down_other))
    grad_hidden, grad_bias_in = hidden_back(grad_made, w_down, slope)
    grad_first_sum, grad_out, grad_mixed, sums_first = out_back(
        grad_hidden, w_in, turn, grad_second, unit, unit_scale, vectors, mixed_slots, w_first
    )
    in_mine, in_other = in_back(first_slots, grad_hidden)
    down, in_mine, in_other, grad_mixed = together((down, in_mine, in_other, grad_mixed))

    corner_down = exchange_sides(build(*alone(corner_out(2, down))))
    inner = (in_mine, exchange_core(in_other))

    def clip_back(clip):
        prob, rel, _ = made[clip]
        return attention_back(clip, joined, gate, rank, prob, rel, grad_mixed)

    backs = [clip_back(0)]
    corner_down, inner, backs, grad_mixed = together((corner_down, inner, backs, grad_mixed))

    corner_down = [(part, 0) for part in corner_down]
    sides_down = exchange_sides(build(*beside(sides_out(2, down, corner_down), corner_out(1, inner))))
    backs += [clip_back(clip) for clip in range(1, clips)]
    grads_joined = [back[0] for back in backs]
    grad_gate_inputs, table_grad, sums_attention = gate_back(
        inputs_low, table, gate, grads_joined, [back[1] for back in backs], [back[2] for back in backs]
    )
    grad_small = pack(shards, turn, sums_attention, sums_first, sums_second, grad_bias_in, table_grad)
    first_mine, first_other, grad_joined = first_back(inputs_slots, grad_out, grad_small, grads_joined)
    sides_down, first_mine, first_other, grad_joined = together((sides_down, first_mine, first_other, grad_joined))

    corner_in = [(part, FF) for part in sides_down]
    first = (first_mine, exchange_core(first_other))
    sides_in = exchange_sides(build(*alone(sides_out(1, inner, corner_in))))
    high_down = scatter_far(2, down, sides_down)
    corner_first = exchange_sides(build(*alone(corner_out(0, first))))
    input_grad = rows_back(grad_joined, w_first, turn, grad_first_sum, grad_gate_inputs)
    first, sides_in, high_down, corner_first, input_grad = together(
        (first, sides_in, high_down, corner_first, input_grad)
    )

    corner_first = [(part, 0) for part in corner_first]
    units = ((first, 0), (inner, 1), (down, 2))

    def own_views(row, column, columns):
        found = []
        for pair, unit in units:
            start, end = max(column, lefts[unit]), min(column + columns, lefts[unit] + widths[unit])
            if start < end:
                found.append((start - column, end - start, both(pair, row, start - lefts[unit])))
        return found

    def own_third(side):
        base = cut_all if side else 0
        items = []
        for i, (column, columns) in enumerate(spans(side)):
            for start, size, views in own_views(3 * eighth, base + column, columns):
                items.append((i * n, start, n, size, views))
        return (third[side][0], items)

    sides_first = exchange_sides(
        build(*beside(sides_out(0, first, corner_first), (own_third(1), own_third(0))))
    )
    high_in = scatter_far(1, inner, sides_in)
    if staged:
        high_down += [exchange(build(high_out(2, down, sides_down, 1, 1, high_down[0]))[0], "dp", 4)]
    weight_rows, momenta_rows, averages_rows = [flat_rows(part, n) for part in (weights, momenta, averages)]
    sides_first, high_in, high_down, weight_rows, momenta_rows, averages_rows = together(
        (sides_first, high_in, high_down, weight_rows, momenta_rows, averages_rows)
    )

    own_outs = []
    for side, row in ((0, eighth), (1, 2 * eighth)):
        items = []
        base = 0 if side == 0 else cut_all
        came = sides_first[1] if side == 0 else sides_first[0]
        edges = [(base + c, w, (came, i * n, widths[0])) for i, (c, w) in enumerate(spans(side))]
        edges.append((cut_all, wide_all - cut_all, None) if side == 0 else (0, cut_all, None))
        for column, columns, view in edges:
            for start, size, views in own_views(row, column, columns):
                if view is not None:
                    views = views + [(view[0], view[1], view[2] + start)]
                items.append((0, column + start, n, size, views))
        own_outs.append(((n, wide_all), items))
    own_sides = exchange_sides(build(*own_outs))
    if staged:
        near, far, farthest = [high_out(0, first, sides_first, d, 1) for d in (1, 2, 3)]
        near_in = high_out(1, inner, sides_in, 1, 1, high_in[0])
        wide = widths[0]
        near = ((n, wide + FF), near[1] + [(0, wide, n, FF, near_in[1][0][4])])
        high_first = [exchange(part, "dp", mask) for part, mask in zip(build(near, far, farthest), (4, 8, 12))]
        high_in += [high_first[0]]
    else:
        high_first = scatter_high(0, first, sides_first)
    comes = (
        [(part, 0) for part in high_first],
        [(part, widths[0] if i else 0) for i, part in enumerate(high_in)],
        [(part, 0) for part in high_down],
    )
    sums = []
    for pair, unit in units:
        views = both(pair, 0, 0) + [(side, 0, lefts[unit]) for side in own_sides]
        sums.append(views + [(part, 0, left) for part, left in comes[unit]])

    learning = rate_scale / math.sqrt(total_tokens)
    momenta_new, averages_new, weights_new = update(
        learning,
        sums,
        weight_rows,
        momenta_rows,
        averages_rows,
        weights.shape[1],
    )
    return (
        activations.reshape(acts.shape),
        input_grad.reshape(acts.shape),
        momenta_new,
        averages_new,
        weights_new,
        weights_new.astype(BF),
    )


def solution(mesh):
    split = ("dp", "fsdp")
    in_specs = (
        P(split, None, None),
        P(split, None, None),
        P(split, None),
        P(split),
        P(split, None),
        P(split, None),
        P(split, None),
    )
    out_specs = (
        P(split, None, None),
        P(split, None, None),
        P(split, None),
        P(split, None),
        P(split, None),
        P(split, None),
    )
    return jax.shard_map(body, mesh=mesh, in_specs=in_specs, out_specs=out_specs, check_vma=False)
```

```python
from functools import partial
import math

import jax
import jax.numpy as jnp
import numpy as np
from jax import lax
from jax.experimental import pallas as pl
from jax.experimental.pallas import tpu as pltpu
from jax.sharding import PartitionSpec as P

D = 768
H = 12
HD = 64
FF = 3072
NB = 320
HALF = NB // 2
P_SIZE = 512
NPOS = 4372
LANES = 128
KEYS = 384
BF = jnp.bfloat16
F32 = jnp.float32

deep_alpha = 24.0**0.25
layer_epsilon = 1e-05
masked_score = -1000000000.0
far_distance = 800
gate_units = 8
momentum_rate = 0.9
average_rate = 0.8
decay_rate = 0.0001
rate_scale = 0.04
far_place = 1 << 20


def bucket_levels(span):
    distance = np.arange(0, span + 1)
    exact = HALF // 2
    logscale = (
        np.log(np.maximum(distance, 1) / exact) / np.log(far_distance / exact) * (HALF - exact)
    )
    beyond = np.minimum(exact + np.floor(logscale).astype(np.int64), HALF - 1)
    return np.where(distance < exact, distance, beyond)


def far_marks():
    levels = bucket_levels(2 * P_SIZE)
    rises = np.diff(levels)
    marks = np.repeat(np.arange(1, 2 * P_SIZE + 1), rises)
    return [int(m) for m in marks[HALF // 2 :]]


def key_ends():
    span = 2 * P_SIZE
    levels = bucket_levels(span)
    offsets = np.arange(-span, span + 1)
    level = levels[np.abs(offsets)]
    keys = np.where(offsets > 0, HALF + level, HALF - 1 - level)
    ends = np.full((KEYS,), far_place // 2, np.int32)
    for key in range(NB - 1):
        below = offsets[keys <= key]
        ends[key] = below.max() if below.size else -(far_place // 2)
    return ends


def exchange(value, axis, mask):
    count = lax.axis_size(axis)
    return lax.ppermute(value, axis, [(i, i ^ mask) for i in range(count)])


def high_bits(count):
    return list(range(2, count.bit_length() - 1))


def exchange_sides(pair):
    return exchange(pair[0], "dp", 1), exchange(pair[1], "dp", 2)


def exchange_core(value):
    return exchange(value, "fsdp", 1)


def slot_order(dp, core, count):
    high = count // 4
    core_step, low, up = np.meshgrid(np.arange(2), np.arange(4), np.arange(high), indexing="ij")
    distance = jnp.asarray((up * 4 + low).reshape(-1).astype(np.int32))
    core_distance = jnp.asarray(core_step.reshape(-1).astype(np.int32))
    return (distance ^ dp) * 2 + (core_distance ^ core)


def prep_kernel(marks, shape_ref, mask_ref, ends_ref, bucket_ref, rank_ref, valid_ref):
    clips, patches = mask_ref.shape
    slots = bucket_ref.shape[1]
    mask = mask_ref[...]
    up = lax.broadcasted_iota(jnp.int32, (patches, patches), 0)
    across = lax.broadcasted_iota(jnp.int32, (patches, patches), 1)
    running = wide_dot(mask.astype(F32).astype(BF), (up <= across).astype(F32).astype(BF))
    ranks = jnp.where(mask == 1, running.astype(jnp.int32) - 1, -1)
    slot = lax.broadcasted_iota(jnp.int32, (slots, patches), 0)
    patch = lax.broadcasted_iota(jnp.int32, (slots, patches), 1)
    pair = lax.broadcasted_iota(jnp.int32, (8, patches), 1)
    halves = jnp.where(lax.broadcasted_iota(jnp.int32, (8, patches), 0) == 0, pair >> 4, pair & 15)
    halves = halves.astype(F32).astype(BF)
    for clip in range(clips):
        found = ranks[clip : clip + 1, :] == slot
        column = jnp.sum(jnp.where(found, patch, 0), axis=1, keepdims=True)
        both = nt(halves, found.astype(F32).astype(BF)).astype(jnp.int32)
        row = 16 * both[0:1, :] + both[1:2, :]
        narrow = shape_ref[clip] > 0
        column = jnp.where(narrow, 8 * (column >> 2) + (column & 3), column)
        row = jnp.where(narrow, 8 * (row >> 2) + (row & 3), row)
        count = jnp.sum(mask[clip : clip + 1, :], axis=1, keepdims=True)
        valid = lax.broadcasted_iota(jnp.int32, (slots, 1), 0) < count
        valid_ref[clip * slots : (clip + 1) * slots, :] = valid.astype(F32)
        offset = column - row
        distance = jnp.abs(offset)
        level = jnp.minimum(distance, HALF // 2)
        for mark in marks:
            level = level + (distance >= mark).astype(jnp.int32)
        bucket_ref[clip] = level + jnp.where(offset > 0, HALF, 0)
        away = jnp.where(valid, offset, far_place)
        for first in range(slots):
            seen = away[:, first : first + 1] <= ends_ref[...]
            rank_ref[clip, first : first + 1, :] = jnp.sum(seen.astype(jnp.int32), axis=0, keepdims=True)


def prep(mask, shape_id, slots):
    clips = mask.shape[0]
    ends = jnp.asarray(key_ends())[None, :]
    return call(
        partial(prep_kernel, far_marks()),
        (mask, ends),
        (
            shaped((clips, slots, slots), jnp.int32),
            shaped((clips, slots, KEYS), jnp.int32),
            shaped((clips * slots, 1), F32),
        ),
        8,
        "prep",
        scalars=(shape_id,),
    )


def position_rows(shards, by_key):
    width = (NPOS + shards - 1) // shards
    index = np.full((24, KEYS), -1, np.int64)
    for head in range(H):
        for lane in range(NB):
            bucket = (HALF - 1 - lane if lane < HALF else lane) if by_key else lane
            index[head, lane] = bucket * H + head
    for unit in range(gate_units):
        index[12 + unit, :HD] = NB * H + np.arange(HD) * gate_units + unit
    index[20, :gate_units] = (NB + 0) * H + HD * gate_units + np.arange(gate_units)
    index[21, :H] = NB * H + (HD + 1) * gate_units + np.arange(H)
    pieces = np.where(index >= 0, index // width, -1).astype(np.int32)
    columns = np.where(index >= 0, 12 * D // shards + index % width, -1).astype(np.int32)
    return jnp.asarray(pieces), jnp.asarray(columns)


def vector_chunks(shards):
    width = 12 * D // shards
    size = math.gcd(width, D)
    each, across = width // size, D // size
    return size, [
        (g // each, g % each * size, g // across, g % across * size) for g in range(12 * across)
    ]


def unpack_kernel(shards, turn_ref, pieces_ref, columns_ref, *refs):
    whole_ref, vectors_ref, bias_ref, table_ref, natural_ref, small_ref = refs
    natural_ref[...] = wide_dot(turn_ref[...], whole_ref[:, 4 * D :])
    each = D // shards
    wide = small_ref.shape[1]
    for k in range(wide // LANES):
        small_ref[:, k * LANES : (k + 1) * LANES] = natural_ref[pl.ds(k, shards, stride=each), :]
    size, chunks = vector_chunks(shards)
    for piece, column, row, place in chunks:
        value = small_ref[piece : piece + 1, column : column + size]
        if row < 8:
            vectors_ref[row : row + 1, place : place + size] = value
        else:
            bias_ref[:, (row - 8) * D + place : (row - 8) * D + place + size] = value
    start = 12 * D // shards // LANES * LANES
    small = small_ref[:, start:].astype(BF)
    piece_ids = lax.broadcasted_iota(jnp.int32, (shards, KEYS), 0)
    column_ids = lax.broadcasted_iota(jnp.int32, (wide - start, KEYS), 0) + start
    for row in range(22):
        chosen = (piece_ids == pieces_ref[row : row + 1, :]).astype(F32).astype(BF)
        spread = tn(small, chosen)
        table_ref[row : row + 1, :] = jnp.sum(
            jnp.where(column_ids == columns_ref[row : row + 1, :], spread, 0.0), axis=0, keepdims=True
        )
    table_ref[22:24, :] = jnp.zeros((2, KEYS), F32)


def small_lanes(shards):
    return -(-(12 * D // shards + (NPOS + shards - 1) // shards) // LANES) * LANES


def unpack(shards, turn, whole):
    pieces, columns = position_rows(shards, False)
    return call(
        partial(unpack_kernel, shards),
        (turn, pieces, columns, whole),
        (shaped((8, D), F32), shaped((1, FF), F32), shaped((24, KEYS), F32)),
        8,
        "unpack",
        scratch=(
            pltpu.VMEM((D, LANES), F32),
            pltpu.VMEM((shards, small_lanes(shards)), F32),
        ),
    )


def pack_kernel(shards, turn_ref, pieces_ref, columns_ref, attention_ref, first_ref, second_ref, bias_ref, table_ref, out_ref, natural_ref, small_ref):
    each = D // shards
    wide = small_ref.shape[1]
    table = table_ref[...]
    lane = lax.broadcasted_iota(jnp.int32, table.shape, 1)
    row_id = lax.broadcasted_iota(jnp.int32, table.shape, 0)
    before = jnp.where((lane > 0) & (row_id < H), pltpu.roll(table, 1, 1), 0.0)
    table = table - before
    piece_ids = lax.broadcasted_iota(jnp.int32, (shards, KEYS), 0)
    start = 12 * D // shards // LANES * LANES
    column_ids = lax.broadcasted_iota(jnp.int32, (wide - start, KEYS), 0) + start
    total = jnp.zeros((shards, wide - start), F32)
    for row in range(22):
        chosen = jnp.where(piece_ids == pieces_ref[row : row + 1, :], table[row : row + 1, :], 0.0).astype(BF)
        spread = (column_ids == columns_ref[row : row + 1, :]).astype(F32).astype(BF)
        total = total + nt(chosen, spread)
    small_ref[...] = jnp.zeros(small_ref.shape, F32)
    small_ref[:, start:] = total
    rows = [(attention_ref, 0), (attention_ref, 1)]
    rows += [(first_ref, i) for i in range(3)] + [(second_ref, i) for i in range(3)]
    size, chunks = vector_chunks(shards)
    for piece, column, row, place in chunks:
        if row < 8:
            ref, at = rows[row]
            value = ref[at : at + 1, place : place + size]
        else:
            value = bias_ref[:, (row - 8) * D + place : (row - 8) * D + place + size]
        small_ref[piece : piece + 1, column : column + size] = value
    natural_ref[...] = jnp.zeros(natural_ref.shape, F32)
    for k in range(wide // LANES):
        natural_ref[pl.ds(k, shards, stride=each), :] = small_ref[:, k * LANES : (k + 1) * LANES]
    out_ref[...] = tn(turn_ref[...], natural_ref[...].astype(BF)).astype(BF)


def pack(shards, turn, sums_attention, sums_first, sums_second, bias, table):
    pieces, columns = position_rows(shards, True)
    return call(
        partial(pack_kernel, shards),
        (turn, pieces, columns, sums_attention, sums_first, sums_second, bias, table),
        (shaped((D, LANES), BF),),
        8,
        "pack",
        scratch=(pltpu.VMEM((D, LANES), F32), pltpu.VMEM((shards, small_lanes(shards)), F32)),
    )[0]


def lookup(table_ref, head, index, block):
    out = None
    for part in range(KEYS // LANES):
        row = jnp.broadcast_to(table_ref[head : head + 1, part * LANES : (part + 1) * LANES], index.shape)
        found = jnp.take_along_axis(row, index, axis=1, mode="promise_in_bounds")
        out = found if out is None else jnp.where(block == part, found, out)
    return out


def nt(a, b):
    return lax.dot_general(a, b, (((1,), (1,)), ((), ())), preferred_element_type=F32)


def tn(a, b):
    return lax.dot_general(a, b, (((0,), (0,)), ((), ())), preferred_element_type=F32)


def vmem(count):
    return [pl.BlockSpec(memory_space=pltpu.VMEM)] * count


def limits(mib):
    return pltpu.CompilerParams(vmem_limit_bytes=mib * 1024 * 1024)


def shaped(shape, dtype):
    return jax.ShapeDtypeStruct(tuple(shape), dtype)


def call(kernel, operands, outs, mib, name, scalars=(), scratch=()):
    return pl.pallas_call(
        kernel,
        out_shape=tuple(outs),
        in_specs=[pl.BlockSpec(memory_space=pltpu.SMEM)] * len(scalars) + vmem(len(operands)),
        out_specs=tuple(vmem(len(outs))),
        scratch_shapes=list(scratch),
        compiler_params=limits(mib),
        cost_estimate=pl.CostEstimate(flops=1, bytes_accessed=1, transcendentals=0),
        name=name,
    )(*scalars, *operands)


def build_kernel(plans, count, *refs):
    sources, outs = refs[:count], refs[count:]
    for out, (whole, items) in zip(outs, plans):
        if not whole:
            out[...] = jnp.zeros(out.shape, out.dtype)
        for row, column, rows, columns, views in items:
            values = [
                sources[which][first : first + rows, left : left + columns] for which, first, left in views
            ]
            if len(values) > 1:
                values = [sum(value.astype(F32) for value in values)]
            out[row : row + rows, column : column + columns] = values[0].astype(out.dtype)


def build(*outs):
    sources, plans = [], []
    for shape, items in outs:
        plan = []
        for row, column, rows, columns, views in items:
            found = []
            for array, first, left in views:
                at = next((i for i, source in enumerate(sources) if source is array), None)
                if at is None:
                    at = len(sources)
                    sources.append(array)
                found.append((at, first, left))
            plan.append((row, column, rows, columns, found))
        plans.append((sum(item[2] * item[3] for item in items) == math.prod(shape), plan))
    return call(
        partial(build_kernel, plans, len(sources)), sources, [shaped(shape, BF) for shape, _ in outs], 8, "build"
    )


def stack(parts):
    items, at = [], 0
    for array, row, rows, column, columns in parts:
        items.append((at, 0, rows, columns, [(array, row, column)]))
        at += rows
    return (at, parts[0][4]), items


def whole_of(array):
    return (array, 0, array.shape[0], 0, array.shape[1])


def normal(entries):
    centre = entries - jnp.mean(entries, axis=-1, keepdims=True)
    scale = lax.rsqrt(jnp.mean(centre * centre, axis=-1, keepdims=True) + layer_epsilon)
    return centre * scale, scale


def normal_back(grad, unit, scale):
    return scale * (
        grad
        - jnp.mean(grad, axis=-1, keepdims=True)
        - unit * jnp.mean(grad * unit, axis=-1, keepdims=True)
    )


def wide_dot(a, b):
    return jnp.dot(a, b, preferred_element_type=F32)


def split(value, count):
    parts = []
    for _ in range(count):
        parts.append(value.astype(BF))
        value = value - parts[-1].astype(F32)
    return parts


def joined_kernel(
    x_ref, turn_ref, vectors_ref, table_ref, whole_ref, slots_ref, joined_ref, gate_ref, logits_ref
):
    slots_ref[...] = wide_dot(x_ref[...], turn_ref[...]).astype(BF)
    for part in range(3):
        cols = slice(part * D, (part + 1) * D)
        made = wide_dot(slots_ref[...], whole_ref[:, cols])
        if part != 1:
            made = made + vectors_ref[part // 2 : part // 2 + 1, :]
        joined_ref[:, cols] = made.astype(BF)
    units = table_ref[12:20, :HD].astype(BF)
    logits_ref[...] = jnp.zeros(logits_ref.shape, F32)
    for head in range(H):
        logits_ref[:, head * gate_units : (head + 1) * gate_units] = (
            nt(x_ref[:, head * HD : (head + 1) * HD], units) + table_ref[20:21, :gate_units]
        )
    up = lax.broadcasted_iota(jnp.int32, (LANES, LANES), 0)
    across = lax.broadcasted_iota(jnp.int32, (LANES, LANES), 1)
    logits = split(logits_ref[...], 3)
    gates = []
    for side in range(2):
        chosen = ((up >> 3) == across) & (((up >> 2) & 1) == side)
        chosen = chosen.astype(F32).astype(BF)
        gates.append(jax.nn.sigmoid(sum(wide_dot(part, chosen) for part in logits)))
    first, second = gates
    gate_ref[0] = first * (second * table_ref[21:22, :LANES] - 1.0) + 2.0
    gate_ref[1] = first
    gate_ref[2] = second


def joined_forward(x, turn, vectors, table, whole):
    rows = x.shape[0]
    return call(
        joined_kernel,
        (x, turn, vectors, table, whole),
        (
            shaped((rows, D), BF),
            shaped((rows, 3 * D), BF),
            shaped((3, rows, LANES), F32),
        ),
        8,
        "joined_forward",
        scratch=(pltpu.VMEM((rows, LANES), F32),),
    )


def attention_kernel(clip, bucket_ref, valid_ref, table_ref, joined_ref, gate_ref, prob_ref, rel_ref, mixed_ref):
    slots = bucket_ref.shape[1]
    rows = slice(clip * slots, (clip + 1) * slots)
    index = bucket_ref[clip] & (LANES - 1)
    block = bucket_ref[clip] >> 7
    valid = valid_ref[rows, :] > 0
    gate = jnp.transpose(gate_ref[0, rows, :])
    for head in range(H):
        rel_ref[head] = lookup(table_ref, head, index, block)
    for head in range(H):
        query = joined_ref[rows, head * HD : (head + 1) * HD]
        key = joined_ref[rows, D + head * HD : D + (head + 1) * HD]
        score = nt(key, query) * (1.0 / math.sqrt(HD)) + gate[head : head + 1, :] * rel_ref[head]
        prob_ref[head] = jnp.where(valid, score, masked_score)
    for first in range(0, H, 4):
        score = prob_ref[first : first + 4]
        power = jnp.exp(score - jnp.max(score, axis=1, keepdims=True))
        prob_ref[first : first + 4] = power * (1.0 / jnp.sum(power, axis=1, keepdims=True))
    for head in range(H):
        value = joined_ref[rows, 2 * D + head * HD : 2 * D + (head + 1) * HD]
        mixed_ref[head * HD : (head + 1) * HD, :] = tn(value, prob_ref[head].astype(BF)).astype(BF)


def attention(clip, bucket, valid, table, joined, gate):
    slots = bucket.shape[1]
    return call(
        partial(attention_kernel, clip),
        (bucket, valid, table, joined, gate),
        (shaped((H, slots, slots), F32), shaped((H, slots, slots), F32), shaped((D, slots), BF)),
        4,
        "attention",
    )


def out_kernel(x_ref, turn_ref, vectors_ref, whole_ref, *refs):
    mixed_ref, unit_ref, scale_ref = refs[-3:]
    at = 0
    for part in refs[:-3]:
        rows = slice(at, at + part.shape[1])
        mixed_ref[rows, :] = tn(part[...], turn_ref[...]).astype(BF)
        at += part.shape[1]
    branch = wide_dot(mixed_ref[...], whole_ref[:, 3 * D : 4 * D]) + vectors_ref[2:3, :]
    unit, scale = normal(deep_alpha * x_ref[...].astype(F32) + branch)
    unit_ref[...] = unit
    scale_ref[...] = scale


def out_forward(x, turn, vectors, whole, mixed):
    rows = x.shape[0]
    return call(
        out_kernel,
        (x, turn, vectors, whole, *mixed),
        (shaped((rows, D), BF), shaped((rows, D), F32), shaped((rows, 1), F32)),
        6,
        "out_forward",
    )


def attention_back_kernel(
    clip, joined_ref, gate_ref, rank_ref, prob_ref, rel_ref, grad_ref, tri_ref,
    joined_grad_ref, gate_grad_ref, table_grad_ref,
):
    slots = rank_ref.shape[1]
    rows = slice(clip * slots, (clip + 1) * slots)
    scale = 1.0 / math.sqrt(HD)
    gate = jnp.transpose(gate_ref[0, rows, :])
    for head in range(H):
        cols = slice(head * HD, (head + 1) * HD)
        key_cols = slice(D + head * HD, D + (head + 1) * HD)
        value_cols = slice(2 * D + head * HD, 2 * D + (head + 1) * HD)
        query = joined_ref[rows, cols]
        key = joined_ref[rows, key_cols]
        value = joined_ref[rows, value_cols]
        grad = grad_ref[rows, cols]
        prob = prob_ref[head]
        joined_grad_ref[:, value_cols] = wide_dot(prob.astype(BF), grad).astype(BF)
        weighted = prob * nt(value, grad)
        low = (weighted - prob * jnp.sum(weighted, axis=0, keepdims=True)).astype(BF)
        joined_grad_ref[:, cols] = (tn(low, key) * scale).astype(BF)
        joined_grad_ref[:, key_cols] = (wide_dot(low, query) * scale).astype(BF)
        wide = low.astype(F32)
        gate_grad_ref[head : head + 1, :] = jnp.sum(wide * rel_ref[head], axis=0, keepdims=True)
        gated = wide * gate[head : head + 1, :]
        high = gated.astype(BF)
        rest = (gated - high.astype(F32)).astype(BF)
        running = tn(high, tri_ref[...]) + tn(rest, tri_ref[...])
        for part in range(KEYS // LANES):
            lanes = slice(part * LANES, (part + 1) * LANES)
            rank = rank_ref[clip, :, lanes]
            found = jnp.take_along_axis(
                running, jnp.maximum(rank - 1, 0), axis=1, mode="promise_in_bounds"
            )
            table_grad_ref[head : head + 1, lanes] = jnp.sum(
                jnp.where(rank > 0, found, 0.0), axis=0, keepdims=True
            )
    table_grad_ref[H:, :] = jnp.zeros((16 - H, KEYS), F32)
    gate_grad_ref[H:, :] = jnp.zeros((16 - H, slots), F32)


def attention_back(clip, joined, gate, rank, prob, rel, grad):
    slots = rank.shape[1]
    tri = jnp.asarray(np.triu(np.ones((slots, slots), np.float32)), BF)
    return call(
        partial(attention_back_kernel, clip),
        (joined, gate, rank, prob, rel, grad, tri),
        (shaped((slots, 3 * D), BF), shaped((16, slots), F32), shaped((16, KEYS), F32)),
        4,
        "attention_back",
    )


def gate_back_kernel(count, x_ref, table_ref, gate_ref, *refs):
    joined_grads, gate_grads, table_grads = refs[:count], refs[count : 2 * count], refs[2 * count : 3 * count]
    x_grad_ref, table_grad_ref, sums_ref = refs[3 * count :]
    table_grad_ref[...] = jnp.zeros(table_grad_ref.shape, F32)
    table_grad_ref[:16, :] = sum(ref[...] for ref in table_grads)
    sums_ref[0:1, :] = sum(jnp.sum(ref[:, :D].astype(F32), axis=0, keepdims=True) for ref in joined_grads)
    sums_ref[1:2, :] = sum(jnp.sum(ref[:, 2 * D :].astype(F32), axis=0, keepdims=True) for ref in joined_grads)
    units = [jnp.sum(table_ref[12 + 4 * i : 16 + 4 * i, :HD], axis=0, keepdims=True) for i in range(2)]
    unit_grads = [jnp.zeros((1, HD), F32), jnp.zeros((1, HD), F32)]
    grad = jnp.concatenate([jnp.transpose(ref[...]) for ref in gate_grads], axis=0)
    first, second = gate_ref[1, :, :16], gate_ref[2, :, :16]
    size = table_ref[21:22, :16]
    grads = (
        grad * (second * size - 1.0) * first * (1.0 - first),
        grad * first * size * second * (1.0 - second),
    )
    table_grad_ref[21:22, :16] = jnp.sum(grad * first * second, axis=0, keepdims=True)
    bias_grads = [jnp.sum(jnp.sum(g, axis=0, keepdims=True), axis=1, keepdims=True) for g in grads]
    for head in range(H):
        cols = slice(head * HD, (head + 1) * HD)
        x = x_ref[:, cols].astype(F32)
        sides = [g[:, head : head + 1] for g in grads]
        x_grad_ref[:, cols] = sides[0] * units[0] + sides[1] * units[1]
        for i in range(2):
            unit_grads[i] = unit_grads[i] + jnp.sum(x * sides[i], axis=0, keepdims=True)
    for unit in range(gate_units):
        table_grad_ref[12 + unit : 13 + unit, :HD] = unit_grads[unit // 4]
        table_grad_ref[20:21, unit : unit + 1] = bias_grads[unit // 4]


def gate_back(x, table, gate, joined_grads, gate_grads, table_grads):
    return call(
        partial(gate_back_kernel, len(joined_grads)),
        (x, table, gate, *joined_grads, *gate_grads, *table_grads),
        (shaped(x.shape, F32), shaped((24, KEYS), F32), shaped((8, D), F32)),
        6,
        "gate_back",
    )


def gelu_pair(u):
    size = jnp.abs(u) * math.sqrt(0.5)
    t = 1.0 / (1.0 + 0.3275911 * size)
    poly = ((((1.061405429 * t - 1.453152027) * t + 1.421413741) * t - 0.284496736) * t + 0.254829592) * t
    bell = jnp.exp(-0.5 * u * u)
    tail = 0.5 * poly * bell
    below = jnp.where(u < 0, tail, 1.0 - tail)
    return u * below, below + u * bell * (1.0 / math.sqrt(2.0 * math.pi))


def hidden_kernel(
    unit_ref, vectors_ref, turn_ref, bias_ref, whole_ref, slots_ref, active_ref, slope_ref
):
    low = (unit_ref[...] * vectors_ref[3:4, :] + vectors_ref[4:5, :]).astype(BF)
    slots_ref[...] = wide_dot(low, turn_ref[...]).astype(BF)
    width = FF // 8
    for block in range(8):
        cols = slice(block * width, (block + 1) * width)
        u = wide_dot(slots_ref[...], whole_ref[:, cols]) + bias_ref[:, cols]
        active, slope = gelu_pair(u)
        active_ref[:, cols] = active.astype(BF)
        slope_ref[:, cols] = slope


def hidden_forward(unit, vectors, turn, bias, whole):
    rows = unit.shape[0]
    return call(
        hidden_kernel,
        (unit, vectors, turn, bias, whole),
        (shaped((rows, D), BF), shaped((rows, FF), BF), shaped((rows, FF), F32)),
        10,
        "hidden_forward",
    )


def turn_kernel(slots, *refs):
    at_ref, active_ref, unit_ref, vectors_ref, valid_ref, cot_ref = refs[:6]
    parts = refs[6:-5]
    whole_ref, out_ref, second_ref, low_ref, sums_ref = refs[-5:]
    for slot, (which, row, rows, column) in enumerate(slots):
        place = pl.multiple_of(at_ref[slot], 16)
        if parts[which].shape[1] == D:
            whole_ref[pl.ds(place, rows), :] = parts[which][row : row + rows, :]
            continue
        blocks = [
            parts[which][row : row + rows, column + j * D : column + (j + 1) * D] for j in range(FF // D)
        ]
        whole_ref[pl.ds(place, rows * len(blocks)), :] = jnp.concatenate(blocks, axis=0)
    made = wide_dot(active_ref[...], whole_ref[...]) + vectors_ref[5:6, :]
    first_norm = unit_ref[...] * vectors_ref[3:4, :] + vectors_ref[4:5, :]
    unit, scale = normal(deep_alpha * first_norm + made.astype(BF).astype(F32))
    valid = valid_ref[...]
    gain = vectors_ref[6:7, :]
    out_ref[...] = ((unit * gain + vectors_ref[7:8, :]) * valid).astype(BF)
    grad = cot_ref[...].astype(F32) * valid
    second = normal_back(grad * gain, unit, scale)
    second_ref[...] = second
    low = second.astype(BF)
    low_ref[...] = low
    sums_ref[0:1, :] = jnp.sum(low.astype(F32), axis=0, keepdims=True)
    sums_ref[1:2, :] = jnp.sum(grad * unit, axis=0, keepdims=True)
    sums_ref[2:3, :] = jnp.sum(grad, axis=0, keepdims=True)


def turn_back(at, slots, active, unit, vectors, valid, cot, parts):
    rows = unit.shape[0]
    return call(
        partial(turn_kernel, slots),
        (active, unit, vectors, valid, cot, *parts),
        (shaped((FF, D), BF), shaped((rows, D), BF), shaped((rows, D), F32), shaped((rows, D), BF), shaped((8, D), F32)),
        10,
        "turn_back",
        scalars=(at,),
    )


def turn_active_kernel(rows, at_ref, active_ref, out_ref, turned_ref):
    for first in range(0, FF, FF // 8):
        cols = slice(first, first + FF // 8)
        turned_ref[cols, :] = jnp.transpose(active_ref[:, cols])
    for slot in range(FF // rows):
        place = pl.multiple_of(at_ref[slot], 16)
        out_ref[slot * rows : (slot + 1) * rows, :] = turned_ref[pl.ds(place, rows), :]


def turn_active(at, rows, active):
    return call(
        partial(turn_active_kernel, rows),
        (active,),
        (shaped((FF, active.shape[0]), BF),),
        8,
        "turn_active",
        scalars=(at,),
        scratch=(pltpu.VMEM((FF, active.shape[0]), BF),),
    )[0]


def down_back_kernel(first, rows, active_ref, low_ref, out_ref):
    chunk = rows * FF // D
    for slot in range(FF // 2 // chunk):
        at = first + slot * chunk
        made = wide_dot(active_ref[at : at + chunk, :], low_ref[...]).astype(BF)
        for j in range(FF // D):
            out_ref[slot * rows : (slot + 1) * rows, j * D : (j + 1) * D] = made[j * rows : (j + 1) * rows, :]


def down_back(half, rows, active, low):
    return call(
        partial(down_back_kernel, half * FF // 2, rows),
        (active, low),
        (shaped((D // 2, FF), BF),),
        6,
        "down_back",
    )[0]


def hidden_back_kernel(low_ref, down_ref, slope_ref, grad_ref, bias_ref):
    width = FF // 8
    for block in range(8):
        cols = slice(block * width, (block + 1) * width)
        grad = (nt(low_ref[...], down_ref[cols, :]) * slope_ref[:, cols]).astype(BF)
        grad_ref[:, cols] = grad
        bias_ref[:, cols] = jnp.sum(grad.astype(F32), axis=0, keepdims=True)


def hidden_back(low, down, slope):
    rows = low.shape[0]
    return call(
        hidden_back_kernel,
        (low, down, slope),
        (shaped((rows, FF), BF), shaped((1, FF), F32)),
        6,
        "hidden_back",
    )


def in_back_kernel(slots_ref, grad_ref, mine_ref, other_ref):
    width = FF // 4
    for block in range(4):
        cols = slice(block * width, (block + 1) * width)
        made = tn(slots_ref[...], grad_ref[:, cols]).astype(BF)
        mine_ref[:, cols] = made[: D // 2]
        other_ref[:, cols] = made[D // 2 :]


def in_back(slots, grad):
    rows = slots.shape[0]
    return call(
        in_back_kernel,
        (slots, grad),
        (shaped((D // 2, FF), BF), shaped((D // 2, FF), BF)),
        6,
        "in_back",
    )


def out_back_kernel(
    grad_ref, in_ref, turn_ref, second_ref, unit_ref, scale_ref, vectors_ref, mixed_ref, out_ref,
    first_ref, weight_ref, mixed_grad_ref, sums_ref,
):
    low = nt(grad_ref[...], in_ref[...]).astype(BF)
    grad = deep_alpha * second_ref[...] + nt(low, turn_ref[...]).astype(BF).astype(F32)
    unit = unit_ref[...]
    first = normal_back(grad * vectors_ref[3:4, :], unit, scale_ref[...])
    first_ref[...] = first
    branch = first.astype(BF)
    sums_ref[0:1, :] = jnp.sum(branch.astype(F32), axis=0, keepdims=True)
    sums_ref[1:2, :] = jnp.sum(grad * unit, axis=0, keepdims=True)
    sums_ref[2:3, :] = jnp.sum(grad, axis=0, keepdims=True)
    weight_ref[...] = tn(mixed_ref[...], branch).astype(BF)
    back = nt(branch, out_ref[:, 3 * D : 4 * D]).astype(BF)
    mixed_grad_ref[...] = nt(back, turn_ref[...]).astype(BF)


def out_back(grad, w_in, turn, second, unit, scale, vectors, mixed, w_first):
    rows = unit.shape[0]
    return call(
        out_back_kernel,
        (grad, w_in, turn, second, unit, scale, vectors, mixed, w_first),
        (shaped((rows, D), F32), shaped((D, D), BF), shaped((rows, D), BF), shaped((8, D), F32)),
        6,
        "out_back",
    )


def first_back_kernel(slots_ref, out_ref, small_ref, *refs):
    *grads, mine_ref, other_ref, grad_ref = refs
    at = 0
    for grad in grads:
        grad_ref[at : at + grad.shape[0], :] = grad[...]
        at += grad.shape[0]
    half = D // 2
    for part in range(3):
        cols = slice(part * D, (part + 1) * D)
        made = tn(slots_ref[...], grad_ref[:, cols]).astype(BF)
        mine_ref[:, cols] = made[:half]
        other_ref[:, cols] = made[half:]
    for ref, rows in ((mine_ref, slice(0, half)), (other_ref, slice(half, D))):
        ref[:, 3 * D : 4 * D] = out_ref[rows, :]
        ref[:, 4 * D :] = small_ref[rows, :]


def first_back(slots, weight_out, small, grads):
    rows = slots.shape[0]
    wide = 4 * D + small.shape[1]
    return call(
        first_back_kernel,
        (slots, weight_out, small, *grads),
        (shaped((D // 2, wide), BF), shaped((D // 2, wide), BF), shaped((rows, 3 * D), BF)),
        6,
        "first_back",
    )


def rows_back_kernel(grad_ref, first_ref, turn_ref, branch_ref, gate_ref, out_ref):
    made = nt(grad_ref[...], first_ref[:, : 3 * D])
    high = made.astype(BF)
    rest = made - high.astype(F32)
    middle = rest.astype(BF)
    last = (rest - middle.astype(F32)).astype(BF)
    turned = nt(high, turn_ref[...]) + nt(middle, turn_ref[...]) + nt(last, turn_ref[...])
    out_ref[...] = turned + deep_alpha * branch_ref[...] + gate_ref[...]


def rows_back(grad, w_first, turn, branch, gate):
    rows = grad.shape[0]
    return call(
        rows_back_kernel,
        (grad, w_first, turn, branch, gate),
        (shaped((rows, D), F32),),
        8,
        "rows_back",
    )[0]


def flat_cuts(each):
    cuts = [(0, row, 0, 3 * D) for row in range(each)]
    cuts += [(0, row, 3 * D, 4 * D) for row in range(each)]
    cuts += [(1, row, 0, FF) for row in range(each)]
    cuts += [(2, row, j * D, (j + 1) * D) for j in range(FF // D) for row in range(each)]
    return cuts + [(0, row, 4 * D, 4 * D + LANES) for row in range(each)]


def flat_runs(each, width):
    at = 0
    for which, row, first, last in flat_cuts(each):
        size = min(last - first, width - at)
        if size > 0:
            yield which, row, first, size, at
        at += last - first


def rows_kernel(flat_ref, first_ref, in_ref, down_ref):
    refs = (first_ref, in_ref, down_ref)
    first_ref[:, 4 * D :] = jnp.zeros((first_ref.shape[0], LANES), F32)
    for which, row, first, size, at in flat_runs(first_ref.shape[0], flat_ref.shape[1]):
        refs[which][row : row + 1, first : first + size] = flat_ref[:, at : at + size]


def pieces_kernel(flat_ref, first_ref, in_ref, down_ref, all_ref, *refs):
    rows_kernel(flat_ref, *refs)
    at = 0
    for ref, low in zip(refs, (first_ref, in_ref, down_ref)):
        low[...] = ref[...].astype(BF)
        all_ref[:, at : at + low.shape[1]] = low[...]
        at += low.shape[1]


def row_widths():
    return (4 * D + LANES, FF, FF)


def flat_rows(flat, each):
    return call(rows_kernel, (flat,), [shaped((each, width), F32) for width in row_widths()], 6, "flat_rows")


def pieces(flat, each):
    widths = row_widths()
    return call(
        pieces_kernel,
        (flat,),
        [shaped((each, width), BF) for width in (*widths, sum(widths))],
        6,
        "pieces",
        scratch=[pltpu.VMEM((each, width), F32) for width in widths],
    )


def update_kernel(learning, plan, count, *refs):
    sums = refs[:count]
    refs = refs[count:]
    weights, momenta, averages, outs, rows = refs[:3], refs[3:6], refs[6:9], refs[9:13], refs[13:]
    for i in range(3):
        each, wide = weights[i].shape
        grad = sum(
            sums[which][row : row + each, column : column + wide].astype(F32) for which, row, column in plan[i]
        )
        weight = weights[i][...]
        decayed = grad + decay_rate * weight
        momentum = momentum_rate * momenta[i][...] + decayed
        weight = weight - learning * (decayed + momentum_rate * momentum)
        rows[i][...] = momentum
        rows[3 + i][...] = average_rate * averages[i][...] + (1.0 - average_rate) * weight
        rows[6 + i][...] = weight
    for out, which in zip(outs, (0, 3, 6, 6)):
        for section, row, first, size, at in flat_runs(rows[0].shape[0], out.shape[1]):
            value = rows[which + section][row : row + 1, first : first + size]
            out[:, at : at + size] = value.astype(out.dtype)


def update(learning, sums, weights, momenta, averages, width):
    arrays, plan = [], []
    for views in sums:
        found = []
        for array, row, column in views:
            at = next((i for i, known in enumerate(arrays) if known is array), None)
            if at is None:
                at = len(arrays)
                arrays.append(array)
            found.append((at, row, column))
        plan.append(found)
    rows = [pltpu.VMEM(part.shape, F32) for part in weights] * 3
    return call(
        partial(update_kernel, learning, plan, len(arrays)),
        [*arrays, *weights, *momenta, *averages],
        (shaped((1, width), F32),) * 3 + (shaped((1, width), BF),),
        8,
        "update",
        scratch=rows,
    )


def body(acts, cotangent, mask, shape_id, weights, momenta, averages):
    shards = lax.axis_size(("dp", "fsdp"))
    count = lax.axis_size("dp")
    dp, core = lax.axis_index("dp"), lax.axis_index("fsdp")
    clips, slots = acts.shape[0], acts.shape[1]
    rows = clips * slots
    total_tokens = rows * shards
    piece_rows = D // shards
    wide_rows = FF // shards
    vector_width = 12 * D // shards
    position_width = (NPOS + shards - 1) // shards
    small_width = vector_width + position_width

    piece_first, piece_in, piece_down, piece_all = pieces(weights, piece_rows)

    order = slot_order(dp, core, count)
    row_order = (order[:, None] * piece_rows + jnp.arange(piece_rows, dtype=jnp.int32)).reshape(-1)
    turn = (jnp.arange(D, dtype=jnp.int32)[:, None] == row_order[None, :]).astype(BF)
    piece_turn = (jnp.arange(shards, dtype=jnp.int32)[:, None] == order[None, :]).astype(BF)

    back_order = jnp.dot(piece_turn.astype(F32), jnp.arange(shards, dtype=F32)).astype(jnp.int32)

    together = lax.optimization_barrier
    bits = high_bits(count)
    staged = len(bits) == 2
    n = piece_rows
    rest = D // 8 - n
    widths = (piece_first.shape[1], FF, FF)
    lefts = (0, widths[0], widths[0] + FF)
    cuts = (13 * LANES, FF // 2, FF // 2)
    wide_all, cut_all = sum(widths), 37 * LANES
    third = (13 * LANES, 12 * LANES, 12 * LANES), (12 * LANES,) * 3
    at = order * wide_rows
    inputs_low = acts.reshape(rows, D)

    def gather_high(piece):
        if staged:
            return [exchange(piece, "dp", d << 2) for d in (1, 2, 3)]
        column = piece
        for bit in bits:
            column = jnp.concatenate([column, exchange(column, "dp", 1 << bit)], axis=0)
        return [column[n:]]

    def thirds(side, views):
        left = widths[0]
        items, column = [], 0
        for i, size in enumerate(third[side]):
            items += views(i * n, left, column, size)
            column += size
        return items

    own_sides = exchange_sides((piece_all, piece_all))
    high_first = gather_high(piece_first)
    own_sides, high_first, piece_in, mask, turn, at = together(
        (own_sides, high_first, piece_in, mask, turn, at)
    )

    items = stack([whole_of(part) for part in high_first])[1]
    sends = build(
        ((rest, widths[0]), items),
        (
            (rest, widths[0] + third[1][0]),
            items + thirds(1, lambda row, left, c, w: [(row, left, n, w, [(own_sides[1], 0, cut_all + c)])]),
        ),
        (
            (rest, widths[0] + third[0][0]),
            items + thirds(0, lambda row, left, c, w: [(row, left, n, w, [(own_sides[0], 0, c)])]),
        ),
    )
    rest_first, sends = sends[0], sends[1:]
    sides_first = exchange_sides(sends)
    high_in = gather_high(piece_in)
    bucket, rank, valid_rows = prep(mask, shape_id, slots)
    sides_first, high_in, piece_down, bucket, rank, valid_rows = together(
        (sides_first, high_in, piece_down, bucket, rank, valid_rows)
    )

    def corner_sends(unit, sides):
        wide, half = widths[unit], cuts[unit]
        return (
            ((rest, wide - half), [(0, 0, rest, wide - half, [(sides[1], 0, half)])]),
            ((rest, half), [(0, 0, rest, half, [(sides[0], 0, 0)])]),
        )

    def corner_items(unit, corner):
        wide, half = widths[unit], cuts[unit]
        (second, left_second), (first, left_first) = corner
        return [
            (0, 0, rest, half, [(first, 0, left_first)]),
            (0, half, rest, wide - half, [(second, 0, left_second)]),
        ]

    def early_rows(unit, piece, high, sides):
        wide = widths[unit]
        return stack([whole_of(piece), whole_of(high)] + [(side, 0, rest, 0, wide) for side in sides])

    def shifted(items, row):
        return [(row + item[0], *item[1:]) for item in items]

    def slots_of(unit, piece, high, sides, corner, early, late):
        wide, left = widths[unit], lefts[unit]
        own_mine, own_other = own
        items = [(0, 0, n, wide, [(piece, 0, 0)]), (n, 0, rest, wide, [(high, 0, 0)])]
        eighth = D // 8
        for i in range(3):
            items.append(((i + 1) * eighth, 0, n, wide, [(own_mine, i * n, left)]))
        for i, side in enumerate(sides):
            items.append(((i + 1) * eighth + n, 0, rest, wide, [(side, 0, 0)]))
        items += shifted(corner_items(unit, corner), 3 * eighth + n)
        base = D // 2
        if not isinstance(early, tuple):
            early = (early, 0), (early, n + rest)
        (one, row_one), (two, row_two) = early
        items.append((base, 0, n, wide, [(one, row_one, 0)]))
        items.append((base + n, 0, rest, wide, [(one, row_one + n, 0)]))
        for i in range(3):
            items.append((base + (i + 1) * eighth, 0, n, wide, [(own_other, i * n, left)]))
            view = (late, 0, 0) if i == 2 else (two, row_two + i * rest, 0)
            items.append((base + (i + 1) * eighth + n, 0, rest, wide, [view]))
        return items

    def own_corner(row, half, side, column):
        return [(row, column + c, n, w, [(side, i * n, widths[0])]) for i, (c, w) in enumerate(half)]

    def spans(side):
        edges = np.cumsum((0, *third[side]))
        return [(int(a), int(b - a)) for a, b in zip(edges[:-1], edges[1:])]

    items = [(0, 0, n, wide_all, [(own_sides[0], 0, 0)]), (n, 0, n, wide_all, [(own_sides[1], 0, 0)])]
    items += own_corner(2 * n, spans(0), sides_first[1], 0) + own_corner(2 * n, spans(1), sides_first[0], cut_all)
    def side_sends(unit, high, sides):
        wide, half = widths[unit - 1], cuts[unit - 1]
        items = stack([whole_of(part) for part in high])[1]
        sends = []
        for width, view in ((wide - half, (sides[1], 0, half)), (half, (sides[0], 0, 0))):
            sends.append(((rest, widths[unit] + width), items + [(0, widths[unit], rest, width, [view])]))
        return [((rest, widths[unit]), items)] + sends

    own_mine, early, rest_in, *sends = build(
        ((3 * n, wide_all), items),
        early_rows(0, piece_first, rest_first, sides_first),
        *side_sends(1, high_in, sides_first),
    )
    sides_in = exchange_sides(sends)
    early_first = exchange_core(early)
    high_down = gather_high(piece_down)
    sides_in, early_first, high_down, own_mine = together((sides_in, early_first, high_down, own_mine))

    corner_first = [(part, FF) for part in sides_in]
    late, rest_down, *sends = build(
        ((rest, widths[0]), corner_items(0, corner_first)), *side_sends(2, high_down, sides_in)
    )
    sides_down = exchange_sides(sends)
    own = (own_mine, exchange_core(own_mine))
    late = exchange_core(late)
    items = slots_of(0, piece_first, rest_first, sides_first, corner_first, early_first, late)
    w_first = build(((D, widths[0]), items))[0]
    early, first_down = build(
        early_rows(1, piece_in, rest_in, sides_in), stack([whole_of(piece_down), whole_of(rest_down)])
    )
    early_in, first_down = exchange_core(early), exchange_core(first_down)
    vectors, bias_in, table = unpack(shards, turn, w_first)
    inputs_slots, joined, gate = joined_forward(inputs_low, turn, vectors, table, w_first)
    made = [attention(clip, bucket, valid_rows, table, joined, gate) for clip in range(clips)]
    mixed_slots, unit, unit_scale = out_forward(inputs_low, turn, vectors, w_first, [m[2] for m in made])
    sides_down, early_in, first_down, unit = together((sides_down, early_in, first_down, unit))

    corner_in = [(part, FF) for part in sides_down]
    late, early, *sends = build(
        ((rest, FF), corner_items(1, corner_in)),
        stack([(side, 0, rest, 0, FF) for side in sides_down]),
        *corner_sends(2, sides_down),
    )
    corner_down = exchange_sides(sends)
    late = exchange_core(late)
    early_down = exchange_core(early)
    items = slots_of(1, piece_in, rest_in, sides_in, corner_in, early_in, late)
    w_in = build(((D, FF), items))[0]
    first_slots, active, slope = hidden_forward(unit, vectors, turn, bias_in, w_in)
    corner_down, early_down, active = together((corner_down, early_down, active))

    corner_down = [(part, 0) for part in corner_down]
    corner = build(((rest, FF), corner_items(2, corner_down)))[0]
    late = exchange_core(corner)
    early_down = (first_down, 0), (early_down, 0)
    items = slots_of(2, piece_down, rest_down, sides_down, [(corner, cuts[2]), (corner, 0)], early_down, late)
    arrays, places = [], [None] * shards
    for row, column, size, _, [(array, first, left)] in items:
        if column:
            continue
        which = next((i for i, known in enumerate(arrays) if known is array), len(arrays))
        if which == len(arrays):
            arrays.append(array)
        for step in range(size // n):
            places[row // n + step] = (which, first + step * n, n, left)
    to = at
    if wide_rows % 16 == 0:
        turned = turn_active(at, wide_rows, active)
        turned, arrays[0] = together((turned, arrays[0]))
    else:
        parts = [arrays[which][row : row + n, left : left + FF] for which, row, _, left in places]
        stacked = jnp.stack(parts).reshape(shards, n, FF // D, D).transpose(0, 2, 1, 3).reshape(shards, wide_rows, D)
        arrays, places = [jnp.take(stacked, back_order, axis=0).reshape(FF, D)], [(0, 0, FF, 0)]
        to = jnp.zeros((1,), jnp.int32)
    w_down, activations, grad_second, grad_made, sums_second = turn_back(
        to, places, active, unit, vectors, valid_rows, cotangent.reshape(rows, D), arrays
    )

    if wide_rows % 16:
        grad_down = tn(active, grad_made).astype(BF).reshape(shards, wide_rows, D)
        grad_down = jnp.take(grad_down, order, axis=0).reshape(shards, FF // D, n, D).transpose(0, 2, 1, 3)
        grad_down = grad_down.reshape(D, FF)
        down_mine, down_other = grad_down[: D // 2], grad_down[D // 2 :]
    else:
        down_other = down_back(1, n, turned, grad_made)
        down_other, grad_made = together((down_other, grad_made))
        down_mine = down_back(0, n, turned, grad_made)

    eighth = D // 8

    def both(pair, row, column):
        return [(array, row, column) for array in pair]

    def corner_out(unit, pair):
        wide, half = widths[unit], cuts[unit]
        row = 3 * eighth + n
        return (
            (wide - half, [(0, 0, rest, wide - half, both(pair, row, half))]),
            (half, [(0, 0, rest, half, both(pair, row, 0))]),
        )

    def sides_out(unit, pair, corner):
        wide, half = widths[unit], cuts[unit]
        (second, left_second), (first, left_first) = corner
        near, side = eighth + n, 2 * eighth + n
        return (
            (
                wide,
                [
                    (0, 0, rest, half, both(pair, near, 0) + [(first, 0, left_first)]),
                    (0, half, rest, wide - half, both(pair, near, half)),
                ],
            ),
            (
                wide,
                [
                    (0, 0, rest, half, both(pair, side, 0)),
                    (0, half, rest, wide - half, both(pair, side, half) + [(second, 0, left_second)]),
                ],
            ),
        )

    def beside(one, two):
        return [
            ((rest, a[0] + b[0]), a[1] + [(item[0], a[0] + item[1], *item[2:]) for item in b[1]])
            for a, b in zip(one, two)
        ]

    def alone(one):
        return [((rest, wide), items) for wide, items in one]

    def column_views(unit, pair, sides, row):
        return both(pair, row, 0) + [(side, row - n, 0) for side in sides]

    def high_out(unit, pair, sides, first, count, *more):
        wide = widths[unit]
        views = column_views(unit, pair, sides, first * n)
        if more:
            views = views + [(more[0], n, 0)]
        return ((count * n, wide), [(0, 0, count * n, wide, views)])

    def scatter_high(unit, pair, sides):
        total = sum(part[n:eighth].astype(F32) for part in pair)
        total = total + sum(side[:, : widths[unit]].astype(F32) for side in sides)
        total = jnp.concatenate([jnp.zeros((n, widths[unit]), F32), total], axis=0)
        for bit in reversed(bits):
            size = total.shape[0] // 2
            total = total[:size] + exchange(total[size:].astype(BF), "dp", 1 << bit).astype(F32)
        return [total]

    def scatter_far(unit, pair, sides):
        if not staged:
            return scatter_high(unit, pair, sides)
        return [exchange(build(high_out(unit, pair, sides, 2, 2))[0], "dp", 8)]

    down = (down_mine, exchange_core(down_other))
    grad_hidden, grad_bias_in = hidden_back(grad_made, w_down, slope)
    in_mine, in_other = in_back(first_slots, grad_hidden)
    down, in_mine, in_other, grad_hidden = together((down, in_mine, in_other, grad_hidden))

    corner_down = exchange_sides(build(*alone(corner_out(2, down))))
    inner = (in_mine, exchange_core(in_other))
    grad_first_sum, grad_out, grad_mixed, sums_first = out_back(
        grad_hidden, w_in, turn, grad_second, unit, unit_scale, vectors, mixed_slots, w_first
    )

    def clip_back(clip):
        prob, rel, _ = made[clip]
        return attention_back(clip, joined, gate, rank, prob, rel, grad_mixed)

    corner_down, inner, grad_mixed = together((corner_down, inner, grad_mixed))

    corner_down = [(part, 0) for part in corner_down]
    sides_down = exchange_sides(build(*beside(sides_out(2, down, corner_down), corner_out(1, inner))))
    backs = [clip_back(clip) for clip in range(clips)]
    grads_joined = [back[0] for back in backs]
    grad_gate_inputs, table_grad, sums_attention = gate_back(
        inputs_low, table, gate, grads_joined, [back[1] for back in backs], [back[2] for back in backs]
    )
    grad_small = pack(shards, turn, sums_attention, sums_first, sums_second, grad_bias_in, table_grad)
    first_mine, first_other, grad_joined = first_back(inputs_slots, grad_out, grad_small, grads_joined)
    sides_down, first_mine, first_other, grad_joined = together((sides_down, first_mine, first_other, grad_joined))

    corner_in = [(part, FF) for part in sides_down]
    first = (first_mine, exchange_core(first_other))
    sides_in = exchange_sides(build(*alone(sides_out(1, inner, corner_in))))
    high_down = scatter_far(2, down, sides_down)
    corner_first = exchange_sides(build(*alone(corner_out(0, first))))
    input_grad = rows_back(grad_joined, w_first, turn, grad_first_sum, grad_gate_inputs)
    first, sides_in, high_down, corner_first, input_grad = together(
        (first, sides_in, high_down, corner_first, input_grad)
    )

    corner_first = [(part, 0) for part in corner_first]
    units = ((first, 0), (inner, 1), (down, 2))

    def own_views(row, column, columns):
        found = []
        for pair, unit in units:
            start, end = max(column, lefts[unit]), min(column + columns, lefts[unit] + widths[unit])
            if start < end:
                found.append((start - column, end - start, both(pair, row, start - lefts[unit])))
        return found

    def own_third(side):
        base = cut_all if side else 0
        items = []
        for i, (column, columns) in enumerate(spans(side)):
            for start, size, views in own_views(3 * eighth, base + column, columns):
                items.append((i * n, start, n, size, views))
        return (third[side][0], items)

    sides_first = exchange_sides(
        build(*beside(sides_out(0, first, corner_first), (own_third(1), own_third(0))))
    )
    high_in = scatter_far(1, inner, sides_in)
    if staged:
        high_down += [exchange(build(high_out(2, down, sides_down, 1, 1, high_down[0]))[0], "dp", 4)]
    weight_rows, momenta_rows, averages_rows = [flat_rows(part, n) for part in (weights, momenta, averages)]
    sides_first, high_in, high_down, weight_rows, momenta_rows, averages_rows = together(
        (sides_first, high_in, high_down, weight_rows, momenta_rows, averages_rows)
    )

    own_outs = []
    for side, row in ((0, eighth), (1, 2 * eighth)):
        items = []
        base = 0 if side == 0 else cut_all
        came = sides_first[1] if side == 0 else sides_first[0]
        edges = [(base + c, w, (came, i * n, widths[0])) for i, (c, w) in enumerate(spans(side))]
        edges.append((cut_all, wide_all - cut_all, None) if side == 0 else (0, cut_all, None))
        for column, columns, view in edges:
            for start, size, views in own_views(row, column, columns):
                if view is not None:
                    views = views + [(view[0], view[1], view[2] + start)]
                items.append((0, column + start, n, size, views))
        own_outs.append(((n, wide_all), items))
    own_sides = exchange_sides(build(*own_outs))
    if staged:
        near, far, farthest = [high_out(0, first, sides_first, d, 1) for d in (1, 2, 3)]
        near_in = high_out(1, inner, sides_in, 1, 1, high_in[0])
        wide = widths[0]
        near = ((n, wide + FF), near[1] + [(0, wide, n, FF, near_in[1][0][4])])
        high_first = [exchange(part, "dp", mask) for part, mask in zip(build(near, far, farthest), (4, 8, 12))]
        high_in += [high_first[0]]
    else:
        high_first = scatter_high(0, first, sides_first)
    comes = (
        [(part, 0) for part in high_first],
        [(part, widths[0] if i else 0) for i, part in enumerate(high_in)],
        [(part, 0) for part in high_down],
    )
    sums = []
    for pair, unit in units:
        views = both(pair, 0, 0) + [(side, 0, lefts[unit]) for side in own_sides]
        sums.append(views + [(part, 0, left) for part, left in comes[unit]])

    learning = rate_scale / math.sqrt(total_tokens)
    momenta_new, averages_new, weights_new, weights_copy = update(
        learning,
        sums,
        weight_rows,
        momenta_rows,
        averages_rows,
        weights.shape[1],
    )
    return (
        activations.reshape(acts.shape),
        input_grad.reshape(acts.shape),
        momenta_new,
        averages_new,
        weights_new,
        weights_copy,
    )


def solution(mesh):
    split = ("dp", "fsdp")
    in_specs = (
        P(split, None, None),
        P(split, None, None),
        P(split, None),
        P(split),
        P(split, None),
        P(split, None),
        P(split, None),
    )
    out_specs = (
        P(split, None, None),
        P(split, None, None),
        P(split, None),
        P(split, None),
        P(split, None),
        P(split, None),
    )
    return jax.shard_map(body, mesh=mesh, in_specs=in_specs, out_specs=out_specs, check_vma=False)
```

```python
from functools import partial
import math

import jax
import jax.numpy as jnp
import numpy as np
from jax import lax
from jax.experimental import pallas as pl
from jax.experimental.pallas import tpu as pltpu
from jax.sharding import PartitionSpec as P

D = 768
H = 12
HD = 64
FF = 3072
NB = 320
HALF = NB // 2
P_SIZE = 512
NPOS = 4372
LANES = 128
KEYS = 384
BF = jnp.bfloat16
F32 = jnp.float32

deep_alpha = 24.0**0.25
layer_epsilon = 1e-05
masked_score = -1000000000.0
far_distance = 800
gate_units = 8
momentum_rate = 0.9
average_rate = 0.8
decay_rate = 0.0001
rate_scale = 0.04
far_place = 1 << 20


def bucket_levels(span):
    distance = np.arange(0, span + 1)
    exact = HALF // 2
    logscale = (
        np.log(np.maximum(distance, 1) / exact) / np.log(far_distance / exact) * (HALF - exact)
    )
    beyond = np.minimum(exact + np.floor(logscale).astype(np.int64), HALF - 1)
    return np.where(distance < exact, distance, beyond)


def far_marks():
    levels = bucket_levels(2 * P_SIZE)
    rises = np.diff(levels)
    marks = np.repeat(np.arange(1, 2 * P_SIZE + 1), rises)
    return [int(m) for m in marks[HALF // 2 :]]


def key_ends():
    span = 2 * P_SIZE
    levels = bucket_levels(span)
    offsets = np.arange(-span, span + 1)
    level = levels[np.abs(offsets)]
    keys = np.where(offsets > 0, HALF + level, HALF - 1 - level)
    ends = np.full((KEYS,), far_place // 2, np.int32)
    for key in range(NB - 1):
        below = offsets[keys <= key]
        ends[key] = below.max() if below.size else -(far_place // 2)
    return ends


def exchange(value, axis, mask):
    count = lax.axis_size(axis)
    return lax.ppermute(value, axis, [(i, i ^ mask) for i in range(count)])


def high_bits(count):
    return list(range(2, count.bit_length() - 1))


def exchange_sides(pair):
    return exchange(pair[0], "dp", 1), exchange(pair[1], "dp", 2)


def exchange_core(value):
    return exchange(value, "fsdp", 1)


def slot_order(dp, core, count):
    high = count // 4
    core_step, low, up = np.meshgrid(np.arange(2), np.arange(4), np.arange(high), indexing="ij")
    distance = jnp.asarray((up * 4 + low).reshape(-1).astype(np.int32))
    core_distance = jnp.asarray(core_step.reshape(-1).astype(np.int32))
    return (distance ^ dp) * 2 + (core_distance ^ core)


def prep_kernel(marks, shape_ref, mask_ref, ends_ref, bucket_ref, rank_ref, valid_ref):
    clips, patches = mask_ref.shape
    slots = bucket_ref.shape[1]
    mask = mask_ref[...]
    up = lax.broadcasted_iota(jnp.int32, (patches, patches), 0)
    across = lax.broadcasted_iota(jnp.int32, (patches, patches), 1)
    running = wide_dot(mask.astype(F32).astype(BF), (up <= across).astype(F32).astype(BF))
    ranks = jnp.where(mask == 1, running.astype(jnp.int32) - 1, -1)
    slot = lax.broadcasted_iota(jnp.int32, (slots, patches), 0)
    patch = lax.broadcasted_iota(jnp.int32, (slots, patches), 1)
    pair = lax.broadcasted_iota(jnp.int32, (8, patches), 1)
    halves = jnp.where(lax.broadcasted_iota(jnp.int32, (8, patches), 0) == 0, pair >> 4, pair & 15)
    halves = halves.astype(F32).astype(BF)
    for clip in range(clips):
        found = ranks[clip : clip + 1, :] == slot
        column = jnp.sum(jnp.where(found, patch, 0), axis=1, keepdims=True)
        both = nt(halves, found.astype(F32).astype(BF)).astype(jnp.int32)
        row = 16 * both[0:1, :] + both[1:2, :]
        narrow = shape_ref[clip] > 0
        column = jnp.where(narrow, 8 * (column >> 2) + (column & 3), column)
        row = jnp.where(narrow, 8 * (row >> 2) + (row & 3), row)
        count = jnp.sum(mask[clip : clip + 1, :], axis=1, keepdims=True)
        valid = lax.broadcasted_iota(jnp.int32, (slots, 1), 0) < count
        valid_ref[clip * slots : (clip + 1) * slots, :] = valid.astype(F32)
        offset = column - row
        distance = jnp.abs(offset)
        level = jnp.minimum(distance, HALF // 2)
        for mark in marks:
            level = level + (distance >= mark).astype(jnp.int32)
        bucket_ref[clip] = level + jnp.where(offset > 0, HALF, 0)
        away = jnp.where(valid, offset, far_place)
        for first in range(slots):
            seen = away[:, first : first + 1] <= ends_ref[...]
            rank_ref[clip, first : first + 1, :] = jnp.sum(seen.astype(jnp.int32), axis=0, keepdims=True)


def prep(mask, shape_id, slots):
    clips = mask.shape[0]
    ends = jnp.asarray(key_ends())[None, :]
    return call(
        partial(prep_kernel, far_marks()),
        (mask, ends),
        (
            shaped((clips, slots, slots), jnp.int32),
            shaped((clips, slots, KEYS), jnp.int32),
            shaped((clips * slots, 1), F32),
        ),
        8,
        "prep",
        scalars=(shape_id,),
    )


def position_rows(shards, by_key):
    width = (NPOS + shards - 1) // shards
    index = np.full((24, KEYS), -1, np.int64)
    for head in range(H):
        for lane in range(NB):
            bucket = (HALF - 1 - lane if lane < HALF else lane) if by_key else lane
            index[head, lane] = bucket * H + head
    for unit in range(gate_units):
        index[12 + unit, :HD] = NB * H + np.arange(HD) * gate_units + unit
    index[20, :gate_units] = (NB + 0) * H + HD * gate_units + np.arange(gate_units)
    index[21, :H] = NB * H + (HD + 1) * gate_units + np.arange(H)
    pieces = np.where(index >= 0, index // width, -1).astype(np.int32)
    columns = np.where(index >= 0, 12 * D // shards + index % width, -1).astype(np.int32)
    return jnp.asarray(pieces), jnp.asarray(columns)


def vector_chunks(shards):
    width = 12 * D // shards
    size = math.gcd(width, D)
    each, across = width // size, D // size
    return size, [
        (g // each, g % each * size, g // across, g % across * size) for g in range(12 * across)
    ]


def unpack_kernel(shards, turn_ref, pieces_ref, columns_ref, *refs):
    whole_ref, vectors_ref, bias_ref, table_ref, natural_ref, small_ref = refs
    natural_ref[...] = wide_dot(turn_ref[...], whole_ref[:, 4 * D :])
    each = D // shards
    wide = small_ref.shape[1]
    for k in range(wide // LANES):
        small_ref[:, k * LANES : (k + 1) * LANES] = natural_ref[pl.ds(k, shards, stride=each), :]
    size, chunks = vector_chunks(shards)
    for piece, column, row, place in chunks:
        value = small_ref[piece : piece + 1, column : column + size]
        if row < 8:
            vectors_ref[row : row + 1, place : place + size] = value
        else:
            bias_ref[:, (row - 8) * D + place : (row - 8) * D + place + size] = value
    start = 12 * D // shards // LANES * LANES
    small = small_ref[:, start:].astype(BF)
    piece_ids = lax.broadcasted_iota(jnp.int32, (shards, KEYS), 0)
    column_ids = lax.broadcasted_iota(jnp.int32, (wide - start, KEYS), 0) + start
    for row in range(22):
        chosen = (piece_ids == pieces_ref[row : row + 1, :]).astype(F32).astype(BF)
        spread = tn(small, chosen)
        table_ref[row : row + 1, :] = jnp.sum(
            jnp.where(column_ids == columns_ref[row : row + 1, :], spread, 0.0), axis=0, keepdims=True
        )
    table_ref[22:24, :] = jnp.zeros((2, KEYS), F32)


def small_lanes(shards):
    return -(-(12 * D // shards + (NPOS + shards - 1) // shards) // LANES) * LANES


def unpack(shards, turn, whole):
    pieces, columns = position_rows(shards, False)
    return call(
        partial(unpack_kernel, shards),
        (turn, pieces, columns, whole),
        (shaped((8, D), F32), shaped((1, FF), F32), shaped((24, KEYS), F32)),
        8,
        "unpack",
        scratch=(
            pltpu.VMEM((D, LANES), F32),
            pltpu.VMEM((shards, small_lanes(shards)), F32),
        ),
    )


def pack_kernel(shards, turn_ref, pieces_ref, columns_ref, attention_ref, first_ref, second_ref, bias_ref, table_ref, out_ref, natural_ref, small_ref):
    each = D // shards
    wide = small_ref.shape[1]
    table = table_ref[...]
    lane = lax.broadcasted_iota(jnp.int32, table.shape, 1)
    row_id = lax.broadcasted_iota(jnp.int32, table.shape, 0)
    before = jnp.where((lane > 0) & (row_id < H), pltpu.roll(table, 1, 1), 0.0)
    table = table - before
    piece_ids = lax.broadcasted_iota(jnp.int32, (shards, KEYS), 0)
    start = 12 * D // shards // LANES * LANES
    column_ids = lax.broadcasted_iota(jnp.int32, (wide - start, KEYS), 0) + start
    total = jnp.zeros((shards, wide - start), F32)
    for row in range(22):
        chosen = jnp.where(piece_ids == pieces_ref[row : row + 1, :], table[row : row + 1, :], 0.0).astype(BF)
        spread = (column_ids == columns_ref[row : row + 1, :]).astype(F32).astype(BF)
        total = total + nt(chosen, spread)
    small_ref[...] = jnp.zeros(small_ref.shape, F32)
    small_ref[:, start:] = total
    rows = [(attention_ref, 0), (attention_ref, 1)]
    rows += [(first_ref, i) for i in range(3)] + [(second_ref, i) for i in range(3)]
    size, chunks = vector_chunks(shards)
    for piece, column, row, place in chunks:
        if row < 8:
            ref, at = rows[row]
            value = ref[at : at + 1, place : place + size]
        else:
            value = bias_ref[:, (row - 8) * D + place : (row - 8) * D + place + size]
        small_ref[piece : piece + 1, column : column + size] = value
    natural_ref[...] = jnp.zeros(natural_ref.shape, F32)
    for k in range(wide // LANES):
        natural_ref[pl.ds(k, shards, stride=each), :] = small_ref[:, k * LANES : (k + 1) * LANES]
    out_ref[...] = tn(turn_ref[...], natural_ref[...].astype(BF)).astype(BF)


def pack(shards, turn, sums_attention, sums_first, sums_second, bias, table):
    pieces, columns = position_rows(shards, True)
    return call(
        partial(pack_kernel, shards),
        (turn, pieces, columns, sums_attention, sums_first, sums_second, bias, table),
        (shaped((D, LANES), BF),),
        8,
        "pack",
        scratch=(pltpu.VMEM((D, LANES), F32), pltpu.VMEM((shards, small_lanes(shards)), F32)),
    )[0]


def lookup(table_ref, head, index, block):
    out = None
    for part in range(KEYS // LANES):
        row = jnp.broadcast_to(table_ref[head : head + 1, part * LANES : (part + 1) * LANES], index.shape)
        found = jnp.take_along_axis(row, index, axis=1, mode="promise_in_bounds")
        out = found if out is None else jnp.where(block == part, found, out)
    return out


def nt(a, b):
    return lax.dot_general(a, b, (((1,), (1,)), ((), ())), preferred_element_type=F32)


def tn(a, b):
    return lax.dot_general(a, b, (((0,), (0,)), ((), ())), preferred_element_type=F32)


def vmem(count):
    return [pl.BlockSpec(memory_space=pltpu.VMEM)] * count


def limits(mib):
    return pltpu.CompilerParams(vmem_limit_bytes=mib * 1024 * 1024)


def shaped(shape, dtype):
    return jax.ShapeDtypeStruct(tuple(shape), dtype)


def call(kernel, operands, outs, mib, name, scalars=(), scratch=()):
    return pl.pallas_call(
        kernel,
        out_shape=tuple(outs),
        in_specs=[pl.BlockSpec(memory_space=pltpu.SMEM)] * len(scalars) + vmem(len(operands)),
        out_specs=tuple(vmem(len(outs))),
        scratch_shapes=list(scratch),
        compiler_params=limits(mib),
        cost_estimate=pl.CostEstimate(flops=1, bytes_accessed=1, transcendentals=0),
        name=name,
    )(*scalars, *operands)


def build_kernel(plans, count, *refs):
    sources, outs = refs[:count], refs[count:]
    for out, (whole, items) in zip(outs, plans):
        if not whole:
            out[...] = jnp.zeros(out.shape, out.dtype)
        for row, column, rows, columns, views in items:
            values = [
                sources[which][first : first + rows, left : left + columns] for which, first, left in views
            ]
            if len(values) > 1:
                values = [sum(value.astype(F32) for value in values)]
            out[row : row + rows, column : column + columns] = values[0].astype(out.dtype)


def build(*outs):
    sources, plans = [], []
    for shape, items in outs:
        plan = []
        for row, column, rows, columns, views in items:
            found = []
            for array, first, left in views:
                at = next((i for i, source in enumerate(sources) if source is array), None)
                if at is None:
                    at = len(sources)
                    sources.append(array)
                found.append((at, first, left))
            plan.append((row, column, rows, columns, found))
        plans.append((sum(item[2] * item[3] for item in items) == math.prod(shape), plan))
    return call(
        partial(build_kernel, plans, len(sources)), sources, [shaped(shape, BF) for shape, _ in outs], 8, "build"
    )


def stack(parts):
    items, at = [], 0
    for array, row, rows, column, columns in parts:
        items.append((at, 0, rows, columns, [(array, row, column)]))
        at += rows
    return (at, parts[0][4]), items


def whole_of(array):
    return (array, 0, array.shape[0], 0, array.shape[1])


def normal(entries):
    centre = entries - jnp.mean(entries, axis=-1, keepdims=True)
    scale = lax.rsqrt(jnp.mean(centre * centre, axis=-1, keepdims=True) + layer_epsilon)
    return centre * scale, scale


def normal_back(grad, unit, scale):
    return scale * (
        grad
        - jnp.mean(grad, axis=-1, keepdims=True)
        - unit * jnp.mean(grad * unit, axis=-1, keepdims=True)
    )


def wide_dot(a, b):
    return jnp.dot(a, b, preferred_element_type=F32)


def split(value, count):
    parts = []
    for _ in range(count):
        parts.append(value.astype(BF))
        value = value - parts[-1].astype(F32)
    return parts


def joined_kernel(
    x_ref, turn_ref, vectors_ref, table_ref, whole_ref, slots_ref, joined_ref, gate_ref, logits_ref
):
    slots_ref[...] = wide_dot(x_ref[...], turn_ref[...]).astype(BF)
    for part in range(3):
        cols = slice(part * D, (part + 1) * D)
        made = wide_dot(slots_ref[...], whole_ref[:, cols])
        if part != 1:
            made = made + vectors_ref[part // 2 : part // 2 + 1, :]
        joined_ref[:, cols] = made.astype(BF)
    units = table_ref[12:20, :HD].astype(BF)
    logits_ref[...] = jnp.zeros(logits_ref.shape, F32)
    for head in range(H):
        logits_ref[:, head * gate_units : (head + 1) * gate_units] = (
            nt(x_ref[:, head * HD : (head + 1) * HD], units) + table_ref[20:21, :gate_units]
        )
    up = lax.broadcasted_iota(jnp.int32, (LANES, LANES), 0)
    across = lax.broadcasted_iota(jnp.int32, (LANES, LANES), 1)
    logits = split(logits_ref[...], 3)
    gates = []
    for side in range(2):
        chosen = ((up >> 3) == across) & (((up >> 2) & 1) == side)
        chosen = chosen.astype(F32).astype(BF)
        gates.append(jax.nn.sigmoid(sum(wide_dot(part, chosen) for part in logits)))
    first, second = gates
    gate_ref[0] = first * (second * table_ref[21:22, :LANES] - 1.0) + 2.0
    gate_ref[1] = first
    gate_ref[2] = second


def joined_forward(x, turn, vectors, table, whole):
    rows = x.shape[0]
    return call(
        joined_kernel,
        (x, turn, vectors, table, whole),
        (
            shaped((rows, D), BF),
            shaped((rows, 3 * D), BF),
            shaped((3, rows, LANES), F32),
        ),
        8,
        "joined_forward",
        scratch=(pltpu.VMEM((rows, LANES), F32),),
    )


def attention_kernel(clip, bucket_ref, valid_ref, table_ref, joined_ref, gate_ref, prob_ref, rel_ref, mixed_ref):
    slots = bucket_ref.shape[1]
    rows = slice(clip * slots, (clip + 1) * slots)
    index = bucket_ref[clip] & (LANES - 1)
    block = bucket_ref[clip] >> 7
    valid = valid_ref[rows, :] > 0
    gate = jnp.transpose(gate_ref[0, rows, :])
    for head in range(H):
        rel_ref[head] = lookup(table_ref, head, index, block)
    for head in range(H):
        query = joined_ref[rows, head * HD : (head + 1) * HD]
        key = joined_ref[rows, D + head * HD : D + (head + 1) * HD]
        score = nt(key, query) * (1.0 / math.sqrt(HD)) + gate[head : head + 1, :] * rel_ref[head]
        prob_ref[head] = jnp.where(valid, score, masked_score)
    for first in range(0, H, 4):
        score = prob_ref[first : first + 4]
        power = jnp.exp(score - jnp.max(score, axis=1, keepdims=True))
        prob_ref[first : first + 4] = power * (1.0 / jnp.sum(power, axis=1, keepdims=True))
    for head in range(H):
        value = joined_ref[rows, 2 * D + head * HD : 2 * D + (head + 1) * HD]
        mixed_ref[head * HD : (head + 1) * HD, :] = tn(value, prob_ref[head].astype(BF)).astype(BF)


def attention(clip, bucket, valid, table, joined, gate):
    slots = bucket.shape[1]
    return call(
        partial(attention_kernel, clip),
        (bucket, valid, table, joined, gate),
        (shaped((H, slots, slots), F32), shaped((H, slots, slots), F32), shaped((D, slots), BF)),
        4,
        "attention",
    )


def out_kernel(x_ref, turn_ref, vectors_ref, whole_ref, *refs):
    mixed_ref, unit_ref, scale_ref = refs[-3:]
    at = 0
    for part in refs[:-3]:
        rows = slice(at, at + part.shape[1])
        mixed_ref[rows, :] = tn(part[...], turn_ref[...]).astype(BF)
        at += part.shape[1]
    branch = wide_dot(mixed_ref[...], whole_ref[:, 3 * D : 4 * D]) + vectors_ref[2:3, :]
    unit, scale = normal(deep_alpha * x_ref[...].astype(F32) + branch)
    unit_ref[...] = unit
    scale_ref[...] = scale


def out_forward(x, turn, vectors, whole, mixed):
    rows = x.shape[0]
    return call(
        out_kernel,
        (x, turn, vectors, whole, *mixed),
        (shaped((rows, D), BF), shaped((rows, D), F32), shaped((rows, 1), F32)),
        6,
        "out_forward",
    )


def attention_back_kernel(
    clip, joined_ref, gate_ref, rank_ref, prob_ref, rel_ref, grad_ref, tri_ref,
    joined_grad_ref, gate_grad_ref, table_grad_ref,
):
    slots = rank_ref.shape[1]
    rows = slice(clip * slots, (clip + 1) * slots)
    scale = 1.0 / math.sqrt(HD)
    gate = jnp.transpose(gate_ref[0, rows, :])
    for head in range(H):
        cols = slice(head * HD, (head + 1) * HD)
        key_cols = slice(D + head * HD, D + (head + 1) * HD)
        value_cols = slice(2 * D + head * HD, 2 * D + (head + 1) * HD)
        query = joined_ref[rows, cols]
        key = joined_ref[rows, key_cols]
        value = joined_ref[rows, value_cols]
        grad = grad_ref[rows, cols]
        prob = prob_ref[head]
        joined_grad_ref[:, value_cols] = wide_dot(prob.astype(BF), grad).astype(BF)
        weighted = prob * nt(value, grad)
        low = (weighted - prob * jnp.sum(weighted, axis=0, keepdims=True)).astype(BF)
        joined_grad_ref[:, cols] = (tn(low, key) * scale).astype(BF)
        joined_grad_ref[:, key_cols] = (wide_dot(low, query) * scale).astype(BF)
        wide = low.astype(F32)
        gate_grad_ref[head : head + 1, :] = jnp.sum(wide * rel_ref[head], axis=0, keepdims=True)
        gated = wide * gate[head : head + 1, :]
        high = gated.astype(BF)
        rest = (gated - high.astype(F32)).astype(BF)
        running = tn(high, tri_ref[...]) + tn(rest, tri_ref[...])
        for part in range(KEYS // LANES):
            lanes = slice(part * LANES, (part + 1) * LANES)
            rank = rank_ref[clip, :, lanes]
            found = jnp.take_along_axis(
                running, jnp.maximum(rank - 1, 0), axis=1, mode="promise_in_bounds"
            )
            table_grad_ref[head : head + 1, lanes] = jnp.sum(
                jnp.where(rank > 0, found, 0.0), axis=0, keepdims=True
            )
    table_grad_ref[H:, :] = jnp.zeros((16 - H, KEYS), F32)
    gate_grad_ref[H:, :] = jnp.zeros((16 - H, slots), F32)


def attention_back(clip, joined, gate, rank, prob, rel, grad):
    slots = rank.shape[1]
    tri = jnp.asarray(np.triu(np.ones((slots, slots), np.float32)), BF)
    return call(
        partial(attention_back_kernel, clip),
        (joined, gate, rank, prob, rel, grad, tri),
        (shaped((slots, 3 * D), BF), shaped((16, slots), F32), shaped((16, KEYS), F32)),
        4,
        "attention_back",
    )


def gate_back_kernel(count, x_ref, table_ref, gate_ref, *refs):
    joined_grads, gate_grads, table_grads = refs[:count], refs[count : 2 * count], refs[2 * count : 3 * count]
    x_grad_ref, table_grad_ref, sums_ref = refs[3 * count :]
    table_grad_ref[...] = jnp.zeros(table_grad_ref.shape, F32)
    table_grad_ref[:16, :] = sum(ref[...] for ref in table_grads)
    sums_ref[0:1, :] = sum(jnp.sum(ref[:, :D].astype(F32), axis=0, keepdims=True) for ref in joined_grads)
    sums_ref[1:2, :] = sum(jnp.sum(ref[:, 2 * D :].astype(F32), axis=0, keepdims=True) for ref in joined_grads)
    units = [jnp.sum(table_ref[12 + 4 * i : 16 + 4 * i, :HD], axis=0, keepdims=True) for i in range(2)]
    unit_grads = [jnp.zeros((1, HD), F32), jnp.zeros((1, HD), F32)]
    grad = jnp.concatenate([jnp.transpose(ref[...]) for ref in gate_grads], axis=0)
    first, second = gate_ref[1, :, :16], gate_ref[2, :, :16]
    size = table_ref[21:22, :16]
    grads = (
        grad * (second * size - 1.0) * first * (1.0 - first),
        grad * first * size * second * (1.0 - second),
    )
    table_grad_ref[21:22, :16] = jnp.sum(grad * first * second, axis=0, keepdims=True)
    bias_grads = [jnp.sum(jnp.sum(g, axis=0, keepdims=True), axis=1, keepdims=True) for g in grads]
    for head in range(H):
        cols = slice(head * HD, (head + 1) * HD)
        x = x_ref[:, cols].astype(F32)
        sides = [g[:, head : head + 1] for g in grads]
        x_grad_ref[:, cols] = sides[0] * units[0] + sides[1] * units[1]
        for i in range(2):
            unit_grads[i] = unit_grads[i] + jnp.sum(x * sides[i], axis=0, keepdims=True)
    for unit in range(gate_units):
        table_grad_ref[12 + unit : 13 + unit, :HD] = unit_grads[unit // 4]
        table_grad_ref[20:21, unit : unit + 1] = bias_grads[unit // 4]


def gate_back(x, table, gate, joined_grads, gate_grads, table_grads):
    return call(
        partial(gate_back_kernel, len(joined_grads)),
        (x, table, gate, *joined_grads, *gate_grads, *table_grads),
        (shaped(x.shape, F32), shaped((24, KEYS), F32), shaped((8, D), F32)),
        6,
        "gate_back",
    )


def gelu_pair(u):
    size = jnp.abs(u) * math.sqrt(0.5)
    t = 1.0 / (1.0 + 0.3275911 * size)
    poly = ((((1.061405429 * t - 1.453152027) * t + 1.421413741) * t - 0.284496736) * t + 0.254829592) * t
    bell = jnp.exp(-0.5 * u * u)
    tail = 0.5 * poly * bell
    below = jnp.where(u < 0, tail, 1.0 - tail)
    return u * below, below + u * bell * (1.0 / math.sqrt(2.0 * math.pi))


def hidden_kernel(
    unit_ref, vectors_ref, turn_ref, bias_ref, whole_ref, slots_ref, active_ref, slope_ref
):
    low = (unit_ref[...] * vectors_ref[3:4, :] + vectors_ref[4:5, :]).astype(BF)
    slots_ref[...] = wide_dot(low, turn_ref[...]).astype(BF)
    width = FF // 8
    for block in range(8):
        cols = slice(block * width, (block + 1) * width)
        u = wide_dot(slots_ref[...], whole_ref[:, cols]) + bias_ref[:, cols]
        active, slope = gelu_pair(u)
        active_ref[:, cols] = active.astype(BF)
        slope_ref[:, cols] = slope


def hidden_forward(unit, vectors, turn, bias, whole):
    rows = unit.shape[0]
    return call(
        hidden_kernel,
        (unit, vectors, turn, bias, whole),
        (shaped((rows, D), BF), shaped((rows, FF), BF), shaped((rows, FF), F32)),
        10,
        "hidden_forward",
    )


def turn_kernel(slots, *refs):
    at_ref, active_ref, unit_ref, vectors_ref, valid_ref, cot_ref = refs[:6]
    parts = refs[6:-5]
    whole_ref, out_ref, second_ref, low_ref, sums_ref = refs[-5:]
    for slot, (which, row, rows, column) in enumerate(slots):
        place = pl.multiple_of(at_ref[slot], 16)
        if parts[which].shape[1] == D:
            whole_ref[pl.ds(place, rows), :] = parts[which][row : row + rows, :]
            continue
        blocks = [
            parts[which][row : row + rows, column + j * D : column + (j + 1) * D] for j in range(FF // D)
        ]
        whole_ref[pl.ds(place, rows * len(blocks)), :] = jnp.concatenate(blocks, axis=0)
    made = wide_dot(active_ref[...], whole_ref[...]) + vectors_ref[5:6, :]
    first_norm = unit_ref[...] * vectors_ref[3:4, :] + vectors_ref[4:5, :]
    unit, scale = normal(deep_alpha * first_norm + made.astype(BF).astype(F32))
    valid = valid_ref[...]
    gain = vectors_ref[6:7, :]
    out_ref[...] = ((unit * gain + vectors_ref[7:8, :]) * valid).astype(BF)
    grad = cot_ref[...].astype(F32) * valid
    second = normal_back(grad * gain, unit, scale)
    second_ref[...] = second
    low = second.astype(BF)
    low_ref[...] = low
    sums_ref[0:1, :] = jnp.sum(low.astype(F32), axis=0, keepdims=True)
    sums_ref[1:2, :] = jnp.sum(grad * unit, axis=0, keepdims=True)
    sums_ref[2:3, :] = jnp.sum(grad, axis=0, keepdims=True)


def turn_back(at, slots, active, unit, vectors, valid, cot, parts):
    rows = unit.shape[0]
    return call(
        partial(turn_kernel, slots),
        (active, unit, vectors, valid, cot, *parts),
        (shaped((FF, D), BF), shaped((rows, D), BF), shaped((rows, D), F32), shaped((rows, D), BF), shaped((8, D), F32)),
        10,
        "turn_back",
        scalars=(at,),
    )


def turn_active_kernel(rows, at_ref, active_ref, out_ref, turned_ref):
    for first in range(0, FF, FF // 8):
        cols = slice(first, first + FF // 8)
        turned_ref[cols, :] = jnp.transpose(active_ref[:, cols])
    for slot in range(FF // rows):
        place = pl.multiple_of(at_ref[slot], 16)
        out_ref[slot * rows : (slot + 1) * rows, :] = turned_ref[pl.ds(place, rows), :]


def turn_active(at, rows, active):
    return call(
        partial(turn_active_kernel, rows),
        (active,),
        (shaped((FF, active.shape[0]), BF),),
        8,
        "turn_active",
        scalars=(at,),
        scratch=(pltpu.VMEM((FF, active.shape[0]), BF),),
    )[0]


def down_back_kernel(first, rows, active_ref, low_ref, out_ref):
    chunk = rows * FF // D
    for slot in range(FF // 2 // chunk):
        at = first + slot * chunk
        made = wide_dot(active_ref[at : at + chunk, :], low_ref[...]).astype(BF)
        for j in range(FF // D):
            out_ref[slot * rows : (slot + 1) * rows, j * D : (j + 1) * D] = made[j * rows : (j + 1) * rows, :]


def down_back(half, rows, active, low):
    return call(
        partial(down_back_kernel, half * FF // 2, rows),
        (active, low),
        (shaped((D // 2, FF), BF),),
        6,
        "down_back",
    )[0]


def hidden_back_kernel(low_ref, down_ref, slope_ref, grad_ref, bias_ref):
    width = FF // 8
    for block in range(8):
        cols = slice(block * width, (block + 1) * width)
        grad = (nt(low_ref[...], down_ref[cols, :]) * slope_ref[:, cols]).astype(BF)
        grad_ref[:, cols] = grad
        bias_ref[:, cols] = jnp.sum(grad.astype(F32), axis=0, keepdims=True)


def hidden_back(low, down, slope):
    rows = low.shape[0]
    return call(
        hidden_back_kernel,
        (low, down, slope),
        (shaped((rows, FF), BF), shaped((1, FF), F32)),
        6,
        "hidden_back",
    )


def in_back_kernel(slots_ref, grad_ref, mine_ref, other_ref):
    width = FF // 4
    for block in range(4):
        cols = slice(block * width, (block + 1) * width)
        made = tn(slots_ref[...], grad_ref[:, cols]).astype(BF)
        mine_ref[:, cols] = made[: D // 2]
        other_ref[:, cols] = made[D // 2 :]


def in_back(slots, grad):
    rows = slots.shape[0]
    return call(
        in_back_kernel,
        (slots, grad),
        (shaped((D // 2, FF), BF), shaped((D // 2, FF), BF)),
        6,
        "in_back",
    )


def out_back_kernel(
    grad_ref, in_ref, turn_ref, second_ref, unit_ref, scale_ref, vectors_ref, mixed_ref, out_ref,
    first_ref, weight_ref, mixed_grad_ref, sums_ref,
):
    low = nt(grad_ref[...], in_ref[...]).astype(BF)
    grad = deep_alpha * second_ref[...] + nt(low, turn_ref[...]).astype(BF).astype(F32)
    unit = unit_ref[...]
    first = normal_back(grad * vectors_ref[3:4, :], unit, scale_ref[...])
    first_ref[...] = first
    branch = first.astype(BF)
    sums_ref[0:1, :] = jnp.sum(branch.astype(F32), axis=0, keepdims=True)
    sums_ref[1:2, :] = jnp.sum(grad * unit, axis=0, keepdims=True)
    sums_ref[2:3, :] = jnp.sum(grad, axis=0, keepdims=True)
    weight_ref[...] = tn(mixed_ref[...], branch).astype(BF)
    back = nt(branch, out_ref[:, 3 * D : 4 * D]).astype(BF)
    mixed_grad_ref[...] = nt(back, turn_ref[...]).astype(BF)


def out_back(grad, w_in, turn, second, unit, scale, vectors, mixed, w_first):
    rows = unit.shape[0]
    return call(
        out_back_kernel,
        (grad, w_in, turn, second, unit, scale, vectors, mixed, w_first),
        (shaped((rows, D), F32), shaped((D, D), BF), shaped((rows, D), BF), shaped((8, D), F32)),
        6,
        "out_back",
    )


def first_back_kernel(slots_ref, out_ref, small_ref, *refs):
    *grads, mine_ref, other_ref, grad_ref = refs
    at = 0
    for grad in grads:
        grad_ref[at : at + grad.shape[0], :] = grad[...]
        at += grad.shape[0]
    half = D // 2
    for part in range(3):
        cols = slice(part * D, (part + 1) * D)
        made = tn(slots_ref[...], grad_ref[:, cols]).astype(BF)
        mine_ref[:, cols] = made[:half]
        other_ref[:, cols] = made[half:]
    for ref, rows in ((mine_ref, slice(0, half)), (other_ref, slice(half, D))):
        ref[:, 3 * D : 4 * D] = out_ref[rows, :]
        ref[:, 4 * D :] = small_ref[rows, :]


def first_back(slots, weight_out, small, grads):
    rows = slots.shape[0]
    wide = 4 * D + small.shape[1]
    return call(
        first_back_kernel,
        (slots, weight_out, small, *grads),
        (shaped((D // 2, wide), BF), shaped((D // 2, wide), BF), shaped((rows, 3 * D), BF)),
        6,
        "first_back",
    )


def rows_back_kernel(grad_ref, first_ref, turn_ref, branch_ref, gate_ref, out_ref):
    made = nt(grad_ref[...], first_ref[:, : 3 * D])
    high = made.astype(BF)
    rest = made - high.astype(F32)
    middle = rest.astype(BF)
    last = (rest - middle.astype(F32)).astype(BF)
    turned = nt(high, turn_ref[...]) + nt(middle, turn_ref[...]) + nt(last, turn_ref[...])
    out_ref[...] = turned + deep_alpha * branch_ref[...] + gate_ref[...]


def rows_back(grad, w_first, turn, branch, gate):
    rows = grad.shape[0]
    return call(
        rows_back_kernel,
        (grad, w_first, turn, branch, gate),
        (shaped((rows, D), F32),),
        8,
        "rows_back",
    )[0]


def flat_cuts(each):
    cuts = [(0, row, 0, 3 * D) for row in range(each)]
    cuts += [(0, row, 3 * D, 4 * D) for row in range(each)]
    cuts += [(1, row, 0, FF) for row in range(each)]
    cuts += [(2, row, j * D, (j + 1) * D) for j in range(FF // D) for row in range(each)]
    return cuts + [(0, row, 4 * D, 4 * D + LANES) for row in range(each)]


def flat_runs(each, width):
    at = 0
    for which, row, first, last in flat_cuts(each):
        size = min(last - first, width - at)
        if size > 0:
            yield which, row, first, size, at
        at += last - first


def rows_kernel(flat_ref, first_ref, in_ref, down_ref):
    refs = (first_ref, in_ref, down_ref)
    first_ref[:, 4 * D :] = jnp.zeros((first_ref.shape[0], LANES), F32)
    for which, row, first, size, at in flat_runs(first_ref.shape[0], flat_ref.shape[1]):
        refs[which][row : row + 1, first : first + size] = flat_ref[:, at : at + size]


def pieces_kernel(flat_ref, first_ref, in_ref, down_ref, all_ref, *refs):
    rows_kernel(flat_ref, *refs)
    at = 0
    for ref, low in zip(refs, (first_ref, in_ref, down_ref)):
        low[...] = ref[...].astype(BF)
        all_ref[:, at : at + low.shape[1]] = low[...]
        at += low.shape[1]


def row_widths():
    return (4 * D + LANES, FF, FF)


def flat_rows(flat, each):
    return call(rows_kernel, (flat,), [shaped((each, width), F32) for width in row_widths()], 6, "flat_rows")


def pieces(flat, each):
    widths = row_widths()
    return call(
        pieces_kernel,
        (flat,),
        [shaped((each, width), BF) for width in (*widths, sum(widths))],
        6,
        "pieces",
        scratch=[pltpu.VMEM((each, width), F32) for width in widths],
    )


def update_kernel(learning, plan, sections, spans, known, count, *refs):
    size = len(sections)
    sums, refs = refs[:count], refs[count:]
    weights, momenta, averages, refs = refs[:size], refs[size : 2 * size], refs[2 * size : 3 * size], refs[3 * size :]
    outs, refs = refs[known : known + 4], refs[known + 4 :]
    rows, flats, arrived = refs[: 3 * size], refs[3 * size : -1], refs[-1]
    for i in range(size):
        each, wide = weights[i].shape
        grad = sum(
            sums[which][row : row + each, column : column + wide].astype(F32) for which, row, column in plan[i]
        )
        weight = weights[i][...]
        decayed = grad + decay_rate * weight
        momentum = momentum_rate * momenta[i][...] + decayed
        weight = weight - learning * (decayed + momentum_rate * momentum)
        rows[i][...] = momentum
        rows[size + i][...] = average_rate * averages[i][...] + (1.0 - average_rate) * weight
        rows[2 * size + i][...] = weight
    each = weights[0].shape[0]
    copies = []
    for out, which in zip(range(4), (0, 1, 2, 2)):
        for span, (first, last) in enumerate(spans):
            flat = flats[out * len(spans) + span]
            for section, row, column, width, at in flat_runs(each, outs[out].shape[1]):
                if section in sections and first <= at < last:
                    value = rows[which * size + sections.index(section)][row : row + 1, column : column + width]
                    flat[:, at - first : at - first + width] = value.astype(flat.dtype)
            copies.append(
                pltpu.make_async_copy(
                    flat, outs[out].at[:, pl.ds(first, last - first)], arrived.at[out * len(spans) + span]
                )
            )
            copies[-1].start()
    for copy in copies:
        copy.wait()


def update(learning, sections, sums, weights, momenta, averages, width, known=()):
    arrays, plan = [], []
    for section in sections:
        found = []
        for array, row, column in sums[section]:
            at = next((i for i, other in enumerate(arrays) if other is array), None)
            if at is None:
                at = len(arrays)
                arrays.append(array)
            found.append((at, row, column))
        plan.append(found)
    each = weights[0].shape[0]
    runs = [(at, at + size) for section, _, _, size, at in flat_runs(each, width) if section in sections]
    spans = []
    for first, last in runs:
        if spans and spans[-1][1] == first:
            spans[-1] = (spans[-1][0], last)
        else:
            spans.append((first, last))
    rows = [[part[section] for section in sections] for part in (weights, momenta, averages)]
    dtypes = (F32, F32, F32, BF)
    operands = [*arrays, *rows[0], *rows[1], *rows[2]]
    anywhere = pl.BlockSpec(memory_space=pl.ANY)
    return pl.pallas_call(
        partial(update_kernel, learning, plan, list(sections), spans, len(known), len(arrays)),
        out_shape=tuple(shaped((1, width), dtype) for dtype in dtypes),
        in_specs=vmem(len(operands)) + [anywhere] * len(known),
        out_specs=(anywhere,) * 4,
        input_output_aliases={len(operands) + i: i for i in range(len(known))},
        scratch_shapes=[pltpu.VMEM(part.shape, F32) for part in rows[0]] * 3
        + [pltpu.VMEM((1, last - first), dtype) for dtype in dtypes for first, last in spans]
        + [pltpu.SemaphoreType.DMA((4 * len(spans),))],
        compiler_params=limits(10),
        cost_estimate=pl.CostEstimate(flops=1, bytes_accessed=1, transcendentals=0),
        name="update",
    )(*operands, *known)


def body(acts, cotangent, mask, shape_id, weights, momenta, averages):
    shards = lax.axis_size(("dp", "fsdp"))
    count = lax.axis_size("dp")
    dp, core = lax.axis_index("dp"), lax.axis_index("fsdp")
    clips, slots = acts.shape[0], acts.shape[1]
    rows = clips * slots
    total_tokens = rows * shards
    piece_rows = D // shards
    wide_rows = FF // shards
    vector_width = 12 * D // shards
    position_width = (NPOS + shards - 1) // shards
    small_width = vector_width + position_width

    piece_first, piece_in, piece_down, piece_all = pieces(weights, piece_rows)

    order = slot_order(dp, core, count)
    row_order = (order[:, None] * piece_rows + jnp.arange(piece_rows, dtype=jnp.int32)).reshape(-1)
    turn = (jnp.arange(D, dtype=jnp.int32)[:, None] == row_order[None, :]).astype(BF)
    piece_turn = (jnp.arange(shards, dtype=jnp.int32)[:, None] == order[None, :]).astype(BF)

    back_order = jnp.dot(piece_turn.astype(F32), jnp.arange(shards, dtype=F32)).astype(jnp.int32)

    together = lax.optimization_barrier
    bits = high_bits(count)
    staged = len(bits) == 2
    n = piece_rows
    rest = D // 8 - n
    widths = (piece_first.shape[1], FF, FF)
    lefts = (0, widths[0], widths[0] + FF)
    cuts = (13 * LANES, FF // 2, FF // 2)
    wide_all, cut_all = sum(widths), 37 * LANES
    third = (13 * LANES, 12 * LANES, 12 * LANES), (12 * LANES,) * 3
    at = order * wide_rows
    inputs_low = acts.reshape(rows, D)

    def gather_high(piece):
        if staged:
            return [exchange(piece, "dp", d << 2) for d in (1, 2, 3)]
        column = piece
        for bit in bits:
            column = jnp.concatenate([column, exchange(column, "dp", 1 << bit)], axis=0)
        return [column[n:]]

    def thirds(side, views):
        left = widths[0]
        items, column = [], 0
        for i, size in enumerate(third[side]):
            items += views(i * n, left, column, size)
            column += size
        return items

    own_sides = exchange_sides((piece_all, piece_all))
    high_first = gather_high(piece_first)
    own_sides, high_first, piece_in, mask, turn, at = together(
        (own_sides, high_first, piece_in, mask, turn, at)
    )

    items = stack([whole_of(part) for part in high_first])[1]
    sends = build(
        ((rest, widths[0]), items),
        (
            (rest, widths[0] + third[1][0]),
            items + thirds(1, lambda row, left, c, w: [(row, left, n, w, [(own_sides[1], 0, cut_all + c)])]),
        ),
        (
            (rest, widths[0] + third[0][0]),
            items + thirds(0, lambda row, left, c, w: [(row, left, n, w, [(own_sides[0], 0, c)])]),
        ),
    )
    rest_first, sends = sends[0], sends[1:]
    sides_first = exchange_sides(sends)
    high_in = gather_high(piece_in)
    bucket, rank, valid_rows = prep(mask, shape_id, slots)
    sides_first, high_in, piece_down, bucket, rank, valid_rows = together(
        (sides_first, high_in, piece_down, bucket, rank, valid_rows)
    )

    def corner_sends(unit, sides):
        wide, half = widths[unit], cuts[unit]
        return (
            ((rest, wide - half), [(0, 0, rest, wide - half, [(sides[1], 0, half)])]),
            ((rest, half), [(0, 0, rest, half, [(sides[0], 0, 0)])]),
        )

    def corner_items(unit, corner):
        wide, half = widths[unit], cuts[unit]
        (second, left_second), (first, left_first) = corner
        return [
            (0, 0, rest, half, [(first, 0, left_first)]),
            (0, half, rest, wide - half, [(second, 0, left_second)]),
        ]

    def early_rows(unit, piece, high, sides):
        wide = widths[unit]
        return stack([whole_of(piece), whole_of(high)] + [(side, 0, rest, 0, wide) for side in sides])

    def shifted(items, row):
        return [(row + item[0], *item[1:]) for item in items]

    def slots_of(unit, piece, high, sides, corner, early, late):
        wide, left = widths[unit], lefts[unit]
        own_mine, own_other = own
        items = [(0, 0, n, wide, [(piece, 0, 0)]), (n, 0, rest, wide, [(high, 0, 0)])]
        eighth = D // 8
        for i in range(3):
            items.append(((i + 1) * eighth, 0, n, wide, [(own_mine, i * n, left)]))
        for i, side in enumerate(sides):
            items.append(((i + 1) * eighth + n, 0, rest, wide, [(side, 0, 0)]))
        items += shifted(corner_items(unit, corner), 3 * eighth + n)
        base = D // 2
        if not isinstance(early, tuple):
            early = (early, 0), (early, n + rest)
        (one, row_one), (two, row_two) = early
        items.append((base, 0, n, wide, [(one, row_one, 0)]))
        items.append((base + n, 0, rest, wide, [(one, row_one + n, 0)]))
        for i in range(3):
            items.append((base + (i + 1) * eighth, 0, n, wide, [(own_other, i * n, left)]))
            view = (late, 0, 0) if i == 2 else (two, row_two + i * rest, 0)
            items.append((base + (i + 1) * eighth + n, 0, rest, wide, [view]))
        return items

    def own_corner(row, half, side, column):
        return [(row, column + c, n, w, [(side, i * n, widths[0])]) for i, (c, w) in enumerate(half)]

    def spans(side):
        edges = np.cumsum((0, *third[side]))
        return [(int(a), int(b - a)) for a, b in zip(edges[:-1], edges[1:])]

    items = [(0, 0, n, wide_all, [(own_sides[0], 0, 0)]), (n, 0, n, wide_all, [(own_sides[1], 0, 0)])]
    items += own_corner(2 * n, spans(0), sides_first[1], 0) + own_corner(2 * n, spans(1), sides_first[0], cut_all)
    def side_sends(unit, high, sides):
        wide, half = widths[unit - 1], cuts[unit - 1]
        items = stack([whole_of(part) for part in high])[1]
        sends = []
        for width, view in ((wide - half, (sides[1], 0, half)), (half, (sides[0], 0, 0))):
            sends.append(((rest, widths[unit] + width), items + [(0, widths[unit], rest, width, [view])]))
        return [((rest, widths[unit]), items)] + sends

    own_mine, early, rest_in, *sends = build(
        ((3 * n, wide_all), items),
        early_rows(0, piece_first, rest_first, sides_first),
        *side_sends(1, high_in, sides_first),
    )
    sides_in = exchange_sides(sends)
    early_first = exchange_core(early)
    high_down = gather_high(piece_down)
    sides_in, early_first, high_down, own_mine = together((sides_in, early_first, high_down, own_mine))

    corner_first = [(part, FF) for part in sides_in]
    late, rest_down, *sends = build(
        ((rest, widths[0]), corner_items(0, corner_first)), *side_sends(2, high_down, sides_in)
    )
    sides_down = exchange_sides(sends)
    own = (own_mine, exchange_core(own_mine))
    late = exchange_core(late)
    items = slots_of(0, piece_first, rest_first, sides_first, corner_first, early_first, late)
    w_first = build(((D, widths[0]), items))[0]
    early, first_down = build(
        early_rows(1, piece_in, rest_in, sides_in), stack([whole_of(piece_down), whole_of(rest_down)])
    )
    early_in, first_down = exchange_core(early), exchange_core(first_down)
    vectors, bias_in, table = unpack(shards, turn, w_first)
    inputs_slots, joined, gate = joined_forward(inputs_low, turn, vectors, table, w_first)
    made = [attention(clip, bucket, valid_rows, table, joined, gate) for clip in range(clips)]
    mixed_slots, unit, unit_scale = out_forward(inputs_low, turn, vectors, w_first, [m[2] for m in made])
    sides_down, early_in, first_down, unit = together((sides_down, early_in, first_down, unit))

    corner_in = [(part, FF) for part in sides_down]
    late, early, *sends = build(
        ((rest, FF), corner_items(1, corner_in)),
        stack([(side, 0, rest, 0, FF) for side in sides_down]),
        *corner_sends(2, sides_down),
    )
    corner_down = exchange_sides(sends)
    late = exchange_core(late)
    early_down = exchange_core(early)
    items = slots_of(1, piece_in, rest_in, sides_in, corner_in, early_in, late)
    w_in = build(((D, FF), items))[0]
    first_slots, active, slope = hidden_forward(unit, vectors, turn, bias_in, w_in)
    corner_down, early_down, active = together((corner_down, early_down, active))

    corner_down = [(part, 0) for part in corner_down]
    corner = build(((rest, FF), corner_items(2, corner_down)))[0]
    late = exchange_core(corner)
    early_down = (first_down, 0), (early_down, 0)
    items = slots_of(2, piece_down, rest_down, sides_down, [(corner, cuts[2]), (corner, 0)], early_down, late)
    arrays, places = [], [None] * shards
    for row, column, size, _, [(array, first, left)] in items:
        if column:
            continue
        which = next((i for i, known in enumerate(arrays) if known is array), len(arrays))
        if which == len(arrays):
            arrays.append(array)
        for step in range(size // n):
            places[row // n + step] = (which, first + step * n, n, left)
    to = at
    if wide_rows % 16 == 0:
        turned = turn_active(at, wide_rows, active)
        turned, arrays[0] = together((turned, arrays[0]))
    else:
        parts = [arrays[which][row : row + n, left : left + FF] for which, row, _, left in places]
        stacked = jnp.stack(parts).reshape(shards, n, FF // D, D).transpose(0, 2, 1, 3).reshape(shards, wide_rows, D)
        arrays, places = [jnp.take(stacked, back_order, axis=0).reshape(FF, D)], [(0, 0, FF, 0)]
        to = jnp.zeros((1,), jnp.int32)
    w_down, activations, grad_second, grad_made, sums_second = turn_back(
        to, places, active, unit, vectors, valid_rows, cotangent.reshape(rows, D), arrays
    )

    if wide_rows % 16:
        grad_down = tn(active, grad_made).astype(BF).reshape(shards, wide_rows, D)
        grad_down = jnp.take(grad_down, order, axis=0).reshape(shards, FF // D, n, D).transpose(0, 2, 1, 3)
        grad_down = grad_down.reshape(D, FF)
        down_mine, down_other = grad_down[: D // 2], grad_down[D // 2 :]
    else:
        down_other = down_back(1, n, turned, grad_made)
        down_other, grad_made = together((down_other, grad_made))
        down_mine = down_back(0, n, turned, grad_made)

    eighth = D // 8

    def both(pair, row, column):
        return [(array, row, column) for array in pair]

    def corner_out(unit, pair):
        wide, half = widths[unit], cuts[unit]
        row = 3 * eighth + n
        return (
            (wide - half, [(0, 0, rest, wide - half, both(pair, row, half))]),
            (half, [(0, 0, rest, half, both(pair, row, 0))]),
        )

    def sides_out(unit, pair, corner):
        wide, half = widths[unit], cuts[unit]
        (second, left_second), (first, left_first) = corner
        near, side = eighth + n, 2 * eighth + n
        return (
            (
                wide,
                [
                    (0, 0, rest, half, both(pair, near, 0) + [(first, 0, left_first)]),
                    (0, half, rest, wide - half, both(pair, near, half)),
                ],
            ),
            (
                wide,
                [
                    (0, 0, rest, half, both(pair, side, 0)),
                    (0, half, rest, wide - half, both(pair, side, half) + [(second, 0, left_second)]),
                ],
            ),
        )

    def beside(one, two):
        return [
            ((rest, a[0] + b[0]), a[1] + [(item[0], a[0] + item[1], *item[2:]) for item in b[1]])
            for a, b in zip(one, two)
        ]

    def alone(one):
        return [((rest, wide), items) for wide, items in one]

    def column_views(unit, pair, sides, row):
        return both(pair, row, 0) + [(side, row - n, 0) for side in sides]

    def high_out(unit, pair, sides, first, count, *more):
        wide = widths[unit]
        views = column_views(unit, pair, sides, first * n)
        if more:
            views = views + [(more[0], n, 0)]
        return ((count * n, wide), [(0, 0, count * n, wide, views)])

    def scatter_high(unit, pair, sides):
        total = sum(part[n:eighth].astype(F32) for part in pair)
        total = total + sum(side[:, : widths[unit]].astype(F32) for side in sides)
        total = jnp.concatenate([jnp.zeros((n, widths[unit]), F32), total], axis=0)
        for bit in reversed(bits):
            size = total.shape[0] // 2
            total = total[:size] + exchange(total[size:].astype(BF), "dp", 1 << bit).astype(F32)
        return [total]

    def scatter_far(unit, pair, sides):
        if not staged:
            return scatter_high(unit, pair, sides)
        return [exchange(build(high_out(unit, pair, sides, 2, 2))[0], "dp", 8)]

    down = (down_mine, exchange_core(down_other))
    grad_hidden, grad_bias_in = hidden_back(grad_made, w_down, slope)
    in_mine, in_other = in_back(first_slots, grad_hidden)
    down, in_mine, in_other, grad_hidden = together((down, in_mine, in_other, grad_hidden))

    corner_down = exchange_sides(build(*alone(corner_out(2, down))))
    inner = (in_mine, exchange_core(in_other))
    grad_first_sum, grad_out, grad_mixed, sums_first = out_back(
        grad_hidden, w_in, turn, grad_second, unit, unit_scale, vectors, mixed_slots, w_first
    )

    def clip_back(clip):
        prob, rel, _ = made[clip]
        return attention_back(clip, joined, gate, rank, prob, rel, grad_mixed)

    corner_down, inner, grad_mixed = together((corner_down, inner, grad_mixed))

    corner_down = [(part, 0) for part in corner_down]
    sides_down = exchange_sides(build(*beside(sides_out(2, down, corner_down), corner_out(1, inner))))
    backs = [clip_back(clip) for clip in range(clips)]
    grads_joined = [back[0] for back in backs]
    grad_gate_inputs, table_grad, sums_attention = gate_back(
        inputs_low, table, gate, grads_joined, [back[1] for back in backs], [back[2] for back in backs]
    )
    grad_small = pack(shards, turn, sums_attention, sums_first, sums_second, grad_bias_in, table_grad)
    first_mine, first_other, grad_joined = first_back(inputs_slots, grad_out, grad_small, grads_joined)
    sides_down, first_mine, first_other, grad_joined = together((sides_down, first_mine, first_other, grad_joined))

    corner_in = [(part, FF) for part in sides_down]
    first = (first_mine, exchange_core(first_other))
    sides_in = exchange_sides(build(*alone(sides_out(1, inner, corner_in))))
    high_down = scatter_far(2, down, sides_down)
    corner_first = exchange_sides(build(*alone(corner_out(0, first))))
    input_grad = rows_back(grad_joined, w_first, turn, grad_first_sum, grad_gate_inputs)
    first, sides_in, high_down, corner_first, input_grad = together(
        (first, sides_in, high_down, corner_first, input_grad)
    )

    corner_first = [(part, 0) for part in corner_first]
    units = ((first, 0), (inner, 1), (down, 2))

    def own_views(row, column, columns):
        found = []
        for pair, unit in units:
            start, end = max(column, lefts[unit]), min(column + columns, lefts[unit] + widths[unit])
            if start < end:
                found.append((start - column, end - start, both(pair, row, start - lefts[unit])))
        return found

    def own_third(side):
        base = cut_all if side else 0
        items = []
        for i, (column, columns) in enumerate(spans(side)):
            for start, size, views in own_views(3 * eighth, base + column, columns):
                items.append((i * n, start, n, size, views))
        return (third[side][0], items)

    sides_first = exchange_sides(
        build(*beside(sides_out(0, first, corner_first), (own_third(1), own_third(0))))
    )
    high_in = scatter_far(1, inner, sides_in)
    if staged:
        high_down += [exchange(build(high_out(2, down, sides_down, 1, 1, high_down[0]))[0], "dp", 4)]
    weight_rows, momenta_rows, averages_rows = [flat_rows(part, n) for part in (weights, momenta, averages)]
    sides_first, high_in, high_down, weight_rows, momenta_rows, averages_rows = together(
        (sides_first, high_in, high_down, weight_rows, momenta_rows, averages_rows)
    )

    own_outs = []
    for side, row in ((0, eighth), (1, 2 * eighth)):
        items = []
        base = 0 if side == 0 else cut_all
        came = sides_first[1] if side == 0 else sides_first[0]
        edges = [(base + c, w, (came, i * n, widths[0])) for i, (c, w) in enumerate(spans(side))]
        edges.append((cut_all, wide_all - cut_all, None) if side == 0 else (0, cut_all, None))
        for column, columns, view in edges:
            for start, size, views in own_views(row, column, columns):
                if view is not None:
                    views = views + [(view[0], view[1], view[2] + start)]
                items.append((0, column + start, n, size, views))
        own_outs.append(((n, wide_all), items))
    own_sides = exchange_sides(build(*own_outs))
    if staged:
        near, far, farthest = [high_out(0, first, sides_first, d, 1) for d in (1, 2, 3)]
        near_in = high_out(1, inner, sides_in, 1, 1, high_in[0])
        wide = widths[0]
        near = ((n, wide + FF), near[1] + [(0, wide, n, FF, near_in[1][0][4])])
        high_first = [exchange(part, "dp", mask) for part, mask in zip(build(near, far, farthest), (4, 8, 12))]
        high_in += [high_first[0]]
    else:
        high_first = scatter_high(0, first, sides_first)
    comes = (
        [(part, 0) for part in high_first],
        [(part, widths[0] if i else 0) for i, part in enumerate(high_in)],
        [(part, 0) for part in high_down],
    )
    sums = []
    for pair, unit in units:
        views = both(pair, 0, 0) + [(side, 0, lefts[unit]) for side in own_sides]
        sums.append(views + [(part, 0, left) for part, left in comes[unit]])

    learning = rate_scale / math.sqrt(total_tokens)
    arguments = (weight_rows, momenta_rows, averages_rows, weights.shape[1])
    known = update(learning, (2,), sums, *arguments)
    known, high_first = together((known, high_first))
    comes = ([(part, 0) for part in high_first], [(high_first[0], widths[0])])
    for section in (0, 1):
        if staged:
            sums[section][-len(comes[section]) :] = [(part, 0, left) for part, left in comes[section]]
    momenta_new, averages_new, weights_new, weights_copy = update(learning, (0, 1), sums, *arguments, known)
    return (
        activations.reshape(acts.shape),
        input_grad.reshape(acts.shape),
        momenta_new,
        averages_new,
        weights_new,
        weights_copy,
    )


def solution(mesh):
    split = ("dp", "fsdp")
    in_specs = (
        P(split, None, None),
        P(split, None, None),
        P(split, None),
        P(split),
        P(split, None),
        P(split, None),
        P(split, None),
    )
    out_specs = (
        P(split, None, None),
        P(split, None, None),
        P(split, None),
        P(split, None),
        P(split, None),
        P(split, None),
    )
    return jax.shard_map(body, mesh=mesh, in_specs=in_specs, out_specs=out_specs, check_vma=False)
```

```python
from functools import partial
import math

import jax
import jax.numpy as jnp
import numpy as np
from jax import lax
from jax.experimental import pallas as pl
from jax.experimental.pallas import tpu as pltpu
from jax.sharding import PartitionSpec as P

D = 768
H = 12
HD = 64
FF = 3072
NB = 320
HALF = NB // 2
P_SIZE = 512
NPOS = 4372
LANES = 128
KEYS = 384
BF = jnp.bfloat16
F32 = jnp.float32

deep_alpha = 24.0**0.25
layer_epsilon = 1e-05
masked_score = -1000000000.0
far_distance = 800
gate_units = 8
momentum_rate = 0.9
average_rate = 0.8
decay_rate = 0.0001
rate_scale = 0.04
far_place = 1 << 20


def bucket_levels(span):
    distance = np.arange(0, span + 1)
    exact = HALF // 2
    logscale = (
        np.log(np.maximum(distance, 1) / exact) / np.log(far_distance / exact) * (HALF - exact)
    )
    beyond = np.minimum(exact + np.floor(logscale).astype(np.int64), HALF - 1)
    return np.where(distance < exact, distance, beyond)


def far_marks():
    levels = bucket_levels(2 * P_SIZE)
    rises = np.diff(levels)
    marks = np.repeat(np.arange(1, 2 * P_SIZE + 1), rises)
    return [int(m) for m in marks[HALF // 2 :]]


def key_ends():
    span = 2 * P_SIZE
    levels = bucket_levels(span)
    offsets = np.arange(-span, span + 1)
    level = levels[np.abs(offsets)]
    keys = np.where(offsets > 0, HALF + level, HALF - 1 - level)
    ends = np.full((KEYS,), far_place // 2, np.int32)
    for key in range(NB - 1):
        below = offsets[keys <= key]
        ends[key] = below.max() if below.size else -(far_place // 2)
    return ends


def exchange(value, axis, mask):
    count = lax.axis_size(axis)
    return lax.ppermute(value, axis, [(i, i ^ mask) for i in range(count)])


def high_bits(count):
    return list(range(2, count.bit_length() - 1))


def exchange_sides(pair):
    return exchange(pair[0], "dp", 1), exchange(pair[1], "dp", 2)


def exchange_core(value):
    return exchange(value, "fsdp", 1)


def slot_order(dp, core, count):
    high = count // 4
    core_step, low, up = np.meshgrid(np.arange(2), np.arange(4), np.arange(high), indexing="ij")
    distance = jnp.asarray((up * 4 + low).reshape(-1).astype(np.int32))
    core_distance = jnp.asarray(core_step.reshape(-1).astype(np.int32))
    return (distance ^ dp) * 2 + (core_distance ^ core)


def prep_kernel(marks, shape_ref, mask_ref, ends_ref, bucket_ref, rank_ref, valid_ref):
    clips, patches = mask_ref.shape
    slots = bucket_ref.shape[1]
    mask = mask_ref[...]
    up = lax.broadcasted_iota(jnp.int32, (patches, patches), 0)
    across = lax.broadcasted_iota(jnp.int32, (patches, patches), 1)
    running = wide_dot(mask.astype(F32).astype(BF), (up <= across).astype(F32).astype(BF))
    ranks = jnp.where(mask == 1, running.astype(jnp.int32) - 1, -1)
    slot = lax.broadcasted_iota(jnp.int32, (slots, patches), 0)
    patch = lax.broadcasted_iota(jnp.int32, (slots, patches), 1)
    pair = lax.broadcasted_iota(jnp.int32, (8, patches), 1)
    halves = jnp.where(lax.broadcasted_iota(jnp.int32, (8, patches), 0) == 0, pair >> 4, pair & 15)
    halves = halves.astype(F32).astype(BF)
    for clip in range(clips):
        found = ranks[clip : clip + 1, :] == slot
        column = jnp.sum(jnp.where(found, patch, 0), axis=1, keepdims=True)
        both = nt(halves, found.astype(F32).astype(BF)).astype(jnp.int32)
        row = 16 * both[0:1, :] + both[1:2, :]
        narrow = shape_ref[clip] > 0
        column = jnp.where(narrow, 8 * (column >> 2) + (column & 3), column)
        row = jnp.where(narrow, 8 * (row >> 2) + (row & 3), row)
        count = jnp.sum(mask[clip : clip + 1, :], axis=1, keepdims=True)
        valid = lax.broadcasted_iota(jnp.int32, (slots, 1), 0) < count
        valid_ref[clip * slots : (clip + 1) * slots, :] = valid.astype(F32)
        offset = column - row
        distance = jnp.abs(offset)
        level = jnp.minimum(distance, HALF // 2)
        for mark in marks:
            level = level + (distance >= mark).astype(jnp.int32)
        bucket_ref[clip] = level + jnp.where(offset > 0, HALF, 0)
        away = jnp.where(valid, offset, far_place)
        for first in range(slots):
            seen = away[:, first : first + 1] <= ends_ref[...]
            rank_ref[clip, first : first + 1, :] = jnp.sum(seen.astype(jnp.int32), axis=0, keepdims=True)


def prep(mask, shape_id, slots):
    clips = mask.shape[0]
    ends = jnp.asarray(key_ends())[None, :]
    return call(
        partial(prep_kernel, far_marks()),
        (mask, ends),
        (
            shaped((clips, slots, slots), jnp.int32),
            shaped((clips, slots, KEYS), jnp.int32),
            shaped((clips * slots, 1), F32),
        ),
        8,
        "prep",
        scalars=(shape_id,),
    )


def position_rows(shards, by_key):
    width = (NPOS + shards - 1) // shards
    index = np.full((24, KEYS), -1, np.int64)
    for head in range(H):
        for lane in range(NB):
            bucket = (HALF - 1 - lane if lane < HALF else lane) if by_key else lane
            index[head, lane] = bucket * H + head
    for unit in range(gate_units):
        index[12 + unit, :HD] = NB * H + np.arange(HD) * gate_units + unit
    index[20, :gate_units] = (NB + 0) * H + HD * gate_units + np.arange(gate_units)
    index[21, :H] = NB * H + (HD + 1) * gate_units + np.arange(H)
    pieces = np.where(index >= 0, index // width, -1).astype(np.int32)
    columns = np.where(index >= 0, 12 * D // shards + index % width, -1).astype(np.int32)
    return jnp.asarray(pieces), jnp.asarray(columns)


def vector_chunks(shards):
    width = 12 * D // shards
    size = math.gcd(width, D)
    each, across = width // size, D // size
    return size, [
        (g // each, g % each * size, g // across, g % across * size) for g in range(12 * across)
    ]


def unpack_kernel(shards, turn_ref, pieces_ref, columns_ref, *refs):
    whole_ref, vectors_ref, bias_ref, table_ref, natural_ref, small_ref = refs
    natural_ref[...] = wide_dot(turn_ref[...], whole_ref[:, 4 * D :])
    each = D // shards
    wide = small_ref.shape[1]
    for k in range(wide // LANES):
        small_ref[:, k * LANES : (k + 1) * LANES] = natural_ref[pl.ds(k, shards, stride=each), :]
    size, chunks = vector_chunks(shards)
    for piece, column, row, place in chunks:
        value = small_ref[piece : piece + 1, column : column + size]
        if row < 8:
            vectors_ref[row : row + 1, place : place + size] = value
        else:
            bias_ref[:, (row - 8) * D + place : (row - 8) * D + place + size] = value
    start = 12 * D // shards // LANES * LANES
    small = small_ref[:, start:].astype(BF)
    piece_ids = lax.broadcasted_iota(jnp.int32, (shards, KEYS), 0)
    column_ids = lax.broadcasted_iota(jnp.int32, (wide - start, KEYS), 0) + start
    for row in range(22):
        chosen = (piece_ids == pieces_ref[row : row + 1, :]).astype(F32).astype(BF)
        spread = tn(small, chosen)
        table_ref[row : row + 1, :] = jnp.sum(
            jnp.where(column_ids == columns_ref[row : row + 1, :], spread, 0.0), axis=0, keepdims=True
        )
    table_ref[22:24, :] = jnp.zeros((2, KEYS), F32)


def small_lanes(shards):
    return -(-(12 * D // shards + (NPOS + shards - 1) // shards) // LANES) * LANES


def unpack(shards, turn, whole):
    pieces, columns = position_rows(shards, False)
    return call(
        partial(unpack_kernel, shards),
        (turn, pieces, columns, whole),
        (shaped((8, D), F32), shaped((1, FF), F32), shaped((24, KEYS), F32)),
        8,
        "unpack",
        scratch=(
            pltpu.VMEM((D, LANES), F32),
            pltpu.VMEM((shards, small_lanes(shards)), F32),
        ),
    )


def pack_kernel(shards, turn_ref, pieces_ref, columns_ref, attention_ref, first_ref, second_ref, bias_ref, table_ref, out_ref, natural_ref, small_ref):
    each = D // shards
    wide = small_ref.shape[1]
    table = table_ref[...]
    lane = lax.broadcasted_iota(jnp.int32, table.shape, 1)
    row_id = lax.broadcasted_iota(jnp.int32, table.shape, 0)
    before = jnp.where((lane > 0) & (row_id < H), pltpu.roll(table, 1, 1), 0.0)
    table = table - before
    piece_ids = lax.broadcasted_iota(jnp.int32, (shards, KEYS), 0)
    start = 12 * D // shards // LANES * LANES
    column_ids = lax.broadcasted_iota(jnp.int32, (wide - start, KEYS), 0) + start
    total = jnp.zeros((shards, wide - start), F32)
    for row in range(22):
        chosen = jnp.where(piece_ids == pieces_ref[row : row + 1, :], table[row : row + 1, :], 0.0).astype(BF)
        spread = (column_ids == columns_ref[row : row + 1, :]).astype(F32).astype(BF)
        total = total + nt(chosen, spread)
    small_ref[...] = jnp.zeros(small_ref.shape, F32)
    small_ref[:, start:] = total
    rows = [(attention_ref, 0), (attention_ref, 1)]
    rows += [(first_ref, i) for i in range(3)] + [(second_ref, i) for i in range(3)]
    size, chunks = vector_chunks(shards)
    for piece, column, row, place in chunks:
        if row < 8:
            ref, at = rows[row]
            value = ref[at : at + 1, place : place + size]
        else:
            value = bias_ref[:, (row - 8) * D + place : (row - 8) * D + place + size]
        small_ref[piece : piece + 1, column : column + size] = value
    natural_ref[...] = jnp.zeros(natural_ref.shape, F32)
    for k in range(wide // LANES):
        natural_ref[pl.ds(k, shards, stride=each), :] = small_ref[:, k * LANES : (k + 1) * LANES]
    out_ref[...] = tn(turn_ref[...], natural_ref[...].astype(BF)).astype(BF)


def pack(shards, turn, sums_attention, sums_first, sums_second, bias, table):
    pieces, columns = position_rows(shards, True)
    return call(
        partial(pack_kernel, shards),
        (turn, pieces, columns, sums_attention, sums_first, sums_second, bias, table),
        (shaped((D, LANES), BF),),
        8,
        "pack",
        scratch=(pltpu.VMEM((D, LANES), F32), pltpu.VMEM((shards, small_lanes(shards)), F32)),
    )[0]


def lookup(table_ref, head, index, block):
    out = None
    for part in range(KEYS // LANES):
        row = jnp.broadcast_to(table_ref[head : head + 1, part * LANES : (part + 1) * LANES], index.shape)
        found = jnp.take_along_axis(row, index, axis=1, mode="promise_in_bounds")
        out = found if out is None else jnp.where(block == part, found, out)
    return out


def nt(a, b):
    return lax.dot_general(a, b, (((1,), (1,)), ((), ())), preferred_element_type=F32)


def tn(a, b):
    return lax.dot_general(a, b, (((0,), (0,)), ((), ())), preferred_element_type=F32)


def vmem(count):
    return [pl.BlockSpec(memory_space=pltpu.VMEM)] * count


def limits(mib):
    return pltpu.CompilerParams(vmem_limit_bytes=mib * 1024 * 1024)


def shaped(shape, dtype):
    return jax.ShapeDtypeStruct(tuple(shape), dtype)


def call(kernel, operands, outs, mib, name, scalars=(), scratch=()):
    return pl.pallas_call(
        kernel,
        out_shape=tuple(outs),
        in_specs=[pl.BlockSpec(memory_space=pltpu.SMEM)] * len(scalars) + vmem(len(operands)),
        out_specs=tuple(vmem(len(outs))),
        scratch_shapes=list(scratch),
        compiler_params=limits(mib),
        cost_estimate=pl.CostEstimate(flops=1, bytes_accessed=1, transcendentals=0),
        name=name,
    )(*scalars, *operands)


def build_kernel(plans, count, *refs):
    sources, outs = refs[:count], refs[count:]
    for out, (whole, items) in zip(outs, plans):
        if not whole:
            out[...] = jnp.zeros(out.shape, out.dtype)
        for row, column, rows, columns, views in items:
            values = [
                sources[which][first : first + rows, left : left + columns] for which, first, left in views
            ]
            if len(values) > 1:
                values = [sum(value.astype(F32) for value in values)]
            out[row : row + rows, column : column + columns] = values[0].astype(out.dtype)


def build(*outs):
    sources, plans = [], []
    for shape, items in outs:
        plan = []
        for row, column, rows, columns, views in items:
            found = []
            for array, first, left in views:
                at = next((i for i, source in enumerate(sources) if source is array), None)
                if at is None:
                    at = len(sources)
                    sources.append(array)
                found.append((at, first, left))
            plan.append((row, column, rows, columns, found))
        plans.append((sum(item[2] * item[3] for item in items) == math.prod(shape), plan))
    return call(
        partial(build_kernel, plans, len(sources)), sources, [shaped(shape, BF) for shape, _ in outs], 8, "build"
    )


def stack(parts):
    items, at = [], 0
    for array, row, rows, column, columns in parts:
        items.append((at, 0, rows, columns, [(array, row, column)]))
        at += rows
    return (at, parts[0][4]), items


def whole_of(array):
    return (array, 0, array.shape[0], 0, array.shape[1])


def normal(entries):
    centre = entries - jnp.mean(entries, axis=-1, keepdims=True)
    scale = lax.rsqrt(jnp.mean(centre * centre, axis=-1, keepdims=True) + layer_epsilon)
    return centre * scale, scale


def normal_back(grad, unit, scale):
    return scale * (
        grad
        - jnp.mean(grad, axis=-1, keepdims=True)
        - unit * jnp.mean(grad * unit, axis=-1, keepdims=True)
    )


def wide_dot(a, b):
    return jnp.dot(a, b, preferred_element_type=F32)


def split(value, count):
    parts = []
    for _ in range(count):
        parts.append(value.astype(BF))
        value = value - parts[-1].astype(F32)
    return parts


def joined_kernel(
    x_ref, turn_ref, vectors_ref, table_ref, whole_ref, slots_ref, joined_ref, gate_ref, logits_ref
):
    slots_ref[...] = wide_dot(x_ref[...], turn_ref[...]).astype(BF)
    for part in range(3):
        cols = slice(part * D, (part + 1) * D)
        made = wide_dot(slots_ref[...], whole_ref[:, cols])
        if part != 1:
            made = made + vectors_ref[part // 2 : part // 2 + 1, :]
        joined_ref[:, cols] = made.astype(BF)
    units = table_ref[12:20, :HD].astype(BF)
    logits_ref[...] = jnp.zeros(logits_ref.shape, F32)
    for head in range(H):
        logits_ref[:, head * gate_units : (head + 1) * gate_units] = (
            nt(x_ref[:, head * HD : (head + 1) * HD], units) + table_ref[20:21, :gate_units]
        )
    up = lax.broadcasted_iota(jnp.int32, (LANES, LANES), 0)
    across = lax.broadcasted_iota(jnp.int32, (LANES, LANES), 1)
    logits = split(logits_ref[...], 3)
    gates = []
    for side in range(2):
        chosen = ((up >> 3) == across) & (((up >> 2) & 1) == side)
        chosen = chosen.astype(F32).astype(BF)
        gates.append(jax.nn.sigmoid(sum(wide_dot(part, chosen) for part in logits)))
    first, second = gates
    gate_ref[0] = first * (second * table_ref[21:22, :LANES] - 1.0) + 2.0
    gate_ref[1] = first
    gate_ref[2] = second


def joined_forward(x, turn, vectors, table, whole):
    rows = x.shape[0]
    return call(
        joined_kernel,
        (x, turn, vectors, table, whole),
        (
            shaped((rows, D), BF),
            shaped((rows, 3 * D), BF),
            shaped((3, rows, LANES), F32),
        ),
        8,
        "joined_forward",
        scratch=(pltpu.VMEM((rows, LANES), F32),),
    )


def attention_kernel(clip, bucket_ref, valid_ref, table_ref, joined_ref, gate_ref, prob_ref, rel_ref, mixed_ref):
    slots = bucket_ref.shape[1]
    rows = slice(clip * slots, (clip + 1) * slots)
    index = bucket_ref[clip] & (LANES - 1)
    block = bucket_ref[clip] >> 7
    valid = valid_ref[rows, :] > 0
    gate = jnp.transpose(gate_ref[0, rows, :])
    for head in range(H):
        rel_ref[head] = lookup(table_ref, head, index, block)
    for head in range(H):
        query = joined_ref[rows, head * HD : (head + 1) * HD]
        key = joined_ref[rows, D + head * HD : D + (head + 1) * HD]
        score = nt(key, query) * (1.0 / math.sqrt(HD)) + gate[head : head + 1, :] * rel_ref[head]
        prob_ref[head] = jnp.where(valid, score, masked_score)
    for first in range(0, H, 4):
        score = prob_ref[first : first + 4]
        power = jnp.exp(score - jnp.max(score, axis=1, keepdims=True))
        prob_ref[first : first + 4] = power * (1.0 / jnp.sum(power, axis=1, keepdims=True))
    for head in range(H):
        value = joined_ref[rows, 2 * D + head * HD : 2 * D + (head + 1) * HD]
        mixed_ref[head * HD : (head + 1) * HD, :] = tn(value, prob_ref[head].astype(BF)).astype(BF)


def attention(clip, bucket, valid, table, joined, gate):
    slots = bucket.shape[1]
    return call(
        partial(attention_kernel, clip),
        (bucket, valid, table, joined, gate),
        (shaped((H, slots, slots), F32), shaped((H, slots, slots), F32), shaped((D, slots), BF)),
        4,
        "attention",
    )


def out_kernel(x_ref, turn_ref, vectors_ref, whole_ref, *refs):
    mixed_ref, unit_ref, scale_ref = refs[-3:]
    at = 0
    for part in refs[:-3]:
        rows = slice(at, at + part.shape[1])
        mixed_ref[rows, :] = tn(part[...], turn_ref[...]).astype(BF)
        at += part.shape[1]
    branch = wide_dot(mixed_ref[...], whole_ref[:, 3 * D : 4 * D]) + vectors_ref[2:3, :]
    unit, scale = normal(deep_alpha * x_ref[...].astype(F32) + branch)
    unit_ref[...] = unit
    scale_ref[...] = scale


def out_forward(x, turn, vectors, whole, mixed):
    rows = x.shape[0]
    return call(
        out_kernel,
        (x, turn, vectors, whole, *mixed),
        (shaped((rows, D), BF), shaped((rows, D), F32), shaped((rows, 1), F32)),
        6,
        "out_forward",
    )


def attention_back_kernel(
    clip, joined_ref, gate_ref, rank_ref, prob_ref, rel_ref, grad_ref, tri_ref,
    joined_grad_ref, gate_grad_ref, table_grad_ref,
):
    slots = rank_ref.shape[1]
    rows = slice(clip * slots, (clip + 1) * slots)
    scale = 1.0 / math.sqrt(HD)
    gate = jnp.transpose(gate_ref[0, rows, :])
    for head in range(H):
        cols = slice(head * HD, (head + 1) * HD)
        key_cols = slice(D + head * HD, D + (head + 1) * HD)
        value_cols = slice(2 * D + head * HD, 2 * D + (head + 1) * HD)
        query = joined_ref[rows, cols]
        key = joined_ref[rows, key_cols]
        value = joined_ref[rows, value_cols]
        grad = grad_ref[rows, cols]
        prob = prob_ref[head]
        joined_grad_ref[:, value_cols] = wide_dot(prob.astype(BF), grad).astype(BF)
        weighted = prob * nt(value, grad)
        low = (weighted - prob * jnp.sum(weighted, axis=0, keepdims=True)).astype(BF)
        joined_grad_ref[:, cols] = (tn(low, key) * scale).astype(BF)
        joined_grad_ref[:, key_cols] = (wide_dot(low, query) * scale).astype(BF)
        wide = low.astype(F32)
        gate_grad_ref[head : head + 1, :] = jnp.sum(wide * rel_ref[head], axis=0, keepdims=True)
        gated = wide * gate[head : head + 1, :]
        high = gated.astype(BF)
        rest = (gated - high.astype(F32)).astype(BF)
        running = tn(high, tri_ref[...]) + tn(rest, tri_ref[...])
        for part in range(KEYS // LANES):
            lanes = slice(part * LANES, (part + 1) * LANES)
            rank = rank_ref[clip, :, lanes]
            found = jnp.take_along_axis(
                running, jnp.maximum(rank - 1, 0), axis=1, mode="promise_in_bounds"
            )
            table_grad_ref[head : head + 1, lanes] = jnp.sum(
                jnp.where(rank > 0, found, 0.0), axis=0, keepdims=True
            )
    table_grad_ref[H:, :] = jnp.zeros((16 - H, KEYS), F32)
    gate_grad_ref[H:, :] = jnp.zeros((16 - H, slots), F32)


def attention_back(clip, joined, gate, rank, prob, rel, grad):
    slots = rank.shape[1]
    tri = jnp.asarray(np.triu(np.ones((slots, slots), np.float32)), BF)
    return call(
        partial(attention_back_kernel, clip),
        (joined, gate, rank, prob, rel, grad, tri),
        (shaped((slots, 3 * D), BF), shaped((16, slots), F32), shaped((16, KEYS), F32)),
        4,
        "attention_back",
    )


def gate_back_kernel(count, x_ref, table_ref, gate_ref, *refs):
    joined_grads, gate_grads, table_grads = refs[:count], refs[count : 2 * count], refs[2 * count : 3 * count]
    x_grad_ref, table_grad_ref, sums_ref = refs[3 * count :]
    table_grad_ref[...] = jnp.zeros(table_grad_ref.shape, F32)
    table_grad_ref[:16, :] = sum(ref[...] for ref in table_grads)
    sums_ref[0:1, :] = sum(jnp.sum(ref[:, :D].astype(F32), axis=0, keepdims=True) for ref in joined_grads)
    sums_ref[1:2, :] = sum(jnp.sum(ref[:, 2 * D :].astype(F32), axis=0, keepdims=True) for ref in joined_grads)
    units = [jnp.sum(table_ref[12 + 4 * i : 16 + 4 * i, :HD], axis=0, keepdims=True) for i in range(2)]
    unit_grads = [jnp.zeros((1, HD), F32), jnp.zeros((1, HD), F32)]
    grad = jnp.concatenate([jnp.transpose(ref[...]) for ref in gate_grads], axis=0)
    first, second = gate_ref[1, :, :16], gate_ref[2, :, :16]
    size = table_ref[21:22, :16]
    grads = (
        grad * (second * size - 1.0) * first * (1.0 - first),
        grad * first * size * second * (1.0 - second),
    )
    table_grad_ref[21:22, :16] = jnp.sum(grad * first * second, axis=0, keepdims=True)
    bias_grads = [jnp.sum(jnp.sum(g, axis=0, keepdims=True), axis=1, keepdims=True) for g in grads]
    for head in range(H):
        cols = slice(head * HD, (head + 1) * HD)
        x = x_ref[:, cols].astype(F32)
        sides = [g[:, head : head + 1] for g in grads]
        x_grad_ref[:, cols] = sides[0] * units[0] + sides[1] * units[1]
        for i in range(2):
            unit_grads[i] = unit_grads[i] + jnp.sum(x * sides[i], axis=0, keepdims=True)
    for unit in range(gate_units):
        table_grad_ref[12 + unit : 13 + unit, :HD] = unit_grads[unit // 4]
        table_grad_ref[20:21, unit : unit + 1] = bias_grads[unit // 4]


def gate_back(x, table, gate, joined_grads, gate_grads, table_grads):
    return call(
        partial(gate_back_kernel, len(joined_grads)),
        (x, table, gate, *joined_grads, *gate_grads, *table_grads),
        (shaped(x.shape, F32), shaped((24, KEYS), F32), shaped((8, D), F32)),
        6,
        "gate_back",
    )


def gelu_pair(u):
    size = jnp.abs(u) * math.sqrt(0.5)
    t = 1.0 / (1.0 + 0.3275911 * size)
    poly = ((((1.061405429 * t - 1.453152027) * t + 1.421413741) * t - 0.284496736) * t + 0.254829592) * t
    bell = jnp.exp(-0.5 * u * u)
    tail = 0.5 * poly * bell
    below = jnp.where(u < 0, tail, 1.0 - tail)
    return u * below, below + u * bell * (1.0 / math.sqrt(2.0 * math.pi))


def hidden_kernel(
    unit_ref, vectors_ref, turn_ref, bias_ref, whole_ref, slots_ref, active_ref, slope_ref
):
    low = (unit_ref[...] * vectors_ref[3:4, :] + vectors_ref[4:5, :]).astype(BF)
    slots_ref[...] = wide_dot(low, turn_ref[...]).astype(BF)
    width = FF // 8
    for block in range(8):
        cols = slice(block * width, (block + 1) * width)
        u = wide_dot(slots_ref[...], whole_ref[:, cols]) + bias_ref[:, cols]
        active, slope = gelu_pair(u)
        active_ref[:, cols] = active.astype(BF)
        slope_ref[:, cols] = slope


def hidden_forward(unit, vectors, turn, bias, whole):
    rows = unit.shape[0]
    return call(
        hidden_kernel,
        (unit, vectors, turn, bias, whole),
        (shaped((rows, D), BF), shaped((rows, FF), BF), shaped((rows, FF), F32)),
        10,
        "hidden_forward",
    )


def turn_kernel(slots, *refs):
    at_ref, active_ref, unit_ref, vectors_ref, valid_ref, cot_ref = refs[:6]
    parts = refs[6:-5]
    whole_ref, out_ref, second_ref, low_ref, sums_ref = refs[-5:]
    for slot, (which, row, rows, column) in enumerate(slots):
        place = pl.multiple_of(at_ref[slot], 16)
        if parts[which].shape[1] == D:
            whole_ref[pl.ds(place, rows), :] = parts[which][row : row + rows, :]
            continue
        blocks = [
            parts[which][row : row + rows, column + j * D : column + (j + 1) * D] for j in range(FF // D)
        ]
        whole_ref[pl.ds(place, rows * len(blocks)), :] = jnp.concatenate(blocks, axis=0)
    made = wide_dot(active_ref[...], whole_ref[...]) + vectors_ref[5:6, :]
    first_norm = unit_ref[...] * vectors_ref[3:4, :] + vectors_ref[4:5, :]
    unit, scale = normal(deep_alpha * first_norm + made.astype(BF).astype(F32))
    valid = valid_ref[...]
    gain = vectors_ref[6:7, :]
    out_ref[...] = ((unit * gain + vectors_ref[7:8, :]) * valid).astype(BF)
    grad = cot_ref[...].astype(F32) * valid
    second = normal_back(grad * gain, unit, scale)
    second_ref[...] = second
    low = second.astype(BF)
    low_ref[...] = low
    sums_ref[0:1, :] = jnp.sum(low.astype(F32), axis=0, keepdims=True)
    sums_ref[1:2, :] = jnp.sum(grad * unit, axis=0, keepdims=True)
    sums_ref[2:3, :] = jnp.sum(grad, axis=0, keepdims=True)


def turn_back(at, slots, active, unit, vectors, valid, cot, parts):
    rows = unit.shape[0]
    return call(
        partial(turn_kernel, slots),
        (active, unit, vectors, valid, cot, *parts),
        (shaped((FF, D), BF), shaped((rows, D), BF), shaped((rows, D), F32), shaped((rows, D), BF), shaped((8, D), F32)),
        10,
        "turn_back",
        scalars=(at,),
    )


def turn_active_kernel(rows, at_ref, active_ref, out_ref, turned_ref):
    for first in range(0, FF, FF // 8):
        cols = slice(first, first + FF // 8)
        turned_ref[cols, :] = jnp.transpose(active_ref[:, cols])
    for slot in range(FF // rows):
        place = pl.multiple_of(at_ref[slot], 16)
        out_ref[slot * rows : (slot + 1) * rows, :] = turned_ref[pl.ds(place, rows), :]


def turn_active(at, rows, active):
    return call(
        partial(turn_active_kernel, rows),
        (active,),
        (shaped((FF, active.shape[0]), BF),),
        8,
        "turn_active",
        scalars=(at,),
        scratch=(pltpu.VMEM((FF, active.shape[0]), BF),),
    )[0]


def down_back_kernel(first, rows, active_ref, low_ref, out_ref):
    chunk = rows * FF // D
    for slot in range(FF // 2 // chunk):
        at = first + slot * chunk
        made = wide_dot(active_ref[at : at + chunk, :], low_ref[...]).astype(BF)
        for j in range(FF // D):
            out_ref[slot * rows : (slot + 1) * rows, j * D : (j + 1) * D] = made[j * rows : (j + 1) * rows, :]


def down_back(half, rows, active, low):
    return call(
        partial(down_back_kernel, half * FF // 2, rows),
        (active, low),
        (shaped((D // 2, FF), BF),),
        6,
        "down_back",
    )[0]


def hidden_back_kernel(low_ref, down_ref, slope_ref, grad_ref, bias_ref):
    width = FF // 8
    for block in range(8):
        cols = slice(block * width, (block + 1) * width)
        grad = (nt(low_ref[...], down_ref[cols, :]) * slope_ref[:, cols]).astype(BF)
        grad_ref[:, cols] = grad
        bias_ref[:, cols] = jnp.sum(grad.astype(F32), axis=0, keepdims=True)


def hidden_back(low, down, slope):
    rows = low.shape[0]
    return call(
        hidden_back_kernel,
        (low, down, slope),
        (shaped((rows, FF), BF), shaped((1, FF), F32)),
        6,
        "hidden_back",
    )


def in_back_kernel(slots_ref, grad_ref, mine_ref, other_ref):
    width = FF // 4
    for block in range(4):
        cols = slice(block * width, (block + 1) * width)
        made = tn(slots_ref[...], grad_ref[:, cols]).astype(BF)
        mine_ref[:, cols] = made[: D // 2]
        other_ref[:, cols] = made[D // 2 :]


def in_back(slots, grad):
    rows = slots.shape[0]
    return call(
        in_back_kernel,
        (slots, grad),
        (shaped((D // 2, FF), BF), shaped((D // 2, FF), BF)),
        6,
        "in_back",
    )


def out_back_kernel(
    grad_ref, in_ref, turn_ref, second_ref, unit_ref, scale_ref, vectors_ref, mixed_ref, out_ref,
    first_ref, weight_ref, mixed_grad_ref, sums_ref,
):
    low = nt(grad_ref[...], in_ref[...]).astype(BF)
    grad = deep_alpha * second_ref[...] + nt(low, turn_ref[...]).astype(BF).astype(F32)
    unit = unit_ref[...]
    first = normal_back(grad * vectors_ref[3:4, :], unit, scale_ref[...])
    first_ref[...] = first
    branch = first.astype(BF)
    sums_ref[0:1, :] = jnp.sum(branch.astype(F32), axis=0, keepdims=True)
    sums_ref[1:2, :] = jnp.sum(grad * unit, axis=0, keepdims=True)
    sums_ref[2:3, :] = jnp.sum(grad, axis=0, keepdims=True)
    weight_ref[...] = tn(mixed_ref[...], branch).astype(BF)
    back = nt(branch, out_ref[:, 3 * D : 4 * D]).astype(BF)
    mixed_grad_ref[...] = nt(back, turn_ref[...]).astype(BF)


def out_back(grad, w_in, turn, second, unit, scale, vectors, mixed, w_first):
    rows = unit.shape[0]
    return call(
        out_back_kernel,
        (grad, w_in, turn, second, unit, scale, vectors, mixed, w_first),
        (shaped((rows, D), F32), shaped((D, D), BF), shaped((rows, D), BF), shaped((8, D), F32)),
        6,
        "out_back",
    )


def first_back_kernel(slots_ref, out_ref, small_ref, *refs):
    *grads, mine_ref, other_ref, grad_ref = refs
    at = 0
    for grad in grads:
        grad_ref[at : at + grad.shape[0], :] = grad[...]
        at += grad.shape[0]
    half = D // 2
    for part in range(3):
        cols = slice(part * D, (part + 1) * D)
        made = tn(slots_ref[...], grad_ref[:, cols]).astype(BF)
        mine_ref[:, cols] = made[:half]
        other_ref[:, cols] = made[half:]
    for ref, rows in ((mine_ref, slice(0, half)), (other_ref, slice(half, D))):
        ref[:, 3 * D : 4 * D] = out_ref[rows, :]
        ref[:, 4 * D :] = small_ref[rows, :]


def first_back(slots, weight_out, small, grads):
    rows = slots.shape[0]
    wide = 4 * D + small.shape[1]
    return call(
        first_back_kernel,
        (slots, weight_out, small, *grads),
        (shaped((D // 2, wide), BF), shaped((D // 2, wide), BF), shaped((rows, 3 * D), BF)),
        6,
        "first_back",
    )


def rows_back_kernel(grad_ref, first_ref, turn_ref, branch_ref, gate_ref, out_ref):
    made = nt(grad_ref[...], first_ref[:, : 3 * D])
    high = made.astype(BF)
    rest = made - high.astype(F32)
    middle = rest.astype(BF)
    last = (rest - middle.astype(F32)).astype(BF)
    turned = nt(high, turn_ref[...]) + nt(middle, turn_ref[...]) + nt(last, turn_ref[...])
    out_ref[...] = turned + deep_alpha * branch_ref[...] + gate_ref[...]


def rows_back(grad, w_first, turn, branch, gate):
    rows = grad.shape[0]
    return call(
        rows_back_kernel,
        (grad, w_first, turn, branch, gate),
        (shaped((rows, D), F32),),
        8,
        "rows_back",
    )[0]


def flat_cuts(each):
    cuts = [(0, row, 0, 3 * D) for row in range(each)]
    cuts += [(0, row, 3 * D, 4 * D) for row in range(each)]
    cuts += [(1, row, 0, FF) for row in range(each)]
    cuts += [(2, row, j * D, (j + 1) * D) for j in range(FF // D) for row in range(each)]
    return cuts + [(0, row, 4 * D, 4 * D + LANES) for row in range(each)]


def flat_runs(each, width):
    at = 0
    for which, row, first, last in flat_cuts(each):
        size = min(last - first, width - at)
        if size > 0:
            yield which, row, first, size, at
        at += last - first


def rows_kernel(flat_ref, first_ref, in_ref, down_ref):
    refs = (first_ref, in_ref, down_ref)
    first_ref[:, 4 * D :] = jnp.zeros((first_ref.shape[0], LANES), F32)
    for which, row, first, size, at in flat_runs(first_ref.shape[0], flat_ref.shape[1]):
        refs[which][row : row + 1, first : first + size] = flat_ref[:, at : at + size]


def pieces_kernel(flat_ref, first_ref, in_ref, down_ref, all_ref, *refs):
    rows_kernel(flat_ref, *refs)
    at = 0
    for ref, low in zip(refs, (first_ref, in_ref, down_ref)):
        low[...] = ref[...].astype(BF)
        all_ref[:, at : at + low.shape[1]] = low[...]
        at += low.shape[1]


def row_widths():
    return (4 * D + LANES, FF, FF)


def flat_rows(flat, each):
    return call(rows_kernel, (flat,), [shaped((each, width), F32) for width in row_widths()], 6, "flat_rows")


def pieces(flat, each):
    widths = row_widths()
    return call(
        pieces_kernel,
        (flat,),
        [shaped((each, width), BF) for width in (*widths, sum(widths))],
        6,
        "pieces",
        scratch=[pltpu.VMEM((each, width), F32) for width in widths],
    )


def update_kernel(learning, plan, sections, spans, known, count, *refs):
    size = len(sections)
    sums, refs = refs[:count], refs[count:]
    weights, momenta, averages, refs = refs[:size], refs[size : 2 * size], refs[2 * size : 3 * size], refs[3 * size :]
    outs, refs = refs[known : known + 4], refs[known + 4 :]
    rows, flats, arrived = refs[: 3 * size], refs[3 * size : -1], refs[-1]
    for i in range(size):
        each, wide = weights[i].shape
        grad = sum(
            sums[which][row : row + each, column : column + wide].astype(F32) for which, row, column in plan[i]
        )
        weight = weights[i][...]
        decayed = grad + decay_rate * weight
        momentum = momentum_rate * momenta[i][...] + decayed
        weight = weight - learning * (decayed + momentum_rate * momentum)
        rows[i][...] = momentum
        rows[size + i][...] = average_rate * averages[i][...] + (1.0 - average_rate) * weight
        rows[2 * size + i][...] = weight
    each = weights[0].shape[0]
    copies = []
    for out, which in zip(range(4), (0, 1, 2, 2)):
        for span, (first, last) in enumerate(spans):
            flat = flats[out * len(spans) + span]
            for section, row, column, width, at in flat_runs(each, outs[out].shape[1]):
                if section in sections and first <= at < last:
                    value = rows[which * size + sections.index(section)][row : row + 1, column : column + width]
                    flat[:, at - first : at - first + width] = value.astype(flat.dtype)
            copies.append(
                pltpu.make_async_copy(
                    flat, outs[out].at[:, pl.ds(first, last - first)], arrived.at[out * len(spans) + span]
                )
            )
            copies[-1].start()
    for copy in copies:
        copy.wait()


def update(learning, sections, sums, weights, momenta, averages, width, known=()):
    arrays, plan = [], []
    for section in sections:
        found = []
        for array, row, column in sums[section]:
            at = next((i for i, other in enumerate(arrays) if other is array), None)
            if at is None:
                at = len(arrays)
                arrays.append(array)
            found.append((at, row, column))
        plan.append(found)
    each = weights[0].shape[0]
    runs = [(at, at + size) for section, _, _, size, at in flat_runs(each, width) if section in sections]
    spans = []
    for first, last in runs:
        if spans and spans[-1][1] == first:
            spans[-1] = (spans[-1][0], last)
        else:
            spans.append((first, last))
    rows = [[part[section] for section in sections] for part in (weights, momenta, averages)]
    dtypes = (F32, F32, F32, BF)
    operands = [*arrays, *rows[0], *rows[1], *rows[2]]
    anywhere = pl.BlockSpec(memory_space=pl.ANY)
    return pl.pallas_call(
        partial(update_kernel, learning, plan, list(sections), spans, len(known), len(arrays)),
        out_shape=tuple(shaped((1, width), dtype) for dtype in dtypes),
        in_specs=vmem(len(operands)) + [anywhere] * len(known),
        out_specs=(anywhere,) * 4,
        input_output_aliases={len(operands) + i: i for i in range(len(known))},
        scratch_shapes=[pltpu.VMEM(part.shape, F32) for part in rows[0]] * 3
        + [pltpu.VMEM((1, last - first), dtype) for dtype in dtypes for first, last in spans]
        + [pltpu.SemaphoreType.DMA((4 * len(spans),))],
        compiler_params=limits(10),
        cost_estimate=pl.CostEstimate(flops=1, bytes_accessed=1, transcendentals=0),
        name="update",
    )(*operands, *known)


def body(acts, cotangent, mask, shape_id, weights, momenta, averages):
    shards = lax.axis_size(("dp", "fsdp"))
    count = lax.axis_size("dp")
    dp, core = lax.axis_index("dp"), lax.axis_index("fsdp")
    clips, slots = acts.shape[0], acts.shape[1]
    rows = clips * slots
    total_tokens = rows * shards
    piece_rows = D // shards
    wide_rows = FF // shards
    vector_width = 12 * D // shards
    position_width = (NPOS + shards - 1) // shards
    small_width = vector_width + position_width

    piece_first, piece_in, piece_down, piece_all = pieces(weights, piece_rows)

    order = slot_order(dp, core, count)
    row_order = (order[:, None] * piece_rows + jnp.arange(piece_rows, dtype=jnp.int32)).reshape(-1)
    turn = (jnp.arange(D, dtype=jnp.int32)[:, None] == row_order[None, :]).astype(BF)
    piece_turn = (jnp.arange(shards, dtype=jnp.int32)[:, None] == order[None, :]).astype(BF)

    back_order = jnp.dot(piece_turn.astype(F32), jnp.arange(shards, dtype=F32)).astype(jnp.int32)

    together = lax.optimization_barrier
    bits = high_bits(count)
    staged = len(bits) == 2
    n = piece_rows
    rest = D // 8 - n
    widths = (piece_first.shape[1], FF, FF)
    lefts = (0, widths[0], widths[0] + FF)
    cuts = (13 * LANES, FF // 2, FF // 2)
    wide_all, cut_all = sum(widths), 37 * LANES
    third = (13 * LANES, 12 * LANES, 12 * LANES), (12 * LANES,) * 3
    at = order * wide_rows
    inputs_low = acts.reshape(rows, D)

    def gather_high(piece):
        if staged:
            return [exchange(piece, "dp", d << 2) for d in (1, 2, 3)]
        column = piece
        for bit in bits:
            column = jnp.concatenate([column, exchange(column, "dp", 1 << bit)], axis=0)
        return [column[n:]]

    def thirds(side, views):
        left = widths[0]
        items, column = [], 0
        for i, size in enumerate(third[side]):
            items += views(i * n, left, column, size)
            column += size
        return items

    own_sides = exchange_sides((piece_all, piece_all))
    high_first = gather_high(piece_first)
    own_sides, high_first, piece_in, mask, turn, at = together(
        (own_sides, high_first, piece_in, mask, turn, at)
    )

    items = stack([whole_of(part) for part in high_first])[1]
    sends = build(
        ((rest, widths[0]), items),
        (
            (rest, widths[0] + third[1][0]),
            items + thirds(1, lambda row, left, c, w: [(row, left, n, w, [(own_sides[1], 0, cut_all + c)])]),
        ),
        (
            (rest, widths[0] + third[0][0]),
            items + thirds(0, lambda row, left, c, w: [(row, left, n, w, [(own_sides[0], 0, c)])]),
        ),
    )
    rest_first, sends = sends[0], sends[1:]
    sides_first = exchange_sides(sends)
    high_in = gather_high(piece_in)
    bucket, rank, valid_rows = prep(mask, shape_id, slots)
    sides_first, high_in, piece_down, bucket, rank, valid_rows = together(
        (sides_first, high_in, piece_down, bucket, rank, valid_rows)
    )

    def corner_sends(unit, sides):
        wide, half = widths[unit], cuts[unit]
        return (
            ((rest, wide - half), [(0, 0, rest, wide - half, [(sides[1], 0, half)])]),
            ((rest, half), [(0, 0, rest, half, [(sides[0], 0, 0)])]),
        )

    def corner_items(unit, corner):
        wide, half = widths[unit], cuts[unit]
        (second, left_second), (first, left_first) = corner
        return [
            (0, 0, rest, half, [(first, 0, left_first)]),
            (0, half, rest, wide - half, [(second, 0, left_second)]),
        ]

    def early_rows(unit, piece, high, sides):
        wide = widths[unit]
        return stack([whole_of(piece), whole_of(high)] + [(side, 0, rest, 0, wide) for side in sides])

    def shifted(items, row):
        return [(row + item[0], *item[1:]) for item in items]

    def slots_of(unit, piece, high, sides, corner, early, late):
        wide, left = widths[unit], lefts[unit]
        own_mine, own_other = own
        items = [(0, 0, n, wide, [(piece, 0, 0)]), (n, 0, rest, wide, [(high, 0, 0)])]
        eighth = D // 8
        for i in range(3):
            items.append(((i + 1) * eighth, 0, n, wide, [(own_mine, i * n, left)]))
        for i, side in enumerate(sides):
            items.append(((i + 1) * eighth + n, 0, rest, wide, [(side, 0, 0)]))
        items += shifted(corner_items(unit, corner), 3 * eighth + n)
        base = D // 2
        if not isinstance(early, tuple):
            early = (early, 0), (early, n + rest)
        (one, row_one), (two, row_two) = early
        items.append((base, 0, n, wide, [(one, row_one, 0)]))
        items.append((base + n, 0, rest, wide, [(one, row_one + n, 0)]))
        for i in range(3):
            items.append((base + (i + 1) * eighth, 0, n, wide, [(own_other, i * n, left)]))
            view = (late, 0, 0) if i == 2 else (two, row_two + i * rest, 0)
            items.append((base + (i + 1) * eighth + n, 0, rest, wide, [view]))
        return items

    def own_corner(row, half, side, column):
        return [(row, column + c, n, w, [(side, i * n, widths[0])]) for i, (c, w) in enumerate(half)]

    def spans(side):
        edges = np.cumsum((0, *third[side]))
        return [(int(a), int(b - a)) for a, b in zip(edges[:-1], edges[1:])]

    items = [(0, 0, n, wide_all, [(own_sides[0], 0, 0)]), (n, 0, n, wide_all, [(own_sides[1], 0, 0)])]
    items += own_corner(2 * n, spans(0), sides_first[1], 0) + own_corner(2 * n, spans(1), sides_first[0], cut_all)
    def side_sends(unit, high, sides):
        wide, half = widths[unit - 1], cuts[unit - 1]
        items = stack([whole_of(part) for part in high])[1]
        sends = []
        for width, view in ((wide - half, (sides[1], 0, half)), (half, (sides[0], 0, 0))):
            sends.append(((rest, widths[unit] + width), items + [(0, widths[unit], rest, width, [view])]))
        return [((rest, widths[unit]), items)] + sends

    own_mine, early, rest_in, *sends = build(
        ((3 * n, wide_all), items),
        early_rows(0, piece_first, rest_first, sides_first),
        *side_sends(1, high_in, sides_first),
    )
    sides_in = exchange_sides(sends)
    early_first = exchange_core(early)
    high_down = gather_high(piece_down)
    sides_in, early_first, high_down, own_mine = together((sides_in, early_first, high_down, own_mine))

    corner_first = [(part, FF) for part in sides_in]
    late, rest_down, *sends = build(
        ((rest, widths[0]), corner_items(0, corner_first)), *side_sends(2, high_down, sides_in)
    )
    sides_down = exchange_sides(sends)
    own = (own_mine, exchange_core(own_mine))
    late = exchange_core(late)
    items = slots_of(0, piece_first, rest_first, sides_first, corner_first, early_first, late)
    w_first = build(((D, widths[0]), items))[0]
    early, first_down = build(
        early_rows(1, piece_in, rest_in, sides_in), stack([whole_of(piece_down), whole_of(rest_down)])
    )
    early_in, first_down = exchange_core(early), exchange_core(first_down)
    vectors, bias_in, table = unpack(shards, turn, w_first)
    inputs_slots, joined, gate = joined_forward(inputs_low, turn, vectors, table, w_first)
    made = [attention(clip, bucket, valid_rows, table, joined, gate) for clip in range(clips)]
    mixed_slots, unit, unit_scale = out_forward(inputs_low, turn, vectors, w_first, [m[2] for m in made])
    sides_down, early_in, first_down, unit = together((sides_down, early_in, first_down, unit))

    corner_in = [(part, FF) for part in sides_down]
    late, early, *sends = build(
        ((rest, FF), corner_items(1, corner_in)),
        stack([(side, 0, rest, 0, FF) for side in sides_down]),
        *corner_sends(2, sides_down),
    )
    corner_down = exchange_sides(sends)
    late = exchange_core(late)
    early_down = exchange_core(early)
    items = slots_of(1, piece_in, rest_in, sides_in, corner_in, early_in, late)
    w_in = build(((D, FF), items))[0]
    first_slots, active, slope = hidden_forward(unit, vectors, turn, bias_in, w_in)
    corner_down, early_down, active = together((corner_down, early_down, active))

    corner_down = [(part, 0) for part in corner_down]
    corner = build(((rest, FF), corner_items(2, corner_down)))[0]
    late = exchange_core(corner)
    early_down = (first_down, 0), (early_down, 0)
    items = slots_of(2, piece_down, rest_down, sides_down, [(corner, cuts[2]), (corner, 0)], early_down, late)
    arrays, places = [], [None] * shards
    for row, column, size, _, [(array, first, left)] in items:
        if column:
            continue
        which = next((i for i, known in enumerate(arrays) if known is array), len(arrays))
        if which == len(arrays):
            arrays.append(array)
        for step in range(size // n):
            places[row // n + step] = (which, first + step * n, n, left)
    to = at
    if wide_rows % 16 == 0:
        turned = turn_active(at, wide_rows, active)
        turned, arrays[0] = together((turned, arrays[0]))
    else:
        parts = [arrays[which][row : row + n, left : left + FF] for which, row, _, left in places]
        stacked = jnp.stack(parts).reshape(shards, n, FF // D, D).transpose(0, 2, 1, 3).reshape(shards, wide_rows, D)
        arrays, places = [jnp.take(stacked, back_order, axis=0).reshape(FF, D)], [(0, 0, FF, 0)]
        to = jnp.zeros((1,), jnp.int32)
    w_down, activations, grad_second, grad_made, sums_second = turn_back(
        to, places, active, unit, vectors, valid_rows, cotangent.reshape(rows, D), arrays
    )

    if wide_rows % 16:
        grad_down = tn(active, grad_made).astype(BF).reshape(shards, wide_rows, D)
        grad_down = jnp.take(grad_down, order, axis=0).reshape(shards, FF // D, n, D).transpose(0, 2, 1, 3)
        grad_down = grad_down.reshape(D, FF)
        down_mine, down_other = grad_down[: D // 2], grad_down[D // 2 :]
    else:
        down_other = down_back(1, n, turned, grad_made)
        down_other, grad_made = together((down_other, grad_made))
        down_mine = down_back(0, n, turned, grad_made)

    eighth = D // 8

    def both(pair, row, column):
        return [(array, row, column) for array in pair]

    def corner_out(unit, pair):
        wide, half = widths[unit], cuts[unit]
        row = 3 * eighth + n
        return (
            (wide - half, [(0, 0, rest, wide - half, both(pair, row, half))]),
            (half, [(0, 0, rest, half, both(pair, row, 0))]),
        )

    def sides_out(unit, pair, corner):
        wide, half = widths[unit], cuts[unit]
        (second, left_second), (first, left_first) = corner
        near, side = eighth + n, 2 * eighth + n
        return (
            (
                wide,
                [
                    (0, 0, rest, half, both(pair, near, 0) + [(first, 0, left_first)]),
                    (0, half, rest, wide - half, both(pair, near, half)),
                ],
            ),
            (
                wide,
                [
                    (0, 0, rest, half, both(pair, side, 0)),
                    (0, half, rest, wide - half, both(pair, side, half) + [(second, 0, left_second)]),
                ],
            ),
        )

    def beside(one, two):
        return [
            ((rest, a[0] + b[0]), a[1] + [(item[0], a[0] + item[1], *item[2:]) for item in b[1]])
            for a, b in zip(one, two)
        ]

    def alone(one):
        return [((rest, wide), items) for wide, items in one]

    def column_views(unit, pair, sides, row):
        return both(pair, row, 0) + [(side, row - n, 0) for side in sides]

    def high_out(unit, pair, sides, first, count, *more):
        wide = widths[unit]
        views = column_views(unit, pair, sides, first * n)
        if more:
            views = views + [(more[0], n, 0)]
        return ((count * n, wide), [(0, 0, count * n, wide, views)])

    def scatter_high(unit, pair, sides):
        total = sum(part[n:eighth].astype(F32) for part in pair)
        total = total + sum(side[:, : widths[unit]].astype(F32) for side in sides)
        total = jnp.concatenate([jnp.zeros((n, widths[unit]), F32), total], axis=0)
        for bit in reversed(bits):
            size = total.shape[0] // 2
            total = total[:size] + exchange(total[size:].astype(BF), "dp", 1 << bit).astype(F32)
        return [total]

    def scatter_far(unit, pair, sides):
        if not staged:
            return scatter_high(unit, pair, sides)
        return [exchange(build(high_out(unit, pair, sides, 2, 2))[0], "dp", 8)]

    down = (down_mine, exchange_core(down_other))
    grad_hidden, grad_bias_in = hidden_back(grad_made, w_down, slope)
    in_mine, in_other = in_back(first_slots, grad_hidden)
    down, in_mine, in_other, grad_hidden = together((down, in_mine, in_other, grad_hidden))

    corner_down = exchange_sides(build(*alone(corner_out(2, down))))
    inner = (in_mine, exchange_core(in_other))
    grad_first_sum, grad_out, grad_mixed, sums_first = out_back(
        grad_hidden, w_in, turn, grad_second, unit, unit_scale, vectors, mixed_slots, w_first
    )

    def clip_back(clip):
        prob, rel, _ = made[clip]
        return attention_back(clip, joined, gate, rank, prob, rel, grad_mixed)

    corner_down, inner, grad_mixed = together((corner_down, inner, grad_mixed))

    corner_down = [(part, 0) for part in corner_down]
    sides_down = exchange_sides(build(*beside(sides_out(2, down, corner_down), corner_out(1, inner))))
    backs = [clip_back(clip) for clip in range(clips)]
    grads_joined = [back[0] for back in backs]
    grad_gate_inputs, table_grad, sums_attention = gate_back(
        inputs_low, table, gate, grads_joined, [back[1] for back in backs], [back[2] for back in backs]
    )
    grad_small = pack(shards, turn, sums_attention, sums_first, sums_second, grad_bias_in, table_grad)
    first_mine, first_other, grad_joined = first_back(inputs_slots, grad_out, grad_small, grads_joined)
    sides_down, first_mine, first_other, grad_joined = together((sides_down, first_mine, first_other, grad_joined))

    corner_in = [(part, FF) for part in sides_down]
    first = (first_mine, exchange_core(first_other))
    sides_in = exchange_sides(build(*alone(sides_out(1, inner, corner_in))))
    high_down = scatter_far(2, down, sides_down)
    corner_first = exchange_sides(build(*alone(corner_out(0, first))))
    input_grad = rows_back(grad_joined, w_first, turn, grad_first_sum, grad_gate_inputs)
    first, sides_in, high_down, corner_first, input_grad = together(
        (first, sides_in, high_down, corner_first, input_grad)
    )

    corner_first = [(part, 0) for part in corner_first]
    units = ((first, 0), (inner, 1), (down, 2))

    def own_views(row, column, columns):
        found = []
        for pair, unit in units:
            start, end = max(column, lefts[unit]), min(column + columns, lefts[unit] + widths[unit])
            if start < end:
                found.append((start - column, end - start, both(pair, row, start - lefts[unit])))
        return found

    def own_third(side):
        base = cut_all if side else 0
        items = []
        for i, (column, columns) in enumerate(spans(side)):
            for start, size, views in own_views(3 * eighth, base + column, columns):
                items.append((i * n, start, n, size, views))
        return (third[side][0], items)

    sides_first = exchange_sides(
        build(*beside(sides_out(0, first, corner_first), (own_third(1), own_third(0))))
    )
    high_in = scatter_far(1, inner, sides_in)
    if staged:
        high_down += [exchange(build(high_out(2, down, sides_down, 1, 1, high_down[0]))[0], "dp", 4)]
    weight_rows, momenta_rows, averages_rows = [flat_rows(part, n) for part in (weights, momenta, averages)]
    sides_first, high_in, high_down, weight_rows, momenta_rows, averages_rows = together(
        (sides_first, high_in, high_down, weight_rows, momenta_rows, averages_rows)
    )

    own_outs = []
    for side, row in ((0, eighth), (1, 2 * eighth)):
        items = []
        base = 0 if side == 0 else cut_all
        came = sides_first[1] if side == 0 else sides_first[0]
        edges = [(base + c, w, (came, i * n, widths[0])) for i, (c, w) in enumerate(spans(side))]
        edges.append((cut_all, wide_all - cut_all, None) if side == 0 else (0, cut_all, None))
        for column, columns, view in edges:
            for start, size, views in own_views(row, column, columns):
                if view is not None:
                    views = views + [(view[0], view[1], view[2] + start)]
                items.append((0, column + start, n, size, views))
        own_outs.append(((n, wide_all), items))
    own_sides = exchange_sides(build(*own_outs))
    if staged:
        near, far, farthest = [high_out(0, first, sides_first, d, 1) for d in (1, 2, 3)]
        near_in = high_out(1, inner, sides_in, 1, 1, high_in[0])
        wide = widths[0]
        near = ((n, wide + FF), near[1] + [(0, wide, n, FF, near_in[1][0][4])])
        high_first = [exchange(part, "dp", mask) for part, mask in zip(build(near, far, farthest), (4, 8, 12))]
        high_in += [high_first[0]]
    else:
        high_first = scatter_high(0, first, sides_first)
    comes = (
        [(part, 0) for part in high_first],
        [(part, widths[0] if i else 0) for i, part in enumerate(high_in)],
        [(part, 0) for part in high_down],
    )
    sums = []
    for pair, unit in units:
        views = both(pair, 0, 0) + [(side, 0, lefts[unit]) for side in own_sides]
        sums.append(views + [(part, 0, left) for part, left in comes[unit]])

    learning = rate_scale / math.sqrt(total_tokens)
    arguments = (weight_rows, momenta_rows, averages_rows, weights.shape[1])
    known = update(learning, (2,), sums, *arguments)
    if staged:
        known, high_first[0] = together((known, high_first[0]))
        sums[1][-1] = (high_first[0], 0, widths[0])
    known = update(learning, (1,), sums, *arguments, known)
    if staged:
        known, high_first = together((known, high_first))
        sums[0][-3:] = [(part, 0, 0) for part in high_first]
    momenta_new, averages_new, weights_new, weights_copy = update(learning, (0,), sums, *arguments, known)
    return (
        activations.reshape(acts.shape),
        input_grad.reshape(acts.shape),
        momenta_new,
        averages_new,
        weights_new,
        weights_copy,
    )


def solution(mesh):
    split = ("dp", "fsdp")
    in_specs = (
        P(split, None, None),
        P(split, None, None),
        P(split, None),
        P(split),
        P(split, None),
        P(split, None),
        P(split, None),
    )
    out_specs = (
        P(split, None, None),
        P(split, None, None),
        P(split, None),
        P(split, None),
        P(split, None),
        P(split, None),
    )
    return jax.shard_map(body, mesh=mesh, in_specs=in_specs, out_specs=out_specs, check_vma=False)
```

```python
from functools import partial
import math

import jax
import jax.numpy as jnp
import numpy as np
from jax import lax
from jax.experimental import pallas as pl
from jax.experimental.pallas import tpu as pltpu
from jax.sharding import PartitionSpec as P

D = 768
H = 12
HD = 64
FF = 3072
NB = 320
HALF = NB // 2
P_SIZE = 512
NPOS = 4372
LANES = 128
KEYS = 384
BF = jnp.bfloat16
F32 = jnp.float32

deep_alpha = 24.0**0.25
layer_epsilon = 1e-05
masked_score = -1000000000.0
far_distance = 800
gate_units = 8
momentum_rate = 0.9
average_rate = 0.8
decay_rate = 0.0001
rate_scale = 0.04
far_place = 1 << 20


def bucket_levels(span):
    distance = np.arange(0, span + 1)
    exact = HALF // 2
    logscale = (
        np.log(np.maximum(distance, 1) / exact) / np.log(far_distance / exact) * (HALF - exact)
    )
    beyond = np.minimum(exact + np.floor(logscale).astype(np.int64), HALF - 1)
    return np.where(distance < exact, distance, beyond)


def far_marks():
    levels = bucket_levels(2 * P_SIZE)
    rises = np.diff(levels)
    marks = np.repeat(np.arange(1, 2 * P_SIZE + 1), rises)
    return [int(m) for m in marks[HALF // 2 :]]


def key_ends():
    span = 2 * P_SIZE
    levels = bucket_levels(span)
    offsets = np.arange(-span, span + 1)
    level = levels[np.abs(offsets)]
    keys = np.where(offsets > 0, HALF + level, HALF - 1 - level)
    ends = np.full((KEYS,), far_place // 2, np.int32)
    for key in range(NB - 1):
        below = offsets[keys <= key]
        ends[key] = below.max() if below.size else -(far_place // 2)
    return ends


def exchange(value, axis, mask):
    count = lax.axis_size(axis)
    return lax.ppermute(value, axis, [(i, i ^ mask) for i in range(count)])


def high_bits(count):
    return list(range(2, count.bit_length() - 1))


def exchange_sides(pair):
    return exchange(pair[0], "dp", 1), exchange(pair[1], "dp", 2)


def exchange_core(value):
    return exchange(value, "fsdp", 1)


def slot_order(dp, core, count):
    high = count // 4
    core_step, low, up = np.meshgrid(np.arange(2), np.arange(4), np.arange(high), indexing="ij")
    distance = jnp.asarray((up * 4 + low).reshape(-1).astype(np.int32))
    core_distance = jnp.asarray(core_step.reshape(-1).astype(np.int32))
    return (distance ^ dp) * 2 + (core_distance ^ core)


def prep_kernel(marks, shape_ref, mask_ref, ends_ref, bucket_ref, rank_ref, valid_ref):
    clips, patches = mask_ref.shape
    slots = bucket_ref.shape[1]
    mask = mask_ref[...]
    up = lax.broadcasted_iota(jnp.int32, (patches, patches), 0)
    across = lax.broadcasted_iota(jnp.int32, (patches, patches), 1)
    running = wide_dot(mask.astype(F32).astype(BF), (up <= across).astype(F32).astype(BF))
    ranks = jnp.where(mask == 1, running.astype(jnp.int32) - 1, -1)
    slot = lax.broadcasted_iota(jnp.int32, (slots, patches), 0)
    patch = lax.broadcasted_iota(jnp.int32, (slots, patches), 1)
    pair = lax.broadcasted_iota(jnp.int32, (8, patches), 1)
    halves = jnp.where(lax.broadcasted_iota(jnp.int32, (8, patches), 0) == 0, pair >> 4, pair & 15)
    halves = halves.astype(F32).astype(BF)
    for clip in range(clips):
        found = ranks[clip : clip + 1, :] == slot
        column = jnp.sum(jnp.where(found, patch, 0), axis=1, keepdims=True)
        both = nt(halves, found.astype(F32).astype(BF)).astype(jnp.int32)
        row = 16 * both[0:1, :] + both[1:2, :]
        narrow = shape_ref[clip] > 0
        column = jnp.where(narrow, 8 * (column >> 2) + (column & 3), column)
        row = jnp.where(narrow, 8 * (row >> 2) + (row & 3), row)
        count = jnp.sum(mask[clip : clip + 1, :], axis=1, keepdims=True)
        valid = lax.broadcasted_iota(jnp.int32, (slots, 1), 0) < count
        valid_ref[clip * slots : (clip + 1) * slots, :] = valid.astype(F32)
        offset = column - row
        distance = jnp.abs(offset)
        level = jnp.minimum(distance, HALF // 2)
        for mark in marks:
            level = level + (distance >= mark).astype(jnp.int32)
        bucket_ref[clip] = level + jnp.where(offset > 0, HALF, 0)
        away = jnp.where(valid, offset, far_place)
        for first in range(slots):
            seen = away[:, first : first + 1] <= ends_ref[...]
            rank_ref[clip, first : first + 1, :] = jnp.sum(seen.astype(jnp.int32), axis=0, keepdims=True)


def prep(mask, shape_id, slots):
    clips = mask.shape[0]
    ends = jnp.asarray(key_ends())[None, :]
    return call(
        partial(prep_kernel, far_marks()),
        (mask, ends),
        (
            shaped((clips, slots, slots), jnp.int32),
            shaped((clips, slots, KEYS), jnp.int32),
            shaped((clips * slots, 1), F32),
        ),
        8,
        "prep",
        scalars=(shape_id,),
    )


def position_rows(shards, by_key):
    width = (NPOS + shards - 1) // shards
    index = np.full((24, KEYS), -1, np.int64)
    for head in range(H):
        for lane in range(NB):
            bucket = (HALF - 1 - lane if lane < HALF else lane) if by_key else lane
            index[head, lane] = bucket * H + head
    for unit in range(gate_units):
        index[12 + unit, :HD] = NB * H + np.arange(HD) * gate_units + unit
    index[20, :gate_units] = (NB + 0) * H + HD * gate_units + np.arange(gate_units)
    index[21, :H] = NB * H + (HD + 1) * gate_units + np.arange(H)
    pieces = np.where(index >= 0, index // width, -1).astype(np.int32)
    columns = np.where(index >= 0, 12 * D // shards + index % width, -1).astype(np.int32)
    return jnp.asarray(pieces), jnp.asarray(columns)


def vector_chunks(shards):
    width = 12 * D // shards
    size = math.gcd(width, D)
    each, across = width // size, D // size
    return size, [
        (g // each, g % each * size, g // across, g % across * size) for g in range(12 * across)
    ]


def unpack_kernel(shards, turn_ref, pieces_ref, columns_ref, *refs):
    whole_ref, vectors_ref, bias_ref, table_ref, natural_ref, small_ref = refs
    natural_ref[...] = wide_dot(turn_ref[...], whole_ref[:, 4 * D :])
    each = D // shards
    wide = small_ref.shape[1]
    for k in range(wide // LANES):
        small_ref[:, k * LANES : (k + 1) * LANES] = natural_ref[pl.ds(k, shards, stride=each), :]
    size, chunks = vector_chunks(shards)
    for piece, column, row, place in chunks:
        value = small_ref[piece : piece + 1, column : column + size]
        if row < 8:
            vectors_ref[row : row + 1, place : place + size] = value
        else:
            bias_ref[:, (row - 8) * D + place : (row - 8) * D + place + size] = value
    start = 12 * D // shards // LANES * LANES
    small = small_ref[:, start:].astype(BF)
    piece_ids = lax.broadcasted_iota(jnp.int32, (shards, KEYS), 0)
    column_ids = lax.broadcasted_iota(jnp.int32, (wide - start, KEYS), 0) + start
    for row in range(22):
        chosen = (piece_ids == pieces_ref[row : row + 1, :]).astype(F32).astype(BF)
        spread = tn(small, chosen)
        table_ref[row : row + 1, :] = jnp.sum(
            jnp.where(column_ids == columns_ref[row : row + 1, :], spread, 0.0), axis=0, keepdims=True
        )
    table_ref[22:24, :] = jnp.zeros((2, KEYS), F32)


def small_lanes(shards):
    return -(-(12 * D // shards + (NPOS + shards - 1) // shards) // LANES) * LANES


def unpack(shards, turn, whole):
    pieces, columns = position_rows(shards, False)
    return call(
        partial(unpack_kernel, shards),
        (turn, pieces, columns, whole),
        (shaped((8, D), F32), shaped((1, FF), F32), shaped((24, KEYS), F32)),
        8,
        "unpack",
        scratch=(
            pltpu.VMEM((D, LANES), F32),
            pltpu.VMEM((shards, small_lanes(shards)), F32),
        ),
    )


def pack_kernel(shards, turn_ref, pieces_ref, columns_ref, attention_ref, first_ref, second_ref, bias_ref, table_ref, out_ref, natural_ref, small_ref):
    each = D // shards
    wide = small_ref.shape[1]
    table = table_ref[...]
    lane = lax.broadcasted_iota(jnp.int32, table.shape, 1)
    row_id = lax.broadcasted_iota(jnp.int32, table.shape, 0)
    before = jnp.where((lane > 0) & (row_id < H), pltpu.roll(table, 1, 1), 0.0)
    table = table - before
    piece_ids = lax.broadcasted_iota(jnp.int32, (shards, KEYS), 0)
    start = 12 * D // shards // LANES * LANES
    column_ids = lax.broadcasted_iota(jnp.int32, (wide - start, KEYS), 0) + start
    total = jnp.zeros((shards, wide - start), F32)
    for row in range(22):
        chosen = jnp.where(piece_ids == pieces_ref[row : row + 1, :], table[row : row + 1, :], 0.0).astype(BF)
        spread = (column_ids == columns_ref[row : row + 1, :]).astype(F32).astype(BF)
        total = total + nt(chosen, spread)
    small_ref[...] = jnp.zeros(small_ref.shape, F32)
    small_ref[:, start:] = total
    rows = [(attention_ref, 0), (attention_ref, 1)]
    rows += [(first_ref, i) for i in range(3)] + [(second_ref, i) for i in range(3)]
    size, chunks = vector_chunks(shards)
    for piece, column, row, place in chunks:
        if row < 8:
            ref, at = rows[row]
            value = ref[at : at + 1, place : place + size]
        else:
            value = bias_ref[:, (row - 8) * D + place : (row - 8) * D + place + size]
        small_ref[piece : piece + 1, column : column + size] = value
    natural_ref[...] = jnp.zeros(natural_ref.shape, F32)
    for k in range(wide // LANES):
        natural_ref[pl.ds(k, shards, stride=each), :] = small_ref[:, k * LANES : (k + 1) * LANES]
    out_ref[...] = tn(turn_ref[...], natural_ref[...].astype(BF)).astype(BF)


def pack(shards, turn, sums_attention, sums_first, sums_second, bias, table):
    pieces, columns = position_rows(shards, True)
    return call(
        partial(pack_kernel, shards),
        (turn, pieces, columns, sums_attention, sums_first, sums_second, bias, table),
        (shaped((D, LANES), BF),),
        8,
        "pack",
        scratch=(pltpu.VMEM((D, LANES), F32), pltpu.VMEM((shards, small_lanes(shards)), F32)),
    )[0]


def lookup(table_ref, head, index, block):
    out = None
    for part in range(KEYS // LANES):
        row = jnp.broadcast_to(table_ref[head : head + 1, part * LANES : (part + 1) * LANES], index.shape)
        found = jnp.take_along_axis(row, index, axis=1, mode="promise_in_bounds")
        out = found if out is None else jnp.where(block == part, found, out)
    return out


def nt(a, b):
    return lax.dot_general(a, b, (((1,), (1,)), ((), ())), preferred_element_type=F32)


def tn(a, b):
    return lax.dot_general(a, b, (((0,), (0,)), ((), ())), preferred_element_type=F32)


def vmem(count):
    return [pl.BlockSpec(memory_space=pltpu.VMEM)] * count


def limits(mib):
    return pltpu.CompilerParams(vmem_limit_bytes=mib * 1024 * 1024)


def shaped(shape, dtype):
    return jax.ShapeDtypeStruct(tuple(shape), dtype)


def call(kernel, operands, outs, mib, name, scalars=(), scratch=()):
    return pl.pallas_call(
        kernel,
        out_shape=tuple(outs),
        in_specs=[pl.BlockSpec(memory_space=pltpu.SMEM)] * len(scalars) + vmem(len(operands)),
        out_specs=tuple(vmem(len(outs))),
        scratch_shapes=list(scratch),
        compiler_params=limits(mib),
        cost_estimate=pl.CostEstimate(flops=1, bytes_accessed=1, transcendentals=0),
        name=name,
    )(*scalars, *operands)


def build_kernel(plans, count, *refs):
    sources, outs = refs[:count], refs[count:]
    for out, (whole, items) in zip(outs, plans):
        if not whole:
            out[...] = jnp.zeros(out.shape, out.dtype)
        for row, column, rows, columns, views in items:
            values = [
                sources[which][first : first + rows, left : left + columns] for which, first, left in views
            ]
            if len(values) > 1:
                values = [sum(value.astype(F32) for value in values)]
            out[row : row + rows, column : column + columns] = values[0].astype(out.dtype)


def build(*outs):
    sources, plans = [], []
    for shape, items in outs:
        plan = []
        for row, column, rows, columns, views in items:
            found = []
            for array, first, left in views:
                at = next((i for i, source in enumerate(sources) if source is array), None)
                if at is None:
                    at = len(sources)
                    sources.append(array)
                found.append((at, first, left))
            plan.append((row, column, rows, columns, found))
        plans.append((sum(item[2] * item[3] for item in items) == math.prod(shape), plan))
    return call(
        partial(build_kernel, plans, len(sources)), sources, [shaped(shape, BF) for shape, _ in outs], 8, "build"
    )


def stack(parts):
    items, at = [], 0
    for array, row, rows, column, columns in parts:
        items.append((at, 0, rows, columns, [(array, row, column)]))
        at += rows
    return (at, parts[0][4]), items


def whole_of(array):
    return (array, 0, array.shape[0], 0, array.shape[1])


def normal(entries):
    centre = entries - jnp.mean(entries, axis=-1, keepdims=True)
    scale = lax.rsqrt(jnp.mean(centre * centre, axis=-1, keepdims=True) + layer_epsilon)
    return centre * scale, scale


def normal_back(grad, unit, scale):
    return scale * (
        grad
        - jnp.mean(grad, axis=-1, keepdims=True)
        - unit * jnp.mean(grad * unit, axis=-1, keepdims=True)
    )


def wide_dot(a, b):
    return jnp.dot(a, b, preferred_element_type=F32)


def split(value, count):
    parts = []
    for _ in range(count):
        parts.append(value.astype(BF))
        value = value - parts[-1].astype(F32)
    return parts


def joined_kernel(
    x_ref, turn_ref, vectors_ref, table_ref, whole_ref, slots_ref, joined_ref, gate_ref, logits_ref
):
    slots_ref[...] = wide_dot(x_ref[...], turn_ref[...]).astype(BF)
    for part in range(3):
        cols = slice(part * D, (part + 1) * D)
        made = wide_dot(slots_ref[...], whole_ref[:, cols])
        if part != 1:
            made = made + vectors_ref[part // 2 : part // 2 + 1, :]
        joined_ref[:, cols] = made.astype(BF)
    units = table_ref[12:20, :HD].astype(BF)
    logits_ref[...] = jnp.zeros(logits_ref.shape, F32)
    for head in range(H):
        logits_ref[:, head * gate_units : (head + 1) * gate_units] = (
            nt(x_ref[:, head * HD : (head + 1) * HD], units) + table_ref[20:21, :gate_units]
        )
    up = lax.broadcasted_iota(jnp.int32, (LANES, LANES), 0)
    across = lax.broadcasted_iota(jnp.int32, (LANES, LANES), 1)
    logits = split(logits_ref[...], 3)
    gates = []
    for side in range(2):
        chosen = ((up >> 3) == across) & (((up >> 2) & 1) == side)
        chosen = chosen.astype(F32).astype(BF)
        gates.append(jax.nn.sigmoid(sum(wide_dot(part, chosen) for part in logits)))
    first, second = gates
    gate_ref[0] = first * (second * table_ref[21:22, :LANES] - 1.0) + 2.0
    gate_ref[1] = first
    gate_ref[2] = second


def joined_forward(x, turn, vectors, table, whole):
    rows = x.shape[0]
    return call(
        joined_kernel,
        (x, turn, vectors, table, whole),
        (
            shaped((rows, D), BF),
            shaped((rows, 3 * D), BF),
            shaped((3, rows, LANES), F32),
        ),
        8,
        "joined_forward",
        scratch=(pltpu.VMEM((rows, LANES), F32),),
    )


def attention_kernel(clip, bucket_ref, valid_ref, table_ref, joined_ref, gate_ref, prob_ref, rel_ref, mixed_ref):
    slots = bucket_ref.shape[1]
    rows = slice(clip * slots, (clip + 1) * slots)
    index = bucket_ref[clip] & (LANES - 1)
    block = bucket_ref[clip] >> 7
    valid = valid_ref[rows, :] > 0
    gate = jnp.transpose(gate_ref[0, rows, :])
    for head in range(H):
        rel_ref[head] = lookup(table_ref, head, index, block)
    for head in range(H):
        query = joined_ref[rows, head * HD : (head + 1) * HD]
        key = joined_ref[rows, D + head * HD : D + (head + 1) * HD]
        score = nt(key, query) * (1.0 / math.sqrt(HD)) + gate[head : head + 1, :] * rel_ref[head]
        prob_ref[head] = jnp.where(valid, score, masked_score)
    for first in range(0, H, 4):
        score = prob_ref[first : first + 4]
        power = jnp.exp(score - jnp.max(score, axis=1, keepdims=True))
        prob_ref[first : first + 4] = power * (1.0 / jnp.sum(power, axis=1, keepdims=True))
    for head in range(H):
        value = joined_ref[rows, 2 * D + head * HD : 2 * D + (head + 1) * HD]
        mixed_ref[head * HD : (head + 1) * HD, :] = tn(value, prob_ref[head].astype(BF)).astype(BF)


def attention(clip, bucket, valid, table, joined, gate):
    slots = bucket.shape[1]
    return call(
        partial(attention_kernel, clip),
        (bucket, valid, table, joined, gate),
        (shaped((H, slots, slots), F32), shaped((H, slots, slots), F32), shaped((D, slots), BF)),
        4,
        "attention",
    )


def out_kernel(x_ref, turn_ref, vectors_ref, whole_ref, *refs):
    mixed_ref, unit_ref, scale_ref = refs[-3:]
    at = 0
    for part in refs[:-3]:
        rows = slice(at, at + part.shape[1])
        mixed_ref[rows, :] = tn(part[...], turn_ref[...]).astype(BF)
        at += part.shape[1]
    branch = wide_dot(mixed_ref[...], whole_ref[:, 3 * D : 4 * D]) + vectors_ref[2:3, :]
    unit, scale = normal(deep_alpha * x_ref[...].astype(F32) + branch)
    unit_ref[...] = unit
    scale_ref[...] = scale


def out_forward(x, turn, vectors, whole, mixed):
    rows = x.shape[0]
    return call(
        out_kernel,
        (x, turn, vectors, whole, *mixed),
        (shaped((rows, D), BF), shaped((rows, D), F32), shaped((rows, 1), F32)),
        6,
        "out_forward",
    )


def attention_back_kernel(
    clip, joined_ref, gate_ref, rank_ref, prob_ref, rel_ref, grad_ref, tri_ref,
    joined_grad_ref, gate_grad_ref, table_grad_ref,
):
    slots = rank_ref.shape[1]
    rows = slice(clip * slots, (clip + 1) * slots)
    scale = 1.0 / math.sqrt(HD)
    gate = jnp.transpose(gate_ref[0, rows, :])
    for head in range(H):
        cols = slice(head * HD, (head + 1) * HD)
        key_cols = slice(D + head * HD, D + (head + 1) * HD)
        value_cols = slice(2 * D + head * HD, 2 * D + (head + 1) * HD)
        query = joined_ref[rows, cols]
        key = joined_ref[rows, key_cols]
        value = joined_ref[rows, value_cols]
        grad = grad_ref[rows, cols]
        prob = prob_ref[head]
        joined_grad_ref[:, value_cols] = wide_dot(prob.astype(BF), grad).astype(BF)
        weighted = prob * nt(value, grad)
        low = (weighted - prob * jnp.sum(weighted, axis=0, keepdims=True)).astype(BF)
        joined_grad_ref[:, cols] = (tn(low, key) * scale).astype(BF)
        joined_grad_ref[:, key_cols] = (wide_dot(low, query) * scale).astype(BF)
        wide = low.astype(F32)
        gate_grad_ref[head : head + 1, :] = jnp.sum(wide * rel_ref[head], axis=0, keepdims=True)
        gated = wide * gate[head : head + 1, :]
        high = gated.astype(BF)
        rest = (gated - high.astype(F32)).astype(BF)
        running = tn(high, tri_ref[...]) + tn(rest, tri_ref[...])
        for part in range(KEYS // LANES):
            lanes = slice(part * LANES, (part + 1) * LANES)
            rank = rank_ref[clip, :, lanes]
            found = jnp.take_along_axis(
                running, jnp.maximum(rank - 1, 0), axis=1, mode="promise_in_bounds"
            )
            table_grad_ref[head : head + 1, lanes] = jnp.sum(
                jnp.where(rank > 0, found, 0.0), axis=0, keepdims=True
            )
    table_grad_ref[H:, :] = jnp.zeros((16 - H, KEYS), F32)
    gate_grad_ref[H:, :] = jnp.zeros((16 - H, slots), F32)


def attention_back(clip, joined, gate, rank, prob, rel, grad):
    slots = rank.shape[1]
    tri = jnp.asarray(np.triu(np.ones((slots, slots), np.float32)), BF)
    return call(
        partial(attention_back_kernel, clip),
        (joined, gate, rank, prob, rel, grad, tri),
        (shaped((slots, 3 * D), BF), shaped((16, slots), F32), shaped((16, KEYS), F32)),
        4,
        "attention_back",
    )


def gate_back_kernel(count, x_ref, table_ref, gate_ref, *refs):
    joined_grads, gate_grads, table_grads = refs[:count], refs[count : 2 * count], refs[2 * count : 3 * count]
    x_grad_ref, table_grad_ref, sums_ref = refs[3 * count :]
    table_grad_ref[...] = jnp.zeros(table_grad_ref.shape, F32)
    table_grad_ref[:16, :] = sum(ref[...] for ref in table_grads)
    sums_ref[0:1, :] = sum(jnp.sum(ref[:, :D].astype(F32), axis=0, keepdims=True) for ref in joined_grads)
    sums_ref[1:2, :] = sum(jnp.sum(ref[:, 2 * D :].astype(F32), axis=0, keepdims=True) for ref in joined_grads)
    units = [jnp.sum(table_ref[12 + 4 * i : 16 + 4 * i, :HD], axis=0, keepdims=True) for i in range(2)]
    unit_grads = [jnp.zeros((1, HD), F32), jnp.zeros((1, HD), F32)]
    grad = jnp.concatenate([jnp.transpose(ref[...]) for ref in gate_grads], axis=0)
    first, second = gate_ref[1, :, :16], gate_ref[2, :, :16]
    size = table_ref[21:22, :16]
    grads = (
        grad * (second * size - 1.0) * first * (1.0 - first),
        grad * first * size * second * (1.0 - second),
    )
    table_grad_ref[21:22, :16] = jnp.sum(grad * first * second, axis=0, keepdims=True)
    bias_grads = [jnp.sum(jnp.sum(g, axis=0, keepdims=True), axis=1, keepdims=True) for g in grads]
    for head in range(H):
        cols = slice(head * HD, (head + 1) * HD)
        x = x_ref[:, cols].astype(F32)
        sides = [g[:, head : head + 1] for g in grads]
        x_grad_ref[:, cols] = sides[0] * units[0] + sides[1] * units[1]
        for i in range(2):
            unit_grads[i] = unit_grads[i] + jnp.sum(x * sides[i], axis=0, keepdims=True)
    for unit in range(gate_units):
        table_grad_ref[12 + unit : 13 + unit, :HD] = unit_grads[unit // 4]
        table_grad_ref[20:21, unit : unit + 1] = bias_grads[unit // 4]


def gate_back(x, table, gate, joined_grads, gate_grads, table_grads):
    return call(
        partial(gate_back_kernel, len(joined_grads)),
        (x, table, gate, *joined_grads, *gate_grads, *table_grads),
        (shaped(x.shape, F32), shaped((24, KEYS), F32), shaped((8, D), F32)),
        6,
        "gate_back",
    )


def gelu_pair(u):
    size = jnp.abs(u) * math.sqrt(0.5)
    t = 1.0 / (1.0 + 0.3275911 * size)
    poly = ((((1.061405429 * t - 1.453152027) * t + 1.421413741) * t - 0.284496736) * t + 0.254829592) * t
    bell = jnp.exp(-0.5 * u * u)
    tail = 0.5 * poly * bell
    below = jnp.where(u < 0, tail, 1.0 - tail)
    return u * below, below + u * bell * (1.0 / math.sqrt(2.0 * math.pi))


def hidden_kernel(
    unit_ref, vectors_ref, turn_ref, bias_ref, whole_ref, slots_ref, active_ref, slope_ref
):
    low = (unit_ref[...] * vectors_ref[3:4, :] + vectors_ref[4:5, :]).astype(BF)
    slots_ref[...] = wide_dot(low, turn_ref[...]).astype(BF)
    width = FF // 8
    for block in range(8):
        cols = slice(block * width, (block + 1) * width)
        u = wide_dot(slots_ref[...], whole_ref[:, cols]) + bias_ref[:, cols]
        active, slope = gelu_pair(u)
        active_ref[:, cols] = active.astype(BF)
        slope_ref[:, cols] = slope


def hidden_forward(unit, vectors, turn, bias, whole):
    rows = unit.shape[0]
    return call(
        hidden_kernel,
        (unit, vectors, turn, bias, whole),
        (shaped((rows, D), BF), shaped((rows, FF), BF), shaped((rows, FF), F32)),
        10,
        "hidden_forward",
    )


def turn_kernel(slots, *refs):
    at_ref, active_ref, unit_ref, vectors_ref, valid_ref, cot_ref = refs[:6]
    parts = refs[6:-5]
    whole_ref, out_ref, second_ref, low_ref, sums_ref = refs[-5:]
    for slot, (which, row, rows, column) in enumerate(slots):
        place = pl.multiple_of(at_ref[slot], 16)
        if parts[which].shape[1] == D:
            whole_ref[pl.ds(place, rows), :] = parts[which][row : row + rows, :]
            continue
        blocks = [
            parts[which][row : row + rows, column + j * D : column + (j + 1) * D] for j in range(FF // D)
        ]
        whole_ref[pl.ds(place, rows * len(blocks)), :] = jnp.concatenate(blocks, axis=0)
    made = wide_dot(active_ref[...], whole_ref[...]) + vectors_ref[5:6, :]
    first_norm = unit_ref[...] * vectors_ref[3:4, :] + vectors_ref[4:5, :]
    unit, scale = normal(deep_alpha * first_norm + made.astype(BF).astype(F32))
    valid = valid_ref[...]
    gain = vectors_ref[6:7, :]
    out_ref[...] = ((unit * gain + vectors_ref[7:8, :]) * valid).astype(BF)
    grad = cot_ref[...].astype(F32) * valid
    second = normal_back(grad * gain, unit, scale)
    second_ref[...] = second
    low = second.astype(BF)
    low_ref[...] = low
    sums_ref[0:1, :] = jnp.sum(low.astype(F32), axis=0, keepdims=True)
    sums_ref[1:2, :] = jnp.sum(grad * unit, axis=0, keepdims=True)
    sums_ref[2:3, :] = jnp.sum(grad, axis=0, keepdims=True)


def turn_back(at, slots, active, unit, vectors, valid, cot, parts):
    rows = unit.shape[0]
    return call(
        partial(turn_kernel, slots),
        (active, unit, vectors, valid, cot, *parts),
        (shaped((FF, D), BF), shaped((rows, D), BF), shaped((rows, D), F32), shaped((rows, D), BF), shaped((8, D), F32)),
        10,
        "turn_back",
        scalars=(at,),
    )


def turn_active_kernel(rows, at_ref, active_ref, out_ref, turned_ref):
    for first in range(0, FF, FF // 8):
        cols = slice(first, first + FF // 8)
        turned_ref[cols, :] = jnp.transpose(active_ref[:, cols])
    for slot in range(FF // rows):
        place = pl.multiple_of(at_ref[slot], 16)
        out_ref[slot * rows : (slot + 1) * rows, :] = turned_ref[pl.ds(place, rows), :]


def turn_active(at, rows, active):
    return call(
        partial(turn_active_kernel, rows),
        (active,),
        (shaped((FF, active.shape[0]), BF),),
        8,
        "turn_active",
        scalars=(at,),
        scratch=(pltpu.VMEM((FF, active.shape[0]), BF),),
    )[0]


def down_back_kernel(ranges, rows, active_ref, low_ref, *outs):
    chunk = rows * FF // D
    for (first, last), out_ref in zip(ranges, outs):
        for slot in range(first, last):
            made = wide_dot(active_ref[slot * chunk : (slot + 1) * chunk, :], low_ref[...]).astype(BF)
            to = (slot - first) * rows
            for j in range(FF // D):
                out_ref[to : to + rows, j * D : (j + 1) * D] = made[j * rows : (j + 1) * rows, :]


def down_back(ranges, rows, active, low):
    return call(
        partial(down_back_kernel, ranges, rows),
        (active, low),
        [shaped(((last - first) * rows, FF), BF) for first, last in ranges],
        6,
        "down_back",
    )


def hidden_back_kernel(low_ref, down_ref, slope_ref, grad_ref, bias_ref):
    width = FF // 8
    for block in range(8):
        cols = slice(block * width, (block + 1) * width)
        grad = (nt(low_ref[...], down_ref[cols, :]) * slope_ref[:, cols]).astype(BF)
        grad_ref[:, cols] = grad
        bias_ref[:, cols] = jnp.sum(grad.astype(F32), axis=0, keepdims=True)


def hidden_back(low, down, slope):
    rows = low.shape[0]
    return call(
        hidden_back_kernel,
        (low, down, slope),
        (shaped((rows, FF), BF), shaped((1, FF), F32)),
        6,
        "hidden_back",
    )


def in_back_kernel(slots_ref, grad_ref, mine_ref, other_ref):
    width = FF // 4
    for block in range(4):
        cols = slice(block * width, (block + 1) * width)
        made = tn(slots_ref[...], grad_ref[:, cols]).astype(BF)
        mine_ref[:, cols] = made[: D // 2]
        other_ref[:, cols] = made[D // 2 :]


def in_back(slots, grad):
    rows = slots.shape[0]
    return call(
        in_back_kernel,
        (slots, grad),
        (shaped((D // 2, FF), BF), shaped((D // 2, FF), BF)),
        6,
        "in_back",
    )


def out_back_kernel(
    grad_ref, in_ref, turn_ref, second_ref, unit_ref, scale_ref, vectors_ref, mixed_ref, out_ref,
    first_ref, weight_ref, mixed_grad_ref, sums_ref,
):
    low = nt(grad_ref[...], in_ref[...]).astype(BF)
    grad = deep_alpha * second_ref[...] + nt(low, turn_ref[...]).astype(BF).astype(F32)
    unit = unit_ref[...]
    first = normal_back(grad * vectors_ref[3:4, :], unit, scale_ref[...])
    first_ref[...] = first
    branch = first.astype(BF)
    sums_ref[0:1, :] = jnp.sum(branch.astype(F32), axis=0, keepdims=True)
    sums_ref[1:2, :] = jnp.sum(grad * unit, axis=0, keepdims=True)
    sums_ref[2:3, :] = jnp.sum(grad, axis=0, keepdims=True)
    weight_ref[...] = tn(mixed_ref[...], branch).astype(BF)
    back = nt(branch, out_ref[:, 3 * D : 4 * D]).astype(BF)
    mixed_grad_ref[...] = nt(back, turn_ref[...]).astype(BF)


def out_back(grad, w_in, turn, second, unit, scale, vectors, mixed, w_first):
    rows = unit.shape[0]
    return call(
        out_back_kernel,
        (grad, w_in, turn, second, unit, scale, vectors, mixed, w_first),
        (shaped((rows, D), F32), shaped((D, D), BF), shaped((rows, D), BF), shaped((8, D), F32)),
        6,
        "out_back",
    )


def first_back_kernel(slots_ref, out_ref, small_ref, *refs):
    *grads, mine_ref, other_ref, grad_ref = refs
    at = 0
    for grad in grads:
        grad_ref[at : at + grad.shape[0], :] = grad[...]
        at += grad.shape[0]
    half = D // 2
    for part in range(3):
        cols = slice(part * D, (part + 1) * D)
        made = tn(slots_ref[...], grad_ref[:, cols]).astype(BF)
        mine_ref[:, cols] = made[:half]
        other_ref[:, cols] = made[half:]
    for ref, rows in ((mine_ref, slice(0, half)), (other_ref, slice(half, D))):
        ref[:, 3 * D : 4 * D] = out_ref[rows, :]
        ref[:, 4 * D :] = small_ref[rows, :]


def first_back(slots, weight_out, small, grads):
    rows = slots.shape[0]
    wide = 4 * D + small.shape[1]
    return call(
        first_back_kernel,
        (slots, weight_out, small, *grads),
        (shaped((D // 2, wide), BF), shaped((D // 2, wide), BF), shaped((rows, 3 * D), BF)),
        6,
        "first_back",
    )


def rows_back_kernel(grad_ref, first_ref, turn_ref, branch_ref, gate_ref, out_ref):
    made = nt(grad_ref[...], first_ref[:, : 3 * D])
    high = made.astype(BF)
    rest = made - high.astype(F32)
    middle = rest.astype(BF)
    last = (rest - middle.astype(F32)).astype(BF)
    turned = nt(high, turn_ref[...]) + nt(middle, turn_ref[...]) + nt(last, turn_ref[...])
    out_ref[...] = turned + deep_alpha * branch_ref[...] + gate_ref[...]


def rows_back(grad, w_first, turn, branch, gate):
    rows = grad.shape[0]
    return call(
        rows_back_kernel,
        (grad, w_first, turn, branch, gate),
        (shaped((rows, D), F32),),
        8,
        "rows_back",
    )[0]


def flat_cuts(each):
    cuts = [(0, row, 0, 3 * D) for row in range(each)]
    cuts += [(0, row, 3 * D, 4 * D) for row in range(each)]
    cuts += [(1, row, 0, FF) for row in range(each)]
    cuts += [(2, row, j * D, (j + 1) * D) for j in range(FF // D) for row in range(each)]
    return cuts + [(0, row, 4 * D, 4 * D + LANES) for row in range(each)]


def flat_runs(each, width):
    at = 0
    for which, row, first, last in flat_cuts(each):
        size = min(last - first, width - at)
        if size > 0:
            yield which, row, first, size, at
        at += last - first


def rows_kernel(flat_ref, first_ref, in_ref, down_ref):
    refs = (first_ref, in_ref, down_ref)
    first_ref[:, 4 * D :] = jnp.zeros((first_ref.shape[0], LANES), F32)
    for which, row, first, size, at in flat_runs(first_ref.shape[0], flat_ref.shape[1]):
        refs[which][row : row + 1, first : first + size] = flat_ref[:, at : at + size]


def pieces_kernel(flat_ref, first_ref, in_ref, down_ref, all_ref, *refs):
    rows_kernel(flat_ref, *refs)
    at = 0
    for ref, low in zip(refs, (first_ref, in_ref, down_ref)):
        low[...] = ref[...].astype(BF)
        all_ref[:, at : at + low.shape[1]] = low[...]
        at += low.shape[1]


def row_widths():
    return (4 * D + LANES, FF, FF)


def flat_rows(flat, each):
    return call(rows_kernel, (flat,), [shaped((each, width), F32) for width in row_widths()], 6, "flat_rows")


def pieces(flat, each):
    widths = row_widths()
    return call(
        pieces_kernel,
        (flat,),
        [shaped((each, width), BF) for width in (*widths, sum(widths))],
        6,
        "pieces",
        scratch=[pltpu.VMEM((each, width), F32) for width in widths],
    )


def update_kernel(learning, plan, sections, spans, known, count, *refs):
    size = len(sections)
    sums, refs = refs[:count], refs[count:]
    weights, momenta, averages, refs = refs[:size], refs[size : 2 * size], refs[2 * size : 3 * size], refs[3 * size :]
    outs, refs = refs[known : known + 4], refs[known + 4 :]
    rows, flats, arrived = refs[: 3 * size], refs[3 * size : -1], refs[-1]
    for i in range(size):
        each, wide = weights[i].shape
        grad = sum(
            sums[which][row : row + each, column : column + wide].astype(F32) for which, row, column in plan[i]
        )
        weight = weights[i][...]
        decayed = grad + decay_rate * weight
        momentum = momentum_rate * momenta[i][...] + decayed
        weight = weight - learning * (decayed + momentum_rate * momentum)
        rows[i][...] = momentum
        rows[size + i][...] = average_rate * averages[i][...] + (1.0 - average_rate) * weight
        rows[2 * size + i][...] = weight
    each = weights[0].shape[0]
    copies = []
    for out, which in zip(range(4), (0, 1, 2, 2)):
        for span, (first, last) in enumerate(spans):
            flat = flats[out * len(spans) + span]
            for section, row, column, width, at in flat_runs(each, outs[out].shape[1]):
                if section in sections and first <= at < last:
                    value = rows[which * size + sections.index(section)][row : row + 1, column : column + width]
                    flat[:, at - first : at - first + width] = value.astype(flat.dtype)
            copies.append(
                pltpu.make_async_copy(
                    flat, outs[out].at[:, pl.ds(first, last - first)], arrived.at[out * len(spans) + span]
                )
            )
            copies[-1].start()
    for copy in copies:
        copy.wait()


def update(learning, sections, sums, weights, momenta, averages, width, known=()):
    arrays, plan = [], []
    for section in sections:
        found = []
        for array, row, column in sums[section]:
            at = next((i for i, other in enumerate(arrays) if other is array), None)
            if at is None:
                at = len(arrays)
                arrays.append(array)
            found.append((at, row, column))
        plan.append(found)
    each = weights[0].shape[0]
    runs = [(at, at + size) for section, _, _, size, at in flat_runs(each, width) if section in sections]
    spans = []
    for first, last in runs:
        if spans and spans[-1][1] == first:
            spans[-1] = (spans[-1][0], last)
        else:
            spans.append((first, last))
    rows = [[part[section] for section in sections] for part in (weights, momenta, averages)]
    dtypes = (F32, F32, F32, BF)
    operands = [*arrays, *rows[0], *rows[1], *rows[2]]
    anywhere = pl.BlockSpec(memory_space=pl.ANY)
    return pl.pallas_call(
        partial(update_kernel, learning, plan, list(sections), spans, len(known), len(arrays)),
        out_shape=tuple(shaped((1, width), dtype) for dtype in dtypes),
        in_specs=vmem(len(operands)) + [anywhere] * len(known),
        out_specs=(anywhere,) * 4,
        input_output_aliases={len(operands) + i: i for i in range(len(known))},
        scratch_shapes=[pltpu.VMEM(part.shape, F32) for part in rows[0]] * 3
        + [pltpu.VMEM((1, last - first), dtype) for dtype in dtypes for first, last in spans]
        + [pltpu.SemaphoreType.DMA((4 * len(spans),))],
        compiler_params=limits(10),
        cost_estimate=pl.CostEstimate(flops=1, bytes_accessed=1, transcendentals=0),
        name="update",
    )(*operands, *known)


def body(acts, cotangent, mask, shape_id, weights, momenta, averages):
    shards = lax.axis_size(("dp", "fsdp"))
    count = lax.axis_size("dp")
    dp, core = lax.axis_index("dp"), lax.axis_index("fsdp")
    clips, slots = acts.shape[0], acts.shape[1]
    rows = clips * slots
    total_tokens = rows * shards
    piece_rows = D // shards
    wide_rows = FF // shards
    vector_width = 12 * D // shards
    position_width = (NPOS + shards - 1) // shards
    small_width = vector_width + position_width

    piece_first, piece_in, piece_down, piece_all = pieces(weights, piece_rows)

    order = slot_order(dp, core, count)
    row_order = (order[:, None] * piece_rows + jnp.arange(piece_rows, dtype=jnp.int32)).reshape(-1)
    turn = (jnp.arange(D, dtype=jnp.int32)[:, None] == row_order[None, :]).astype(BF)
    piece_turn = (jnp.arange(shards, dtype=jnp.int32)[:, None] == order[None, :]).astype(BF)

    back_order = jnp.dot(piece_turn.astype(F32), jnp.arange(shards, dtype=F32)).astype(jnp.int32)

    together = lax.optimization_barrier
    bits = high_bits(count)
    staged = len(bits) == 2
    n = piece_rows
    rest = D // 8 - n
    widths = (piece_first.shape[1], FF, FF)
    lefts = (0, widths[0], widths[0] + FF)
    cuts = (13 * LANES, FF // 2, FF // 2)
    wide_all, cut_all = sum(widths), 37 * LANES
    third = (13 * LANES, 12 * LANES, 12 * LANES), (12 * LANES,) * 3
    at = order * wide_rows
    inputs_low = acts.reshape(rows, D)

    def gather_high(piece, direct=False):
        if staged:
            if direct:
                return [exchange(piece, "dp", d << 2) for d in (1, 2, 3)]
            two = exchange(piece, "dp", 8)
            return [exchange(piece, "dp", 4), two, exchange(two, "dp", 4)]
        column = piece
        for bit in bits:
            column = jnp.concatenate([column, exchange(column, "dp", 1 << bit)], axis=0)
        return [column[n:]]

    def thirds(side, views):
        left = widths[0]
        items, column = [], 0
        for i, size in enumerate(third[side]):
            items += views(i * n, left, column, size)
            column += size
        return items

    own_sides = exchange_sides((piece_all, piece_all))
    high_first = gather_high(piece_first)
    own_sides, high_first, piece_in, mask, turn, at = together(
        (own_sides, high_first, piece_in, mask, turn, at)
    )

    items = stack([whole_of(part) for part in high_first])[1]
    sends = build(
        ((rest, widths[0]), items),
        (
            (rest, widths[0] + third[1][0]),
            items + thirds(1, lambda row, left, c, w: [(row, left, n, w, [(own_sides[1], 0, cut_all + c)])]),
        ),
        (
            (rest, widths[0] + third[0][0]),
            items + thirds(0, lambda row, left, c, w: [(row, left, n, w, [(own_sides[0], 0, c)])]),
        ),
    )
    rest_first, sends = sends[0], sends[1:]
    sides_first = exchange_sides(sends)
    high_in = gather_high(piece_in, True)
    bucket, rank, valid_rows = prep(mask, shape_id, slots)
    sides_first, high_in, piece_down, bucket, rank, valid_rows = together(
        (sides_first, high_in, piece_down, bucket, rank, valid_rows)
    )

    def corner_sends(unit, sides):
        wide, half = widths[unit], cuts[unit]
        return (
            ((rest, wide - half), [(0, 0, rest, wide - half, [(sides[1], 0, half)])]),
            ((rest, half), [(0, 0, rest, half, [(sides[0], 0, 0)])]),
        )

    def corner_items(unit, corner):
        wide, half = widths[unit], cuts[unit]
        (second, left_second), (first, left_first) = corner
        return [
            (0, 0, rest, half, [(first, 0, left_first)]),
            (0, half, rest, wide - half, [(second, 0, left_second)]),
        ]

    def early_rows(unit, piece, high, sides):
        wide = widths[unit]
        return stack([whole_of(piece), whole_of(high)] + [(side, 0, rest, 0, wide) for side in sides])

    def shifted(items, row):
        return [(row + item[0], *item[1:]) for item in items]

    def slots_of(unit, piece, high, sides, corner, early, late):
        wide, left = widths[unit], lefts[unit]
        own_mine, own_other = own
        items = [(0, 0, n, wide, [(piece, 0, 0)]), (n, 0, rest, wide, [(high, 0, 0)])]
        eighth = D // 8
        for i in range(3):
            items.append(((i + 1) * eighth, 0, n, wide, [(own_mine, i * n, left)]))
        for i, side in enumerate(sides):
            items.append(((i + 1) * eighth + n, 0, rest, wide, [(side, 0, 0)]))
        items += shifted(corner_items(unit, corner), 3 * eighth + n)
        base = D // 2
        if not isinstance(early, tuple):
            early = (early, 0), (early, n + rest)
        (one, row_one), (two, row_two) = early
        items.append((base, 0, n, wide, [(one, row_one, 0)]))
        items.append((base + n, 0, rest, wide, [(one, row_one + n, 0)]))
        for i in range(3):
            items.append((base + (i + 1) * eighth, 0, n, wide, [(own_other, i * n, left)]))
            view = late if i == 2 else (two, row_two + i * rest, 0)
            items.append((base + (i + 1) * eighth + n, 0, rest, wide, [view]))
        return items

    def own_corner(row, half, side, column):
        return [(row, column + c, n, w, [(side, i * n, widths[0])]) for i, (c, w) in enumerate(half)]

    def spans(side):
        edges = np.cumsum((0, *third[side]))
        return [(int(a), int(b - a)) for a, b in zip(edges[:-1], edges[1:])]

    items = [(0, 0, n, wide_all, [(own_sides[0], 0, 0)]), (n, 0, n, wide_all, [(own_sides[1], 0, 0)])]
    items += own_corner(2 * n, spans(0), sides_first[1], 0) + own_corner(2 * n, spans(1), sides_first[0], cut_all)
    def side_sends(unit, high, sides):
        wide, half = widths[unit - 1], cuts[unit - 1]
        items = stack([whole_of(part) for part in high])[1]
        sends = []
        for width, view in ((wide - half, (sides[1], 0, half)), (half, (sides[0], 0, 0))):
            sends.append(((rest, widths[unit] + width), items + [(0, widths[unit], rest, width, [view])]))
        return [((rest, widths[unit]), items)] + sends

    own_mine, early, rest_in, *sends = build(
        ((3 * n, wide_all), items),
        early_rows(0, piece_first, rest_first, sides_first),
        *side_sends(1, high_in, sides_first),
    )
    sides_in = exchange_sides(sends)
    early_first = exchange_core(early)
    high_down = gather_high(piece_down)
    sides_in, early_first, high_down, own_mine = together((sides_in, early_first, high_down, own_mine))

    corner_first = [(part, FF) for part in sides_in]
    items = stack([whole_of(own_mine)])[1]
    items += [(row, wide_all + column, *more) for row, column, *more in corner_items(0, corner_first)]
    late, rest_down, *sends = build(
        ((rest, wide_all + widths[0]), items), *side_sends(2, high_down, sides_in)
    )
    sides_down = exchange_sides(sends)
    late = exchange_core(late)
    own = (own_mine, late)
    items = slots_of(0, piece_first, rest_first, sides_first, corner_first, early_first, (late, 0, wide_all))
    w_first = build(((D, widths[0]), items))[0]
    early, first_down = build(
        early_rows(1, piece_in, rest_in, sides_in), stack([whole_of(piece_down), whole_of(rest_down)])
    )
    early_in, first_down = exchange_core(early), exchange_core(first_down)
    vectors, bias_in, table = unpack(shards, turn, w_first)
    inputs_slots, joined, gate = joined_forward(inputs_low, turn, vectors, table, w_first)
    made = [attention(clip, bucket, valid_rows, table, joined, gate) for clip in range(clips)]
    mixed_slots, unit, unit_scale = out_forward(inputs_low, turn, vectors, w_first, [m[2] for m in made])
    sides_down, early_in, first_down, unit = together((sides_down, early_in, first_down, unit))

    corner_in = [(part, FF) for part in sides_down]
    late, early, *sends = build(
        ((rest, FF), corner_items(1, corner_in)),
        stack([(side, 0, rest, 0, FF) for side in sides_down]),
        *corner_sends(2, sides_down),
    )
    corner_down = exchange_sides(sends)
    late = exchange_core(late)
    early_down = exchange_core(early)
    items = slots_of(1, piece_in, rest_in, sides_in, corner_in, early_in, (late, 0, 0))
    w_in = build(((D, FF), items))[0]
    first_slots, active, slope = hidden_forward(unit, vectors, turn, bias_in, w_in)
    corner_down, early_down, active = together((corner_down, early_down, active))

    corner_down = [(part, 0) for part in corner_down]
    corner = build(((rest, FF), corner_items(2, corner_down)))[0]
    late = exchange_core(corner)
    early_down = (first_down, 0), (early_down, 0)
    items = slots_of(2, piece_down, rest_down, sides_down, [(corner, cuts[2]), (corner, 0)], early_down, (late, 0, 0))
    arrays, places = [], [None] * shards
    for row, column, size, _, [(array, first, left)] in items:
        if column:
            continue
        which = next((i for i, known in enumerate(arrays) if known is array), len(arrays))
        if which == len(arrays):
            arrays.append(array)
        for step in range(size // n):
            places[row // n + step] = (which, first + step * n, n, left)
    to = at
    if wide_rows % 16 == 0:
        turned = turn_active(at, wide_rows, active)
        turned, arrays[0] = together((turned, arrays[0]))
    else:
        parts = [arrays[which][row : row + n, left : left + FF] for which, row, _, left in places]
        stacked = jnp.stack(parts).reshape(shards, n, FF // D, D).transpose(0, 2, 1, 3).reshape(shards, wide_rows, D)
        arrays, places = [jnp.take(stacked, back_order, axis=0).reshape(FF, D)], [(0, 0, FF, 0)]
        to = jnp.zeros((1,), jnp.int32)
    w_down, activations, grad_second, grad_made, sums_second = turn_back(
        to, places, active, unit, vectors, valid_rows, cotangent.reshape(rows, D), arrays
    )

    if wide_rows % 16:
        grad_down = tn(active, grad_made).astype(BF).reshape(shards, wide_rows, D)
        grad_down = jnp.take(grad_down, order, axis=0).reshape(shards, FF // D, n, D).transpose(0, 2, 1, 3)
        grad_down = grad_down.reshape(D, FF)
        at_last = D // 2 - rest
        down_main, down_last, other_main, other_last = (
            grad_down[:at_last], grad_down[at_last : D // 2], grad_down[D // 2 : D // 2 + at_last], grad_down[D // 2 + at_last :]
        )
    else:
        half_slots, last_slots = shards // 2, rest // n
        down_last, other_last = down_back(
            ((half_slots - last_slots, half_slots), (shards - last_slots, shards)), n, turned, grad_made
        )
        down_last, other_last, grad_made = together((down_last, other_last, grad_made))
        other_main = down_back(((half_slots, shards - last_slots),), n, turned, grad_made)[0]
        down_main = None

    eighth = D // 8

    def both(pair, row, column):
        views = []
        for array in pair:
            if isinstance(array, tuple):
                main, last = array
                at = D // 2 - rest
                views.append((last, row - at, column) if row >= at else (main, row, column))
            else:
                views.append((array, row, column))
        return views

    def corner_out(unit, pair):
        wide, half = widths[unit], cuts[unit]
        row = 3 * eighth + n
        return (
            (wide - half, [(0, 0, rest, wide - half, both(pair, row, half))]),
            (half, [(0, 0, rest, half, both(pair, row, 0))]),
        )

    def sides_out(unit, pair, corner):
        wide, half = widths[unit], cuts[unit]
        (second, left_second), (first, left_first) = corner
        near, side = eighth + n, 2 * eighth + n
        return (
            (
                wide,
                [
                    (0, 0, rest, half, both(pair, near, 0) + [(first, 0, left_first)]),
                    (0, half, rest, wide - half, both(pair, near, half)),
                ],
            ),
            (
                wide,
                [
                    (0, 0, rest, half, both(pair, side, 0)),
                    (0, half, rest, wide - half, both(pair, side, half) + [(second, 0, left_second)]),
                ],
            ),
        )

    def beside(one, two):
        return [
            ((rest, a[0] + b[0]), a[1] + [(item[0], a[0] + item[1], *item[2:]) for item in b[1]])
            for a, b in zip(one, two)
        ]

    def alone(one):
        return [((rest, wide), items) for wide, items in one]

    def column_views(unit, pair, sides, row):
        return both(pair, row, 0) + [(side, row - n, 0) for side in sides]

    def high_out(unit, pair, sides, first, count, *more):
        wide = widths[unit]
        views = column_views(unit, pair, sides, first * n)
        if more:
            views = views + [(more[0], n, 0)]
        return ((count * n, wide), [(0, 0, count * n, wide, views)])

    def scatter_high(unit, pair, sides):
        wide = widths[unit]
        total = build(((rest, wide), [(0, 0, rest, wide, column_views(unit, pair, sides, n))]))[0].astype(F32)
        total = jnp.concatenate([jnp.zeros((n, widths[unit]), F32), total], axis=0)
        for bit in reversed(bits):
            size = total.shape[0] // 2
            total = total[:size] + exchange(total[size:].astype(BF), "dp", 1 << bit).astype(F32)
        return [total]

    def scatter_far(unit, pair, sides):
        if not staged:
            return scatter_high(unit, pair, sides)
        return [exchange(build(high_out(unit, pair, sides, 2, 2))[0], "dp", 8)]

    other_last = exchange_core(other_last)
    grad_hidden, grad_bias_in = hidden_back(grad_made, w_down, slope)
    in_mine, in_other = in_back(first_slots, grad_hidden)
    down_last, other_last, other_main, in_mine, in_other, grad_hidden, grad_made = together(
        (down_last, other_last, other_main, in_mine, in_other, grad_hidden, grad_made)
    )

    corner_down = exchange_sides(build(*alone(corner_out(2, ((None, down_last), (None, other_last))))))
    inner = (in_mine, exchange_core(in_other))
    other_main = exchange_core(other_main)
    if down_main is None:
        down_main = down_back(((0, half_slots - last_slots),), n, turned, grad_made)[0]
    grad_first_sum, grad_out, grad_mixed, sums_first = out_back(
        grad_hidden, w_in, turn, grad_second, unit, unit_scale, vectors, mixed_slots, w_first
    )

    def clip_back(clip):
        prob, rel, _ = made[clip]
        return attention_back(clip, joined, gate, rank, prob, rel, grad_mixed)

    corner_down, inner, other_main, down_main, grad_mixed = together(
        (corner_down, inner, other_main, down_main, grad_mixed)
    )
    down = ((down_main, down_last), (other_main, other_last))

    corner_down = [(part, 0) for part in corner_down]
    sides_down = exchange_sides(build(*beside(sides_out(2, down, corner_down), corner_out(1, inner))))
    backs = [clip_back(clip) for clip in range(clips)]
    grads_joined = [back[0] for back in backs]
    grad_gate_inputs, table_grad, sums_attention = gate_back(
        inputs_low, table, gate, grads_joined, [back[1] for back in backs], [back[2] for back in backs]
    )
    grad_small = pack(shards, turn, sums_attention, sums_first, sums_second, grad_bias_in, table_grad)
    first_mine, first_other, grad_joined = first_back(inputs_slots, grad_out, grad_small, grads_joined)
    sides_down, first_mine, first_other, grad_joined = together((sides_down, first_mine, first_other, grad_joined))

    corner_in = [(part, FF) for part in sides_down]
    first = (first_mine, exchange_core(first_other))
    sides_in = exchange_sides(build(*alone(sides_out(1, inner, corner_in))))
    high_down = scatter_far(2, down, sides_down)
    corner_first = exchange_sides(build(*alone(corner_out(0, first))))
    input_grad = rows_back(grad_joined, w_first, turn, grad_first_sum, grad_gate_inputs)
    first, sides_in, high_down, corner_first, input_grad = together(
        (first, sides_in, high_down, corner_first, input_grad)
    )

    corner_first = [(part, 0) for part in corner_first]
    units = ((first, 0), (inner, 1), (down, 2))

    def own_views(row, column, columns):
        found = []
        for pair, unit in units:
            start, end = max(column, lefts[unit]), min(column + columns, lefts[unit] + widths[unit])
            if start < end:
                found.append((start - column, end - start, both(pair, row, start - lefts[unit])))
        return found

    def own_third(side):
        base = cut_all if side else 0
        items = []
        for i, (column, columns) in enumerate(spans(side)):
            for start, size, views in own_views(3 * eighth, base + column, columns):
                items.append((i * n, start, n, size, views))
        return (third[side][0], items)

    sides_first = exchange_sides(
        build(*beside(sides_out(0, first, corner_first), (own_third(1), own_third(0))))
    )
    high_in = scatter_far(1, inner, sides_in)
    if staged:
        high_down += [exchange(build(high_out(2, down, sides_down, 1, 1, high_down[0]))[0], "dp", 4)]
    weight_rows, momenta_rows, averages_rows = [flat_rows(part, n) for part in (weights, momenta, averages)]
    sides_first, high_in, high_down, weight_rows, momenta_rows, averages_rows = together(
        (sides_first, high_in, high_down, weight_rows, momenta_rows, averages_rows)
    )

    own_outs = []
    for side, row in ((0, eighth), (1, 2 * eighth)):
        items = []
        base = 0 if side == 0 else cut_all
        came = sides_first[1] if side == 0 else sides_first[0]
        edges = [(base + c, w, (came, i * n, widths[0])) for i, (c, w) in enumerate(spans(side))]
        edges.append((cut_all, wide_all - cut_all, None) if side == 0 else (0, cut_all, None))
        for column, columns, view in edges:
            for start, size, views in own_views(row, column, columns):
                if view is not None:
                    views = views + [(view[0], view[1], view[2] + start)]
                items.append((0, column + start, n, size, views))
        own_outs.append(((n, wide_all), items))
    own_sides = exchange_sides(build(*own_outs))
    if staged:
        near, far, farthest = [high_out(0, first, sides_first, d, 1) for d in (1, 2, 3)]
        near_in = high_out(1, inner, sides_in, 1, 1, high_in[0])
        wide = widths[0]
        near = ((n, wide + FF), near[1] + [(0, wide, n, FF, near_in[1][0][4])])
        high_first = [exchange(part, "dp", mask) for part, mask in zip(build(near, far, farthest), (4, 8, 12))]
        high_in += [high_first[0]]
    else:
        high_first = scatter_high(0, first, sides_first)
    comes = (
        [(part, 0) for part in high_first],
        [(part, widths[0] if i else 0) for i, part in enumerate(high_in)],
        [(part, 0) for part in high_down],
    )
    sums = []
    for pair, unit in units:
        views = both(pair, 0, 0) + [(side, 0, lefts[unit]) for side in own_sides]
        sums.append(views + [(part, 0, left) for part, left in comes[unit]])

    learning = rate_scale / math.sqrt(total_tokens)
    arguments = (weight_rows, momenta_rows, averages_rows, weights.shape[1])
    known = update(learning, (2,), sums, *arguments)
    if staged:
        known, high_first[0] = together((known, high_first[0]))
        sums[1][-1] = (high_first[0], 0, widths[0])
    known = update(learning, (1,), sums, *arguments, known)
    if staged:
        known, high_first = together((known, high_first))
        sums[0][-3:] = [(part, 0, 0) for part in high_first]
    momenta_new, averages_new, weights_new, weights_copy = update(learning, (0,), sums, *arguments, known)
    return (
        activations.reshape(acts.shape),
        input_grad.reshape(acts.shape),
        momenta_new,
        averages_new,
        weights_new,
        weights_copy,
    )


def solution(mesh):
    split = ("dp", "fsdp")
    in_specs = (
        P(split, None, None),
        P(split, None, None),
        P(split, None),
        P(split),
        P(split, None),
        P(split, None),
        P(split, None),
    )
    out_specs = (
        P(split, None, None),
        P(split, None, None),
        P(split, None),
        P(split, None),
        P(split, None),
        P(split, None),
    )
    return jax.shard_map(body, mesh=mesh, in_specs=in_specs, out_specs=out_specs, check_vma=False)
```

```python
from functools import partial
import math

import jax
import jax.numpy as jnp
import numpy as np
from jax import lax
from jax.experimental import pallas as pl
from jax.experimental.pallas import tpu as pltpu
from jax.sharding import PartitionSpec as P

D = 768
H = 12
HD = 64
FF = 3072
NB = 320
HALF = NB // 2
P_SIZE = 512
NPOS = 4372
LANES = 128
KEYS = 384
BF = jnp.bfloat16
F32 = jnp.float32

deep_alpha = 24.0**0.25
layer_epsilon = 1e-05
masked_score = -1000000000.0
far_distance = 800
gate_units = 8
momentum_rate = 0.9
average_rate = 0.8
decay_rate = 0.0001
rate_scale = 0.04
far_place = 1 << 20


def bucket_levels(span):
    distance = np.arange(0, span + 1)
    exact = HALF // 2
    logscale = (
        np.log(np.maximum(distance, 1) / exact) / np.log(far_distance / exact) * (HALF - exact)
    )
    beyond = np.minimum(exact + np.floor(logscale).astype(np.int64), HALF - 1)
    return np.where(distance < exact, distance, beyond)


def far_marks():
    levels = bucket_levels(2 * P_SIZE)
    rises = np.diff(levels)
    marks = np.repeat(np.arange(1, 2 * P_SIZE + 1), rises)
    return [int(m) for m in marks[HALF // 2 :]]


def key_ends():
    span = 2 * P_SIZE
    levels = bucket_levels(span)
    offsets = np.arange(-span, span + 1)
    level = levels[np.abs(offsets)]
    keys = np.where(offsets > 0, HALF + level, HALF - 1 - level)
    ends = np.full((KEYS,), far_place // 2, np.int32)
    for key in range(NB - 1):
        below = offsets[keys <= key]
        ends[key] = below.max() if below.size else -(far_place // 2)
    return ends


def exchange(value, axis, mask):
    count = lax.axis_size(axis)
    return lax.ppermute(value, axis, [(i, i ^ mask) for i in range(count)])


def high_bits(count):
    return list(range(2, count.bit_length() - 1))


def exchange_sides(pair):
    return exchange(pair[0], "dp", 1), exchange(pair[1], "dp", 2)


def exchange_core(value):
    return exchange(value, "fsdp", 1)


def slot_order(dp, core, count):
    high = count // 4
    core_step, low, up = np.meshgrid(np.arange(2), np.arange(4), np.arange(high), indexing="ij")
    distance = jnp.asarray((up * 4 + low).reshape(-1).astype(np.int32))
    core_distance = jnp.asarray(core_step.reshape(-1).astype(np.int32))
    return (distance ^ dp) * 2 + (core_distance ^ core)


def prep_kernel(marks, shape_ref, mask_ref, ends_ref, bucket_ref, rank_ref, valid_ref):
    clips, patches = mask_ref.shape
    slots = bucket_ref.shape[1]
    mask = mask_ref[...]
    up = lax.broadcasted_iota(jnp.int32, (patches, patches), 0)
    across = lax.broadcasted_iota(jnp.int32, (patches, patches), 1)
    running = wide_dot(mask.astype(F32).astype(BF), (up <= across).astype(F32).astype(BF))
    ranks = jnp.where(mask == 1, running.astype(jnp.int32) - 1, -1)
    slot = lax.broadcasted_iota(jnp.int32, (slots, patches), 0)
    patch = lax.broadcasted_iota(jnp.int32, (slots, patches), 1)
    pair = lax.broadcasted_iota(jnp.int32, (8, patches), 1)
    halves = jnp.where(lax.broadcasted_iota(jnp.int32, (8, patches), 0) == 0, pair >> 4, pair & 15)
    halves = halves.astype(F32).astype(BF)
    for clip in range(clips):
        found = ranks[clip : clip + 1, :] == slot
        column = jnp.sum(jnp.where(found, patch, 0), axis=1, keepdims=True)
        both = nt(halves, found.astype(F32).astype(BF)).astype(jnp.int32)
        row = 16 * both[0:1, :] + both[1:2, :]
        narrow = shape_ref[clip] > 0
        column = jnp.where(narrow, 8 * (column >> 2) + (column & 3), column)
        row = jnp.where(narrow, 8 * (row >> 2) + (row & 3), row)
        count = jnp.sum(mask[clip : clip + 1, :], axis=1, keepdims=True)
        valid = lax.broadcasted_iota(jnp.int32, (slots, 1), 0) < count
        valid_ref[clip * slots : (clip + 1) * slots, :] = valid.astype(F32)
        offset = column - row
        distance = jnp.abs(offset)
        level = jnp.minimum(distance, HALF // 2)
        for mark in marks:
            level = level + (distance >= mark).astype(jnp.int32)
        bucket_ref[clip] = level + jnp.where(offset > 0, HALF, 0)
        away = jnp.where(valid, offset, far_place)
        for first in range(slots):
            seen = away[:, first : first + 1] <= ends_ref[...]
            rank_ref[clip, first : first + 1, :] = jnp.sum(seen.astype(jnp.int32), axis=0, keepdims=True)


def prep(mask, shape_id, slots):
    clips = mask.shape[0]
    ends = jnp.asarray(key_ends())[None, :]
    return call(
        partial(prep_kernel, far_marks()),
        (mask, ends),
        (
            shaped((clips, slots, slots), jnp.int32),
            shaped((clips, slots, KEYS), jnp.int32),
            shaped((clips * slots, 1), F32),
        ),
        8,
        "prep",
        scalars=(shape_id,),
    )


def position_rows(shards, by_key):
    width = (NPOS + shards - 1) // shards
    index = np.full((24, KEYS), -1, np.int64)
    for head in range(H):
        for lane in range(NB):
            bucket = (HALF - 1 - lane if lane < HALF else lane) if by_key else lane
            index[head, lane] = bucket * H + head
    for unit in range(gate_units):
        index[12 + unit, :HD] = NB * H + np.arange(HD) * gate_units + unit
    index[20, :gate_units] = (NB + 0) * H + HD * gate_units + np.arange(gate_units)
    index[21, :H] = NB * H + (HD + 1) * gate_units + np.arange(H)
    pieces = np.where(index >= 0, index // width, -1).astype(np.int32)
    columns = np.where(index >= 0, 12 * D // shards + index % width, -1).astype(np.int32)
    return jnp.asarray(pieces), jnp.asarray(columns)


def vector_chunks(shards):
    width = 12 * D // shards
    size = math.gcd(width, D)
    each, across = width // size, D // size
    return size, [
        (g // each, g % each * size, g // across, g % across * size) for g in range(12 * across)
    ]


def unpack_kernel(shards, turn_ref, pieces_ref, columns_ref, *refs):
    whole_ref, vectors_ref, bias_ref, table_ref, natural_ref, small_ref = refs
    natural_ref[...] = wide_dot(turn_ref[...], whole_ref[:, 4 * D :])
    each = D // shards
    wide = small_ref.shape[1]
    for k in range(wide // LANES):
        small_ref[:, k * LANES : (k + 1) * LANES] = natural_ref[pl.ds(k, shards, stride=each), :]
    size, chunks = vector_chunks(shards)
    for piece, column, row, place in chunks:
        value = small_ref[piece : piece + 1, column : column + size]
        if row < 8:
            vectors_ref[row : row + 1, place : place + size] = value
        else:
            bias_ref[:, (row - 8) * D + place : (row - 8) * D + place + size] = value
    start = 12 * D // shards // LANES * LANES
    small = small_ref[:, start:].astype(BF)
    piece_ids = lax.broadcasted_iota(jnp.int32, (shards, KEYS), 0)
    column_ids = lax.broadcasted_iota(jnp.int32, (wide - start, KEYS), 0) + start
    for row in range(22):
        chosen = (piece_ids == pieces_ref[row : row + 1, :]).astype(F32).astype(BF)
        spread = tn(small, chosen)
        table_ref[row : row + 1, :] = jnp.sum(
            jnp.where(column_ids == columns_ref[row : row + 1, :], spread, 0.0), axis=0, keepdims=True
        )
    table_ref[22:24, :] = jnp.zeros((2, KEYS), F32)


def small_lanes(shards):
    return -(-(12 * D // shards + (NPOS + shards - 1) // shards) // LANES) * LANES


def unpack(shards, turn, whole):
    pieces, columns = position_rows(shards, False)
    return call(
        partial(unpack_kernel, shards),
        (turn, pieces, columns, whole),
        (shaped((8, D), F32), shaped((1, FF), F32), shaped((24, KEYS), F32)),
        8,
        "unpack",
        scratch=(
            pltpu.VMEM((D, LANES), F32),
            pltpu.VMEM((shards, small_lanes(shards)), F32),
        ),
    )


def pack_kernel(shards, turn_ref, pieces_ref, columns_ref, attention_ref, first_ref, second_ref, bias_ref, table_ref, out_ref, natural_ref, small_ref):
    each = D // shards
    wide = small_ref.shape[1]
    table = table_ref[...]
    lane = lax.broadcasted_iota(jnp.int32, table.shape, 1)
    row_id = lax.broadcasted_iota(jnp.int32, table.shape, 0)
    before = jnp.where((lane > 0) & (row_id < H), pltpu.roll(table, 1, 1), 0.0)
    table = table - before
    piece_ids = lax.broadcasted_iota(jnp.int32, (shards, KEYS), 0)
    start = 12 * D // shards // LANES * LANES
    column_ids = lax.broadcasted_iota(jnp.int32, (wide - start, KEYS), 0) + start
    total = jnp.zeros((shards, wide - start), F32)
    for row in range(22):
        chosen = jnp.where(piece_ids == pieces_ref[row : row + 1, :], table[row : row + 1, :], 0.0).astype(BF)
        spread = (column_ids == columns_ref[row : row + 1, :]).astype(F32).astype(BF)
        total = total + nt(chosen, spread)
    small_ref[...] = jnp.zeros(small_ref.shape, F32)
    small_ref[:, start:] = total
    rows = [(attention_ref, 0), (attention_ref, 1)]
    rows += [(first_ref, i) for i in range(3)] + [(second_ref, i) for i in range(3)]
    size, chunks = vector_chunks(shards)
    for piece, column, row, place in chunks:
        if row < 8:
            ref, at = rows[row]
            value = ref[at : at + 1, place : place + size]
        else:
            value = bias_ref[:, (row - 8) * D + place : (row - 8) * D + place + size]
        small_ref[piece : piece + 1, column : column + size] = value
    natural_ref[...] = jnp.zeros(natural_ref.shape, F32)
    for k in range(wide // LANES):
        natural_ref[pl.ds(k, shards, stride=each), :] = small_ref[:, k * LANES : (k + 1) * LANES]
    out_ref[...] = tn(turn_ref[...], natural_ref[...].astype(BF)).astype(BF)


def pack(shards, turn, sums_attention, sums_first, sums_second, bias, table):
    pieces, columns = position_rows(shards, True)
    return call(
        partial(pack_kernel, shards),
        (turn, pieces, columns, sums_attention, sums_first, sums_second, bias, table),
        (shaped((D, LANES), BF),),
        8,
        "pack",
        scratch=(pltpu.VMEM((D, LANES), F32), pltpu.VMEM((shards, small_lanes(shards)), F32)),
    )[0]


def lookup(table_ref, head, index, block):
    out = None
    for part in range(KEYS // LANES):
        row = jnp.broadcast_to(table_ref[head : head + 1, part * LANES : (part + 1) * LANES], index.shape)
        found = jnp.take_along_axis(row, index, axis=1, mode="promise_in_bounds")
        out = found if out is None else jnp.where(block == part, found, out)
    return out


def nt(a, b):
    return lax.dot_general(a, b, (((1,), (1,)), ((), ())), preferred_element_type=F32)


def tn(a, b):
    return lax.dot_general(a, b, (((0,), (0,)), ((), ())), preferred_element_type=F32)


def vmem(count):
    return [pl.BlockSpec(memory_space=pltpu.VMEM)] * count


def limits(mib):
    return pltpu.CompilerParams(vmem_limit_bytes=mib * 1024 * 1024)


def shaped(shape, dtype):
    return jax.ShapeDtypeStruct(tuple(shape), dtype)


def call(kernel, operands, outs, mib, name, scalars=(), scratch=()):
    return pl.pallas_call(
        kernel,
        out_shape=tuple(outs),
        in_specs=[pl.BlockSpec(memory_space=pltpu.SMEM)] * len(scalars) + vmem(len(operands)),
        out_specs=tuple(vmem(len(outs))),
        scratch_shapes=list(scratch),
        compiler_params=limits(mib),
        cost_estimate=pl.CostEstimate(flops=1, bytes_accessed=1, transcendentals=0),
        name=name,
    )(*scalars, *operands)


def build_kernel(plans, count, *refs):
    sources, outs = refs[:count], refs[count:]
    for out, (whole, items) in zip(outs, plans):
        if not whole:
            out[...] = jnp.zeros(out.shape, out.dtype)
        for row, column, rows, columns, views in items:
            values = [
                sources[which][first : first + rows, left : left + columns] for which, first, left in views
            ]
            if len(values) > 1:
                values = [sum(value.astype(F32) for value in values)]
            out[row : row + rows, column : column + columns] = values[0].astype(out.dtype)


def build(*outs):
    sources, plans = [], []
    for shape, items in outs:
        plan = []
        for row, column, rows, columns, views in items:
            found = []
            for array, first, left in views:
                at = next((i for i, source in enumerate(sources) if source is array), None)
                if at is None:
                    at = len(sources)
                    sources.append(array)
                found.append((at, first, left))
            plan.append((row, column, rows, columns, found))
        plans.append((sum(item[2] * item[3] for item in items) == math.prod(shape), plan))
    return call(
        partial(build_kernel, plans, len(sources)), sources, [shaped(shape, BF) for shape, _ in outs], 8, "build"
    )


def stack(parts):
    items, at = [], 0
    for array, row, rows, column, columns in parts:
        items.append((at, 0, rows, columns, [(array, row, column)]))
        at += rows
    return (at, parts[0][4]), items


def whole_of(array):
    return (array, 0, array.shape[0], 0, array.shape[1])


def normal(entries):
    centre = entries - jnp.mean(entries, axis=-1, keepdims=True)
    scale = lax.rsqrt(jnp.mean(centre * centre, axis=-1, keepdims=True) + layer_epsilon)
    return centre * scale, scale


def normal_back(grad, unit, scale):
    return scale * (
        grad
        - jnp.mean(grad, axis=-1, keepdims=True)
        - unit * jnp.mean(grad * unit, axis=-1, keepdims=True)
    )


def wide_dot(a, b):
    return jnp.dot(a, b, preferred_element_type=F32)


def split(value, count):
    parts = []
    for _ in range(count):
        parts.append(value.astype(BF))
        value = value - parts[-1].astype(F32)
    return parts


def joined_kernel(
    x_ref, turn_ref, vectors_ref, table_ref, whole_ref, slots_ref, joined_ref, gate_ref, logits_ref
):
    slots_ref[...] = wide_dot(x_ref[...], turn_ref[...]).astype(BF)
    for part in range(3):
        cols = slice(part * D, (part + 1) * D)
        made = wide_dot(slots_ref[...], whole_ref[:, cols])
        if part != 1:
            made = made + vectors_ref[part // 2 : part // 2 + 1, :]
        joined_ref[:, cols] = made.astype(BF)
    units = table_ref[12:20, :HD].astype(BF)
    logits_ref[...] = jnp.zeros(logits_ref.shape, F32)
    for head in range(H):
        logits_ref[:, head * gate_units : (head + 1) * gate_units] = (
            nt(x_ref[:, head * HD : (head + 1) * HD], units) + table_ref[20:21, :gate_units]
        )
    up = lax.broadcasted_iota(jnp.int32, (LANES, LANES), 0)
    across = lax.broadcasted_iota(jnp.int32, (LANES, LANES), 1)
    logits = split(logits_ref[...], 3)
    gates = []
    for side in range(2):
        chosen = ((up >> 3) == across) & (((up >> 2) & 1) == side)
        chosen = chosen.astype(F32).astype(BF)
        gates.append(jax.nn.sigmoid(sum(wide_dot(part, chosen) for part in logits)))
    first, second = gates
    gate_ref[0] = first * (second * table_ref[21:22, :LANES] - 1.0) + 2.0
    gate_ref[1] = first
    gate_ref[2] = second


def joined_forward(x, turn, vectors, table, whole):
    rows = x.shape[0]
    return call(
        joined_kernel,
        (x, turn, vectors, table, whole),
        (
            shaped((rows, D), BF),
            shaped((rows, 3 * D), BF),
            shaped((3, rows, LANES), F32),
        ),
        8,
        "joined_forward",
        scratch=(pltpu.VMEM((rows, LANES), F32),),
    )


def attention_kernel(clip, bucket_ref, valid_ref, table_ref, joined_ref, gate_ref, prob_ref, rel_ref, mixed_ref):
    slots = bucket_ref.shape[1]
    rows = slice(clip * slots, (clip + 1) * slots)
    index = bucket_ref[clip] & (LANES - 1)
    block = bucket_ref[clip] >> 7
    valid = valid_ref[rows, :] > 0
    gate = jnp.transpose(gate_ref[0, rows, :])
    for head in range(H):
        rel_ref[head] = lookup(table_ref, head, index, block)
    for head in range(H):
        query = joined_ref[rows, head * HD : (head + 1) * HD]
        key = joined_ref[rows, D + head * HD : D + (head + 1) * HD]
        score = nt(key, query) * (1.0 / math.sqrt(HD)) + gate[head : head + 1, :] * rel_ref[head]
        prob_ref[head] = jnp.where(valid, score, masked_score)
    for first in range(0, H, 4):
        score = prob_ref[first : first + 4]
        power = jnp.exp(score - jnp.max(score, axis=1, keepdims=True))
        prob_ref[first : first + 4] = power * (1.0 / jnp.sum(power, axis=1, keepdims=True))
    for head in range(H):
        value = joined_ref[rows, 2 * D + head * HD : 2 * D + (head + 1) * HD]
        mixed_ref[head * HD : (head + 1) * HD, :] = tn(value, prob_ref[head].astype(BF)).astype(BF)


def attention(clip, bucket, valid, table, joined, gate):
    slots = bucket.shape[1]
    return call(
        partial(attention_kernel, clip),
        (bucket, valid, table, joined, gate),
        (shaped((H, slots, slots), F32), shaped((H, slots, slots), F32), shaped((D, slots), BF)),
        4,
        "attention",
    )


def out_kernel(x_ref, turn_ref, vectors_ref, whole_ref, *refs):
    mixed_ref, unit_ref, scale_ref = refs[-3:]
    at = 0
    for part in refs[:-3]:
        rows = slice(at, at + part.shape[1])
        mixed_ref[rows, :] = tn(part[...], turn_ref[...]).astype(BF)
        at += part.shape[1]
    branch = wide_dot(mixed_ref[...], whole_ref[:, 3 * D : 4 * D]) + vectors_ref[2:3, :]
    unit, scale = normal(deep_alpha * x_ref[...].astype(F32) + branch)
    unit_ref[...] = unit
    scale_ref[...] = scale


def out_forward(x, turn, vectors, whole, mixed):
    rows = x.shape[0]
    return call(
        out_kernel,
        (x, turn, vectors, whole, *mixed),
        (shaped((rows, D), BF), shaped((rows, D), F32), shaped((rows, 1), F32)),
        6,
        "out_forward",
    )


def attention_back_kernel(
    clip, joined_ref, gate_ref, rank_ref, prob_ref, rel_ref, grad_ref, tri_ref,
    joined_grad_ref, gate_grad_ref, table_grad_ref,
):
    slots = rank_ref.shape[1]
    rows = slice(clip * slots, (clip + 1) * slots)
    scale = 1.0 / math.sqrt(HD)
    gate = jnp.transpose(gate_ref[0, rows, :])
    for head in range(H):
        cols = slice(head * HD, (head + 1) * HD)
        key_cols = slice(D + head * HD, D + (head + 1) * HD)
        value_cols = slice(2 * D + head * HD, 2 * D + (head + 1) * HD)
        query = joined_ref[rows, cols]
        key = joined_ref[rows, key_cols]
        value = joined_ref[rows, value_cols]
        grad = grad_ref[rows, cols]
        prob = prob_ref[head]
        joined_grad_ref[:, value_cols] = wide_dot(prob.astype(BF), grad).astype(BF)
        weighted = prob * nt(value, grad)
        low = (weighted - prob * jnp.sum(weighted, axis=0, keepdims=True)).astype(BF)
        joined_grad_ref[:, cols] = (tn(low, key) * scale).astype(BF)
        joined_grad_ref[:, key_cols] = (wide_dot(low, query) * scale).astype(BF)
        wide = low.astype(F32)
        gate_grad_ref[head : head + 1, :] = jnp.sum(wide * rel_ref[head], axis=0, keepdims=True)
        gated = wide * gate[head : head + 1, :]
        high = gated.astype(BF)
        rest = (gated - high.astype(F32)).astype(BF)
        running = tn(high, tri_ref[...]) + tn(rest, tri_ref[...])
        for part in range(KEYS // LANES):
            lanes = slice(part * LANES, (part + 1) * LANES)
            rank = rank_ref[clip, :, lanes]
            found = jnp.take_along_axis(
                running, jnp.maximum(rank - 1, 0), axis=1, mode="promise_in_bounds"
            )
            table_grad_ref[head : head + 1, lanes] = jnp.sum(
                jnp.where(rank > 0, found, 0.0), axis=0, keepdims=True
            )
    table_grad_ref[H:, :] = jnp.zeros((16 - H, KEYS), F32)
    gate_grad_ref[H:, :] = jnp.zeros((16 - H, slots), F32)


def attention_back(clip, joined, gate, rank, prob, rel, grad):
    slots = rank.shape[1]
    tri = jnp.asarray(np.triu(np.ones((slots, slots), np.float32)), BF)
    return call(
        partial(attention_back_kernel, clip),
        (joined, gate, rank, prob, rel, grad, tri),
        (shaped((slots, 3 * D), BF), shaped((16, slots), F32), shaped((16, KEYS), F32)),
        4,
        "attention_back",
    )


def gate_back_kernel(count, x_ref, table_ref, gate_ref, *refs):
    joined_grads, gate_grads, table_grads = refs[:count], refs[count : 2 * count], refs[2 * count : 3 * count]
    x_grad_ref, table_grad_ref, sums_ref = refs[3 * count :]
    table_grad_ref[...] = jnp.zeros(table_grad_ref.shape, F32)
    table_grad_ref[:16, :] = sum(ref[...] for ref in table_grads)
    sums_ref[0:1, :] = sum(jnp.sum(ref[:, :D].astype(F32), axis=0, keepdims=True) for ref in joined_grads)
    sums_ref[1:2, :] = sum(jnp.sum(ref[:, 2 * D :].astype(F32), axis=0, keepdims=True) for ref in joined_grads)
    units = [jnp.sum(table_ref[12 + 4 * i : 16 + 4 * i, :HD], axis=0, keepdims=True) for i in range(2)]
    unit_grads = [jnp.zeros((1, HD), F32), jnp.zeros((1, HD), F32)]
    grad = jnp.concatenate([jnp.transpose(ref[...]) for ref in gate_grads], axis=0)
    first, second = gate_ref[1, :, :16], gate_ref[2, :, :16]
    size = table_ref[21:22, :16]
    grads = (
        grad * (second * size - 1.0) * first * (1.0 - first),
        grad * first * size * second * (1.0 - second),
    )
    table_grad_ref[21:22, :16] = jnp.sum(grad * first * second, axis=0, keepdims=True)
    bias_grads = [jnp.sum(jnp.sum(g, axis=0, keepdims=True), axis=1, keepdims=True) for g in grads]
    for head in range(H):
        cols = slice(head * HD, (head + 1) * HD)
        x = x_ref[:, cols].astype(F32)
        sides = [g[:, head : head + 1] for g in grads]
        x_grad_ref[:, cols] = sides[0] * units[0] + sides[1] * units[1]
        for i in range(2):
            unit_grads[i] = unit_grads[i] + jnp.sum(x * sides[i], axis=0, keepdims=True)
    for unit in range(gate_units):
        table_grad_ref[12 + unit : 13 + unit, :HD] = unit_grads[unit // 4]
        table_grad_ref[20:21, unit : unit + 1] = bias_grads[unit // 4]


def gate_back(x, table, gate, joined_grads, gate_grads, table_grads):
    return call(
        partial(gate_back_kernel, len(joined_grads)),
        (x, table, gate, *joined_grads, *gate_grads, *table_grads),
        (shaped(x.shape, F32), shaped((24, KEYS), F32), shaped((8, D), F32)),
        6,
        "gate_back",
    )


def gelu_pair(u):
    size = jnp.abs(u) * math.sqrt(0.5)
    t = 1.0 / (1.0 + 0.3275911 * size)
    poly = ((((1.061405429 * t - 1.453152027) * t + 1.421413741) * t - 0.284496736) * t + 0.254829592) * t
    bell = jnp.exp(-0.5 * u * u)
    tail = 0.5 * poly * bell
    below = jnp.where(u < 0, tail, 1.0 - tail)
    return u * below, below + u * bell * (1.0 / math.sqrt(2.0 * math.pi))


def hidden_kernel(
    unit_ref, vectors_ref, turn_ref, bias_ref, whole_ref, slots_ref, active_ref, slope_ref
):
    low = (unit_ref[...] * vectors_ref[3:4, :] + vectors_ref[4:5, :]).astype(BF)
    slots_ref[...] = wide_dot(low, turn_ref[...]).astype(BF)
    width = FF // 8
    for block in range(8):
        cols = slice(block * width, (block + 1) * width)
        u = wide_dot(slots_ref[...], whole_ref[:, cols]) + bias_ref[:, cols]
        active, slope = gelu_pair(u)
        active_ref[:, cols] = active.astype(BF)
        slope_ref[:, cols] = slope


def hidden_forward(unit, vectors, turn, bias, whole):
    rows = unit.shape[0]
    return call(
        hidden_kernel,
        (unit, vectors, turn, bias, whole),
        (shaped((rows, D), BF), shaped((rows, FF), BF), shaped((rows, FF), F32)),
        10,
        "hidden_forward",
    )


def layer_turn(made, unit_ref, vectors_ref, valid_ref, cot_ref, out_ref, second_ref, low_ref, sums_ref):
    made = made + vectors_ref[5:6, :]
    first_norm = unit_ref[...] * vectors_ref[3:4, :] + vectors_ref[4:5, :]
    unit, scale = normal(deep_alpha * first_norm + made.astype(BF).astype(F32))
    valid = valid_ref[...]
    gain = vectors_ref[6:7, :]
    out_ref[...] = ((unit * gain + vectors_ref[7:8, :]) * valid).astype(BF)
    grad = cot_ref[...].astype(F32) * valid
    second = normal_back(grad * gain, unit, scale)
    second_ref[...] = second
    low = second.astype(BF)
    low_ref[...] = low
    sums_ref[0:1, :] = jnp.sum(low.astype(F32), axis=0, keepdims=True)
    sums_ref[1:2, :] = jnp.sum(grad * unit, axis=0, keepdims=True)
    sums_ref[2:3, :] = jnp.sum(grad, axis=0, keepdims=True)


def turn_kernel(slots, ranges, each, *refs):
    at_ref, active_ref, unit_ref, vectors_ref, valid_ref, cot_ref = refs[:6]
    count = 5 + len(ranges)
    parts = refs[6:-count]
    whole_ref, out_ref, second_ref, low_ref, sums_ref, *corners = refs[-count:]
    for slot, (which, row, rows, column) in enumerate(slots):
        place = pl.multiple_of(at_ref[slot], 16)
        if parts[which].shape[1] == D:
            whole_ref[pl.ds(place, rows), :] = parts[which][row : row + rows, :]
            continue
        blocks = [
            parts[which][row : row + rows, column + j * D : column + (j + 1) * D] for j in range(FF // D)
        ]
        whole_ref[pl.ds(place, rows * len(blocks)), :] = jnp.concatenate(blocks, axis=0)
    made = wide_dot(active_ref[...], whole_ref[...])
    layer_turn(made, unit_ref, vectors_ref, valid_ref, cot_ref, out_ref, second_ref, low_ref, sums_ref)
    if ranges:
        for half in range(2):
            down_back_kernel(ranges[half : half + 1], each, parts[half - 2], low_ref, corners[half])


def turn_back(at, slots, active, unit, vectors, valid, cot, parts, turned=None, ranges=(), each=0):
    rows = unit.shape[0]
    outs = [shaped((FF, D), BF), shaped((rows, D), BF), shaped((rows, D), F32), shaped((rows, D), BF)]
    outs.append(shaped((8, D), F32))
    outs += [shaped(((last - first) * each, FF), BF) for first, last in ranges]
    extra = [turned, turned] if ranges else []
    return call(
        partial(turn_kernel, slots, ranges, each),
        (active, unit, vectors, valid, cot, *parts, *extra),
        outs,
        10,
        "turn_back",
        scalars=(at,),
    )


def place_slots(slots, parts, at_ref, first, whole_ref):
    for slot, (which, row, rows, column) in enumerate(slots):
        place = pl.multiple_of(at_ref[first + slot], 16)
        blocks = [
            parts[which][row : row + rows, column + j * D : column + (j + 1) * D] for j in range(FF // D)
        ]
        whole_ref[pl.ds(place, rows * len(blocks)), :] = jnp.concatenate(blocks, axis=0)


def partial_kernel(slots, late, at_ref, active_ref, *refs):
    *parts, whole_ref, made_ref = refs
    place_slots(slots, parts, at_ref, 0, whole_ref)
    chunk = FF // (len(slots) + late)
    for slot in range(len(slots), len(slots) + late):
        place = pl.multiple_of(at_ref[slot], 16)
        whole_ref[pl.ds(place, chunk), :] = jnp.zeros((chunk, D), BF)
    made_ref[...] = wide_dot(active_ref[...], whole_ref[...])


def partial_down(at, slots, late, active, parts):
    return call(
        partial(partial_kernel, slots, late),
        (active, *parts),
        (shaped((FF, D), BF), shaped((active.shape[0], D), F32)),
        8,
        "partial_down",
        scalars=(at,),
    )


def last_kernel(slots, first, ranges, each, *refs):
    at_ref, made_ref, unit_ref, vectors_ref, valid_ref, cot_ref, turned_ref, late_ref, _ = refs[:9]
    whole_ref, out_ref, second_ref, low_ref, sums_ref, *corners, rows_ref = refs[9:]
    place_slots(slots, [late_ref], at_ref, first, whole_ref)
    chunk = each * FF // D
    for slot, (_, row, rows, column) in enumerate(slots):
        for j in range(FF // D):
            at = slot * chunk + j * rows
            rows_ref[at : at + rows, :] = late_ref[row : row + rows, column + j * D : column + (j + 1) * D]
    made = made_ref[...] + tn(turned_ref[first * chunk :, :], rows_ref[...])
    layer_turn(made, unit_ref, vectors_ref, valid_ref, cot_ref, out_ref, second_ref, low_ref, sums_ref)
    for half in range(2):
        down_back_kernel(ranges[half : half + 1], each, turned_ref, low_ref, corners[half])


def last_turn(at, slots, first, made, unit, vectors, valid, cot, turned, late, whole, ranges, each):
    rows = unit.shape[0]
    outs = [shaped((FF, D), BF), shaped((rows, D), BF), shaped((rows, D), F32), shaped((rows, D), BF)]
    outs.append(shaped((8, D), F32))
    outs += [shaped(((last - begin) * each, FF), BF) for begin, last in ranges]
    operands = (made, unit, vectors, valid, cot, turned, late, whole)
    return pl.pallas_call(
        partial(last_kernel, slots, first, ranges, each),
        out_shape=tuple(outs),
        in_specs=[pl.BlockSpec(memory_space=pltpu.SMEM)] + vmem(len(operands)),
        out_specs=tuple(vmem(len(outs))),
        input_output_aliases={8: 0},
        scratch_shapes=[pltpu.VMEM((len(slots) * each * FF // D, D), BF)],
        compiler_params=limits(8),
        cost_estimate=pl.CostEstimate(flops=1, bytes_accessed=1, transcendentals=0),
        name="last_turn",
    )(at, *operands)


def turn_active_kernel(rows, at_ref, active_ref, out_ref, turned_ref):
    for first in range(0, FF, FF // 8):
        cols = slice(first, first + FF // 8)
        turned_ref[cols, :] = jnp.transpose(active_ref[:, cols])
    for slot in range(FF // rows):
        place = pl.multiple_of(at_ref[slot], 16)
        out_ref[slot * rows : (slot + 1) * rows, :] = turned_ref[pl.ds(place, rows), :]


def turn_active(at, rows, active):
    return call(
        partial(turn_active_kernel, rows),
        (active,),
        (shaped((FF, active.shape[0]), BF),),
        8,
        "turn_active",
        scalars=(at,),
        scratch=(pltpu.VMEM((FF, active.shape[0]), BF),),
    )[0]


def down_back_kernel(ranges, rows, active_ref, low_ref, *outs):
    chunk = rows * FF // D
    for (first, last), out_ref in zip(ranges, outs):
        for slot in range(first, last):
            made = wide_dot(active_ref[slot * chunk : (slot + 1) * chunk, :], low_ref[...]).astype(BF)
            to = (slot - first) * rows
            for j in range(FF // D):
                out_ref[to : to + rows, j * D : (j + 1) * D] = made[j * rows : (j + 1) * rows, :]


def down_back(ranges, rows, active, low):
    return call(
        partial(down_back_kernel, ranges, rows),
        (active, low),
        [shaped(((last - first) * rows, FF), BF) for first, last in ranges],
        6,
        "down_back",
    )


def hidden_back_kernel(low_ref, down_ref, slope_ref, grad_ref, bias_ref):
    width = FF // 8
    for block in range(8):
        cols = slice(block * width, (block + 1) * width)
        grad = (nt(low_ref[...], down_ref[cols, :]) * slope_ref[:, cols]).astype(BF)
        grad_ref[:, cols] = grad
        bias_ref[:, cols] = jnp.sum(grad.astype(F32), axis=0, keepdims=True)


def hidden_back(low, down, slope):
    rows = low.shape[0]
    return call(
        hidden_back_kernel,
        (low, down, slope),
        (shaped((rows, FF), BF), shaped((1, FF), F32)),
        6,
        "hidden_back",
    )


def in_back_kernel(slots_ref, grad_ref, mine_ref, other_ref):
    width = FF // 4
    for block in range(4):
        cols = slice(block * width, (block + 1) * width)
        made = tn(slots_ref[...], grad_ref[:, cols]).astype(BF)
        mine_ref[:, cols] = made[: D // 2]
        other_ref[:, cols] = made[D // 2 :]


def inner_back_kernel(ranges, each, turned_ref, low_ref, down_ref, slope_ref, slots_ref, main_ref, grad_ref, bias_ref, mine_ref, other_ref):
    down_back_kernel(ranges, each, turned_ref, low_ref, main_ref)
    hidden_back_kernel(low_ref, down_ref, slope_ref, grad_ref, bias_ref)
    in_back_kernel(slots_ref, grad_ref, mine_ref, other_ref)


def inner_back(ranges, each, turned, low, down, slope, slots):
    rows, half = low.shape[0], shaped((D // 2, FF), BF)
    main = shaped(((ranges[0][1] - ranges[0][0]) * each, FF), BF)
    return call(
        partial(inner_back_kernel, ranges, each),
        (turned, low, down, slope, slots),
        (main, shaped((rows, FF), BF), shaped((1, FF), F32), half, half),
        8,
        "inner_back",
    )


def in_back(slots, grad):
    rows = slots.shape[0]
    return call(
        in_back_kernel,
        (slots, grad),
        (shaped((D // 2, FF), BF), shaped((D // 2, FF), BF)),
        6,
        "in_back",
    )


def out_back_kernel(
    grad_ref, in_ref, turn_ref, second_ref, unit_ref, scale_ref, vectors_ref, mixed_ref, out_ref,
    first_ref, weight_ref, mixed_grad_ref, sums_ref,
):
    low = nt(grad_ref[...], in_ref[...]).astype(BF)
    grad = deep_alpha * second_ref[...] + nt(low, turn_ref[...]).astype(BF).astype(F32)
    unit = unit_ref[...]
    first = normal_back(grad * vectors_ref[3:4, :], unit, scale_ref[...])
    first_ref[...] = first
    branch = first.astype(BF)
    sums_ref[0:1, :] = jnp.sum(branch.astype(F32), axis=0, keepdims=True)
    sums_ref[1:2, :] = jnp.sum(grad * unit, axis=0, keepdims=True)
    sums_ref[2:3, :] = jnp.sum(grad, axis=0, keepdims=True)
    weight_ref[...] = tn(mixed_ref[...], branch).astype(BF)
    back = nt(branch, out_ref[:, 3 * D : 4 * D]).astype(BF)
    mixed_grad_ref[...] = nt(back, turn_ref[...]).astype(BF)


def out_back(grad, w_in, turn, second, unit, scale, vectors, mixed, w_first):
    rows = unit.shape[0]
    return call(
        out_back_kernel,
        (grad, w_in, turn, second, unit, scale, vectors, mixed, w_first),
        (shaped((rows, D), F32), shaped((D, D), BF), shaped((rows, D), BF), shaped((8, D), F32)),
        6,
        "out_back",
    )


def first_back_kernel(slots_ref, out_ref, small_ref, *refs):
    *grads, mine_ref, other_ref, grad_ref = refs
    at = 0
    for grad in grads:
        grad_ref[at : at + grad.shape[0], :] = grad[...]
        at += grad.shape[0]
    half = D // 2
    for part in range(3):
        cols = slice(part * D, (part + 1) * D)
        made = tn(slots_ref[...], grad_ref[:, cols]).astype(BF)
        mine_ref[:, cols] = made[:half]
        other_ref[:, cols] = made[half:]
    for ref, rows in ((mine_ref, slice(0, half)), (other_ref, slice(half, D))):
        ref[:, 3 * D : 4 * D] = out_ref[rows, :]
        ref[:, 4 * D :] = small_ref[rows, :]


def first_back(slots, weight_out, small, grads):
    rows = slots.shape[0]
    wide = 4 * D + small.shape[1]
    return call(
        first_back_kernel,
        (slots, weight_out, small, *grads),
        (shaped((D // 2, wide), BF), shaped((D // 2, wide), BF), shaped((rows, 3 * D), BF)),
        6,
        "first_back",
    )


def rows_back_kernel(grad_ref, first_ref, turn_ref, branch_ref, gate_ref, out_ref):
    made = nt(grad_ref[...], first_ref[:, : 3 * D])
    high = made.astype(BF)
    rest = made - high.astype(F32)
    middle = rest.astype(BF)
    last = (rest - middle.astype(F32)).astype(BF)
    turned = nt(high, turn_ref[...]) + nt(middle, turn_ref[...]) + nt(last, turn_ref[...])
    out_ref[...] = turned + deep_alpha * branch_ref[...] + gate_ref[...]


def rows_back(grad, w_first, turn, branch, gate):
    rows = grad.shape[0]
    return call(
        rows_back_kernel,
        (grad, w_first, turn, branch, gate),
        (shaped((rows, D), F32),),
        8,
        "rows_back",
    )[0]


def flat_cuts(each):
    cuts = [(0, row, 0, 3 * D) for row in range(each)]
    cuts += [(0, row, 3 * D, 4 * D) for row in range(each)]
    cuts += [(1, row, 0, FF) for row in range(each)]
    cuts += [(2, row, j * D, (j + 1) * D) for j in range(FF // D) for row in range(each)]
    return cuts + [(0, row, 4 * D, 4 * D + LANES) for row in range(each)]


def flat_runs(each, width):
    at = 0
    for which, row, first, last in flat_cuts(each):
        size = min(last - first, width - at)
        if size > 0:
            yield which, row, first, size, at
        at += last - first


def rows_kernel(flat_ref, first_ref, in_ref, down_ref):
    refs = (first_ref, in_ref, down_ref)
    first_ref[:, 4 * D :] = jnp.zeros((first_ref.shape[0], LANES), F32)
    for which, row, first, size, at in flat_runs(first_ref.shape[0], flat_ref.shape[1]):
        refs[which][row : row + 1, first : first + size] = flat_ref[:, at : at + size]


def pieces_kernel(flat_ref, first_ref, in_ref, down_ref, all_ref, *refs):
    rows_kernel(flat_ref, *refs)
    at = 0
    for ref, low in zip(refs, (first_ref, in_ref, down_ref)):
        low[...] = ref[...].astype(BF)
        all_ref[:, at : at + low.shape[1]] = low[...]
        at += low.shape[1]


def row_widths():
    return (4 * D + LANES, FF, FF)


def flat_rows(flat, each):
    return call(rows_kernel, (flat,), [shaped((each, width), F32) for width in row_widths()], 6, "flat_rows")


def pieces(flat, each):
    widths = row_widths()
    return call(
        pieces_kernel,
        (flat,),
        [shaped((each, width), BF) for width in (*widths, sum(widths))],
        6,
        "pieces",
        scratch=[pltpu.VMEM((each, width), F32) for width in widths],
    )


def update_kernel(learning, plan, sections, spans, known, count, *refs):
    size = len(sections)
    sums, refs = refs[:count], refs[count:]
    weights, momenta, averages, refs = refs[:size], refs[size : 2 * size], refs[2 * size : 3 * size], refs[3 * size :]
    outs, refs = refs[known : known + 4], refs[known + 4 :]
    rows, flats, arrived = refs[: 3 * size], refs[3 * size : -1], refs[-1]
    for i in range(size):
        each, wide = weights[i].shape
        grad = sum(
            sums[which][row : row + each, column : column + wide].astype(F32) for which, row, column in plan[i]
        )
        weight = weights[i][...]
        decayed = grad + decay_rate * weight
        momentum = momentum_rate * momenta[i][...] + decayed
        weight = weight - learning * (decayed + momentum_rate * momentum)
        rows[i][...] = momentum
        rows[size + i][...] = average_rate * averages[i][...] + (1.0 - average_rate) * weight
        rows[2 * size + i][...] = weight
    each = weights[0].shape[0]
    copies = []
    for out, which in zip(range(4), (0, 1, 2, 2)):
        for span, (first, last) in enumerate(spans):
            flat = flats[out * len(spans) + span]
            for section, row, column, width, at in flat_runs(each, outs[out].shape[1]):
                if section in sections and first <= at < last:
                    value = rows[which * size + sections.index(section)][row : row + 1, column : column + width]
                    flat[:, at - first : at - first + width] = value.astype(flat.dtype)
            copies.append(
                pltpu.make_async_copy(
                    flat, outs[out].at[:, pl.ds(first, last - first)], arrived.at[out * len(spans) + span]
                )
            )
            copies[-1].start()
    for copy in copies:
        copy.wait()


def update(learning, sections, sums, weights, momenta, averages, width, known=()):
    arrays, plan = [], []
    for section in sections:
        found = []
        for array, row, column in sums[section]:
            at = next((i for i, other in enumerate(arrays) if other is array), None)
            if at is None:
                at = len(arrays)
                arrays.append(array)
            found.append((at, row, column))
        plan.append(found)
    each = weights[0].shape[0]
    runs = [(at, at + size) for section, _, _, size, at in flat_runs(each, width) if section in sections]
    spans = []
    for first, last in runs:
        if spans and spans[-1][1] == first:
            spans[-1] = (spans[-1][0], last)
        else:
            spans.append((first, last))
    rows = [[part[section] for section in sections] for part in (weights, momenta, averages)]
    dtypes = (F32, F32, F32, BF)
    operands = [*arrays, *rows[0], *rows[1], *rows[2]]
    anywhere = pl.BlockSpec(memory_space=pl.ANY)
    return pl.pallas_call(
        partial(update_kernel, learning, plan, list(sections), spans, len(known), len(arrays)),
        out_shape=tuple(shaped((1, width), dtype) for dtype in dtypes),
        in_specs=vmem(len(operands)) + [anywhere] * len(known),
        out_specs=(anywhere,) * 4,
        input_output_aliases={len(operands) + i: i for i in range(len(known))},
        scratch_shapes=[pltpu.VMEM(part.shape, F32) for part in rows[0]] * 3
        + [pltpu.VMEM((1, last - first), dtype) for dtype in dtypes for first, last in spans]
        + [pltpu.SemaphoreType.DMA((4 * len(spans),))],
        compiler_params=limits(10),
        cost_estimate=pl.CostEstimate(flops=1, bytes_accessed=1, transcendentals=0),
        name="update",
    )(*operands, *known)


def body(acts, cotangent, mask, shape_id, weights, momenta, averages):
    shards = lax.axis_size(("dp", "fsdp"))
    count = lax.axis_size("dp")
    dp, core = lax.axis_index("dp"), lax.axis_index("fsdp")
    clips, slots = acts.shape[0], acts.shape[1]
    rows = clips * slots
    total_tokens = rows * shards
    piece_rows = D // shards
    wide_rows = FF // shards
    vector_width = 12 * D // shards
    position_width = (NPOS + shards - 1) // shards
    small_width = vector_width + position_width

    piece_first, piece_in, piece_down, piece_all = pieces(weights, piece_rows)

    order = slot_order(dp, core, count)
    row_order = (order[:, None] * piece_rows + jnp.arange(piece_rows, dtype=jnp.int32)).reshape(-1)
    turn = (jnp.arange(D, dtype=jnp.int32)[:, None] == row_order[None, :]).astype(BF)
    piece_turn = (jnp.arange(shards, dtype=jnp.int32)[:, None] == order[None, :]).astype(BF)

    back_order = jnp.dot(piece_turn.astype(F32), jnp.arange(shards, dtype=F32)).astype(jnp.int32)

    together = lax.optimization_barrier
    bits = high_bits(count)
    staged = len(bits) == 2
    n = piece_rows
    rest = D // 8 - n
    widths = (piece_first.shape[1], FF, FF)
    lefts = (0, widths[0], widths[0] + FF)
    cuts = (13 * LANES, FF // 2, FF // 2)
    wide_all, cut_all = sum(widths), 37 * LANES
    third = (13 * LANES, 12 * LANES, 12 * LANES), (12 * LANES,) * 3
    at = order * wide_rows
    inputs_low = acts.reshape(rows, D)

    def gather_high(piece, direct=False):
        if staged:
            if direct:
                return [exchange(piece, "dp", d << 2) for d in (1, 2, 3)]
            two = exchange(piece, "dp", 8)
            return [exchange(piece, "dp", 4), two, exchange(two, "dp", 4)]
        column = piece
        for bit in bits:
            column = jnp.concatenate([column, exchange(column, "dp", 1 << bit)], axis=0)
        return [column[n:]]

    def thirds(side, views):
        left = widths[0]
        items, column = [], 0
        for i, size in enumerate(third[side]):
            items += views(i * n, left, column, size)
            column += size
        return items

    own_sides = exchange_sides((piece_all, piece_all))
    high_first = gather_high(piece_first)
    own_sides, high_first, piece_in, mask, turn, at = together(
        (own_sides, high_first, piece_in, mask, turn, at)
    )

    items = stack([whole_of(part) for part in high_first])[1]
    sends = build(
        ((rest, widths[0]), items),
        (
            (rest, widths[0] + third[1][0]),
            items + thirds(1, lambda row, left, c, w: [(row, left, n, w, [(own_sides[1], 0, cut_all + c)])]),
        ),
        (
            (rest, widths[0] + third[0][0]),
            items + thirds(0, lambda row, left, c, w: [(row, left, n, w, [(own_sides[0], 0, c)])]),
        ),
    )
    rest_first, sends = sends[0], sends[1:]
    sides_first = exchange_sides(sends)
    high_in = gather_high(piece_in, True)
    bucket, rank, valid_rows = prep(mask, shape_id, slots)
    sides_first, high_in, piece_down, bucket, rank, valid_rows = together(
        (sides_first, high_in, piece_down, bucket, rank, valid_rows)
    )

    def corner_sends(unit, sides):
        wide, half = widths[unit], cuts[unit]
        return (
            ((rest, wide - half), [(0, 0, rest, wide - half, [(sides[1], 0, half)])]),
            ((rest, half), [(0, 0, rest, half, [(sides[0], 0, 0)])]),
        )

    def corner_items(unit, corner):
        wide, half = widths[unit], cuts[unit]
        (second, left_second), (first, left_first) = corner
        return [
            (0, 0, rest, half, [(first, 0, left_first)]),
            (0, half, rest, wide - half, [(second, 0, left_second)]),
        ]

    def early_rows(unit, piece, high, sides):
        wide = widths[unit]
        return stack([whole_of(piece), whole_of(high)] + [(side, 0, rest, 0, wide) for side in sides])

    def shifted(items, row):
        return [(row + item[0], *item[1:]) for item in items]

    def slots_of(unit, piece, high, sides, corner, early, late):
        wide, left = widths[unit], lefts[unit]
        own_mine, own_other = own
        items = [(0, 0, n, wide, [(piece, 0, 0)]), (n, 0, rest, wide, [(high, 0, 0)])]
        eighth = D // 8
        for i in range(3):
            items.append(((i + 1) * eighth, 0, n, wide, [(own_mine, i * n, left)]))
        for i, side in enumerate(sides):
            items.append(((i + 1) * eighth + n, 0, rest, wide, [(side, 0, 0)]))
        items += shifted(corner_items(unit, corner), 3 * eighth + n)
        base = D // 2
        if not isinstance(early, tuple):
            early = (early, 0), (early, n + rest)
        (one, row_one), (two, row_two) = early
        items.append((base, 0, n, wide, [(one, row_one, 0)]))
        items.append((base + n, 0, rest, wide, [(one, row_one + n, 0)]))
        for i in range(3):
            items.append((base + (i + 1) * eighth, 0, n, wide, [(own_other, i * n, left)]))
            view = late if i == 2 else (two, row_two + i * rest, 0)
            items.append((base + (i + 1) * eighth + n, 0, rest, wide, [view]))
        return items

    def own_corner(row, half, side, column):
        return [(row, column + c, n, w, [(side, i * n, widths[0])]) for i, (c, w) in enumerate(half)]

    def spans(side):
        edges = np.cumsum((0, *third[side]))
        return [(int(a), int(b - a)) for a, b in zip(edges[:-1], edges[1:])]

    items = [(0, 0, n, wide_all, [(own_sides[0], 0, 0)]), (n, 0, n, wide_all, [(own_sides[1], 0, 0)])]
    items += own_corner(2 * n, spans(0), sides_first[1], 0) + own_corner(2 * n, spans(1), sides_first[0], cut_all)
    def side_sends(unit, high, sides):
        wide, half = widths[unit - 1], cuts[unit - 1]
        items = stack([whole_of(part) for part in high])[1]
        sends = []
        for width, view in ((wide - half, (sides[1], 0, half)), (half, (sides[0], 0, 0))):
            sends.append(((rest, widths[unit] + width), items + [(0, widths[unit], rest, width, [view])]))
        return [((rest, widths[unit]), items)] + sends

    own_mine, early, rest_in, *sends = build(
        ((3 * n, wide_all), items),
        early_rows(0, piece_first, rest_first, sides_first),
        *side_sends(1, high_in, sides_first),
    )
    sides_in = exchange_sides(sends)
    early_first = exchange_core(early)
    high_down = gather_high(piece_down)
    sides_in, early_first, high_down, own_mine = together((sides_in, early_first, high_down, own_mine))

    corner_first = [(part, FF) for part in sides_in]
    items = stack([whole_of(own_mine)])[1]
    items += [(row, wide_all + column, *more) for row, column, *more in corner_items(0, corner_first)]
    late, rest_down, *sends = build(
        ((rest, wide_all + widths[0]), items), *side_sends(2, high_down, sides_in)
    )
    sides_down = exchange_sides(sends)
    late = exchange_core(late)
    own = (own_mine, late)
    items = slots_of(0, piece_first, rest_first, sides_first, corner_first, early_first, (late, 0, wide_all))
    w_first = build(((D, widths[0]), items))[0]
    early, first_down = build(
        early_rows(1, piece_in, rest_in, sides_in), stack([whole_of(piece_down), whole_of(rest_down)])
    )
    early_in, first_down = exchange_core(early), exchange_core(first_down)
    vectors, bias_in, table = unpack(shards, turn, w_first)
    inputs_slots, joined, gate = joined_forward(inputs_low, turn, vectors, table, w_first)
    made = [attention(clip, bucket, valid_rows, table, joined, gate) for clip in range(clips)]
    mixed_slots, unit, unit_scale = out_forward(inputs_low, turn, vectors, w_first, [m[2] for m in made])
    sides_down, early_in, first_down, unit = together((sides_down, early_in, first_down, unit))

    corner_in = [(part, FF) for part in sides_down]
    late, early, *sends = build(
        ((rest, FF), corner_items(1, corner_in)),
        stack([(side, 0, rest, 0, FF) for side in sides_down]),
        *corner_sends(2, sides_down),
    )
    corner_down = exchange_sides(sends)
    late = exchange_core(late)
    early_down = exchange_core(early)
    items = slots_of(1, piece_in, rest_in, sides_in, corner_in, early_in, (late, 0, 0))
    w_in = build(((D, FF), items))[0]
    first_slots, active, slope = hidden_forward(unit, vectors, turn, bias_in, w_in)
    turned = turn_active(at, wide_rows, active) if wide_rows % 16 == 0 else active
    corner_down, early_down, active, turned = together((corner_down, early_down, active, turned))

    corner_down = [(part, 0) for part in corner_down]
    corner = build(((rest, FF), corner_items(2, corner_down)))[0]
    late = exchange_core(corner)
    early_down = (first_down, 0), (early_down, 0)
    items = slots_of(2, piece_down, rest_down, sides_down, [(corner, cuts[2]), (corner, 0)], early_down, (late, 0, 0))
    arrays, places = [], [None] * shards
    for row, column, size, _, [(array, first, left)] in items:
        if column:
            continue
        which = next((i for i, known in enumerate(arrays) if known is array), len(arrays))
        if which == len(arrays):
            arrays.append(array)
        for step in range(size // n):
            places[row // n + step] = (which, first + step * n, n, left)
    cot = cotangent.reshape(rows, D)
    half_slots, last_slots = shards // 2, rest // n
    if wide_rows % 16:
        parts = [arrays[which][row : row + n, left : left + FF] for which, row, _, left in places]
        stacked = jnp.stack(parts).reshape(shards, n, FF // D, D).transpose(0, 2, 1, 3).reshape(shards, wide_rows, D)
        arrays, places = [jnp.take(stacked, back_order, axis=0).reshape(FF, D)], [(0, 0, FF, 0)]
        w_down, activations, grad_second, grad_made, sums_second = turn_back(
            jnp.zeros((1,), jnp.int32), places, active, unit, vectors, valid_rows, cot, arrays
        )
    else:
        first_late = shards - last_slots
        ahead = sorted({place[0] for place in places[:first_late]})
        slots_ahead = [(ahead.index(place[0]), *place[1:]) for place in places[:first_late]]
        slots_late = [(0, *place[1:]) for place in places[first_late:]]
        w_down, made_down = partial_down(at, slots_ahead, last_slots, active, [arrays[i] for i in ahead])
        w_down, made_down, late = together((w_down, made_down, late))
        ranges = ((half_slots - last_slots, half_slots), (first_late, shards))
        w_down, activations, grad_second, grad_made, sums_second, *lasts = last_turn(
            at, slots_late, first_late, made_down, unit, vectors, valid_rows, cot, turned, late, w_down, ranges, n
        )

    if wide_rows % 16:
        grad_down = tn(active, grad_made).astype(BF).reshape(shards, wide_rows, D)
        grad_down = jnp.take(grad_down, order, axis=0).reshape(shards, FF // D, n, D).transpose(0, 2, 1, 3)
        grad_down = grad_down.reshape(D, FF)
        at_last = D // 2 - rest
        down_main, down_last, other_main, other_last = (
            grad_down[:at_last], grad_down[at_last : D // 2], grad_down[D // 2 : D // 2 + at_last], grad_down[D // 2 + at_last :]
        )
    else:
        down_last, other_last, grad_made = together((*lasts, grad_made))

    eighth = D // 8

    def both(pair, row, column):
        views = []
        for array in pair:
            if isinstance(array, tuple):
                main, last = array
                at = D // 2 - rest
                views.append((last, row - at, column) if row >= at else (main, row, column))
            else:
                views.append((array, row, column))
        return views

    def corner_out(unit, pair):
        wide, half = widths[unit], cuts[unit]
        row = 3 * eighth + n
        return (
            (wide - half, [(0, 0, rest, wide - half, both(pair, row, half))]),
            (half, [(0, 0, rest, half, both(pair, row, 0))]),
        )

    def sides_out(unit, pair, corner):
        wide, half = widths[unit], cuts[unit]
        (second, left_second), (first, left_first) = corner
        near, side = eighth + n, 2 * eighth + n
        return (
            (
                wide,
                [
                    (0, 0, rest, half, both(pair, near, 0) + [(first, 0, left_first)]),
                    (0, half, rest, wide - half, both(pair, near, half)),
                ],
            ),
            (
                wide,
                [
                    (0, 0, rest, half, both(pair, side, 0)),
                    (0, half, rest, wide - half, both(pair, side, half) + [(second, 0, left_second)]),
                ],
            ),
        )

    def beside(one, two):
        return [
            ((rest, a[0] + b[0]), a[1] + [(item[0], a[0] + item[1], *item[2:]) for item in b[1]])
            for a, b in zip(one, two)
        ]

    def alone(one):
        return [((rest, wide), items) for wide, items in one]

    def column_views(unit, pair, sides, row):
        return both(pair, row, 0) + [(side, row - n, 0) for side in sides]

    def high_out(unit, pair, sides, first, count, *more):
        wide = widths[unit]
        views = column_views(unit, pair, sides, first * n)
        if more:
            views = views + [(more[0], n, 0)]
        return ((count * n, wide), [(0, 0, count * n, wide, views)])

    def scatter_high(unit, pair, sides):
        wide = widths[unit]
        total = build(((rest, wide), [(0, 0, rest, wide, column_views(unit, pair, sides, n))]))[0].astype(F32)
        total = jnp.concatenate([jnp.zeros((n, widths[unit]), F32), total], axis=0)
        for bit in reversed(bits):
            size = total.shape[0] // 2
            total = total[:size] + exchange(total[size:].astype(BF), "dp", 1 << bit).astype(F32)
        return [total]

    def scatter_far(unit, pair, sides):
        if not staged:
            return scatter_high(unit, pair, sides)
        return [exchange(build(high_out(unit, pair, sides, 2, 2))[0], "dp", 8)]

    other_last = exchange_core(other_last)
    if wide_rows % 16:
        grad_hidden, grad_bias_in = hidden_back(grad_made, w_down, slope)
        in_mine, in_other = in_back(first_slots, grad_hidden)
    else:
        other_main, grad_hidden, grad_bias_in, in_mine, in_other = inner_back(
            ((half_slots, shards - last_slots),), n, turned, grad_made, w_down, slope, first_slots
        )
    down_last, other_last, other_main, in_mine, in_other, grad_hidden, grad_made = together(
        (down_last, other_last, other_main, in_mine, in_other, grad_hidden, grad_made)
    )

    corner_down = exchange_sides(build(*alone(corner_out(2, ((None, down_last), (None, other_last))))))
    inner = (in_mine, exchange_core(in_other))
    other_main = exchange_core(other_main)
    if wide_rows % 16 == 0:
        down_main = down_back(((0, half_slots - last_slots),), n, turned, grad_made)[0]
    grad_first_sum, grad_out, grad_mixed, sums_first = out_back(
        grad_hidden, w_in, turn, grad_second, unit, unit_scale, vectors, mixed_slots, w_first
    )

    def clip_back(clip):
        prob, rel, _ = made[clip]
        return attention_back(clip, joined, gate, rank, prob, rel, grad_mixed)

    corner_down, inner, other_main, down_main, grad_mixed = together(
        (corner_down, inner, other_main, down_main, grad_mixed)
    )
    down = ((down_main, down_last), (other_main, other_last))

    corner_down = [(part, 0) for part in corner_down]
    sides_down = exchange_sides(build(*beside(sides_out(2, down, corner_down), corner_out(1, inner))))
    backs = [clip_back(clip) for clip in range(clips)]
    grads_joined = [back[0] for back in backs]
    grad_gate_inputs, table_grad, sums_attention = gate_back(
        inputs_low, table, gate, grads_joined, [back[1] for back in backs], [back[2] for back in backs]
    )
    grad_small = pack(shards, turn, sums_attention, sums_first, sums_second, grad_bias_in, table_grad)
    first_mine, first_other, grad_joined = first_back(inputs_slots, grad_out, grad_small, grads_joined)
    sides_down, first_mine, first_other, grad_joined = together((sides_down, first_mine, first_other, grad_joined))

    corner_in = [(part, FF) for part in sides_down]
    first = (first_mine, exchange_core(first_other))
    sides_in = exchange_sides(build(*alone(sides_out(1, inner, corner_in))))
    high_down = scatter_far(2, down, sides_down)
    corner_first = exchange_sides(build(*alone(corner_out(0, first))))
    input_grad = rows_back(grad_joined, w_first, turn, grad_first_sum, grad_gate_inputs)
    first, sides_in, high_down, corner_first, input_grad = together(
        (first, sides_in, high_down, corner_first, input_grad)
    )

    corner_first = [(part, 0) for part in corner_first]
    units = ((first, 0), (inner, 1), (down, 2))

    def own_views(row, column, columns):
        found = []
        for pair, unit in units:
            start, end = max(column, lefts[unit]), min(column + columns, lefts[unit] + widths[unit])
            if start < end:
                found.append((start - column, end - start, both(pair, row, start - lefts[unit])))
        return found

    def own_third(side):
        base = cut_all if side else 0
        items = []
        for i, (column, columns) in enumerate(spans(side)):
            for start, size, views in own_views(3 * eighth, base + column, columns):
                items.append((i * n, start, n, size, views))
        return (third[side][0], items)

    sides_first = exchange_sides(
        build(*beside(sides_out(0, first, corner_first), (own_third(1), own_third(0))))
    )
    high_in = scatter_far(1, inner, sides_in)
    if staged:
        high_down += [exchange(build(high_out(2, down, sides_down, 1, 1, high_down[0]))[0], "dp", 4)]
    weight_rows, momenta_rows, averages_rows = [flat_rows(part, n) for part in (weights, momenta, averages)]
    sides_first, high_in, high_down, weight_rows, momenta_rows, averages_rows = together(
        (sides_first, high_in, high_down, weight_rows, momenta_rows, averages_rows)
    )

    own_outs = []
    for side, row in ((0, eighth), (1, 2 * eighth)):
        items = []
        base = 0 if side == 0 else cut_all
        came = sides_first[1] if side == 0 else sides_first[0]
        edges = [(base + c, w, (came, i * n, widths[0])) for i, (c, w) in enumerate(spans(side))]
        edges.append((cut_all, wide_all - cut_all, None) if side == 0 else (0, cut_all, None))
        for column, columns, view in edges:
            for start, size, views in own_views(row, column, columns):
                if view is not None:
                    views = views + [(view[0], view[1], view[2] + start)]
                items.append((0, column + start, n, size, views))
        own_outs.append(((n, wide_all), items))
    own_sides = exchange_sides(build(*own_outs))
    if staged:
        near, far, farthest = [high_out(0, first, sides_first, d, 1) for d in (1, 2, 3)]
        near_in = high_out(1, inner, sides_in, 1, 1, high_in[0])
        wide = widths[0]
        near = ((n, wide + FF), near[1] + [(0, wide, n, FF, near_in[1][0][4])])
        high_first = [exchange(part, "dp", mask) for part, mask in zip(build(near, far, farthest), (4, 8, 12))]
        high_in += [high_first[0]]
    else:
        high_first = scatter_high(0, first, sides_first)
    comes = (
        [(part, 0) for part in high_first],
        [(part, widths[0] if i else 0) for i, part in enumerate(high_in)],
        [(part, 0) for part in high_down],
    )
    sums = []
    for pair, unit in units:
        views = both(pair, 0, 0) + [(side, 0, lefts[unit]) for side in own_sides]
        sums.append(views + [(part, 0, left) for part, left in comes[unit]])

    learning = rate_scale / math.sqrt(total_tokens)
    arguments = (weight_rows, momenta_rows, averages_rows, weights.shape[1])
    known = update(learning, (2,), sums, *arguments)
    if staged:
        known, high_first[0] = together((known, high_first[0]))
        sums[1][-1] = (high_first[0], 0, widths[0])
    known = update(learning, (1,), sums, *arguments, known)
    if staged:
        known, high_first = together((known, high_first))
        sums[0][-3:] = [(part, 0, 0) for part in high_first]
    momenta_new, averages_new, weights_new, weights_copy = update(learning, (0,), sums, *arguments, known)
    return (
        activations.reshape(acts.shape),
        input_grad.reshape(acts.shape),
        momenta_new,
        averages_new,
        weights_new,
        weights_copy,
    )


def solution(mesh):
    split = ("dp", "fsdp")
    in_specs = (
        P(split, None, None),
        P(split, None, None),
        P(split, None),
        P(split),
        P(split, None),
        P(split, None),
        P(split, None),
    )
    out_specs = (
        P(split, None, None),
        P(split, None, None),
        P(split, None),
        P(split, None),
        P(split, None),
        P(split, None),
    )
    return jax.shard_map(body, mesh=mesh, in_specs=in_specs, out_specs=out_specs, check_vma=False)
```

```python
from functools import partial
import math

import jax
import jax.numpy as jnp
import numpy as np
from jax import lax
from jax.experimental import pallas as pl
from jax.experimental.pallas import tpu as pltpu
from jax.sharding import PartitionSpec as P

D = 768
H = 12
HD = 64
FF = 3072
NB = 320
HALF = NB // 2
P_SIZE = 512
NPOS = 4372
LANES = 128
KEYS = 384
BF = jnp.bfloat16
F32 = jnp.float32

deep_alpha = 24.0**0.25
layer_epsilon = 1e-05
masked_score = -1000000000.0
far_distance = 800
gate_units = 8
momentum_rate = 0.9
average_rate = 0.8
decay_rate = 0.0001
rate_scale = 0.04
far_place = 1 << 20


def bucket_levels(span):
    distance = np.arange(0, span + 1)
    exact = HALF // 2
    logscale = (
        np.log(np.maximum(distance, 1) / exact) / np.log(far_distance / exact) * (HALF - exact)
    )
    beyond = np.minimum(exact + np.floor(logscale).astype(np.int64), HALF - 1)
    return np.where(distance < exact, distance, beyond)


def far_marks():
    levels = bucket_levels(2 * P_SIZE)
    rises = np.diff(levels)
    marks = np.repeat(np.arange(1, 2 * P_SIZE + 1), rises)
    return [int(m) for m in marks[HALF // 2 :]]


def key_ends():
    span = 2 * P_SIZE
    levels = bucket_levels(span)
    offsets = np.arange(-span, span + 1)
    level = levels[np.abs(offsets)]
    keys = np.where(offsets > 0, HALF + level, HALF - 1 - level)
    ends = np.full((KEYS,), far_place // 2, np.int32)
    for key in range(NB - 1):
        below = offsets[keys <= key]
        ends[key] = below.max() if below.size else -(far_place // 2)
    return ends


def exchange(value, axis, mask):
    count = lax.axis_size(axis)
    return lax.ppermute(value, axis, [(i, i ^ mask) for i in range(count)])


def high_bits(count):
    return list(range(2, count.bit_length() - 1))


def exchange_sides(pair):
    return exchange(pair[0], "dp", 1), exchange(pair[1], "dp", 2)


def exchange_core(value):
    return exchange(value, "fsdp", 1)


def slot_order(dp, core, count):
    high = count // 4
    core_step, low, up = np.meshgrid(np.arange(2), np.arange(4), np.arange(high), indexing="ij")
    distance = jnp.asarray((up * 4 + low).reshape(-1).astype(np.int32))
    core_distance = jnp.asarray(core_step.reshape(-1).astype(np.int32))
    return (distance ^ dp) * 2 + (core_distance ^ core)


def prep_kernel(marks, shape_ref, mask_ref, ends_ref, bucket_ref, rank_ref, valid_ref):
    clips, patches = mask_ref.shape
    slots = bucket_ref.shape[1]
    mask = mask_ref[...]
    up = lax.broadcasted_iota(jnp.int32, (patches, patches), 0)
    across = lax.broadcasted_iota(jnp.int32, (patches, patches), 1)
    running = wide_dot(mask.astype(F32).astype(BF), (up <= across).astype(F32).astype(BF))
    ranks = jnp.where(mask == 1, running.astype(jnp.int32) - 1, -1)
    slot = lax.broadcasted_iota(jnp.int32, (slots, patches), 0)
    patch = lax.broadcasted_iota(jnp.int32, (slots, patches), 1)
    pair = lax.broadcasted_iota(jnp.int32, (8, patches), 1)
    halves = jnp.where(lax.broadcasted_iota(jnp.int32, (8, patches), 0) == 0, pair >> 4, pair & 15)
    halves = halves.astype(F32).astype(BF)
    for clip in range(clips):
        found = ranks[clip : clip + 1, :] == slot
        column = jnp.sum(jnp.where(found, patch, 0), axis=1, keepdims=True)
        both = nt(halves, found.astype(F32).astype(BF)).astype(jnp.int32)
        row = 16 * both[0:1, :] + both[1:2, :]
        narrow = shape_ref[clip] > 0
        column = jnp.where(narrow, 8 * (column >> 2) + (column & 3), column)
        row = jnp.where(narrow, 8 * (row >> 2) + (row & 3), row)
        count = jnp.sum(mask[clip : clip + 1, :], axis=1, keepdims=True)
        valid = lax.broadcasted_iota(jnp.int32, (slots, 1), 0) < count
        valid_ref[clip * slots : (clip + 1) * slots, :] = valid.astype(F32)
        offset = column - row
        distance = jnp.abs(offset)
        level = jnp.minimum(distance, HALF // 2)
        for mark in marks:
            level = level + (distance >= mark).astype(jnp.int32)
        bucket_ref[clip] = level + jnp.where(offset > 0, HALF, 0)
        away = jnp.where(valid, offset, far_place)
        for first in range(slots):
            seen = away[:, first : first + 1] <= ends_ref[...]
            rank_ref[clip, first : first + 1, :] = jnp.sum(seen.astype(jnp.int32), axis=0, keepdims=True)


def prep(mask, shape_id, slots):
    clips = mask.shape[0]
    ends = jnp.asarray(key_ends())[None, :]
    return call(
        partial(prep_kernel, far_marks()),
        (mask, ends),
        (
            shaped((clips, slots, slots), jnp.int32),
            shaped((clips, slots, KEYS), jnp.int32),
            shaped((clips * slots, 1), F32),
        ),
        8,
        "prep",
        scalars=(shape_id,),
    )


def position_rows(shards, by_key):
    width = (NPOS + shards - 1) // shards
    index = np.full((24, KEYS), -1, np.int64)
    for head in range(H):
        for lane in range(NB):
            bucket = (HALF - 1 - lane if lane < HALF else lane) if by_key else lane
            index[head, lane] = bucket * H + head
    for unit in range(gate_units):
        index[12 + unit, :HD] = NB * H + np.arange(HD) * gate_units + unit
    index[20, :gate_units] = (NB + 0) * H + HD * gate_units + np.arange(gate_units)
    index[21, :H] = NB * H + (HD + 1) * gate_units + np.arange(H)
    pieces = np.where(index >= 0, index // width, -1).astype(np.int32)
    columns = np.where(index >= 0, 12 * D // shards + index % width, -1).astype(np.int32)
    return jnp.asarray(pieces), jnp.asarray(columns)


def vector_chunks(shards):
    width = 12 * D // shards
    size = math.gcd(width, D)
    each, across = width // size, D // size
    return size, [
        (g // each, g % each * size, g // across, g % across * size) for g in range(12 * across)
    ]


def unpack_kernel(shards, turn_ref, pieces_ref, columns_ref, *refs):
    whole_ref, vectors_ref, bias_ref, table_ref, natural_ref, small_ref = refs
    natural_ref[...] = wide_dot(turn_ref[...], whole_ref[:, 4 * D :])
    each = D // shards
    wide = small_ref.shape[1]
    for k in range(wide // LANES):
        small_ref[:, k * LANES : (k + 1) * LANES] = natural_ref[pl.ds(k, shards, stride=each), :]
    size, chunks = vector_chunks(shards)
    for piece, column, row, place in chunks:
        value = small_ref[piece : piece + 1, column : column + size]
        if row < 8:
            vectors_ref[row : row + 1, place : place + size] = value
        else:
            bias_ref[:, (row - 8) * D + place : (row - 8) * D + place + size] = value
    start = 12 * D // shards // LANES * LANES
    small = small_ref[:, start:].astype(BF)
    piece_ids = lax.broadcasted_iota(jnp.int32, (shards, KEYS), 0)
    column_ids = lax.broadcasted_iota(jnp.int32, (wide - start, KEYS), 0) + start
    for row in range(22):
        chosen = (piece_ids == pieces_ref[row : row + 1, :]).astype(F32).astype(BF)
        spread = tn(small, chosen)
        table_ref[row : row + 1, :] = jnp.sum(
            jnp.where(column_ids == columns_ref[row : row + 1, :], spread, 0.0), axis=0, keepdims=True
        )
    table_ref[22:24, :] = jnp.zeros((2, KEYS), F32)


def small_lanes(shards):
    return -(-(12 * D // shards + (NPOS + shards - 1) // shards) // LANES) * LANES


def unpack(shards, turn, whole):
    pieces, columns = position_rows(shards, False)
    return call(
        partial(unpack_kernel, shards),
        (turn, pieces, columns, whole),
        (shaped((8, D), F32), shaped((1, FF), F32), shaped((24, KEYS), F32)),
        8,
        "unpack",
        scratch=(
            pltpu.VMEM((D, LANES), F32),
            pltpu.VMEM((shards, small_lanes(shards)), F32),
        ),
    )


def pack_kernel(shards, turn_ref, pieces_ref, columns_ref, attention_ref, first_ref, second_ref, bias_ref, table_ref, out_ref, natural_ref, small_ref):
    each = D // shards
    wide = small_ref.shape[1]
    table = table_ref[...]
    lane = lax.broadcasted_iota(jnp.int32, table.shape, 1)
    row_id = lax.broadcasted_iota(jnp.int32, table.shape, 0)
    before = jnp.where((lane > 0) & (row_id < H), pltpu.roll(table, 1, 1), 0.0)
    table = table - before
    piece_ids = lax.broadcasted_iota(jnp.int32, (shards, KEYS), 0)
    start = 12 * D // shards // LANES * LANES
    column_ids = lax.broadcasted_iota(jnp.int32, (wide - start, KEYS), 0) + start
    total = jnp.zeros((shards, wide - start), F32)
    for row in range(22):
        chosen = jnp.where(piece_ids == pieces_ref[row : row + 1, :], table[row : row + 1, :], 0.0).astype(BF)
        spread = (column_ids == columns_ref[row : row + 1, :]).astype(F32).astype(BF)
        total = total + nt(chosen, spread)
    small_ref[...] = jnp.zeros(small_ref.shape, F32)
    small_ref[:, start:] = total
    rows = [(attention_ref, 0), (attention_ref, 1)]
    rows += [(first_ref, i) for i in range(3)] + [(second_ref, i) for i in range(3)]
    size, chunks = vector_chunks(shards)
    for piece, column, row, place in chunks:
        if row < 8:
            ref, at = rows[row]
            value = ref[at : at + 1, place : place + size]
        else:
            value = bias_ref[:, (row - 8) * D + place : (row - 8) * D + place + size]
        small_ref[piece : piece + 1, column : column + size] = value
    natural_ref[...] = jnp.zeros(natural_ref.shape, F32)
    for k in range(wide // LANES):
        natural_ref[pl.ds(k, shards, stride=each), :] = small_ref[:, k * LANES : (k + 1) * LANES]
    out_ref[...] = tn(turn_ref[...], natural_ref[...].astype(BF)).astype(BF)


def pack(shards, turn, sums_attention, sums_first, sums_second, bias, table):
    pieces, columns = position_rows(shards, True)
    return call(
        partial(pack_kernel, shards),
        (turn, pieces, columns, sums_attention, sums_first, sums_second, bias, table),
        (shaped((D, LANES), BF),),
        8,
        "pack",
        scratch=(pltpu.VMEM((D, LANES), F32), pltpu.VMEM((shards, small_lanes(shards)), F32)),
    )[0]


def lookup(table_ref, head, index, block):
    out = None
    for part in range(KEYS // LANES):
        row = jnp.broadcast_to(table_ref[head : head + 1, part * LANES : (part + 1) * LANES], index.shape)
        found = jnp.take_along_axis(row, index, axis=1, mode="promise_in_bounds")
        out = found if out is None else jnp.where(block == part, found, out)
    return out


def nt(a, b):
    return lax.dot_general(a, b, (((1,), (1,)), ((), ())), preferred_element_type=F32)


def tn(a, b):
    return lax.dot_general(a, b, (((0,), (0,)), ((), ())), preferred_element_type=F32)


def vmem(count):
    return [pl.BlockSpec(memory_space=pltpu.VMEM)] * count


def limits(mib):
    return pltpu.CompilerParams(vmem_limit_bytes=mib * 1024 * 1024)


def shaped(shape, dtype):
    return jax.ShapeDtypeStruct(tuple(shape), dtype)


def call(kernel, operands, outs, mib, name, scalars=(), scratch=()):
    return pl.pallas_call(
        kernel,
        out_shape=tuple(outs),
        in_specs=[pl.BlockSpec(memory_space=pltpu.SMEM)] * len(scalars) + vmem(len(operands)),
        out_specs=tuple(vmem(len(outs))),
        scratch_shapes=list(scratch),
        compiler_params=limits(mib),
        cost_estimate=pl.CostEstimate(flops=1, bytes_accessed=1, transcendentals=0),
        name=name,
    )(*scalars, *operands)


def build_kernel(plans, count, *refs):
    sources, outs = refs[:count], refs[count:]
    for out, (whole, items) in zip(outs, plans):
        if not whole:
            out[...] = jnp.zeros(out.shape, out.dtype)
        for row, column, rows, columns, views in items:
            values = [
                sources[which][first : first + rows, left : left + columns] for which, first, left in views
            ]
            if len(values) > 1:
                values = [sum(value.astype(F32) for value in values)]
            out[row : row + rows, column : column + columns] = values[0].astype(out.dtype)


def build(*outs):
    sources, plans = [], []
    for shape, items in outs:
        plan = []
        for row, column, rows, columns, views in items:
            found = []
            for array, first, left in views:
                at = next((i for i, source in enumerate(sources) if source is array), None)
                if at is None:
                    at = len(sources)
                    sources.append(array)
                found.append((at, first, left))
            plan.append((row, column, rows, columns, found))
        plans.append((sum(item[2] * item[3] for item in items) == math.prod(shape), plan))
    return call(
        partial(build_kernel, plans, len(sources)), sources, [shaped(shape, BF) for shape, _ in outs], 8, "build"
    )


def stack(parts):
    items, at = [], 0
    for array, row, rows, column, columns in parts:
        items.append((at, 0, rows, columns, [(array, row, column)]))
        at += rows
    return (at, parts[0][4]), items


def whole_of(array):
    return (array, 0, array.shape[0], 0, array.shape[1])


def normal(entries):
    centre = entries - jnp.mean(entries, axis=-1, keepdims=True)
    scale = lax.rsqrt(jnp.mean(centre * centre, axis=-1, keepdims=True) + layer_epsilon)
    return centre * scale, scale


def normal_back(grad, unit, scale):
    return scale * (
        grad
        - jnp.mean(grad, axis=-1, keepdims=True)
        - unit * jnp.mean(grad * unit, axis=-1, keepdims=True)
    )


def wide_dot(a, b):
    return jnp.dot(a, b, preferred_element_type=F32)


def split(value, count):
    parts = []
    for _ in range(count):
        parts.append(value.astype(BF))
        value = value - parts[-1].astype(F32)
    return parts


def joined_kernel(
    x_ref, turn_ref, vectors_ref, table_ref, whole_ref, slots_ref, joined_ref, gate_ref, logits_ref
):
    slots_ref[...] = wide_dot(x_ref[...], turn_ref[...]).astype(BF)
    for part in range(3):
        cols = slice(part * D, (part + 1) * D)
        made = wide_dot(slots_ref[...], whole_ref[:, cols])
        if part != 1:
            made = made + vectors_ref[part // 2 : part // 2 + 1, :]
        joined_ref[:, cols] = made.astype(BF)
    units = table_ref[12:20, :HD].astype(BF)
    logits_ref[...] = jnp.zeros(logits_ref.shape, F32)
    for head in range(H):
        logits_ref[:, head * gate_units : (head + 1) * gate_units] = (
            nt(x_ref[:, head * HD : (head + 1) * HD], units) + table_ref[20:21, :gate_units]
        )
    up = lax.broadcasted_iota(jnp.int32, (LANES, LANES), 0)
    across = lax.broadcasted_iota(jnp.int32, (LANES, LANES), 1)
    logits = split(logits_ref[...], 3)
    gates = []
    for side in range(2):
        chosen = ((up >> 3) == across) & (((up >> 2) & 1) == side)
        chosen = chosen.astype(F32).astype(BF)
        gates.append(jax.nn.sigmoid(sum(wide_dot(part, chosen) for part in logits)))
    first, second = gates
    gate_ref[0] = first * (second * table_ref[21:22, :LANES] - 1.0) + 2.0
    gate_ref[1] = first
    gate_ref[2] = second


def joined_forward(x, turn, vectors, table, whole):
    rows = x.shape[0]
    return call(
        joined_kernel,
        (x, turn, vectors, table, whole),
        (
            shaped((rows, D), BF),
            shaped((rows, 3 * D), BF),
            shaped((3, rows, LANES), F32),
        ),
        8,
        "joined_forward",
        scratch=(pltpu.VMEM((rows, LANES), F32),),
    )


def attention_kernel(clip, bucket_ref, valid_ref, table_ref, joined_ref, gate_ref, prob_ref, rel_ref, mixed_ref):
    slots = bucket_ref.shape[1]
    rows = slice(clip * slots, (clip + 1) * slots)
    index = bucket_ref[clip] & (LANES - 1)
    block = bucket_ref[clip] >> 7
    valid = valid_ref[rows, :] > 0
    gate = jnp.transpose(gate_ref[0, rows, :])
    for head in range(H):
        rel_ref[head] = lookup(table_ref, head, index, block)
    for head in range(H):
        query = joined_ref[rows, head * HD : (head + 1) * HD]
        key = joined_ref[rows, D + head * HD : D + (head + 1) * HD]
        score = nt(key, query) * (1.0 / math.sqrt(HD)) + gate[head : head + 1, :] * rel_ref[head]
        prob_ref[head] = jnp.where(valid, score, masked_score)
    for first in range(0, H, 4):
        score = prob_ref[first : first + 4]
        power = jnp.exp(score - jnp.max(score, axis=1, keepdims=True))
        prob_ref[first : first + 4] = power * (1.0 / jnp.sum(power, axis=1, keepdims=True))
    for head in range(H):
        value = joined_ref[rows, 2 * D + head * HD : 2 * D + (head + 1) * HD]
        mixed_ref[head * HD : (head + 1) * HD, :] = tn(value, prob_ref[head].astype(BF)).astype(BF)


def attention(clip, bucket, valid, table, joined, gate):
    slots = bucket.shape[1]
    return call(
        partial(attention_kernel, clip),
        (bucket, valid, table, joined, gate),
        (shaped((H, slots, slots), F32), shaped((H, slots, slots), F32), shaped((D, slots), BF)),
        4,
        "attention",
    )


def out_kernel(x_ref, turn_ref, vectors_ref, whole_ref, *refs):
    mixed_ref, unit_ref, scale_ref, slots_ref = refs[-4:]
    at = 0
    for part in refs[:-4]:
        rows = slice(at, at + part.shape[1])
        mixed_ref[rows, :] = tn(part[...], turn_ref[...]).astype(BF)
        at += part.shape[1]
    branch = wide_dot(mixed_ref[...], whole_ref[:, 3 * D : 4 * D]) + vectors_ref[2:3, :]
    unit, scale = normal(deep_alpha * x_ref[...].astype(F32) + branch)
    unit_ref[...] = unit
    scale_ref[...] = scale
    low = (unit * vectors_ref[3:4, :] + vectors_ref[4:5, :]).astype(BF)
    slots_ref[...] = wide_dot(low, turn_ref[...]).astype(BF)


def out_forward(x, turn, vectors, whole, mixed):
    rows = x.shape[0]
    return call(
        out_kernel,
        (x, turn, vectors, whole, *mixed),
        (shaped((rows, D), BF), shaped((rows, D), F32), shaped((rows, 1), F32), shaped((rows, D), BF)),
        6,
        "out_forward",
    )


def attention_back_kernel(
    clip, joined_ref, gate_ref, rank_ref, prob_ref, rel_ref, grad_ref, tri_ref,
    joined_grad_ref, gate_grad_ref, table_grad_ref,
):
    slots = rank_ref.shape[1]
    rows = slice(clip * slots, (clip + 1) * slots)
    scale = 1.0 / math.sqrt(HD)
    gate = jnp.transpose(gate_ref[0, rows, :])
    for head in range(H):
        cols = slice(head * HD, (head + 1) * HD)
        key_cols = slice(D + head * HD, D + (head + 1) * HD)
        value_cols = slice(2 * D + head * HD, 2 * D + (head + 1) * HD)
        query = joined_ref[rows, cols]
        key = joined_ref[rows, key_cols]
        value = joined_ref[rows, value_cols]
        grad = grad_ref[rows, cols]
        prob = prob_ref[head]
        joined_grad_ref[:, value_cols] = wide_dot(prob.astype(BF), grad).astype(BF)
        weighted = prob * nt(value, grad)
        low = (weighted - prob * jnp.sum(weighted, axis=0, keepdims=True)).astype(BF)
        joined_grad_ref[:, cols] = (tn(low, key) * scale).astype(BF)
        joined_grad_ref[:, key_cols] = (wide_dot(low, query) * scale).astype(BF)
        wide = low.astype(F32)
        gate_grad_ref[head : head + 1, :] = jnp.sum(wide * rel_ref[head], axis=0, keepdims=True)
        gated = wide * gate[head : head + 1, :]
        high = gated.astype(BF)
        rest = (gated - high.astype(F32)).astype(BF)
        running = tn(high, tri_ref[...]) + tn(rest, tri_ref[...])
        for part in range(KEYS // LANES):
            lanes = slice(part * LANES, (part + 1) * LANES)
            rank = rank_ref[clip, :, lanes]
            found = jnp.take_along_axis(
                running, jnp.maximum(rank - 1, 0), axis=1, mode="promise_in_bounds"
            )
            table_grad_ref[head : head + 1, lanes] = jnp.sum(
                jnp.where(rank > 0, found, 0.0), axis=0, keepdims=True
            )
    table_grad_ref[H:, :] = jnp.zeros((16 - H, KEYS), F32)
    gate_grad_ref[H:, :] = jnp.zeros((16 - H, slots), F32)


def attention_back(clip, joined, gate, rank, prob, rel, grad):
    slots = rank.shape[1]
    tri = jnp.asarray(np.triu(np.ones((slots, slots), np.float32)), BF)
    return call(
        partial(attention_back_kernel, clip),
        (joined, gate, rank, prob, rel, grad, tri),
        (shaped((slots, 3 * D), BF), shaped((16, slots), F32), shaped((16, KEYS), F32)),
        4,
        "attention_back",
    )


def gate_back_kernel(count, x_ref, table_ref, gate_ref, *refs):
    joined_grads, gate_grads, table_grads = refs[:count], refs[count : 2 * count], refs[2 * count : 3 * count]
    x_grad_ref, table_grad_ref, sums_ref = refs[3 * count :]
    table_grad_ref[...] = jnp.zeros(table_grad_ref.shape, F32)
    table_grad_ref[:16, :] = sum(ref[...] for ref in table_grads)
    sums_ref[0:1, :] = sum(jnp.sum(ref[:, :D].astype(F32), axis=0, keepdims=True) for ref in joined_grads)
    sums_ref[1:2, :] = sum(jnp.sum(ref[:, 2 * D :].astype(F32), axis=0, keepdims=True) for ref in joined_grads)
    units = [jnp.sum(table_ref[12 + 4 * i : 16 + 4 * i, :HD], axis=0, keepdims=True) for i in range(2)]
    unit_grads = [jnp.zeros((1, HD), F32), jnp.zeros((1, HD), F32)]
    grad = jnp.concatenate([jnp.transpose(ref[...]) for ref in gate_grads], axis=0)
    first, second = gate_ref[1, :, :16], gate_ref[2, :, :16]
    size = table_ref[21:22, :16]
    grads = (
        grad * (second * size - 1.0) * first * (1.0 - first),
        grad * first * size * second * (1.0 - second),
    )
    table_grad_ref[21:22, :16] = jnp.sum(grad * first * second, axis=0, keepdims=True)
    bias_grads = [jnp.sum(jnp.sum(g, axis=0, keepdims=True), axis=1, keepdims=True) for g in grads]
    for head in range(H):
        cols = slice(head * HD, (head + 1) * HD)
        x = x_ref[:, cols].astype(F32)
        sides = [g[:, head : head + 1] for g in grads]
        x_grad_ref[:, cols] = sides[0] * units[0] + sides[1] * units[1]
        for i in range(2):
            unit_grads[i] = unit_grads[i] + jnp.sum(x * sides[i], axis=0, keepdims=True)
    for unit in range(gate_units):
        table_grad_ref[12 + unit : 13 + unit, :HD] = unit_grads[unit // 4]
        table_grad_ref[20:21, unit : unit + 1] = bias_grads[unit // 4]


def gate_back(x, table, gate, joined_grads, gate_grads, table_grads):
    return call(
        partial(gate_back_kernel, len(joined_grads)),
        (x, table, gate, *joined_grads, *gate_grads, *table_grads),
        (shaped(x.shape, F32), shaped((24, KEYS), F32), shaped((8, D), F32)),
        6,
        "gate_back",
    )


def gelu_pair(u):
    size = jnp.abs(u) * math.sqrt(0.5)
    t = 1.0 / (1.0 + 0.3275911 * size)
    poly = ((((1.061405429 * t - 1.453152027) * t + 1.421413741) * t - 0.284496736) * t + 0.254829592) * t
    bell = jnp.exp(-0.5 * u * u)
    tail = 0.5 * poly * bell
    below = jnp.where(u < 0, tail, 1.0 - tail)
    return u * below, below + u * bell * (1.0 / math.sqrt(2.0 * math.pi))


def hidden_kernel(slots_ref, bias_ref, whole_ref, active_ref, slope_ref):
    width = FF // 8
    for block in range(8):
        cols = slice(block * width, (block + 1) * width)
        u = wide_dot(slots_ref[...], whole_ref[:, cols]) + bias_ref[:, cols]
        active, slope = gelu_pair(u)
        active_ref[:, cols] = active.astype(BF)
        slope_ref[:, cols] = slope


def hidden_forward(slots, bias, whole):
    rows = slots.shape[0]
    return call(
        hidden_kernel,
        (slots, bias, whole),
        (shaped((rows, FF), BF), shaped((rows, FF), F32)),
        10,
        "hidden_forward",
    )


def layer_turn(made, unit_ref, vectors_ref, valid_ref, cot_ref, out_ref, second_ref, low_ref, sums_ref):
    made = made + vectors_ref[5:6, :]
    first_norm = unit_ref[...] * vectors_ref[3:4, :] + vectors_ref[4:5, :]
    unit, scale = normal(deep_alpha * first_norm + made.astype(BF).astype(F32))
    valid = valid_ref[...]
    gain = vectors_ref[6:7, :]
    out_ref[...] = ((unit * gain + vectors_ref[7:8, :]) * valid).astype(BF)
    grad = cot_ref[...].astype(F32) * valid
    second = normal_back(grad * gain, unit, scale)
    second_ref[...] = second
    low = second.astype(BF)
    low_ref[...] = low
    sums_ref[0:1, :] = jnp.sum(low.astype(F32), axis=0, keepdims=True)
    sums_ref[1:2, :] = jnp.sum(grad * unit, axis=0, keepdims=True)
    sums_ref[2:3, :] = jnp.sum(grad, axis=0, keepdims=True)


def turn_kernel(slots, ranges, each, *refs):
    at_ref, active_ref, unit_ref, vectors_ref, valid_ref, cot_ref = refs[:6]
    count = 5 + len(ranges)
    parts = refs[6:-count]
    whole_ref, out_ref, second_ref, low_ref, sums_ref, *corners = refs[-count:]
    for slot, (which, row, rows, column) in enumerate(slots):
        place = pl.multiple_of(at_ref[slot], 16)
        if parts[which].shape[1] == D:
            whole_ref[pl.ds(place, rows), :] = parts[which][row : row + rows, :]
            continue
        blocks = [
            parts[which][row : row + rows, column + j * D : column + (j + 1) * D] for j in range(FF // D)
        ]
        whole_ref[pl.ds(place, rows * len(blocks)), :] = jnp.concatenate(blocks, axis=0)
    made = wide_dot(active_ref[...], whole_ref[...])
    layer_turn(made, unit_ref, vectors_ref, valid_ref, cot_ref, out_ref, second_ref, low_ref, sums_ref)
    if ranges:
        for half in range(2):
            down_back_kernel(ranges[half : half + 1], each, parts[half - 2], low_ref, corners[half])


def turn_back(at, slots, active, unit, vectors, valid, cot, parts, turned=None, ranges=(), each=0):
    rows = unit.shape[0]
    outs = [shaped((FF, D), BF), shaped((rows, D), BF), shaped((rows, D), F32), shaped((rows, D), BF)]
    outs.append(shaped((8, D), F32))
    outs += [shaped(((last - first) * each, FF), BF) for first, last in ranges]
    extra = [turned, turned] if ranges else []
    return call(
        partial(turn_kernel, slots, ranges, each),
        (active, unit, vectors, valid, cot, *parts, *extra),
        outs,
        10,
        "turn_back",
        scalars=(at,),
    )


def place_slots(slots, parts, at_ref, first, whole_ref):
    for slot, (which, row, rows, column) in enumerate(slots):
        place = pl.multiple_of(at_ref[first + slot], 16)
        blocks = [
            parts[which][row : row + rows, column + j * D : column + (j + 1) * D] for j in range(FF // D)
        ]
        whole_ref[pl.ds(place, rows * len(blocks)), :] = jnp.concatenate(blocks, axis=0)


def partial_kernel(slots, late, at_ref, active_ref, *refs):
    *parts, whole_ref, made_ref = refs
    place_slots(slots, parts, at_ref, 0, whole_ref)
    chunk = FF // (len(slots) + late)
    for slot in range(len(slots), len(slots) + late):
        place = pl.multiple_of(at_ref[slot], 16)
        whole_ref[pl.ds(place, chunk), :] = jnp.zeros((chunk, D), BF)
    made_ref[...] = wide_dot(active_ref[...], whole_ref[...])


def partial_down(at, slots, late, active, parts):
    return call(
        partial(partial_kernel, slots, late),
        (active, *parts),
        (shaped((FF, D), BF), shaped((active.shape[0], D), F32)),
        8,
        "partial_down",
        scalars=(at,),
    )


def last_kernel(slots, first, ranges, each, *refs):
    at_ref, made_ref, unit_ref, vectors_ref, valid_ref, cot_ref, turned_ref, late_ref, _ = refs[:9]
    whole_ref, out_ref, second_ref, low_ref, sums_ref, *corners, rows_ref = refs[9:]
    place_slots(slots, [late_ref], at_ref, first, whole_ref)
    chunk = each * FF // D
    for slot, (_, row, rows, column) in enumerate(slots):
        for j in range(FF // D):
            at = slot * chunk + j * rows
            rows_ref[at : at + rows, :] = late_ref[row : row + rows, column + j * D : column + (j + 1) * D]
    made = made_ref[...] + tn(turned_ref[first * chunk :, :], rows_ref[...])
    layer_turn(made, unit_ref, vectors_ref, valid_ref, cot_ref, out_ref, second_ref, low_ref, sums_ref)
    for half in range(2):
        down_back_kernel(ranges[half : half + 1], each, turned_ref, low_ref, corners[half])


def last_turn(at, slots, first, made, unit, vectors, valid, cot, turned, late, whole, ranges, each):
    rows = unit.shape[0]
    outs = [shaped((FF, D), BF), shaped((rows, D), BF), shaped((rows, D), F32), shaped((rows, D), BF)]
    outs.append(shaped((8, D), F32))
    outs += [shaped(((last - begin) * each, FF), BF) for begin, last in ranges]
    operands = (made, unit, vectors, valid, cot, turned, late, whole)
    return pl.pallas_call(
        partial(last_kernel, slots, first, ranges, each),
        out_shape=tuple(outs),
        in_specs=[pl.BlockSpec(memory_space=pltpu.SMEM)] + vmem(len(operands)),
        out_specs=tuple(vmem(len(outs))),
        input_output_aliases={8: 0},
        scratch_shapes=[pltpu.VMEM((len(slots) * each * FF // D, D), BF)],
        compiler_params=limits(8),
        cost_estimate=pl.CostEstimate(flops=1, bytes_accessed=1, transcendentals=0),
        name="last_turn",
    )(at, *operands)


def turn_active_kernel(rows, at_ref, active_ref, out_ref, turned_ref):
    for first in range(0, FF, FF // 8):
        cols = slice(first, first + FF // 8)
        turned_ref[cols, :] = jnp.transpose(active_ref[:, cols])
    for slot in range(FF // rows):
        place = pl.multiple_of(at_ref[slot], 16)
        out_ref[slot * rows : (slot + 1) * rows, :] = turned_ref[pl.ds(place, rows), :]


def turn_active(at, rows, active):
    return call(
        partial(turn_active_kernel, rows),
        (active,),
        (shaped((FF, active.shape[0]), BF),),
        8,
        "turn_active",
        scalars=(at,),
        scratch=(pltpu.VMEM((FF, active.shape[0]), BF),),
    )[0]


def down_back_kernel(ranges, rows, active_ref, low_ref, *outs):
    chunk = rows * FF // D
    for (first, last), out_ref in zip(ranges, outs):
        for slot in range(first, last):
            made = wide_dot(active_ref[slot * chunk : (slot + 1) * chunk, :], low_ref[...]).astype(BF)
            to = (slot - first) * rows
            for j in range(FF // D):
                out_ref[to : to + rows, j * D : (j + 1) * D] = made[j * rows : (j + 1) * rows, :]


def down_back(ranges, rows, active, low):
    return call(
        partial(down_back_kernel, ranges, rows),
        (active, low),
        [shaped(((last - first) * rows, FF), BF) for first, last in ranges],
        6,
        "down_back",
    )


def hidden_back_kernel(low_ref, down_ref, slope_ref, grad_ref, bias_ref):
    width = FF // 8
    for block in range(8):
        cols = slice(block * width, (block + 1) * width)
        grad = (nt(low_ref[...], down_ref[cols, :]) * slope_ref[:, cols]).astype(BF)
        grad_ref[:, cols] = grad
        bias_ref[:, cols] = jnp.sum(grad.astype(F32), axis=0, keepdims=True)


def hidden_back(low, down, slope):
    rows = low.shape[0]
    return call(
        hidden_back_kernel,
        (low, down, slope),
        (shaped((rows, FF), BF), shaped((1, FF), F32)),
        6,
        "hidden_back",
    )


def in_back_kernel(slots_ref, grad_ref, mine_ref, other_ref):
    width = FF // 4
    for block in range(4):
        cols = slice(block * width, (block + 1) * width)
        made = tn(slots_ref[...], grad_ref[:, cols]).astype(BF)
        mine_ref[:, cols] = made[: D // 2]
        other_ref[:, cols] = made[D // 2 :]


def inner_back_kernel(ranges, each, turned_ref, low_ref, down_ref, slope_ref, slots_ref, main_ref, grad_ref, bias_ref, mine_ref, other_ref):
    down_back_kernel(ranges, each, turned_ref, low_ref, main_ref)
    hidden_back_kernel(low_ref, down_ref, slope_ref, grad_ref, bias_ref)
    in_back_kernel(slots_ref, grad_ref, mine_ref, other_ref)


def inner_back(ranges, each, turned, low, down, slope, slots):
    rows, half = low.shape[0], shaped((D // 2, FF), BF)
    main = shaped(((ranges[0][1] - ranges[0][0]) * each, FF), BF)
    return call(
        partial(inner_back_kernel, ranges, each),
        (turned, low, down, slope, slots),
        (main, shaped((rows, FF), BF), shaped((1, FF), F32), half, half),
        8,
        "inner_back",
    )


def in_back(slots, grad):
    rows = slots.shape[0]
    return call(
        in_back_kernel,
        (slots, grad),
        (shaped((D // 2, FF), BF), shaped((D // 2, FF), BF)),
        6,
        "in_back",
    )


def out_back_kernel(
    grad_ref, in_ref, turn_ref, second_ref, unit_ref, scale_ref, vectors_ref, mixed_ref, out_ref,
    first_ref, weight_ref, mixed_grad_ref, sums_ref,
):
    low = nt(grad_ref[...], in_ref[...]).astype(BF)
    grad = deep_alpha * second_ref[...] + nt(low, turn_ref[...]).astype(BF).astype(F32)
    unit = unit_ref[...]
    first = normal_back(grad * vectors_ref[3:4, :], unit, scale_ref[...])
    first_ref[...] = first
    branch = first.astype(BF)
    sums_ref[0:1, :] = jnp.sum(branch.astype(F32), axis=0, keepdims=True)
    sums_ref[1:2, :] = jnp.sum(grad * unit, axis=0, keepdims=True)
    sums_ref[2:3, :] = jnp.sum(grad, axis=0, keepdims=True)
    weight_ref[...] = tn(mixed_ref[...], branch).astype(BF)
    back = nt(branch, out_ref[:, 3 * D : 4 * D]).astype(BF)
    mixed_grad_ref[...] = nt(back, turn_ref[...]).astype(BF)


def out_back(grad, w_in, turn, second, unit, scale, vectors, mixed, w_first):
    rows = unit.shape[0]
    return call(
        out_back_kernel,
        (grad, w_in, turn, second, unit, scale, vectors, mixed, w_first),
        (shaped((rows, D), F32), shaped((D, D), BF), shaped((rows, D), BF), shaped((8, D), F32)),
        6,
        "out_back",
    )


def first_back_kernel(slots_ref, out_ref, small_ref, *refs):
    *grads, mine_ref, other_ref, grad_ref = refs
    at = 0
    for grad in grads:
        grad_ref[at : at + grad.shape[0], :] = grad[...]
        at += grad.shape[0]
    half = D // 2
    for part in range(3):
        cols = slice(part * D, (part + 1) * D)
        made = tn(slots_ref[...], grad_ref[:, cols]).astype(BF)
        mine_ref[:, cols] = made[:half]
        other_ref[:, cols] = made[half:]
    for ref, rows in ((mine_ref, slice(0, half)), (other_ref, slice(half, D))):
        ref[:, 3 * D : 4 * D] = out_ref[rows, :]
        ref[:, 4 * D :] = small_ref[rows, :]


def first_back(slots, weight_out, small, grads):
    rows = slots.shape[0]
    wide = 4 * D + small.shape[1]
    return call(
        first_back_kernel,
        (slots, weight_out, small, *grads),
        (shaped((D // 2, wide), BF), shaped((D // 2, wide), BF), shaped((rows, 3 * D), BF)),
        6,
        "first_back",
    )


def rows_back_kernel(grad_ref, first_ref, turn_ref, branch_ref, gate_ref, out_ref):
    made = nt(grad_ref[...], first_ref[:, : 3 * D])
    high = made.astype(BF)
    rest = made - high.astype(F32)
    middle = rest.astype(BF)
    last = (rest - middle.astype(F32)).astype(BF)
    turned = nt(high, turn_ref[...]) + nt(middle, turn_ref[...]) + nt(last, turn_ref[...])
    out_ref[...] = turned + deep_alpha * branch_ref[...] + gate_ref[...]


def rows_back(grad, w_first, turn, branch, gate):
    rows = grad.shape[0]
    return call(
        rows_back_kernel,
        (grad, w_first, turn, branch, gate),
        (shaped((rows, D), F32),),
        8,
        "rows_back",
    )[0]


def flat_cuts(each):
    cuts = [(0, row, 0, 3 * D) for row in range(each)]
    cuts += [(0, row, 3 * D, 4 * D) for row in range(each)]
    cuts += [(1, row, 0, FF) for row in range(each)]
    cuts += [(2, row, j * D, (j + 1) * D) for j in range(FF // D) for row in range(each)]
    return cuts + [(0, row, 4 * D, 4 * D + LANES) for row in range(each)]


def flat_runs(each, width):
    at = 0
    for which, row, first, last in flat_cuts(each):
        size = min(last - first, width - at)
        if size > 0:
            yield which, row, first, size, at
        at += last - first


def rows_kernel(flat_ref, first_ref, in_ref, down_ref):
    refs = (first_ref, in_ref, down_ref)
    first_ref[:, 4 * D :] = jnp.zeros((first_ref.shape[0], LANES), F32)
    for which, row, first, size, at in flat_runs(first_ref.shape[0], flat_ref.shape[1]):
        refs[which][row : row + 1, first : first + size] = flat_ref[:, at : at + size]


def pieces_kernel(flat_ref, first_ref, in_ref, down_ref, all_ref, *refs):
    rows_kernel(flat_ref, *refs)
    at = 0
    for ref, low in zip(refs, (first_ref, in_ref, down_ref)):
        low[...] = ref[...].astype(BF)
        all_ref[:, at : at + low.shape[1]] = low[...]
        at += low.shape[1]


def row_widths():
    return (4 * D + LANES, FF, FF)


def flat_rows(flat, each):
    return call(rows_kernel, (flat,), [shaped((each, width), F32) for width in row_widths()], 6, "flat_rows")


def pieces(flat, each):
    widths = row_widths()
    return call(
        pieces_kernel,
        (flat,),
        [shaped((each, width), BF) for width in (*widths, sum(widths))],
        6,
        "pieces",
        scratch=[pltpu.VMEM((each, width), F32) for width in widths],
    )


def update_kernel(learning, plan, sections, spans, known, count, *refs):
    size = len(sections)
    sums, refs = refs[:count], refs[count:]
    weights, momenta, averages, refs = refs[:size], refs[size : 2 * size], refs[2 * size : 3 * size], refs[3 * size :]
    outs, refs = refs[known : known + 4], refs[known + 4 :]
    rows, flats, arrived = refs[: 3 * size], refs[3 * size : -1], refs[-1]
    for i in range(size):
        each, wide = weights[i].shape
        grad = sum(
            sums[which][row : row + each, column : column + wide].astype(F32) for which, row, column in plan[i]
        )
        weight = weights[i][...]
        decayed = grad + decay_rate * weight
        momentum = momentum_rate * momenta[i][...] + decayed
        weight = weight - learning * (decayed + momentum_rate * momentum)
        rows[i][...] = momentum
        rows[size + i][...] = average_rate * averages[i][...] + (1.0 - average_rate) * weight
        rows[2 * size + i][...] = weight
    each = weights[0].shape[0]
    copies = []
    for out, which in zip(range(4), (0, 1, 2, 2)):
        for span, (first, last) in enumerate(spans):
            flat = flats[out * len(spans) + span]
            for section, row, column, width, at in flat_runs(each, outs[out].shape[1]):
                if section in sections and first <= at < last:
                    value = rows[which * size + sections.index(section)][row : row + 1, column : column + width]
                    flat[:, at - first : at - first + width] = value.astype(flat.dtype)
            copies.append(
                pltpu.make_async_copy(
                    flat, outs[out].at[:, pl.ds(first, last - first)], arrived.at[out * len(spans) + span]
                )
            )
            copies[-1].start()
    for copy in copies:
        copy.wait()


def update(learning, sections, sums, weights, momenta, averages, width, known=()):
    arrays, plan = [], []
    for section in sections:
        found = []
        for array, row, column in sums[section]:
            at = next((i for i, other in enumerate(arrays) if other is array), None)
            if at is None:
                at = len(arrays)
                arrays.append(array)
            found.append((at, row, column))
        plan.append(found)
    each = weights[0].shape[0]
    runs = [(at, at + size) for section, _, _, size, at in flat_runs(each, width) if section in sections]
    spans = []
    for first, last in runs:
        if spans and spans[-1][1] == first:
            spans[-1] = (spans[-1][0], last)
        else:
            spans.append((first, last))
    rows = [[part[section] for section in sections] for part in (weights, momenta, averages)]
    dtypes = (F32, F32, F32, BF)
    operands = [*arrays, *rows[0], *rows[1], *rows[2]]
    anywhere = pl.BlockSpec(memory_space=pl.ANY)
    return pl.pallas_call(
        partial(update_kernel, learning, plan, list(sections), spans, len(known), len(arrays)),
        out_shape=tuple(shaped((1, width), dtype) for dtype in dtypes),
        in_specs=vmem(len(operands)) + [anywhere] * len(known),
        out_specs=(anywhere,) * 4,
        input_output_aliases={len(operands) + i: i for i in range(len(known))},
        scratch_shapes=[pltpu.VMEM(part.shape, F32) for part in rows[0]] * 3
        + [pltpu.VMEM((1, last - first), dtype) for dtype in dtypes for first, last in spans]
        + [pltpu.SemaphoreType.DMA((4 * len(spans),))],
        compiler_params=limits(10),
        cost_estimate=pl.CostEstimate(flops=1, bytes_accessed=1, transcendentals=0),
        name="update",
    )(*operands, *known)


def body(acts, cotangent, mask, shape_id, weights, momenta, averages):
    shards = lax.axis_size(("dp", "fsdp"))
    count = lax.axis_size("dp")
    dp, core = lax.axis_index("dp"), lax.axis_index("fsdp")
    clips, slots = acts.shape[0], acts.shape[1]
    rows = clips * slots
    total_tokens = rows * shards
    piece_rows = D // shards
    wide_rows = FF // shards
    vector_width = 12 * D // shards
    position_width = (NPOS + shards - 1) // shards
    small_width = vector_width + position_width

    piece_first, piece_in, piece_down, piece_all = pieces(weights, piece_rows)

    order = slot_order(dp, core, count)
    row_order = (order[:, None] * piece_rows + jnp.arange(piece_rows, dtype=jnp.int32)).reshape(-1)
    turn = (jnp.arange(D, dtype=jnp.int32)[:, None] == row_order[None, :]).astype(BF)
    piece_turn = (jnp.arange(shards, dtype=jnp.int32)[:, None] == order[None, :]).astype(BF)

    back_order = jnp.dot(piece_turn.astype(F32), jnp.arange(shards, dtype=F32)).astype(jnp.int32)

    together = lax.optimization_barrier
    bits = high_bits(count)
    staged = len(bits) == 2
    n = piece_rows
    rest = D // 8 - n
    widths = (piece_first.shape[1], FF, FF)
    lefts = (0, widths[0], widths[0] + FF)
    cuts = (13 * LANES, FF // 2, FF // 2)
    wide_all, cut_all = sum(widths), 37 * LANES
    third = (13 * LANES, 12 * LANES, 12 * LANES), (12 * LANES,) * 3
    at = order * wide_rows
    inputs_low = acts.reshape(rows, D)

    def gather_high(piece, direct=False):
        if staged:
            if direct:
                return [exchange(piece, "dp", d << 2) for d in (1, 2, 3)]
            two = exchange(piece, "dp", 8)
            return [exchange(piece, "dp", 4), two, exchange(two, "dp", 4)]
        column = piece
        for bit in bits:
            column = jnp.concatenate([column, exchange(column, "dp", 1 << bit)], axis=0)
        return [column[n:]]

    def thirds(side, views):
        left = widths[0]
        items, column = [], 0
        for i, size in enumerate(third[side]):
            items += views(i * n, left, column, size)
            column += size
        return items

    own_sides = exchange_sides((piece_all, piece_all))
    high_first = gather_high(piece_first)
    own_sides, high_first, piece_in, mask, turn, at = together(
        (own_sides, high_first, piece_in, mask, turn, at)
    )

    items = stack([whole_of(part) for part in high_first])[1]
    sends = build(
        ((rest, widths[0]), items),
        (
            (rest, widths[0] + third[1][0]),
            items + thirds(1, lambda row, left, c, w: [(row, left, n, w, [(own_sides[1], 0, cut_all + c)])]),
        ),
        (
            (rest, widths[0] + third[0][0]),
            items + thirds(0, lambda row, left, c, w: [(row, left, n, w, [(own_sides[0], 0, c)])]),
        ),
    )
    rest_first, sends = sends[0], sends[1:]
    sides_first = exchange_sides(sends)
    high_in = gather_high(piece_in, True)
    bucket, rank, valid_rows = prep(mask, shape_id, slots)
    sides_first, high_in, piece_down, bucket, rank, valid_rows = together(
        (sides_first, high_in, piece_down, bucket, rank, valid_rows)
    )

    def corner_sends(unit, sides):
        wide, half = widths[unit], cuts[unit]
        return (
            ((rest, wide - half), [(0, 0, rest, wide - half, [(sides[1], 0, half)])]),
            ((rest, half), [(0, 0, rest, half, [(sides[0], 0, 0)])]),
        )

    def corner_items(unit, corner):
        wide, half = widths[unit], cuts[unit]
        (second, left_second), (first, left_first) = corner
        return [
            (0, 0, rest, half, [(first, 0, left_first)]),
            (0, half, rest, wide - half, [(second, 0, left_second)]),
        ]

    def early_rows(unit, piece, high, sides):
        wide = widths[unit]
        return stack([whole_of(piece), whole_of(high)] + [(side, 0, rest, 0, wide) for side in sides])

    def shifted(items, row):
        return [(row + item[0], *item[1:]) for item in items]

    def slots_of(unit, piece, high, sides, corner, early, late):
        wide, left = widths[unit], lefts[unit]
        own_mine, own_other = own
        items = [(0, 0, n, wide, [(piece, 0, 0)]), (n, 0, rest, wide, [(high, 0, 0)])]
        eighth = D // 8
        for i in range(3):
            items.append(((i + 1) * eighth, 0, n, wide, [(own_mine, i * n, left)]))
        for i, side in enumerate(sides):
            items.append(((i + 1) * eighth + n, 0, rest, wide, [(side, 0, 0)]))
        items += shifted(corner_items(unit, corner), 3 * eighth + n)
        base = D // 2
        if not isinstance(early, tuple):
            early = (early, 0), (early, n + rest)
        (one, row_one), (two, row_two) = early
        items.append((base, 0, n, wide, [(one, row_one, 0)]))
        items.append((base + n, 0, rest, wide, [(one, row_one + n, 0)]))
        for i in range(3):
            items.append((base + (i + 1) * eighth, 0, n, wide, [(own_other, i * n, left)]))
            view = late if i == 2 else (two, row_two + i * rest, 0)
            items.append((base + (i + 1) * eighth + n, 0, rest, wide, [view]))
        return items

    def own_corner(row, half, side, column):
        return [(row, column + c, n, w, [(side, i * n, widths[0])]) for i, (c, w) in enumerate(half)]

    def spans(side):
        edges = np.cumsum((0, *third[side]))
        return [(int(a), int(b - a)) for a, b in zip(edges[:-1], edges[1:])]

    items = [(0, 0, n, wide_all, [(own_sides[0], 0, 0)]), (n, 0, n, wide_all, [(own_sides[1], 0, 0)])]
    items += own_corner(2 * n, spans(0), sides_first[1], 0) + own_corner(2 * n, spans(1), sides_first[0], cut_all)
    def side_sends(unit, high, sides):
        wide, half = widths[unit - 1], cuts[unit - 1]
        items = stack([whole_of(part) for part in high])[1]
        sends = []
        for width, view in ((wide - half, (sides[1], 0, half)), (half, (sides[0], 0, 0))):
            sends.append(((rest, widths[unit] + width), items + [(0, widths[unit], rest, width, [view])]))
        return [((rest, widths[unit]), items)] + sends

    own_mine, early, rest_in, *sends = build(
        ((3 * n, wide_all), items),
        early_rows(0, piece_first, rest_first, sides_first),
        *side_sends(1, high_in, sides_first),
    )
    sides_in = exchange_sides(sends)
    early_first = exchange_core(early)
    high_down = gather_high(piece_down)
    sides_in, early_first, high_down, own_mine = together((sides_in, early_first, high_down, own_mine))

    corner_first = [(part, FF) for part in sides_in]
    items = stack([whole_of(own_mine)])[1]
    items += [(row, wide_all + column, *more) for row, column, *more in corner_items(0, corner_first)]
    late, rest_down, *sends = build(
        ((rest, wide_all + widths[0]), items), *side_sends(2, high_down, sides_in)
    )
    sides_down = exchange_sides(sends)
    late = exchange_core(late)
    own = (own_mine, late)
    items = slots_of(0, piece_first, rest_first, sides_first, corner_first, early_first, (late, 0, wide_all))
    w_first = build(((D, widths[0]), items))[0]
    early, first_down = build(
        early_rows(1, piece_in, rest_in, sides_in), stack([whole_of(piece_down), whole_of(rest_down)])
    )
    early_in, first_down = exchange_core(early), exchange_core(first_down)
    vectors, bias_in, table = unpack(shards, turn, w_first)
    inputs_slots, joined, gate = joined_forward(inputs_low, turn, vectors, table, w_first)
    made = [attention(clip, bucket, valid_rows, table, joined, gate) for clip in range(clips)]
    mixed_slots, unit, unit_scale, first_slots = out_forward(inputs_low, turn, vectors, w_first, [m[2] for m in made])
    sides_down, early_in, first_down, unit = together((sides_down, early_in, first_down, unit))

    corner_in = [(part, FF) for part in sides_down]
    late, early, *sends = build(
        ((rest, FF), corner_items(1, corner_in)),
        stack([(side, 0, rest, 0, FF) for side in sides_down]),
        *corner_sends(2, sides_down),
    )
    corner_down = exchange_sides(sends)
    late = exchange_core(late)
    early_down = exchange_core(early)
    items = slots_of(1, piece_in, rest_in, sides_in, corner_in, early_in, (late, 0, 0))
    w_in = build(((D, FF), items))[0]
    active, slope = hidden_forward(first_slots, bias_in, w_in)
    turned = turn_active(at, wide_rows, active) if wide_rows % 16 == 0 else active
    corner_down, early_down, active, turned = together((corner_down, early_down, active, turned))

    corner_down = [(part, 0) for part in corner_down]
    corner = build(((rest, FF), corner_items(2, corner_down)))[0]
    late = exchange_core(corner)
    early_down = (first_down, 0), (early_down, 0)
    items = slots_of(2, piece_down, rest_down, sides_down, [(corner, cuts[2]), (corner, 0)], early_down, (late, 0, 0))
    arrays, places = [], [None] * shards
    for row, column, size, _, [(array, first, left)] in items:
        if column:
            continue
        which = next((i for i, known in enumerate(arrays) if known is array), len(arrays))
        if which == len(arrays):
            arrays.append(array)
        for step in range(size // n):
            places[row // n + step] = (which, first + step * n, n, left)
    cot = cotangent.reshape(rows, D)
    half_slots, last_slots = shards // 2, rest // n
    if wide_rows % 16:
        parts = [arrays[which][row : row + n, left : left + FF] for which, row, _, left in places]
        stacked = jnp.stack(parts).reshape(shards, n, FF // D, D).transpose(0, 2, 1, 3).reshape(shards, wide_rows, D)
        arrays, places = [jnp.take(stacked, back_order, axis=0).reshape(FF, D)], [(0, 0, FF, 0)]
        w_down, activations, grad_second, grad_made, sums_second = turn_back(
            jnp.zeros((1,), jnp.int32), places, active, unit, vectors, valid_rows, cot, arrays
        )
    else:
        first_late = shards - last_slots
        ahead = sorted({place[0] for place in places[:first_late]})
        slots_ahead = [(ahead.index(place[0]), *place[1:]) for place in places[:first_late]]
        slots_late = [(0, *place[1:]) for place in places[first_late:]]
        w_down, made_down = partial_down(at, slots_ahead, last_slots, active, [arrays[i] for i in ahead])
        w_down, made_down, late = together((w_down, made_down, late))
        ranges = ((half_slots - last_slots, half_slots), (first_late, shards))
        w_down, activations, grad_second, grad_made, sums_second, *lasts = last_turn(
            at, slots_late, first_late, made_down, unit, vectors, valid_rows, cot, turned, late, w_down, ranges, n
        )

    if wide_rows % 16:
        grad_down = tn(active, grad_made).astype(BF).reshape(shards, wide_rows, D)
        grad_down = jnp.take(grad_down, order, axis=0).reshape(shards, FF // D, n, D).transpose(0, 2, 1, 3)
        grad_down = grad_down.reshape(D, FF)
        at_last = D // 2 - rest
        down_main, down_last, other_main, other_last = (
            grad_down[:at_last], grad_down[at_last : D // 2], grad_down[D // 2 : D // 2 + at_last], grad_down[D // 2 + at_last :]
        )
    else:
        down_last, other_last, grad_made = together((*lasts, grad_made))

    eighth = D // 8

    def both(pair, row, column):
        views = []
        for array in pair:
            if isinstance(array, tuple):
                main, last = array
                at = D // 2 - rest
                views.append((last, row - at, column) if row >= at else (main, row, column))
            else:
                views.append((array, row, column))
        return views

    def corner_out(unit, pair):
        wide, half = widths[unit], cuts[unit]
        row = 3 * eighth + n
        return (
            (wide - half, [(0, 0, rest, wide - half, both(pair, row, half))]),
            (half, [(0, 0, rest, half, both(pair, row, 0))]),
        )

    def sides_out(unit, pair, corner):
        wide, half = widths[unit], cuts[unit]
        (second, left_second), (first, left_first) = corner
        near, side = eighth + n, 2 * eighth + n
        return (
            (
                wide,
                [
                    (0, 0, rest, half, both(pair, near, 0) + [(first, 0, left_first)]),
                    (0, half, rest, wide - half, both(pair, near, half)),
                ],
            ),
            (
                wide,
                [
                    (0, 0, rest, half, both(pair, side, 0)),
                    (0, half, rest, wide - half, both(pair, side, half) + [(second, 0, left_second)]),
                ],
            ),
        )

    def beside(one, two):
        return [
            ((rest, a[0] + b[0]), a[1] + [(item[0], a[0] + item[1], *item[2:]) for item in b[1]])
            for a, b in zip(one, two)
        ]

    def alone(one):
        return [((rest, wide), items) for wide, items in one]

    def column_views(unit, pair, sides, row):
        return both(pair, row, 0) + [(side, row - n, 0) for side in sides]

    def high_out(unit, pair, sides, first, count, *more):
        wide = widths[unit]
        views = column_views(unit, pair, sides, first * n)
        if more:
            views = views + [(more[0], n, 0)]
        return ((count * n, wide), [(0, 0, count * n, wide, views)])

    def scatter_high(unit, pair, sides):
        wide = widths[unit]
        total = build(((rest, wide), [(0, 0, rest, wide, column_views(unit, pair, sides, n))]))[0].astype(F32)
        total = jnp.concatenate([jnp.zeros((n, widths[unit]), F32), total], axis=0)
        for bit in reversed(bits):
            size = total.shape[0] // 2
            total = total[:size] + exchange(total[size:].astype(BF), "dp", 1 << bit).astype(F32)
        return [total]

    def scatter_far(unit, pair, sides):
        if not staged:
            return scatter_high(unit, pair, sides)
        return [exchange(build(high_out(unit, pair, sides, 2, 2))[0], "dp", 8)]

    other_last = exchange_core(other_last)
    if wide_rows % 16:
        grad_hidden, grad_bias_in = hidden_back(grad_made, w_down, slope)
        in_mine, in_other = in_back(first_slots, grad_hidden)
    else:
        other_main, grad_hidden, grad_bias_in, in_mine, in_other = inner_back(
            ((half_slots, shards - last_slots),), n, turned, grad_made, w_down, slope, first_slots
        )
    down_last, other_last, other_main, in_mine, in_other, grad_hidden, grad_made = together(
        (down_last, other_last, other_main, in_mine, in_other, grad_hidden, grad_made)
    )

    corner_down = exchange_sides(build(*alone(corner_out(2, ((None, down_last), (None, other_last))))))
    inner = (in_mine, exchange_core(in_other))
    other_main = exchange_core(other_main)
    if wide_rows % 16 == 0:
        down_main = down_back(((0, half_slots - last_slots),), n, turned, grad_made)[0]
    grad_first_sum, grad_out, grad_mixed, sums_first = out_back(
        grad_hidden, w_in, turn, grad_second, unit, unit_scale, vectors, mixed_slots, w_first
    )

    def clip_back(clip):
        prob, rel, _ = made[clip]
        return attention_back(clip, joined, gate, rank, prob, rel, grad_mixed)

    corner_down, inner, other_main, down_main, grad_mixed = together(
        (corner_down, inner, other_main, down_main, grad_mixed)
    )
    down = ((down_main, down_last), (other_main, other_last))

    corner_down = [(part, 0) for part in corner_down]
    sides_down = exchange_sides(build(*beside(sides_out(2, down, corner_down), corner_out(1, inner))))
    backs = [clip_back(clip) for clip in range(clips)]
    grads_joined = [back[0] for back in backs]
    grad_gate_inputs, table_grad, sums_attention = gate_back(
        inputs_low, table, gate, grads_joined, [back[1] for back in backs], [back[2] for back in backs]
    )
    grad_small = pack(shards, turn, sums_attention, sums_first, sums_second, grad_bias_in, table_grad)
    first_mine, first_other, grad_joined = first_back(inputs_slots, grad_out, grad_small, grads_joined)
    sides_down, first_mine, first_other, grad_joined = together((sides_down, first_mine, first_other, grad_joined))

    corner_in = [(part, FF) for part in sides_down]
    first = (first_mine, exchange_core(first_other))
    sides_in = exchange_sides(build(*alone(sides_out(1, inner, corner_in))))
    high_down = scatter_far(2, down, sides_down)
    corner_first = exchange_sides(build(*alone(corner_out(0, first))))
    input_grad = rows_back(grad_joined, w_first, turn, grad_first_sum, grad_gate_inputs)
    first, sides_in, high_down, corner_first, input_grad = together(
        (first, sides_in, high_down, corner_first, input_grad)
    )

    corner_first = [(part, 0) for part in corner_first]
    units = ((first, 0), (inner, 1), (down, 2))

    def own_views(row, column, columns):
        found = []
        for pair, unit in units:
            start, end = max(column, lefts[unit]), min(column + columns, lefts[unit] + widths[unit])
            if start < end:
                found.append((start - column, end - start, both(pair, row, start - lefts[unit])))
        return found

    def own_third(side):
        base = cut_all if side else 0
        items = []
        for i, (column, columns) in enumerate(spans(side)):
            for start, size, views in own_views(3 * eighth, base + column, columns):
                items.append((i * n, start, n, size, views))
        return (third[side][0], items)

    sides_first = exchange_sides(
        build(*beside(sides_out(0, first, corner_first), (own_third(1), own_third(0))))
    )
    high_in = scatter_far(1, inner, sides_in)
    if staged:
        high_down += [exchange(build(high_out(2, down, sides_down, 1, 1, high_down[0]))[0], "dp", 4)]
    weight_rows, momenta_rows, averages_rows = [flat_rows(part, n) for part in (weights, momenta, averages)]
    sides_first, high_in, high_down, weight_rows, momenta_rows, averages_rows = together(
        (sides_first, high_in, high_down, weight_rows, momenta_rows, averages_rows)
    )

    own_outs = []
    for side, row in ((0, eighth), (1, 2 * eighth)):
        items = []
        base = 0 if side == 0 else cut_all
        came = sides_first[1] if side == 0 else sides_first[0]
        edges = [(base + c, w, (came, i * n, widths[0])) for i, (c, w) in enumerate(spans(side))]
        edges.append((cut_all, wide_all - cut_all, None) if side == 0 else (0, cut_all, None))
        for column, columns, view in edges:
            for start, size, views in own_views(row, column, columns):
                if view is not None:
                    views = views + [(view[0], view[1], view[2] + start)]
                items.append((0, column + start, n, size, views))
        own_outs.append(((n, wide_all), items))
    own_sides = exchange_sides(build(*own_outs))
    if staged:
        near, far, farthest = [high_out(0, first, sides_first, d, 1) for d in (1, 2, 3)]
        near_in = high_out(1, inner, sides_in, 1, 1, high_in[0])
        wide = widths[0]
        near = ((n, wide + FF), near[1] + [(0, wide, n, FF, near_in[1][0][4])])
        high_first = [exchange(part, "dp", mask) for part, mask in zip(build(near, far, farthest), (4, 8, 12))]
        high_in += [high_first[0]]
    else:
        high_first = scatter_high(0, first, sides_first)
    comes = (
        [(part, 0) for part in high_first],
        [(part, widths[0] if i else 0) for i, part in enumerate(high_in)],
        [(part, 0) for part in high_down],
    )
    sums = []
    for pair, unit in units:
        views = both(pair, 0, 0) + [(side, 0, lefts[unit]) for side in own_sides]
        sums.append(views + [(part, 0, left) for part, left in comes[unit]])

    learning = rate_scale / math.sqrt(total_tokens)
    arguments = (weight_rows, momenta_rows, averages_rows, weights.shape[1])
    known = update(learning, (2,), sums, *arguments)
    if staged:
        known, high_first[0] = together((known, high_first[0]))
        sums[1][-1] = (high_first[0], 0, widths[0])
    known = update(learning, (1,), sums, *arguments, known)
    if staged:
        known, high_first = together((known, high_first))
        sums[0][-3:] = [(part, 0, 0) for part in high_first]
    momenta_new, averages_new, weights_new, weights_copy = update(learning, (0,), sums, *arguments, known)
    return (
        activations.reshape(acts.shape),
        input_grad.reshape(acts.shape),
        momenta_new,
        averages_new,
        weights_new,
        weights_copy,
    )


def solution(mesh):
    split = ("dp", "fsdp")
    in_specs = (
        P(split, None, None),
        P(split, None, None),
        P(split, None),
        P(split),
        P(split, None),
        P(split, None),
        P(split, None),
    )
    out_specs = (
        P(split, None, None),
        P(split, None, None),
        P(split, None),
        P(split, None),
        P(split, None),
        P(split, None),
    )
    return jax.shard_map(body, mesh=mesh, in_specs=in_specs, out_specs=out_specs, check_vma=False)
```
